32 devices in a mesh: groups: 2 (over y), sec: 4 (over z), strip: 4 (over x, core).
Axes of the slice: x: 2, y: 2, z: 4, core: 2. Of those that a mesh axis runs over, the one named last changes fastest.
Arguments:
- sections: bfloat16 [4, 256, 1024], P('sec', 'strip', 'groups'), parts along dimension 2, may hold values from -40 to 40
- mask_fine: int32 [4, 8, 32], P('sec', 'strip', 'groups'), parts along dimension 2, may hold values 0 or 1
- mask_coarse: int32 [4, 4, 16], P('sec', 'strip', 'groups'), parts along dimension 2, may hold values 0 or 1
Outputs:
- corr_fine: float32 [4, 2, 8, 32, 1024], P('sec', None, 'strip', 'groups'), parts along dimension 3
- corr_coarse: float32 [4, 2, 4, 16, 1024], P('sec', None, 'strip', 'groups'), parts along dimension 3
The draws below stay inside these ranges and needn't reach their ends.
There are 2 independent parts, one for each index of `groups`. The reference program is written for one: setup_inputs(seed, part) draws one part's arguments, and reference() takes and returns one part's arrays. A program takes and returns all parts, laid end to end along the dimension named above; each array names one. Nothing has to cross between parts.
All inputs are finite; a program needn't handle non-finite values. No bound on the sum of `mask_fine` or of `mask_coarse` on one device may be relied on, other than what follows from the above.
Results may differ from the reference program's by a relative error of at most 0.0039.
Values may be sent and summed in bfloat16 or wider, within the bound.
No kernel may reach another device: no remote copies, remote signals or barrier semaphores. Data moves between devices by JAX's collectives and lax.ppermute only.
A program may use at most 64 MiB of HBM per device.

```python
import jax
import jax.numpy as jnp
from jax import lax

PATCH = 64
STRIDE = 32
WINDOW = 32
WIDTH = 512
NZ = 4
H = 256


def draw_sections(key, part):
    key_noise, key_rows, key_cols = jax.random.split(key, 3)
    row_scale = jnp.exp(jax.random.uniform(key_rows, (NZ, H, 1), jnp.float32, 0.0, jnp.log(10.0)))
    col_scale = jnp.exp(jax.random.uniform(key_cols, (NZ, 1, WIDTH), jnp.float32, 0.0, jnp.log(10.0)))
    scaling = jnp.sqrt(row_scale * col_scale)
    section_image = jax.random.normal(key_noise, (NZ, H, WIDTH), jnp.float32) * scaling
    return jnp.clip(section_image, -40.0, 40.0).astype(jnp.bfloat16)


def set_ends(drawn, rng, low, top_value):
    index_at = [jax.random.randint(jax.random.fold_in(rng, axis), (), 0, length) for axis, length in enumerate(drawn.shape)]
    main_axis = drawn.shape.index(max(drawn.shape))
    beside = index_at[:main_axis] + [(index_at[main_axis] + 1) % drawn.shape[main_axis]] + index_at[main_axis + 1:]
    return drawn.at[tuple(index_at)].set(low).at[tuple(beside)].set(top_value)


def setup_inputs(seed: int = 0, part: int = 0) -> dict:
    splits = jax.random.split(jax.random.key(seed), 4)
    part_keys = jax.random.split(jax.random.fold_in(splits[3], part), 4)
    return {
        "sections": draw_sections(jax.random.fold_in(jax.random.fold_in(splits[3], part), 71), part),
        "mask_fine": set_ends((jax.random.randint(part_keys[1], (NZ, H // STRIDE, WIDTH // STRIDE), 0, 4) < 3).astype(jnp.int32), jax.random.fold_in(part_keys[1], 1), 0, 1),
        "mask_coarse": set_ends((jax.random.randint(part_keys[2], (NZ, H // (2 * STRIDE), WIDTH // (2 * STRIDE)), 0, 4) < 3).astype(jnp.int32), jax.random.fold_in(part_keys[2], 1), 0, 1),
    }


def make_patches(section_image, patch_rows, patch_cols):
    blocks = section_image.reshape(patch_rows + 1, STRIDE, patch_cols + 1, STRIDE)
    tall_blocks = jnp.concatenate([blocks[:-1], blocks[1:]], axis=1)
    wide_blocks = jnp.concatenate([tall_blocks[:, :, :-1], tall_blocks[:, :, 1:]], axis=3)
    return wide_blocks.transpose(1, 3, 0, 2).reshape(PATCH, PATCH, patch_rows * patch_cols)

def level_patches(extended):
    strip_rows = extended.shape[0] - PATCH
    section_width = extended.shape[1]
    fine_img = jnp.pad(extended[:strip_rows + STRIDE], ((0, 0), (0, STRIDE)))
    pooled = extended.reshape(extended.shape[0] // 2, 2, section_width // 2, 2).mean(axis=(1, 3))
    coarse_img = jnp.pad(pooled, ((0, 0), (0, STRIDE)))
    fine_patches = make_patches(fine_img, strip_rows // STRIDE, section_width // STRIDE)
    coarse_patches = make_patches(coarse_img, strip_rows // (2 * STRIDE), section_width // (2 * STRIDE))
    return jnp.concatenate([fine_patches, coarse_patches], axis=2)

def section_spectra(section_image):
    extended = jnp.pad(section_image.astype(jnp.float32), ((0, PATCH), (0, 0)))
    patches = level_patches(extended)
    centered = patches - lax.optimization_barrier(jnp.mean(patches, axis=(0, 1)))
    unit_patch = centered / jnp.sqrt(lax.optimization_barrier(jnp.mean(centered * centered, axis=(0, 1))) + 1e-05)
    spectrum = jnp.fft.fft2(unit_patch, axes=(0, 1))
    return jnp.stack([spectrum.real, spectrum.imag]).astype(jnp.bfloat16)

def window_correlation(own_spec, other_spec):
    own_spec = own_spec.astype(jnp.float32)
    other_spec = other_spec.astype(jnp.float32)
    cross_real = own_spec[0] * other_spec[0] + own_spec[1] * other_spec[1]
    cross_imag = own_spec[0] * other_spec[1] - own_spec[1] * other_spec[0]
    cross_spec = cross_real + 1j * cross_imag
    full_map = jnp.fft.ifft2(cross_spec, axes=(0, 1)).real
    shift_index = ((jnp.arange(WINDOW) - WINDOW // 2) % PATCH).astype(jnp.int32)
    picked = jnp.take(jnp.take(full_map, shift_index, axis=0), shift_index, axis=1)
    return picked / PATCH

def reference(sections, mask_fine, mask_coarse):
    spectra_all = lax.map(section_spectra, sections)
    zero_sections = jnp.zeros((2,) + spectra_all.shape[1:], spectra_all.dtype)
    padded = jnp.concatenate([spectra_all, zero_sections], axis=0)
    fine_rows = H // STRIDE
    fine_cols = WIDTH // STRIDE
    coarse_rows = H // (2 * STRIDE)
    coarse_cols = WIDTH // (2 * STRIDE)
    fine_count = fine_rows * fine_cols

    def one_section(section_items):
        own_spec, first_spec, second_spec, fine_mask, coarse_mask = section_items
        corr_maps = jnp.stack([window_correlation(own_spec, first_spec), window_correlation(own_spec, second_spec)])
        flat_maps = corr_maps.reshape(2, WINDOW * WINDOW, -1)
        fine_out = flat_maps[:, :, :fine_count].reshape(2, WINDOW * WINDOW, fine_rows, fine_cols).transpose(0, 2, 3, 1)
        coarse_out = flat_maps[:, :, fine_count:].reshape(2, WINDOW * WINDOW, coarse_rows, coarse_cols).transpose(0, 2, 3, 1)
        fine_out = fine_out * fine_mask.astype(jnp.float32)[None, :, :, None]
        coarse_out = coarse_out * coarse_mask.astype(jnp.float32)[None, :, :, None]
        return (fine_out, coarse_out)
    corr_fine, corr_coarse = lax.map(one_section, (padded[:NZ], padded[1:NZ + 1], padded[2:NZ + 2], mask_fine, mask_coarse))
    return (corr_fine, corr_coarse)
```

```python
import functools

import jax
import jax.numpy as jnp
import numpy as np
from jax import lax
from jax.experimental import pallas as pl
from jax.experimental.pallas import tpu as pltpu
from jax.sharding import PartitionSpec as P

PATCH = 64
STRIDE = 32
WINDOW = 32
HALF = PATCH // 2
LANES = 128
NYQ = 16

f32 = jnp.float32
bf16 = jnp.bfloat16


def shifted(value, axis, steps):
    count = lax.axis_size(axis)
    leading, last = (max(0, -steps), min(count, count - steps))
    return lax.ppermute(value, axis, [(source, source + steps) for source in range(leading, last)])


def wave(phase):
    turns = np.arange(PATCH) * (2 * np.pi / PATCH)
    cos = np.round(np.cos(turns), 14)
    sin = np.round(np.sin(turns), 14)
    phase = np.mod(phase, PATCH)
    return cos[phase], sin[phase]


def split_table(table):
    high = table.astype(jnp.bfloat16)
    low = (table - high.astype(np.float64)).astype(jnp.bfloat16)
    return high, low


def row_table(strip_rows):
    ext = strip_rows + PATCH
    fine, coarse = strip_rows // STRIDE, strip_rows // (2 * STRIDE)
    k = np.arange(HALF)[:, None]
    cos_rows, sin_rows, nyquist = [], [], np.zeros((NYQ, ext))
    for block in range(fine + coarse):
        cos = np.zeros((HALF, ext))
        sin = np.zeros((HALF, ext))
        if block < fine:
            x, first, scale = np.arange(PATCH), block * STRIDE, 1.0
        else:
            x, first, scale = np.arange(2 * PATCH) // 2, (block - fine) * 2 * STRIDE, 0.5
        c, s = wave(k * x[None, :])
        cos[:, first : first + x.size] = c * scale
        sin[:, first : first + x.size] = s * scale
        nyquist[block, first : first + x.size] = wave(HALF * x)[0] * scale
        cos_rows.append(cos)
        sin_rows.append(sin)
    table = np.concatenate(
        cos_rows[:fine] + [nyquist] + cos_rows[fine:] + sin_rows[:fine] + [np.zeros((NYQ, ext))] + sin_rows[fine:]
    )
    high, low = split_table(table)
    return np.concatenate([high, low], axis=1)


def stacked(table):
    high, low = split_table(table)
    return np.concatenate([high, high, low], axis=0)


def fine_table():
    c, s = wave(np.arange(PATCH)[:, None] * np.arange(PATCH)[None, :])
    table = np.zeros((2, 2, PATCH, 2, 2, PATCH))
    for p in range(2):
        table[0, p, :, 0, p] = c
        table[1, p, :, 0, p] = -s
        table[0, p, :, 1, p] = -s
        table[1, p, :, 1, p] = -c
    return stacked(table.reshape(4 * PATCH, 4 * PATCH))


def coarse_table():
    c, s = wave((np.arange(2 * PATCH) // 2)[:, None] * np.arange(PATCH)[None, :])
    table = np.zeros((2, 2, 2 * PATCH, 2, 2, PATCH))
    for p in range(2):
        table[p, 0, :, 0, p] = 0.5 * c
        table[p, 1, :, 0, p] = -0.5 * s
        table[p, 0, :, 1, p] = -0.5 * s
        table[p, 1, :, 1, p] = -0.5 * c
    return stacked(table.reshape(8 * PATCH, 4 * PATCH))


def shift_table():
    t = np.arange(WINDOW) - WINDOW // 2
    c, s = wave(np.arange(PATCH)[:, None] * t[None, :])
    table = np.zeros((2, 2, 2, PATCH, 2, 4, WINDOW))
    for odd in range(2):
        for p in range(2):
            table[odd, 0, p, :, 0, 2 * p + odd] = c
            table[odd, 1, p, :, 0, 2 * p + odd] = -s
            table[odd, 0, p, :, 1, 2 * p + odd] = s
            table[odd, 1, p, :, 1, 2 * p + odd] = c
    return stacked(table.reshape(8 * PATCH, 8 * WINDOW))


def map_table(blocks):
    shift = np.arange(WINDOW) - WINDOW // 2
    c, s = wave(shift[:, None] * np.arange(HALF)[None, :])
    weight = np.where(np.arange(HALF) == 0, 1.0, 2.0) / PATCH**3
    rows = []
    for block in range(blocks):
        nyquist = np.zeros((WINDOW, NYQ))
        nyquist[:, block] = wave(HALF * shift)[0] / PATCH**3
        high, low = split_table(np.concatenate([c * weight, -s * weight, nyquist], axis=1))
        top = np.concatenate([high, high], axis=1)
        bottom = np.concatenate([low, np.zeros_like(low)], axis=1)
        rows.append(np.concatenate([top, bottom], axis=0))
    return np.stack(rows)


def split(value):
    high = value.astype(bf16)
    return high, (value - high.astype(f32)).astype(bf16)


def dot(left, right):
    return jnp.dot(left, right, preferred_element_type=f32)


def dot3(value, table_ref):
    high, low = split(value)
    return dot(jnp.concatenate([high, low, high], axis=1), table_ref[...])


def kernel(
    fine, coarse, quads_fine, quads_coarse,
    own, rim, near, rim_near, far, rim_far, mask_ref,
    row_ref, fine_ref, coarse_ref, shift_ref, map_ref,
    out_fine, out_coarse,
    t_ref, spec_fine, spec_coarse, maps_ref,
):
    width = own.shape[1]
    fine_rows = fine * HALF
    fine_all = fine_rows + NYQ
    coarse_rows = coarse * HALF
    half_rows = fine_all + coarse_rows
    sub = lax.broadcasted_iota(jnp.int32, (8, LANES), 0)
    lane = lax.broadcasted_iota(jnp.int32, (8, LANES), 1)
    dc = (sub == 0) & (lane % PATCH == 0)
    group = lax.broadcasted_iota(jnp.int32, (LANES, LANES), 0) // PATCH
    same = group == lax.broadcasted_iota(jnp.int32, (LANES, LANES), 1) // PATCH
    ones = jnp.where(same, 1.0, 0.0).astype(bf16)
    ones = jnp.concatenate([ones, ones], axis=0)

    for z, (top, bottom) in enumerate(((own, rim), (near, rim_near), (far, rim_far))):
        x = jnp.concatenate([top[...], bottom[...]], axis=0)
        t = dot(row_ref[...], jnp.concatenate([x, x], axis=0))
        t_ref[z, :, :width] = t
        t_ref[z, :, width:] = jnp.zeros((2 * half_rows, LANES), f32)

    def power(values, first, nyquist_row):
        re, im = values[:, :LANES], values[:, LANES:]
        q = re * re + im * im
        total = None
        for r in range(0, HALF, 8):
            part = q[first + r : first + r + 8]
            if r == 0:
                part = jnp.where(dc, 0.0, part)
                head = jnp.where(sub == 0, part, 0.0)
            total = part if total is None else total + part
        tail = q[nyquist_row[0] : nyquist_row[0] + 8]
        return 2.0 * total - head + jnp.where(sub == nyquist_row[1], tail, 0.0)

    def normalise(spec_ref, z, tiles, blocks, block_first, nyquist_first, first_block, first_mask):
        rows = len(blocks)
        sums = []
        for tile in range(tiles):
            values = spec_ref[z, tile]
            for b in range(rows):
                sums.append(power(values, block_first + b * HALF, (nyquist_first, first_block + b)))
        stack = jnp.concatenate(sums, axis=0)
        high, low = split(stack)
        stack = dot(jnp.concatenate([high, low], axis=1), ones)
        for tile in range(tiles):
            values = spec_ref[z, tile]
            scales = []
            for b in range(rows):
                at = (tile * rows + b) * 8
                total = jnp.sum(stack[at : at + 8], axis=0, keepdims=True)
                scale = 1.0 / jnp.sqrt(total * (1.0 / PATCH**4) + 1e-05)
                if z == 0:
                    m = first_mask + tile * rows + b
                    scale = scale * mask_ref[m : m + 1, :]
                scales.append(jnp.concatenate([scale, scale], axis=1))
            parts = {}
            for b in range(rows):
                first = block_first + b * HALF
                block = values[first : first + HALF]
                head = jnp.where(jnp.concatenate([dc, dc], axis=1), 0.0, block[:8])
                block = jnp.concatenate([head, block[8:]], axis=0)
                parts[first] = block * scales[b]
            nyq = values[nyquist_first : nyquist_first + NYQ]
            row = lax.broadcasted_iota(jnp.int32, (NYQ, 2 * LANES), 0)
            scaled = jnp.zeros_like(nyq)
            for b in range(rows):
                scaled = jnp.where(row == first_block + b, nyq * scales[b], scaled)
            parts[nyquist_first] = scaled
            result = jnp.concatenate([parts[first] for first in sorted(parts)], axis=0)
            spec_ref[z, tile] = result.astype(bf16).astype(f32)

    for z in range(3):
        for m in range(quads_fine):
            for odd in range(2):
                at = LANES * m + STRIDE * odd
                value = jnp.concatenate(
                    [t_ref[z, :fine_all, at : at + LANES],
                     t_ref[z, half_rows : half_rows + fine_all, at : at + LANES]], axis=1)
                spec_fine[z, 2 * m + odd] = dot3(value, fine_ref)
        for n in range(quads_coarse):
            for odd in range(2):
                pieces = []
                for p in range(2):
                    at = 2 * LANES * n + LANES * p + 2 * STRIDE * odd
                    pieces += [t_ref[z, fine_rows:half_rows, at : at + LANES],
                               t_ref[z, half_rows + fine_rows : 2 * half_rows, at : at + LANES]]
                spec_coarse[z, 2 * n + odd] = dot3(jnp.concatenate(pieces, axis=1), coarse_ref)
        normalise(spec_fine, z, 2 * quads_fine, range(fine), 0, fine_rows, 0, 0)
        normalise(spec_coarse, z, 2 * quads_coarse, range(coarse), NYQ, 0, fine, 2 * quads_fine * fine)

    def cross(spec_ref, d, tile):
        a, b = spec_ref[0, tile], spec_ref[d, tile]
        ar, ai, br, bi = a[:, :LANES], a[:, LANES:], b[:, :LANES], b[:, LANES:]
        return [ar * br + ai * bi, ar * bi - ai * br]

    def tile_index(d, level, b, quad):
        index = (b * 2 + d) * quads_fine + quad
        if level:
            index = 2 * fine * quads_fine + (b * 2 + d) * quads_coarse + quad
        return index

    for level, (spec_ref, quads, blocks, first, nyquist, first_block) in enumerate((
        (spec_fine, quads_fine, fine, 0, fine_rows, 0),
        (spec_coarse, quads_coarse, coarse, NYQ, 0, fine),
    )):
        columns = [[] for _ in range(blocks)]
        for d in range(2):
            for quad in range(quads):
                value = jnp.concatenate(
                    cross(spec_ref, d + 1, 2 * quad) + cross(spec_ref, d + 1, 2 * quad + 1), axis=1)
                y = dot3(value, shift_ref)
                for b in range(blocks):
                    at = first + b * HALF
                    stack = jnp.concatenate(
                        [y[at : at + HALF, :LANES], y[at : at + HALF, LANES:],
                         y[nyquist : nyquist + NYQ, :LANES]], axis=0)
                    high, low = split(stack)
                    columns[b].append(jnp.concatenate([high, low], axis=0))
        for b in range(blocks):
            both = dot(map_ref[first_block + b], jnp.concatenate(columns[b], axis=1))
            maps = both[:WINDOW] + both[WINDOW:]
            for d in range(2):
                for quad in range(quads):
                    at = (d * quads + quad) * LANES
                    maps_ref[tile_index(d, level, b, quad)] = maps[:, at : at + LANES]

    lanes = lax.broadcasted_iota(jnp.int32, (maps_ref.shape[0], LANES), 1) // WINDOW
    for big in range(WINDOW // 4):
        rows = [maps_ref[:, 4 * big + r, :] for r in range(4)]
        for g in range(4):
            value = None
            for r in range(4):
                moved = rows[r] if r == g else pltpu.roll(rows[r], (WINDOW * (r - g)) % LANES, 1)
                value = moved if value is None else jnp.where(lanes == r, moved, value)
            at = big * LANES
            for level, (out, quads, blocks) in enumerate((
                (out_fine, quads_fine, fine), (out_coarse, quads_coarse, coarse))):
                for d in range(2):
                    for b in range(blocks):
                        start = tile_index(d, level, b, 0)
                        for quad in range(quads):
                            row = 4 * quad + g
                            out[0, d, b, row : row + 1, at : at + LANES] = value[start + quad : start + quad + 1]


def correlate(own, rim, near, rim_near, far, rim_far, masks, fine, coarse):
    strip_rows, width = own.shape
    quads_fine = width // STRIDE // 4
    quads_coarse = width // (2 * STRIDE) // 4
    tables = (row_table(strip_rows), fine_table(), coarse_table(), shift_table(), map_table(fine + coarse))
    half_rows = (fine + coarse) * HALF + NYQ
    whole = pl.BlockSpec(memory_space=pltpu.VMEM)
    return pl.pallas_call(
        functools.partial(kernel, fine, coarse, quads_fine, quads_coarse),
        out_shape=(
            jax.ShapeDtypeStruct((1, 2, fine, 4 * quads_fine, WINDOW * WINDOW), f32),
            jax.ShapeDtypeStruct((1, 2, coarse, 4 * quads_coarse, WINDOW * WINDOW), f32),
        ),
        in_specs=[whole] * (7 + len(tables)),
        out_specs=(whole, whole),
        scratch_shapes=[
            pltpu.VMEM((3, 2 * half_rows, width + LANES), f32),
            pltpu.VMEM((3, 2 * quads_fine, fine * HALF + NYQ, 2 * LANES), f32),
            pltpu.VMEM((3, 2 * quads_coarse, coarse * HALF + NYQ, 2 * LANES), f32),
            pltpu.VMEM((2 * (fine * quads_fine + coarse * quads_coarse), WINDOW, LANES), f32),
        ],
        compiler_params=pltpu.CompilerParams(vmem_limit_bytes=32 * 1024 * 1024),
    )(own, rim, near, rim_near, far, rim_far, masks, *(jnp.asarray(table) for table in tables))


def mask_rows(mask):
    blocks, patches = mask.shape
    quads = patches // 4
    tiles = mask.astype(f32).reshape(blocks, quads, 2, 2).transpose(1, 3, 0, 2)
    return jnp.repeat(tiles.reshape(2 * quads * blocks, 2), PATCH, axis=1)


def local(sections, mask_fine, mask_coarse):
    rim = shifted(sections, "strip", -1)
    near = shifted(sections, "sec", -1)
    far = shifted(sections, "sec", -2)
    rim_near = shifted(near, "strip", -1)
    rim_far = shifted(far, "strip", -1)
    masks = jnp.concatenate([mask_rows(mask_fine[0]), mask_rows(mask_coarse[0])], axis=0)
    return correlate(
        sections[0], rim[0], near[0], rim_near[0], far[0], rim_far[0], masks,
        mask_fine.shape[1], mask_coarse.shape[1])


def solution(mesh):
    in_specs = (
        P("sec", "strip", "groups"),
        P("sec", "strip", "groups"),
        P("sec", "strip", "groups"),
    )
    out_specs = (P("sec", None, "strip", "groups", None), P("sec", None, "strip", "groups", None))
    return jax.shard_map(local, mesh=mesh, in_specs=in_specs, out_specs=out_specs, check_vma=False)
```

```python
import functools

import jax
import jax.numpy as jnp
import numpy as np
from jax import lax
from jax.experimental import pallas as pl
from jax.experimental.pallas import tpu as pltpu
from jax.sharding import PartitionSpec as P

PATCH = 64
STRIDE = 32
WINDOW = 32
HALF = PATCH // 2
LANES = 128
NYQ = 16

f32 = jnp.float32
bf16 = jnp.bfloat16


def shifted(value, axis, steps):
    count = lax.axis_size(axis)
    leading, last = (max(0, -steps), min(count, count - steps))
    return lax.ppermute(value, axis, [(source, source + steps) for source in range(leading, last)])


def wave(phase):
    turns = np.arange(PATCH) * (2 * np.pi / PATCH)
    cos = np.round(np.cos(turns), 14)
    sin = np.round(np.sin(turns), 14)
    phase = np.mod(phase, PATCH)
    return cos[phase], sin[phase]


def split_table(table):
    high = table.astype(jnp.bfloat16)
    low = (table - high.astype(np.float64)).astype(jnp.bfloat16)
    return high, low


def row_table(strip_rows):
    ext = strip_rows + PATCH
    fine, coarse = strip_rows // STRIDE, strip_rows // (2 * STRIDE)
    k = np.arange(HALF)[:, None]
    cos_rows, sin_rows, nyquist = [], [], np.zeros((NYQ, ext))
    for block in range(fine + coarse):
        cos = np.zeros((HALF, ext))
        sin = np.zeros((HALF, ext))
        if block < fine:
            x, first, scale = np.arange(PATCH), block * STRIDE, 1.0
        else:
            x, first, scale = np.arange(2 * PATCH) // 2, (block - fine) * 2 * STRIDE, 0.5
        c, s = wave(k * x[None, :])
        cos[:, first : first + x.size] = c * scale
        sin[:, first : first + x.size] = s * scale
        nyquist[block, first : first + x.size] = wave(HALF * x)[0] * scale
        cos_rows.append(cos)
        sin_rows.append(sin)
    table = np.concatenate(
        cos_rows[:fine] + [nyquist] + cos_rows[fine:] + sin_rows[:fine] + [np.zeros((NYQ, ext))] + sin_rows[fine:]
    )
    high, low = split_table(table)
    return np.concatenate([high, low], axis=1)


def stacked(table):
    return np.concatenate(split_table(table), axis=0)


def fine_table():
    c, s = wave(np.arange(PATCH)[:, None] * np.arange(PATCH)[None, :])
    table = np.zeros((2, 2, PATCH, 2, 2, PATCH))
    for p in range(2):
        table[0, p, :, 0, p] = c
        table[1, p, :, 0, p] = -s
        table[0, p, :, 1, p] = -s
        table[1, p, :, 1, p] = -c
    return stacked(table.reshape(4 * PATCH, 4 * PATCH))


def coarse_table():
    c, s = wave((np.arange(2 * PATCH) // 2)[:, None] * np.arange(PATCH)[None, :])
    table = np.zeros((2, 2, 2 * PATCH, 2, 2, PATCH))
    for p in range(2):
        table[p, 0, :, 0, p] = 0.5 * c
        table[p, 1, :, 0, p] = -0.5 * s
        table[p, 0, :, 1, p] = -0.5 * s
        table[p, 1, :, 1, p] = -0.5 * c
    return stacked(table.reshape(8 * PATCH, 4 * PATCH))


def shift_table():
    t = np.arange(WINDOW) - WINDOW // 2
    c, s = wave(np.arange(PATCH)[:, None] * t[None, :])
    table = np.zeros((2, 2, 2, PATCH, 2, 4, WINDOW))
    for odd in range(2):
        for p in range(2):
            table[odd, 0, p, :, 0, 2 * p + odd] = c
            table[odd, 1, p, :, 0, 2 * p + odd] = -s
            table[odd, 0, p, :, 1, 2 * p + odd] = s
            table[odd, 1, p, :, 1, 2 * p + odd] = c
    return stacked(table.reshape(8 * PATCH, 8 * WINDOW))


def map_table(blocks):
    shift = np.arange(WINDOW) - WINDOW // 2
    c, s = wave(shift[:, None] * np.arange(HALF)[None, :])
    weight = np.where(np.arange(HALF) == 0, 1.0, 2.0) / PATCH**3
    rows = []
    for block in range(blocks):
        nyquist = np.zeros((WINDOW, NYQ))
        nyquist[:, block] = wave(HALF * shift)[0] / PATCH**3
        high, low = split_table(np.concatenate([c * weight, -s * weight, nyquist], axis=1))
        top = np.concatenate([high, high], axis=1)
        bottom = np.concatenate([low, np.zeros_like(low)], axis=1)
        rows += [top, bottom]
    return np.concatenate(rows)


def all_tables(strip_rows, blocks):
    tables = [row_table(strip_rows), fine_table(), coarse_table(), shift_table(), map_table(blocks)]
    width = max(table.shape[1] for table in tables)
    places = np.cumsum([0] + [table.shape[0] for table in tables])[:-1]
    padded = [np.pad(table, ((0, 0), (0, width - table.shape[1]))) for table in tables]
    return np.concatenate(padded), tuple(int(place) for place in places)


def split(value):
    high = value.astype(bf16)
    return high, (value - high.astype(f32)).astype(bf16)


def dot(left, right):
    return jnp.dot(left, right, preferred_element_type=f32)


def dot3(value, table_ref, at):
    high, low = split(value)
    depth = value.shape[1]
    table_high = table_ref[at : at + depth]
    table_low = table_ref[at + depth : at + 2 * depth]
    return dot(
        jnp.concatenate([high, low, high], axis=1),
        jnp.concatenate([table_high, table_high, table_low], axis=0))


def kernel(
    fine, coarse, quads_fine, quads_coarse, places,
    strips, rims, mask_fine, mask_coarse, table_ref,
    out_fine, out_coarse,
    t_ref, spec_fine, spec_coarse, maps_ref, rows_ref,
):
    width = strips.shape[2]
    row_at, fine_at, coarse_at, shift_at, map_at = places
    fine_rows = fine * HALF
    fine_all = fine_rows + NYQ
    coarse_rows = coarse * HALF
    half_rows = fine_all + coarse_rows
    sub = lax.broadcasted_iota(jnp.int32, (8, LANES), 0)
    lane = lax.broadcasted_iota(jnp.int32, (8, LANES), 1)
    dc = (sub == 0) & (lane % PATCH == 0)
    group = lax.broadcasted_iota(jnp.int32, (LANES, LANES), 0) // PATCH
    same = group == lax.broadcasted_iota(jnp.int32, (LANES, LANES), 1) // PATCH
    ones = jnp.where(same, 1.0, 0.0).astype(bf16)
    ones = jnp.concatenate([ones, ones], axis=0)

    for z in range(3):
        x = jnp.concatenate([strips[z], rims[z]], axis=0)
        t = dot(table_ref[row_at : row_at + 2 * half_rows], jnp.concatenate([x, x], axis=0))
        t_ref[z, :, :width] = t
        t_ref[z, :, width:] = jnp.zeros((2 * half_rows, LANES), f32)

    def power(values, first, nyquist_row):
        re, im = values[:, :LANES], values[:, LANES:]
        q = re * re + im * im
        total = None
        for r in range(0, HALF, 8):
            part = q[first + r : first + r + 8]
            if r == 0:
                part = jnp.where(dc, 0.0, part)
                head = jnp.where(sub == 0, part, 0.0)
            total = part if total is None else total + part
        tail = q[nyquist_row[0] : nyquist_row[0] + 8]
        return 2.0 * total - head + jnp.where(sub == nyquist_row[1], tail, 0.0)

    def normalise(spec_ref, z, tiles, blocks, block_first, nyquist_first, first_block, mask_ref):
        rows = len(blocks)
        sums = []
        for tile in range(tiles):
            values = spec_ref[z, tile]
            for b in range(rows):
                sums.append(power(values, block_first + b * HALF, (nyquist_first, first_block + b)))
        stack = jnp.concatenate(sums, axis=0)
        high, low = split(stack)
        stack = dot(jnp.concatenate([high, low], axis=1), ones)
        for tile in range(tiles):
            values = spec_ref[z, tile]
            scales = []
            for b in range(rows):
                at = (tile * rows + b) * 8
                total = jnp.sum(stack[at : at + 8], axis=0, keepdims=True)
                scale = 1.0 / jnp.sqrt(total * (1.0 / PATCH**4) + 1e-05)
                if z == 0:
                    patch = 4 * (tile // 2) + tile % 2
                    kept = jnp.where(lane[:1] < PATCH, mask_ref[0, b, patch], mask_ref[0, b, patch + 2])
                    scale = scale * kept.astype(f32)
                scales.append(jnp.concatenate([scale, scale], axis=1))
            parts = {}
            for b in range(rows):
                first = block_first + b * HALF
                block = values[first : first + HALF]
                head = jnp.where(jnp.concatenate([dc, dc], axis=1), 0.0, block[:8])
                block = jnp.concatenate([head, block[8:]], axis=0)
                parts[first] = block * scales[b]
            nyq = values[nyquist_first : nyquist_first + NYQ]
            row = lax.broadcasted_iota(jnp.int32, (NYQ, 2 * LANES), 0)
            scaled = jnp.zeros_like(nyq)
            for b in range(rows):
                scaled = jnp.where(row == first_block + b, nyq * scales[b], scaled)
            parts[nyquist_first] = scaled
            result = jnp.concatenate([parts[first] for first in sorted(parts)], axis=0)
            spec_ref[z, tile] = result.astype(bf16).astype(f32)

    for z in range(3):
        for m in range(quads_fine):
            for odd in range(2):
                at = LANES * m + STRIDE * odd
                value = jnp.concatenate(
                    [t_ref[z, :fine_all, at : at + LANES],
                     t_ref[z, half_rows : half_rows + fine_all, at : at + LANES]], axis=1)
                spec_fine[z, 2 * m + odd] = dot3(value, table_ref, fine_at)
        for n in range(quads_coarse):
            for odd in range(2):
                pieces = []
                for p in range(2):
                    at = 2 * LANES * n + LANES * p + 2 * STRIDE * odd
                    pieces += [t_ref[z, fine_rows:half_rows, at : at + LANES],
                               t_ref[z, half_rows + fine_rows : 2 * half_rows, at : at + LANES]]
                spec_coarse[z, 2 * n + odd] = dot3(jnp.concatenate(pieces, axis=1), table_ref, coarse_at)
        normalise(spec_fine, z, 2 * quads_fine, range(fine), 0, fine_rows, 0, mask_fine)
        normalise(spec_coarse, z, 2 * quads_coarse, range(coarse), NYQ, 0, fine, mask_coarse)

    def cross(spec_ref, d, tile):
        a, b = spec_ref[0, tile], spec_ref[d, tile]
        ar, ai, br, bi = a[:, :LANES], a[:, LANES:], b[:, :LANES], b[:, LANES:]
        return [ar * br + ai * bi, ar * bi - ai * br]

    def tile_index(d, level, b, quad):
        index = (b * 2 + d) * quads_fine + quad
        if level:
            index = 2 * fine * quads_fine + (b * 2 + d) * quads_coarse + quad
        return index

    for level, (spec_ref, quads, blocks, first, nyquist, first_block) in enumerate((
        (spec_fine, quads_fine, fine, 0, fine_rows, 0),
        (spec_coarse, quads_coarse, coarse, NYQ, 0, fine),
    )):
        columns = [[] for _ in range(blocks)]
        for d in range(2):
            for quad in range(quads):
                value = jnp.concatenate(
                    cross(spec_ref, d + 1, 2 * quad) + cross(spec_ref, d + 1, 2 * quad + 1), axis=1)
                y = dot3(value, table_ref, shift_at)
                for b in range(blocks):
                    at = first + b * HALF
                    stack = jnp.concatenate(
                        [y[at : at + HALF, :LANES], y[at : at + HALF, LANES:],
                         y[nyquist : nyquist + NYQ, :LANES]], axis=0)
                    high, low = split(stack)
                    columns[b].append(jnp.concatenate([high, low], axis=0))
        for b in range(blocks):
            at = map_at + 2 * WINDOW * (first_block + b)
            columns_b = jnp.concatenate(columns[b], axis=1)
            both = dot(table_ref[at : at + 2 * WINDOW, : columns_b.shape[0]], columns_b)
            maps = both[:WINDOW] + both[WINDOW:]
            for d in range(2):
                for quad in range(quads):
                    at = (d * quads + quad) * LANES
                    maps_ref[tile_index(d, level, b, quad)] = maps[:, at : at + LANES]

    lanes = lax.broadcasted_iota(jnp.int32, (maps_ref.shape[0], LANES), 1) // WINDOW
    for big in range(WINDOW // 4):
        rows = [maps_ref[:, 4 * big + r, :] for r in range(4)]
        for g in range(4):
            value = None
            for r in range(4):
                moved = rows[r] if r == g else pltpu.roll(rows[r], (WINDOW * (r - g)) % LANES, 1)
                value = moved if value is None else jnp.where(lanes == r, moved, value)
            rows_ref[big, pl.ds(g, maps_ref.shape[0], stride=4), :] = value
        for out, level, quads, blocks in ((out_fine, 0, quads_fine, fine), (out_coarse, 1, quads_coarse, coarse)):
            for d in range(2):
                for b in range(blocks):
                    at = 4 * tile_index(d, level, b, 0)
                    out[0, d, b, :, big * LANES : (big + 1) * LANES] = rows_ref[big, at : at + 4 * quads]


def correlate(strips, rims, mask_fine, mask_coarse):
    strip_rows, width = strips.shape[1:]
    fine, coarse = mask_fine.shape[1], mask_coarse.shape[1]
    quads_fine = width // STRIDE // 4
    quads_coarse = width // (2 * STRIDE) // 4
    table, places = all_tables(strip_rows, fine + coarse)
    half_rows = (fine + coarse) * HALF + NYQ
    tiles = 2 * (fine * quads_fine + coarse * quads_coarse)
    whole = pl.BlockSpec(memory_space=pltpu.VMEM)
    scalars = pl.BlockSpec(memory_space=pltpu.SMEM)
    return pl.pallas_call(
        functools.partial(kernel, fine, coarse, quads_fine, quads_coarse, places),
        out_shape=(
            jax.ShapeDtypeStruct((1, 2, fine, 4 * quads_fine, WINDOW * WINDOW), f32),
            jax.ShapeDtypeStruct((1, 2, coarse, 4 * quads_coarse, WINDOW * WINDOW), f32),
        ),
        in_specs=[whole, whole, scalars, scalars, whole],
        out_specs=(whole, whole),
        scratch_shapes=[
            pltpu.VMEM((3, 2 * half_rows, width + LANES), f32),
            pltpu.VMEM((3, 2 * quads_fine, fine * HALF + NYQ, 2 * LANES), f32),
            pltpu.VMEM((3, 2 * quads_coarse, coarse * HALF + NYQ, 2 * LANES), f32),
            pltpu.VMEM((tiles, WINDOW, LANES), f32),
            pltpu.VMEM((WINDOW // 4, 4 * tiles, LANES), f32),
        ],
        compiler_params=pltpu.CompilerParams(vmem_limit_bytes=32 * 1024 * 1024),
    )(strips, rims, mask_fine, mask_coarse, jnp.asarray(table))


def local(sections, mask_fine, mask_coarse):
    near = shifted(sections, "sec", -1)
    far = shifted(sections, "sec", -2)
    strips = jnp.concatenate([sections, near, far], axis=0)
    rims = shifted(strips, "strip", -1)
    return correlate(strips, rims, mask_fine, mask_coarse)


def solution(mesh):
    in_specs = (
        P("sec", "strip", "groups"),
        P("sec", "strip", "groups"),
        P("sec", "strip", "groups"),
    )
    out_specs = (P("sec", None, "strip", "groups", None), P("sec", None, "strip", "groups", None))
    return jax.shard_map(local, mesh=mesh, in_specs=in_specs, out_specs=out_specs, check_vma=False)
```

```python
import functools

import jax
import jax.numpy as jnp
import numpy as np
from jax import lax
from jax.experimental import pallas as pl
from jax.experimental.pallas import tpu as pltpu
from jax.sharding import PartitionSpec as P

PATCH = 64
STRIDE = 32
WINDOW = 32
HALF = PATCH // 2
LANES = 128
NYQ = 16

f32 = jnp.float32
bf16 = jnp.bfloat16


def from_device(value, sec_steps, strip_steps):
    secs, strips = lax.axis_size("sec"), lax.axis_size("strip")
    pairs = []
    for sec in range(secs - sec_steps):
        for strip in range(strips - strip_steps):
            pairs.append(((sec + sec_steps) * strips + strip + strip_steps, sec * strips + strip))
    return lax.ppermute(value, ("sec", "strip"), pairs)


def wave(phase):
    turns = np.arange(PATCH) * (2 * np.pi / PATCH)
    cos = np.round(np.cos(turns), 14)
    sin = np.round(np.sin(turns), 14)
    phase = np.mod(phase, PATCH)
    return cos[phase], sin[phase]


def split_table(table):
    high = table.astype(jnp.bfloat16)
    low = (table - high.astype(np.float64)).astype(jnp.bfloat16)
    return high, low


def row_table(ext, fine, coarse):
    k = np.arange(HALF)[:, None]
    cos_rows, sin_rows, nyquist = [], [], np.zeros((NYQ, ext))
    blocks = [(b * STRIDE, 1) for b in fine] + [(b * 2 * STRIDE, 2) for b in coarse]
    for at, (first, pool) in enumerate(blocks):
        cos = np.zeros((HALF, ext))
        sin = np.zeros((HALF, ext))
        x = np.arange(pool * PATCH) // pool
        c, s = wave(k * x[None, :])
        cos[:, first : first + x.size] = c / pool
        sin[:, first : first + x.size] = s / pool
        nyquist[at, first : first + x.size] = wave(HALF * x)[0] / pool
        cos_rows.append(cos)
        sin_rows.append(sin)
    n = len(fine)
    table = np.concatenate(
        cos_rows[:n] + [nyquist] + cos_rows[n:] + sin_rows[:n] + [np.zeros((NYQ, ext))] + sin_rows[n:])
    return np.concatenate(split_table(table), axis=1)


def stacked(table):
    return np.concatenate(split_table(table), axis=0)


def fine_table():
    c, s = wave(np.arange(PATCH)[:, None] * np.arange(PATCH)[None, :])
    table = np.zeros((2, 2, PATCH, 2, 2, PATCH))
    for p in range(2):
        table[0, p, :, 0, p] = c
        table[1, p, :, 0, p] = -s
        table[0, p, :, 1, p] = -s
        table[1, p, :, 1, p] = -c
    return stacked(table.reshape(4 * PATCH, 4 * PATCH))


def coarse_table():
    c, s = wave((np.arange(2 * PATCH) // 2)[:, None] * np.arange(PATCH)[None, :])
    table = np.zeros((2, 2, 2 * PATCH, 2, 2, PATCH))
    for p in range(2):
        table[p, 0, :, 0, p] = 0.5 * c
        table[p, 1, :, 0, p] = -0.5 * s
        table[p, 0, :, 1, p] = -0.5 * s
        table[p, 1, :, 1, p] = -0.5 * c
    return stacked(table.reshape(8 * PATCH, 4 * PATCH))


def shift_table():
    t = np.arange(WINDOW) - WINDOW // 2
    c, s = wave(np.arange(PATCH)[:, None] * t[None, :])
    table = np.zeros((2, 2, 2, PATCH, 2, 4, WINDOW))
    for odd in range(2):
        for p in range(2):
            table[odd, 0, p, :, 0, 2 * p + odd] = c
            table[odd, 1, p, :, 0, 2 * p + odd] = -s
            table[odd, 0, p, :, 1, 2 * p + odd] = s
            table[odd, 1, p, :, 1, 2 * p + odd] = c
    return stacked(table.reshape(8 * PATCH, 8 * WINDOW))


def map_table(blocks):
    shift = np.arange(WINDOW) - WINDOW // 2
    c, s = wave(shift[:, None] * np.arange(HALF)[None, :])
    weight = np.where(np.arange(HALF) == 0, 1.0, 2.0) / PATCH**3
    rows = []
    for block in range(blocks):
        nyquist = np.zeros((WINDOW, NYQ))
        nyquist[:, block] = wave(HALF * shift)[0] / PATCH**3
        high, low = split_table(np.concatenate([c * weight, -s * weight, nyquist], axis=1))
        rows += [np.concatenate([high, high], axis=1), np.concatenate([low, np.zeros_like(low)], axis=1)]
    return np.concatenate(rows)


def all_tables(ext, groups):
    tables = [row_table(ext, *group) for group in groups]
    tables += [fine_table(), shift_table(), map_table(max(len(f) + len(c) for f, c in groups)), coarse_table()]
    width = max(table.shape[1] for table in tables)
    places = np.cumsum([0] + [table.shape[0] for table in tables])
    padded = [np.pad(table, ((0, 0), (0, width - table.shape[1]))) for table in tables]
    return np.concatenate(padded), [int(place) for place in places]


def split(value):
    high = value.astype(bf16)
    return high, (value - high.astype(f32)).astype(bf16)


def dot(left, right):
    return jnp.dot(left, right, preferred_element_type=f32)


def dot3(high, low, table_ref, at):
    depth = high.shape[1]
    table_high = table_ref[at : at + depth]
    table_low = table_ref[at + depth : at + 2 * depth]
    return dot(
        jnp.concatenate([high, low, high], axis=1),
        jnp.concatenate([table_high, table_high, table_low], axis=0))


def power(values, first, nyquist, block, dc, sub):
    re, im = values[:, :LANES], values[:, LANES:]
    q = re * re + im * im
    total = None
    for r in range(0, HALF, 8):
        part = q[first + r : first + r + 8]
        if r == 0:
            part = jnp.where(dc, 0.0, part)
            head = jnp.where(sub == 0, part, 0.0)
        total = part if total is None else total + part
    return 2.0 * total - head + jnp.where(sub == block, q[nyquist : nyquist + 8], 0.0)


def normalise(spec_ref, z, tiles, rows, block_first, nyquist, first_block):
    sub = lax.broadcasted_iota(jnp.int32, (8, LANES), 0)
    lane = lax.broadcasted_iota(jnp.int32, (8, LANES), 1)
    dc = (sub == 0) & (lane % PATCH == 0)
    dc_both = jnp.concatenate([dc, dc], axis=1)
    group = lax.broadcasted_iota(jnp.int32, (LANES, LANES), 0) // PATCH
    same = group == lax.broadcasted_iota(jnp.int32, (LANES, LANES), 1) // PATCH
    ones = jnp.where(same, 1.0, 0.0).astype(bf16)
    sums = []
    for tile in range(tiles):
        values = spec_ref[z, tile]
        for b in range(rows):
            sums.append(power(values, block_first + b * HALF, nyquist, first_block + b, dc, sub))
    high, low = split(jnp.concatenate(sums, axis=0))
    stack = dot(jnp.concatenate([high, low], axis=1), jnp.concatenate([ones, ones], axis=0))
    nyquist_row = lax.broadcasted_iota(jnp.int32, (NYQ, 2 * LANES), 0)
    for tile in range(tiles):
        values = spec_ref[z, tile]
        parts = {}
        nyq = values[nyquist : nyquist + NYQ]
        scaled = jnp.zeros_like(nyq)
        for b in range(rows):
            at = (tile * rows + b) * 8
            total = jnp.sum(stack[at : at + 8], axis=0, keepdims=True)
            scale = 1.0 / jnp.sqrt(total * (1.0 / PATCH**4) + 1e-05)
            scale = jnp.concatenate([scale, scale], axis=1)
            first = block_first + b * HALF
            block = values[first : first + HALF]
            block = jnp.concatenate([jnp.where(dc_both, 0.0, block[:8]), block[8:]], axis=0)
            parts[first] = block * scale
            scaled = jnp.where(nyquist_row == first_block + b, nyq * scale, scaled)
        parts[nyquist] = scaled
        result = jnp.concatenate([parts[first] for first in sorted(parts)], axis=0)
        spec_ref[z, tile] = result.astype(bf16).astype(f32)


def maps_of(fine, coarse, width, strips, masks, table_ref, places, outs, scratch):
    row_at, fine_at, shift_at, map_at, coarse_at = places
    high_ref, low_ref, spec_fine, spec_coarse, maps_ref, rows_ref = scratch
    quads_fine, quads_coarse = width // STRIDE // 4, width // (2 * STRIDE) // 4
    fine_rows = fine * HALF
    fine_all = fine_rows + NYQ
    half_rows = fine_all + coarse * HALF
    levels = [(spec_fine, quads_fine, fine, 0, fine_rows, 0)]
    if coarse:
        levels.append((spec_coarse, quads_coarse, coarse, NYQ, 0, fine))

    for z in range(3):
        x = strips(z)
        t = dot(table_ref[row_at : row_at + 2 * half_rows, : 2 * x.shape[0]], jnp.concatenate([x, x], axis=0))
        for ref, half in zip((high_ref, low_ref), split(t)):
            ref[:, :width] = half
            ref[:, width:] = jnp.zeros((2 * half_rows, LANES), bf16)

        def windows(first, last, starts):
            result = []
            for ref in (high_ref, low_ref):
                pieces = []
                for tile in starts:
                    columns = []
                    for at in tile:
                        columns += [ref[first:last, at : at + LANES],
                                    ref[half_rows + first : half_rows + last, at : at + LANES]]
                    pieces.append(jnp.concatenate(columns, axis=1))
                result.append(jnp.concatenate(pieces, axis=0))
            return result

        starts = [[LANES * m + STRIDE * odd] for m in range(quads_fine) for odd in range(2)]
        f = dot3(*windows(0, fine_all, starts), table_ref, fine_at)
        for tile in range(len(starts)):
            spec_fine[z, tile] = f[tile * fine_all : (tile + 1) * fine_all]
        normalise(spec_fine, z, len(starts), fine, 0, fine_rows, 0)
        if coarse:
            starts = [[2 * LANES * n + LANES * p + 2 * STRIDE * odd for p in range(2)]
                      for n in range(quads_coarse) for odd in range(2)]
            f = dot3(*windows(fine_rows, half_rows, starts), table_ref, coarse_at)
            rows = half_rows - fine_rows
            for tile in range(len(starts)):
                spec_coarse[z, tile] = f[tile * rows : (tile + 1) * rows]
            normalise(spec_coarse, z, len(starts), coarse, NYQ, 0, fine)

    values = []
    for spec_ref, quads, blocks, first, nyquist, first_block in levels:
        for d in range(2):
            for quad in range(quads):
                columns = []
                for odd in range(2):
                    a, b = spec_ref[0, 2 * quad + odd], spec_ref[d + 1, 2 * quad + odd]
                    ar, ai, br, bi = a[:, :LANES], a[:, LANES:], b[:, :LANES], b[:, LANES:]
                    columns += [ar * br + ai * bi, ar * bi - ai * br]
                values.append(jnp.concatenate(columns, axis=1))
    y = dot3(*split(jnp.concatenate(values, axis=0)), table_ref, shift_at)

    starts = {}
    at = tile = 0
    for level, (spec_ref, quads, blocks, first, nyquist, first_block) in enumerate(levels):
        rows = blocks * HALF + NYQ
        for b in range(blocks):
            columns = []
            for i in range(2 * quads):
                top = at + i * rows + first + b * HALF
                nyq = at + i * rows + nyquist
                stack = jnp.concatenate(
                    [y[top : top + HALF, :LANES], y[top : top + HALF, LANES:], y[nyq : nyq + NYQ, :LANES]], axis=0)
                columns.append(jnp.concatenate(split(stack), axis=0))
            columns = jnp.concatenate(columns, axis=1)
            table = map_at + 2 * WINDOW * (first_block + b)
            both = dot(table_ref[table : table + 2 * WINDOW, : columns.shape[0]], columns)
            maps = both[:WINDOW] + both[WINDOW:]
            for i in range(2 * quads):
                maps_ref[tile + i] = maps[:, i * LANES : (i + 1) * LANES]
            for d in range(2):
                starts[level, d, b] = tile + d * quads
            tile += 2 * quads
        at += 2 * quads * rows

    kept = [jnp.transpose(mask) for mask in masks()]
    lanes = lax.broadcasted_iota(jnp.int32, (tile, LANES), 1) // WINDOW
    for big in range(WINDOW // 4):
        rows = [maps_ref[:, 4 * big + r, :] for r in range(4)]
        for g in range(4):
            value = None
            for r in range(4):
                moved = rows[r] if r == g else pltpu.roll(rows[r], (WINDOW * (r - g)) % LANES, 1)
                value = moved if value is None else jnp.where(lanes == r, moved, value)
            rows_ref[big, pl.ds(g, tile, stride=4), :] = value
        for level, out in enumerate(outs):
            quads, blocks = levels[level][1:3]
            for b in range(blocks):
                column = kept[level][: 4 * quads, b : b + 1]
                for d in range(2):
                    at = 4 * starts[level, d, b]
                    out[d, b, :, big * LANES : (big + 1) * LANES] = rows_ref[big, at : at + 4 * quads] * column


def mask_tile(mask_ref, pad_ref, first, count):
    pad_ref[...] = jnp.zeros(pad_ref.shape, f32)
    pad_ref[:count, : mask_ref.shape[2]] = mask_ref[0, first : first + count].astype(f32)
    return pad_ref[...]


def inner_kernel(
    fine, width, places,
    own_hbm, near, far, mask_hbm, table_hbm,
    out_hbm, table_ref,
    own, mask, pad, high_ref, low_ref, spec_fine, maps_ref, rows_ref, out, sems,
):
    own_copy = pltpu.make_async_copy(own_hbm, own, sems.at[0])
    mask_copy = pltpu.make_async_copy(mask_hbm, mask, sems.at[1])
    own_copy.start()
    mask_copy.start()
    row_at, fine_at, shift_at, map_at, coarse_at = places
    cuts = [0, fine_at, shift_at, coarse_at, table_hbm.shape[0]]
    copies = []
    for i in range(4):
        piece = pl.ds(cuts[i], cuts[i + 1] - cuts[i])
        copies.append(pltpu.make_async_copy(table_hbm.at[piece], table_ref.at[piece], sems.at[2 + i]))
        copies[-1].start()
    own_copy.wait()
    mask_copy.wait()
    for copy in copies:
        copy.wait()
    strips = (own, near, far)
    maps_of(
        fine, 0, width, lambda z: strips[z][0], lambda: [mask_tile(mask, pad, 0, fine)],
        table_ref, places, [out], (high_ref, low_ref, spec_fine, None, maps_ref, rows_ref))
    stores = [
        pltpu.make_async_copy(out.at[d], out_hbm.at[0, d, pl.ds(0, fine)], sems.at[d]) for d in range(2)]
    for store in stores:
        store.start()
    for store in stores:
        store.wait()


def outer_kernel(
    first, fine, coarse, width, places,
    own_hbm, near, far, rim, rim_near, rim_far, mask_hbm, mask_coarse_hbm, table_ref, part_hbm,
    out_hbm, out_coarse_hbm,
    own, mask, mask_coarse, pad, pad_coarse, high_ref, low_ref, spec_fine, spec_coarse, maps_ref, rows_ref,
    out, out_coarse, sems,
):
    loads = [
        pltpu.make_async_copy(own_hbm, own, sems.at[0]),
        pltpu.make_async_copy(mask_hbm, mask, sems.at[1]),
        pltpu.make_async_copy(mask_coarse_hbm, mask_coarse, sems.at[2]),
    ]
    for load in loads:
        load.start()
    for load in loads:
        load.wait()
    strips, rims = (own, near, far), (rim, rim_near, rim_far)
    maps_of(
        fine, coarse, width, lambda z: jnp.concatenate([strips[z][0], rims[z][0]], axis=0),
        lambda: [mask_tile(mask, pad, first, fine), mask_tile(mask_coarse, pad_coarse, 0, coarse)],
        table_ref, places, [out, out_coarse], (high_ref, low_ref, spec_fine, spec_coarse, maps_ref, rows_ref))
    stores = []
    for d in range(2):
        stores.append(pltpu.make_async_copy(out.at[d], out_hbm.at[0, d, pl.ds(first, fine)], sems.at[2 * d]))
        stores.append(pltpu.make_async_copy(out_coarse.at[d], out_coarse_hbm.at[0, d], sems.at[2 * d + 1]))
    for store in stores:
        store.start()
    for store in stores:
        store.wait()


def scratch_of(fine, coarse, width):
    quads_fine, quads_coarse = width // STRIDE // 4, width // (2 * STRIDE) // 4
    half_rows = (fine + coarse) * HALF + NYQ
    tiles = 2 * (fine * quads_fine + coarse * quads_coarse)
    shapes = [
        pltpu.VMEM((2 * half_rows, width + LANES), bf16),
        pltpu.VMEM((2 * half_rows, width + LANES), bf16),
        pltpu.VMEM((3, 2 * quads_fine, fine * HALF + NYQ, 2 * LANES), f32),
    ]
    if coarse:
        shapes.append(pltpu.VMEM((3, 2 * quads_coarse, coarse * HALF + NYQ, 2 * LANES), f32))
    shapes += [
        pltpu.VMEM((tiles, WINDOW, LANES), f32),
        pltpu.VMEM((WINDOW // 4, 4 * tiles, LANES), f32),
        pltpu.VMEM((2, fine, 4 * quads_fine, WINDOW * WINDOW), f32),
    ]
    if coarse:
        shapes.append(pltpu.VMEM((2, coarse, 4 * quads_coarse, WINDOW * WINDOW), f32))
    return shapes


def correlate(own, near, far, rims, mask_fine, mask_coarse):
    strip_rows, width = own.shape[1:]
    fine, coarse = mask_fine.shape[1], mask_coarse.shape[1]
    inner = fine - 1
    table, places = all_tables(
        strip_rows + PATCH, [(range(inner), []), (range(inner, fine), range(coarse))])
    ext = strip_rows + PATCH
    table[: places[1], strip_rows : 2 * strip_rows] = table[: places[1], ext : ext + strip_rows]
    row_in, row_out, fine_at, shift_at, map_at, coarse_at, _ = places
    hbm = pl.BlockSpec(memory_space=pltpu.HBM)
    vmem = pl.BlockSpec(memory_space=pltpu.VMEM)
    params = pltpu.CompilerParams(vmem_limit_bytes=24 * 1024 * 1024)
    out_fine = jax.ShapeDtypeStruct((1, 2, fine, width // STRIDE, WINDOW * WINDOW), f32)
    out_coarse = jax.ShapeDtypeStruct((1, 2, coarse, width // (2 * STRIDE), WINDOW * WINDOW), f32)

    part, tables = pl.pallas_call(
        functools.partial(inner_kernel, inner, width, (row_in, fine_at, shift_at, map_at, coarse_at)),
        out_shape=(out_fine, jax.ShapeDtypeStruct(table.shape, bf16)),
        in_specs=[hbm, vmem, vmem, hbm, hbm],
        out_specs=(hbm, vmem),
        scratch_shapes=[
            pltpu.VMEM(own.shape, bf16),
            pltpu.VMEM(mask_fine.shape, jnp.int32),
            pltpu.VMEM((8, LANES), f32),
            *scratch_of(inner, 0, width),
            pltpu.SemaphoreType.DMA((6,)),
        ],
        compiler_params=params,
        cost_estimate=pl.CostEstimate(flops=3 * 10**9, bytes_accessed=4 * 10**6, transcendentals=0),
        name="inner_blocks",
    )(own, near, far, mask_fine, jnp.asarray(table))
    return pl.pallas_call(
        functools.partial(
            outer_kernel, inner, fine - inner, coarse, width, (row_out, fine_at, shift_at, map_at, coarse_at)),
        out_shape=(out_fine, out_coarse),
        in_specs=[hbm, vmem, vmem, vmem, vmem, vmem, hbm, hbm, vmem, hbm],
        out_specs=(hbm, hbm),
        scratch_shapes=[
            pltpu.VMEM(own.shape, bf16),
            pltpu.VMEM(mask_fine.shape, jnp.int32),
            pltpu.VMEM(mask_coarse.shape, jnp.int32),
            pltpu.VMEM((8, LANES), f32),
            pltpu.VMEM((8, LANES), f32),
            *scratch_of(fine - inner, coarse, width),
            pltpu.SemaphoreType.DMA((4,)),
        ],
        input_output_aliases={9: 0},
        compiler_params=params,
        cost_estimate=pl.CostEstimate(flops=4 * 10**9, bytes_accessed=4 * 10**6, transcendentals=0),
        name="outer_blocks",
    )(own, near, far, *rims, mask_fine, mask_coarse, tables, part)


def local(sections, mask_fine, mask_coarse):
    far = from_device(sections, 2, 0)
    near = from_device(sections, 1, 0)
    rims = [from_device(sections, 0, 1), from_device(sections, 1, 1), from_device(sections, 2, 1)]
    return correlate(sections, near, far, rims, mask_fine, mask_coarse)


def solution(mesh):
    in_specs = (
        P("sec", "strip", "groups"),
        P("sec", "strip", "groups"),
        P("sec", "strip", "groups"),
    )
    out_specs = (P("sec", None, "strip", "groups", None), P("sec", None, "strip", "groups", None))
    return jax.shard_map(local, mesh=mesh, in_specs=in_specs, out_specs=out_specs, check_vma=False)
```

```python
import functools

import jax
import jax.numpy as jnp
import numpy as np
from jax import lax
from jax.experimental import pallas as pl
from jax.experimental.pallas import tpu as pltpu
from jax.sharding import PartitionSpec as P

PATCH = 64
STRIDE = 32
WINDOW = 32
HALF = PATCH // 2
LANES = 128
NYQ = 16

f32 = jnp.float32
bf16 = jnp.bfloat16


def from_device(value, sec_steps, strip_steps):
    secs, strips = lax.axis_size("sec"), lax.axis_size("strip")
    pairs = []
    for sec in range(secs - sec_steps):
        for strip in range(strips - strip_steps):
            pairs.append(((sec + sec_steps) * strips + strip + strip_steps, sec * strips + strip))
    return lax.ppermute(value, ("sec", "strip"), pairs)


def wave(phase):
    turns = np.arange(PATCH) * (2 * np.pi / PATCH)
    cos = np.round(np.cos(turns), 14)
    sin = np.round(np.sin(turns), 14)
    phase = np.mod(phase, PATCH)
    return cos[phase], sin[phase]


def split_table(table):
    high = table.astype(jnp.bfloat16)
    low = (table - high.astype(np.float64)).astype(jnp.bfloat16)
    return high, low


def stacked(table):
    return np.concatenate(split_table(table), axis=0)


def fine_table():
    c, s = wave(np.arange(PATCH)[:, None] * np.arange(PATCH)[None, :])
    table = np.zeros((2, 2, PATCH, 2, 2, PATCH))
    for p in range(2):
        table[0, p, :, 0, p] = c
        table[1, p, :, 0, p] = -s
        table[0, p, :, 1, p] = -s
        table[1, p, :, 1, p] = -c
    return stacked(table.reshape(4 * PATCH, 4 * PATCH))


def coarse_table():
    c, s = wave((np.arange(2 * PATCH) // 2)[:, None] * np.arange(PATCH)[None, :])
    table = np.zeros((2, 2, 2 * PATCH, 2, 2, PATCH))
    for p in range(2):
        table[p, 0, :, 0, p] = 0.5 * c
        table[p, 1, :, 0, p] = -0.5 * s
        table[p, 0, :, 1, p] = -0.5 * s
        table[p, 1, :, 1, p] = -0.5 * c
    return stacked(table.reshape(8 * PATCH, 4 * PATCH))


def shift_table():
    t = np.arange(WINDOW) - WINDOW // 2
    c, s = wave(np.arange(PATCH)[:, None] * t[None, :])
    table = np.zeros((2, 2, 2, PATCH, 2, 4, WINDOW))
    for odd in range(2):
        for p in range(2):
            table[odd, 0, p, :, 0, 2 * p + odd] = c
            table[odd, 1, p, :, 0, 2 * p + odd] = -s
            table[odd, 0, p, :, 1, 2 * p + odd] = s
            table[odd, 1, p, :, 1, 2 * p + odd] = c
    return stacked(table.reshape(8 * PATCH, 8 * WINDOW))


def map_table(blocks):
    shift = np.arange(WINDOW) - WINDOW // 2
    c, s = wave(shift[:, None] * np.arange(HALF)[None, :])
    weight = np.where(np.arange(HALF) == 0, 1.0, 2.0) / PATCH**3
    rows = []
    for block in range(blocks):
        nyquist = np.zeros((WINDOW, NYQ))
        nyquist[:, block] = wave(HALF * shift)[0] / PATCH**3
        high, low = split_table(np.concatenate([c * weight, -s * weight, nyquist], axis=1))
        rows += [np.concatenate([high, high], axis=1), np.concatenate([low, np.zeros_like(low)], axis=1)]
    return np.concatenate(rows)


def all_tables(blocks):
    tables = [fine_table(), coarse_table(), shift_table(), map_table(blocks)]
    width = max(table.shape[1] for table in tables)
    places = np.cumsum([0] + [table.shape[0] for table in tables])
    padded = [np.pad(table, ((0, 0), (0, width - table.shape[1]))) for table in tables]
    return np.concatenate(padded), [int(place) for place in places]


def split(value):
    high = value.astype(bf16)
    return high, (value - high.astype(f32)).astype(bf16)


def dot(left, right):
    return jnp.dot(left, right, preferred_element_type=f32)


def dot3(high, low, table_ref, at):
    depth = high.shape[1]
    table_high = table_ref[at : at + depth]
    table_low = table_ref[at + depth : at + 2 * depth]
    return dot(
        jnp.concatenate([high, low, high], axis=1),
        jnp.concatenate([table_high, table_high, table_low], axis=0))


def cosine(turns):
    turns = turns + PATCH // 4
    part = (turns & (HALF - 1)) - PATCH // 4
    angle = part.astype(f32) * (2 * np.pi / PATCH)
    square = angle * angle
    value = jnp.full(square.shape, 1.0 / 479001600, f32)
    for term in (-1.0 / 3628800, 1.0 / 40320, -1.0 / 720, 1.0 / 24, -0.5, 1.0):
        value = value * square + term
    return jnp.where((turns & HALF) == 0, value, -value)


def write_row_table(row_ref, fine, coarse):
    ext = row_ref.shape[1] // 2
    half_rows = row_ref.shape[0] // 2
    blocks = [(b * HALF, b * STRIDE, 0) for b in range(fine)]
    blocks += [(fine * HALF + NYQ + b * HALF, b * 2 * STRIDE, 1) for b in range(coarse)]

    def put(at, value):
        high, low = split(value)
        row_ref[at : at + value.shape[0], :ext] = high
        row_ref[at : at + value.shape[0], ext:] = low

    k = lax.broadcasted_iota(jnp.int32, (HALF, ext), 0)
    column = lax.broadcasted_iota(jnp.int32, (HALF, ext), 1)
    row = lax.broadcasted_iota(jnp.int32, (NYQ, ext), 0)
    nyquist = jnp.zeros((NYQ, ext), f32)
    for number, (at, first, pool) in enumerate(blocks):
        x = column - first
        kept = jnp.where((x >= 0) & (x < PATCH << pool), 1.0 / (1 << pool), 0.0)
        turns = k * (x >> pool)
        put(at, cosine(turns) * kept)
        put(half_rows + at, cosine(turns - PATCH // 4) * kept)
        wave_half = cosine((x[:NYQ] >> pool) * HALF) * kept[:NYQ]
        nyquist = jnp.where(row == number, wave_half, nyquist)
    put(fine * HALF, nyquist)
    put(half_rows + fine * HALF, jnp.zeros((NYQ, ext), f32))


def all_rows(value):
    for step in (4, 2, 1):
        value = value + pltpu.roll(value, step, 0)
    return value


class Level:
    def __init__(self, blocks, quads, first, nyquist, number, start, table):
        self.blocks, self.quads, self.tiles = blocks, quads, 2 * quads
        self.first, self.nyquist, self.number = first, nyquist, number
        self.rows = blocks * HALF + NYQ
        self.start = start
        self.table = table


def levels_of(fine, coarse, width, places):
    fine_at, coarse_at = places[0], places[1]
    return [
        Level(fine, width // STRIDE // 4, 0, fine * HALF, 0, 0, fine_at),
        Level(coarse, width // (2 * STRIDE) // 4, NYQ, 0, fine, fine * HALF, coarse_at),
    ]


def transform_rows(x, row_ref, t_ref, halves):
    width = x.shape[1]
    t_ref[...] = dot(row_ref[...], jnp.concatenate([x, x], axis=0))
    for r in range(0, t_ref.shape[0], 16):
        for ref, half in zip(halves, split(t_ref[r : r + 16])):
            ref[r : r + 16, :width] = half
            ref[r : r + 16, width:] = jnp.zeros((16, LANES), bf16)


def transform_columns(level, pool, halves, left, f_ref, spec_ref, table_ref):
    half_rows = halves[0].shape[0] // 2
    rows, size = level.rows, pool * LANES
    for source, target in zip(halves, left):
        for tile in range(level.tiles):
            for p in range(pool):
                at = size * (tile // 2) + LANES * p + pool * STRIDE * (tile % 2)
                for half in range(2):
                    target[tile * rows : (tile + 1) * rows, (2 * p + half) * LANES : (2 * p + half + 1) * LANES] = (
                        source[half * half_rows + level.start : half * half_rows + level.start + rows, at : at + LANES])
    f_ref[...] = dot3(left[0][...], left[1][...], table_ref, level.table)

    sub = lax.broadcasted_iota(jnp.int32, (8, LANES), 0)
    lane = lax.broadcasted_iota(jnp.int32, (8, LANES), 1)
    dc = (sub == 0) & (lane % PATCH == 0)
    dc_both = jnp.concatenate([dc, dc], axis=1)
    group = lax.broadcasted_iota(jnp.int32, (LANES, LANES), 0) // PATCH
    same = group == lax.broadcasted_iota(jnp.int32, (LANES, LANES), 1) // PATCH
    ones = jnp.where(same, 1.0, 0.0).astype(bf16)
    sums = []
    for tile in range(level.tiles):
        base = tile * rows
        for b in range(level.blocks):
            total = None
            for r in range(0, HALF, 8):
                at = base + level.first + b * HALF + r
                re, im = f_ref[at : at + 8, :LANES], f_ref[at : at + 8, LANES:]
                part = re * re + im * im
                if r == 0:
                    part = jnp.where(dc, 0.0, part)
                    head = jnp.where(sub == 0, part, 0.0)
                total = part if total is None else total + part
            at = base + level.nyquist
            re, im = f_ref[at : at + 8, :LANES], f_ref[at : at + 8, LANES:]
            tail = jnp.where(sub == level.number + b, re * re + im * im, 0.0)
            sums.append(2.0 * total - head + tail)
    high, low = split(jnp.concatenate(sums, axis=0))
    sums = dot(jnp.concatenate([high, low], axis=1), jnp.concatenate([ones, ones], axis=0))
    for tile in range(level.tiles):
        base = tile * rows
        at = base + level.nyquist
        nyq = f_ref[at : at + 8]
        scaled = jnp.zeros_like(nyq)
        for b in range(level.blocks):
            number = (tile * level.blocks + b) * 8
            scale = lax.rsqrt(all_rows(sums[number : number + 8]) * (1.0 / PATCH**4) + 1e-05)
            scale = jnp.concatenate([scale, scale], axis=1)
            first = level.first + b * HALF
            for r in range(0, HALF, 16):
                at = base + first + r
                head = f_ref[at : at + 8]
                if r == 0:
                    head = jnp.where(dc_both, 0.0, head)
                both = jnp.concatenate([head * scale, f_ref[at + 8 : at + 16] * scale], axis=0)
                spec_ref[at : at + 16] = both.astype(bf16)
            scaled = jnp.where(sub[:, :1] == level.number + b, nyq * scale, scaled)
        at = base + level.nyquist
        spec_ref[at : at + 16] = jnp.concatenate([scaled, jnp.zeros_like(scaled)], axis=0).astype(bf16)


def correlate_pair(levels, own_specs, other_specs, masks, table_ref, shift_at, map_at, scratch, outs):
    high_ref, low_ref, y_ref, maps_ref, rows_ref = scratch[:5]
    stacks = scratch[5:]
    base = 0
    for level, own, other in zip(levels, own_specs, other_specs):
        for tile in range(level.tiles):
            quad, odd = divmod(tile, 2)
            for r in range(0, level.rows, 16):
                at = tile * level.rows + r
                a, b = own[at : at + 16].astype(f32), other[at : at + 16].astype(f32)
                ar, ai, br, bi = a[:, :LANES], a[:, LANES:], b[:, :LANES], b[:, LANES:]
                cross = jnp.concatenate([ar * br + ai * bi, ar * bi - ai * br], axis=1)
                to = base + quad * level.rows + r
                for ref, half in zip((high_ref, low_ref), split(cross)):
                    ref[to : to + 16, 2 * odd * LANES : 2 * (odd + 1) * LANES] = half
        base += level.quads * level.rows
    y_ref[...] = dot3(high_ref[...], low_ref[...], table_ref, shift_at)
    base = tile = 0
    starts = {}
    for index, level in enumerate(levels):
        for b in range(level.blocks):
            stack_ref = stacks[level.number + b]
            for quad in range(level.quads):
                row = base + quad * level.rows
                top, nyq = row + level.first + b * HALF, row + level.nyquist
                for at, value in (
                    (0, y_ref[top : top + HALF, :LANES]),
                    (HALF, y_ref[top : top + HALF, LANES:]),
                    (2 * HALF, y_ref[nyq : nyq + NYQ, :LANES]),
                ):
                    for half, part in enumerate(split(value)):
                        to = half * (2 * HALF + NYQ) + at
                        stack_ref[to : to + value.shape[0], quad * LANES : (quad + 1) * LANES] = part
            table = map_at + 2 * WINDOW * (level.number + b)
            depth, columns = stack_ref.shape
            both = dot(table_ref[table : table + 2 * WINDOW, :depth], stack_ref[...])
            maps = both[:WINDOW] + both[WINDOW:]
            for quad in range(level.quads):
                maps_ref[tile + quad] = maps[:, quad * LANES : (quad + 1) * LANES]
            starts[index, b] = tile
            tile += level.quads
        base += level.quads * level.rows
    kept = [jnp.transpose(mask) for mask in masks]
    lanes = lax.broadcasted_iota(jnp.int32, (tile, LANES), 1) // WINDOW
    for big in range(WINDOW // 4):
        rows = [maps_ref[:, 4 * big + r, :] for r in range(4)]
        for g in range(4):
            value = None
            for r in range(4):
                moved = rows[r] if r == g else pltpu.roll(rows[r], (WINDOW * (r - g)) % LANES, 1)
                value = moved if value is None else jnp.where(lanes == r, moved, value)
            rows_ref[big, pl.ds(g, tile, stride=4), :] = value
        for index, (level, out) in enumerate(zip(levels, outs)):
            for b in range(level.blocks):
                column = kept[index][: 4 * level.quads, b : b + 1]
                at = 4 * starts[index, b]
                out[b, :, big * LANES : (big + 1) * LANES] = rows_ref[big, at : at + 4 * level.quads] * column


def mask_tile(mask_ref, pad_ref):
    pad_ref[...] = jnp.zeros(pad_ref.shape, f32)
    pad_ref[: mask_ref.shape[1], : mask_ref.shape[2]] = mask_ref[0].astype(f32)
    return pad_ref[...]


def near_kernel(
    fine, coarse, places,
    own_hbm, near, rim, rim_near, mask_hbm, mask_coarse_hbm, table_hbm,
    row_ref, table_ref, own_fine, own_coarse, map_fine, map_coarse,
    own, mask, mask_coarse, pad, pad_coarse, t_ref, t_high, t_low, left_high, left_low, coarse_high, coarse_low,
    f_fine, f_coarse, near_fine, near_coarse, *rest,
):
    sems = rest[-1]
    loads = [
        pltpu.make_async_copy(own_hbm, own, sems.at[0]),
        pltpu.make_async_copy(mask_hbm, mask, sems.at[1]),
        pltpu.make_async_copy(mask_coarse_hbm, mask_coarse, sems.at[2]),
    ]
    fine_at, coarse_at, shift_at, map_at, end = places
    for i, (first, last) in enumerate(((fine_at, coarse_at), (coarse_at, shift_at), (shift_at, end))):
        piece = pl.ds(first, last - first)
        loads.append(pltpu.make_async_copy(table_hbm.at[piece], table_ref.at[piece], sems.at[3 + i]))
    for load in loads:
        load.start()
    write_row_table(row_ref, fine, coarse)
    levels = levels_of(fine, coarse, near.shape[2], places)
    specs = ((near_fine, near_coarse), (own_fine, own_coarse))
    for z in range(2):
        if z == 1:
            loads[0].wait()
        strips = ((near, rim_near), (own, rim))[z]
        x = jnp.concatenate([strips[0][0], strips[1][0]], axis=0)
        transform_rows(x, row_ref, t_ref.at[z], (t_high.at[z], t_low.at[z]))
    loads[3].wait()
    for z in range(2):
        transform_columns(
            levels[0], 1, (t_high.at[z], t_low.at[z]), (left_high.at[z], left_low.at[z]), f_fine.at[z],
            specs[z][0], table_ref)
    loads[4].wait()
    for z in range(2):
        transform_columns(
            levels[1], 2, (t_high.at[z], t_low.at[z]), (coarse_high.at[z], coarse_low.at[z]), f_coarse.at[z],
            specs[z][1], table_ref)
    loads[5].wait()
    loads[1].wait()
    loads[2].wait()
    correlate_pair(
        levels, specs[1], specs[0], (mask_tile(mask, pad), mask_tile(mask_coarse, pad_coarse)),
        table_ref, shift_at, map_at, rest[:-1], (map_fine, map_coarse))


def far_kernel(
    fine, coarse, places,
    far, row_ref, table_ref, own_fine, own_coarse, map_fine, map_coarse, mask_hbm, mask_coarse_hbm,
    out_fine, out_coarse,
    mask, mask_coarse, pad, pad_coarse, t_ref, t_high, t_low, left_high, left_low, coarse_high, coarse_low,
    f_fine, f_coarse, far_fine, far_coarse, last_fine, last_coarse, *rest,
):
    sems = rest[-1]
    loads = [
        pltpu.make_async_copy(mask_hbm, mask, sems.at[0]),
        pltpu.make_async_copy(mask_coarse_hbm, mask_coarse, sems.at[1]),
    ]
    stores = [
        pltpu.make_async_copy(map_fine, out_fine.at[0, 0], sems.at[2]),
        pltpu.make_async_copy(map_coarse, out_coarse.at[0, 0], sems.at[3]),
    ]
    for copy in loads + stores:
        copy.start()
    fine_at, coarse_at, shift_at, map_at, end = places
    levels = levels_of(fine, coarse, far.shape[2], places)
    x = jnp.concatenate([far[0], far[1]], axis=0)
    transform_rows(x, row_ref, t_ref.at[0], (t_high.at[0], t_low.at[0]))
    transform_columns(
        levels[0], 1, (t_high.at[0], t_low.at[0]), (left_high.at[0], left_low.at[0]), f_fine.at[0], far_fine, table_ref)
    transform_columns(
        levels[1], 2, (t_high.at[0], t_low.at[0]), (coarse_high.at[0], coarse_low.at[0]), f_coarse.at[0],
        far_coarse, table_ref)
    for load in loads:
        load.wait()
    correlate_pair(
        levels, (own_fine, own_coarse), (far_fine, far_coarse),
        (mask_tile(mask, pad), mask_tile(mask_coarse, pad_coarse)),
        table_ref, shift_at, map_at, rest[:-1], (last_fine, last_coarse))
    last = [
        pltpu.make_async_copy(last_fine, out_fine.at[0, 1], sems.at[4]),
        pltpu.make_async_copy(last_coarse, out_coarse.at[0, 1], sems.at[5]),
    ]
    for copy in last:
        copy.start()
    for copy in stores + last:
        copy.wait()


def correlate(own, near, rim, rim_near, far, mask_fine, mask_coarse):
    strip_rows, width = own.shape[1:]
    fine, coarse = mask_fine.shape[1], mask_coarse.shape[1]
    ext = strip_rows + PATCH
    table, places = all_tables(fine + coarse)
    levels = levels_of(fine, coarse, width, places)
    half_rows = (fine + coarse) * HALF + NYQ
    tiles = sum(level.blocks * level.quads for level in levels)
    spec_shapes = [(level.tiles * level.rows, 2 * LANES) for level in levels]
    map_shapes = [(level.blocks, 4 * level.quads, WINDOW * WINDOW) for level in levels]
    cross_rows = sum(level.quads * level.rows for level in levels)

    def scratch(sections):
        def many(shape, dtype):
            return pltpu.VMEM((sections,) + shape, dtype)

        return [
            many((2 * half_rows, width), f32),
            many((2 * half_rows, width + LANES), bf16),
            many((2 * half_rows, width + LANES), bf16),
            many(spec_shapes[0], bf16),
            many(spec_shapes[0], bf16),
            many((spec_shapes[1][0], 4 * LANES), bf16),
            many((spec_shapes[1][0], 4 * LANES), bf16),
            many(spec_shapes[0], f32),
            many(spec_shapes[1], f32),
            pltpu.VMEM(spec_shapes[0], bf16),
            pltpu.VMEM(spec_shapes[1], bf16),
        ]

    pair_scratch = [
        pltpu.VMEM((cross_rows, 4 * LANES), bf16),
        pltpu.VMEM((cross_rows, 4 * LANES), bf16),
        pltpu.VMEM((cross_rows, 2 * LANES), f32),
        pltpu.VMEM((tiles, WINDOW, LANES), f32),
        pltpu.VMEM((WINDOW // 4, 4 * tiles, LANES), f32),
        *(pltpu.VMEM((4 * HALF + 2 * NYQ, level.quads * LANES), bf16) for level in levels for _ in range(level.blocks)),
        pltpu.SemaphoreType.DMA((6,)),
    ]
    mask_scratch = [
        pltpu.VMEM(mask_fine.shape, jnp.int32),
        pltpu.VMEM(mask_coarse.shape, jnp.int32),
        pltpu.VMEM((8, LANES), f32),
        pltpu.VMEM((8, LANES), f32),
    ]
    hbm = pl.BlockSpec(memory_space=pltpu.HBM)
    vmem = pl.BlockSpec(memory_space=pltpu.VMEM)
    params = pltpu.CompilerParams(vmem_limit_bytes=24 * 1024 * 1024)
    own, table, mask_fine, mask_coarse = (
        pltpu.with_memory_space_constraint(value, pltpu.HBM)
        for value in (own, jnp.asarray(table), mask_fine, mask_coarse))

    handed = pl.pallas_call(
        functools.partial(near_kernel, fine, coarse, places),
        out_shape=(
            jax.ShapeDtypeStruct((2 * half_rows, 2 * ext), bf16),
            jax.ShapeDtypeStruct(table.shape, bf16),
            *(jax.ShapeDtypeStruct(shape, bf16) for shape in spec_shapes),
            *(jax.ShapeDtypeStruct(shape, f32) for shape in map_shapes),
        ),
        in_specs=[hbm, vmem, vmem, vmem, hbm, hbm, hbm],
        out_specs=(vmem,) * 6,
        scratch_shapes=[pltpu.VMEM(own.shape, bf16), *mask_scratch, *scratch(2), *pair_scratch],
        compiler_params=params,
        cost_estimate=pl.CostEstimate(flops=4 * 10**9, bytes_accessed=4 * 10**6, transcendentals=0),
        name="near_maps",
    )(own, near, rim, rim_near, mask_fine, mask_coarse, table)
    return pl.pallas_call(
        functools.partial(far_kernel, fine, coarse, places),
        out_shape=tuple(jax.ShapeDtypeStruct((1, 2) + shape, f32) for shape in map_shapes),
        in_specs=[vmem] * 7 + [hbm, hbm],
        out_specs=(hbm, hbm),
        scratch_shapes=[
            *mask_scratch, *scratch(1), *(pltpu.VMEM(shape, f32) for shape in map_shapes), *pair_scratch],
        compiler_params=params,
        cost_estimate=pl.CostEstimate(flops=3 * 10**9, bytes_accessed=4 * 10**6, transcendentals=0),
        name="far_maps",
    )(far, *handed, mask_fine, mask_coarse)


def local(sections, mask_fine, mask_coarse):
    near = from_device(sections, 1, 0)
    rim_near = from_device(sections, 1, 1)
    rim = from_device(sections, 0, 1)
    far = from_device(jnp.concatenate([near, rim_near], axis=0), 1, 0)
    return correlate(sections, near, rim, rim_near, far, mask_fine, mask_coarse)


def solution(mesh):
    in_specs = (
        P("sec", "strip", "groups"),
        P("sec", "strip", "groups"),
        P("sec", "strip", "groups"),
    )
    out_specs = (P("sec", None, "strip", "groups", None), P("sec", None, "strip", "groups", None))
    return jax.shard_map(local, mesh=mesh, in_specs=in_specs, out_specs=out_specs, check_vma=False)
```

```python
import functools

import jax
import jax.numpy as jnp
import numpy as np
from jax import lax
from jax.experimental import pallas as pl
from jax.experimental.pallas import tpu as pltpu
from jax.sharding import PartitionSpec as P

PATCH = 64
STRIDE = 32
WINDOW = 32
HALF = PATCH // 2
LANES = 128
NYQ = 16

f32 = jnp.float32
bf16 = jnp.bfloat16


def from_device(value, sec_steps, strip_steps):
    secs, strips = lax.axis_size("sec"), lax.axis_size("strip")
    pairs = []
    for sec in range(secs - sec_steps):
        for strip in range(strips - strip_steps):
            pairs.append(((sec + sec_steps) * strips + strip + strip_steps, sec * strips + strip))
    return lax.ppermute(value, ("sec", "strip"), pairs)


def wave(phase):
    turns = np.arange(PATCH) * (2 * np.pi / PATCH)
    cos = np.round(np.cos(turns), 14)
    sin = np.round(np.sin(turns), 14)
    phase = np.mod(phase, PATCH)
    return cos[phase], sin[phase]


def split_table(table):
    high = table.astype(jnp.bfloat16)
    low = (table - high.astype(np.float64)).astype(jnp.bfloat16)
    return high, low


def stacked(table):
    return np.concatenate(split_table(table), axis=0)


def fine_table():
    c, s = wave(np.arange(PATCH)[:, None] * np.arange(PATCH)[None, :])
    table = np.zeros((2, 2, PATCH, 2, 2, PATCH))
    for p in range(2):
        table[0, p, :, 0, p] = c
        table[1, p, :, 0, p] = -s
        table[0, p, :, 1, p] = -s
        table[1, p, :, 1, p] = -c
    return stacked(table.reshape(4 * PATCH, 4 * PATCH))


def coarse_table():
    c, s = wave((np.arange(2 * PATCH) // 2)[:, None] * np.arange(PATCH)[None, :])
    table = np.zeros((2, 2, 2 * PATCH, 2, 2, PATCH))
    for p in range(2):
        table[p, 0, :, 0, p] = 0.5 * c
        table[p, 1, :, 0, p] = -0.5 * s
        table[p, 0, :, 1, p] = -0.5 * s
        table[p, 1, :, 1, p] = -0.5 * c
    return stacked(table.reshape(8 * PATCH, 4 * PATCH))


def shift_table():
    t = np.arange(WINDOW) - WINDOW // 2
    c, s = wave(np.arange(PATCH)[:, None] * t[None, :])
    table = np.zeros((2, 2, 2, PATCH, 2, 4, WINDOW))
    for odd in range(2):
        for p in range(2):
            table[odd, 0, p, :, 0, 2 * p + odd] = c
            table[odd, 1, p, :, 0, 2 * p + odd] = -s
            table[odd, 0, p, :, 1, 2 * p + odd] = s
            table[odd, 1, p, :, 1, 2 * p + odd] = c
    return stacked(table.reshape(8 * PATCH, 8 * WINDOW))


def map_table(blocks):
    shift = np.arange(WINDOW) - WINDOW // 2
    c, s = wave(shift[:, None] * np.arange(HALF)[None, :])
    weight = np.where(np.arange(HALF) == 0, 1.0, 2.0) / PATCH**3
    rows = []
    for block in range(blocks):
        nyquist = np.zeros((WINDOW, NYQ))
        nyquist[:, block] = wave(HALF * shift)[0] / PATCH**3
        high, low = split_table(np.concatenate([c * weight, -s * weight, nyquist], axis=1))
        rows += [np.concatenate([high, high], axis=1), np.concatenate([low, np.zeros_like(low)], axis=1)]
    return np.concatenate(rows)


def all_tables(blocks):
    tables = [fine_table(), coarse_table(), shift_table(), map_table(blocks)]
    width = max(table.shape[1] for table in tables)
    places = np.cumsum([0] + [table.shape[0] for table in tables])
    padded = [np.pad(table, ((0, 0), (0, width - table.shape[1]))) for table in tables]
    return np.concatenate(padded), [int(place) for place in places]


def split(value):
    high = value.astype(bf16)
    return high, (value - high.astype(f32)).astype(bf16)


def dot(left, right):
    return jnp.dot(left, right, preferred_element_type=f32)


def dot3(high, low, table_ref, at):
    depth = high.shape[1]
    table_high = table_ref[at : at + depth]
    table_low = table_ref[at + depth : at + 2 * depth]
    return dot(
        jnp.concatenate([high, low, high], axis=1),
        jnp.concatenate([table_high, table_high, table_low], axis=0))


def cosine(turns):
    turns = turns + PATCH // 4
    part = (turns & (HALF - 1)) - PATCH // 4
    angle = part.astype(f32) * (2 * np.pi / PATCH)
    square = angle * angle
    value = jnp.full(square.shape, 1.0 / 479001600, f32)
    for term in (-1.0 / 3628800, 1.0 / 40320, -1.0 / 720, 1.0 / 24, -0.5, 1.0):
        value = value * square + term
    return jnp.where((turns & HALF) == 0, value, -value)


def write_row_table(row_ref, fine, coarse):
    ext = row_ref.shape[1] // 2
    half_rows = row_ref.shape[0] // 2
    blocks = [(b * HALF, b * STRIDE, 0) for b in range(fine)]
    blocks += [(fine * HALF + NYQ + b * HALF, b * 2 * STRIDE, 1) for b in range(coarse)]

    def put(at, value):
        high, low = split(value)
        row_ref[at : at + value.shape[0], :ext] = high
        row_ref[at : at + value.shape[0], ext:] = low

    k = lax.broadcasted_iota(jnp.int32, (HALF, ext), 0)
    column = lax.broadcasted_iota(jnp.int32, (HALF, ext), 1)
    row = lax.broadcasted_iota(jnp.int32, (NYQ, ext), 0)
    nyquist = jnp.zeros((NYQ, ext), f32)
    for number, (at, first, pool) in enumerate(blocks):
        x = column - first
        kept = jnp.where((x >= 0) & (x < PATCH << pool), 1.0 / (1 << pool), 0.0)
        turns = k * (x >> pool)
        put(at, cosine(turns) * kept)
        put(half_rows + at, cosine(turns - PATCH // 4) * kept)
        wave_half = cosine((x[:NYQ] >> pool) * HALF) * kept[:NYQ]
        nyquist = jnp.where(row == number, wave_half, nyquist)
    put(fine * HALF, nyquist)
    put(half_rows + fine * HALF, jnp.zeros((NYQ, ext), f32))


def all_rows(value):
    for step in (4, 2, 1):
        value = value + pltpu.roll(value, step, 0)
    return value


class Level:
    def __init__(self, pool, blocks, quads, first, nyquist, number, start, table):
        self.pool = pool
        self.blocks, self.quads, self.tiles = blocks, quads, 2 * quads
        self.first, self.nyquist, self.number = first, nyquist, number
        self.rows = blocks * HALF + NYQ
        self.start = start
        self.table = table


def levels_of(fine, coarse, width, places):
    fine_at, coarse_at = places[0], places[1]
    return [
        Level(1, fine, width // STRIDE // 4, 0, fine * HALF, 0, 0, fine_at),
        Level(2, coarse, width // (2 * STRIDE) // 4, NYQ, 0, fine, fine * HALF, coarse_at),
    ]


def transform_rows(x, row_ref, t_ref, halves):
    width = x.shape[1]
    t_ref[...] = dot(row_ref[...], jnp.concatenate([x, x], axis=0))
    for r in range(0, t_ref.shape[0], 16):
        for ref, half in zip(halves, split(t_ref[r : r + 16])):
            ref[r : r + 16, :width] = half
            ref[r : r + 16, width:] = jnp.zeros((16, LANES), bf16)


def gather_windows(level, halves, left):
    half_rows = halves[0].shape[0] // 2
    rows, pool = level.rows, level.pool
    for source, target in zip(halves, left):
        for tile in range(level.tiles):
            for p in range(pool):
                at = pool * LANES * (tile // 2) + LANES * p + pool * STRIDE * (tile % 2)
                for half in range(2):
                    target[tile * rows : (tile + 1) * rows, (2 * p + half) * LANES : (2 * p + half + 1) * LANES] = (
                        source[half * half_rows + level.start : half * half_rows + level.start + rows, at : at + LANES])


def spectrum_power(level, f_ref):
    sub = lax.broadcasted_iota(jnp.int32, (8, LANES), 0)
    lane = lax.broadcasted_iota(jnp.int32, (8, LANES), 1)
    dc = (sub == 0) & (lane % PATCH == 0)
    group = lax.broadcasted_iota(jnp.int32, (LANES, LANES), 0) // PATCH
    same = group == lax.broadcasted_iota(jnp.int32, (LANES, LANES), 1) // PATCH
    ones = jnp.where(same, 1.0, 0.0).astype(bf16)
    sums = []
    for tile in range(level.tiles):
        base = tile * level.rows
        for b in range(level.blocks):
            total = None
            for r in range(0, HALF, 8):
                at = base + level.first + b * HALF + r
                re, im = f_ref[at : at + 8, :LANES], f_ref[at : at + 8, LANES:]
                part = re * re + im * im
                if r == 0:
                    part = jnp.where(dc, 0.0, part)
                    head = jnp.where(sub == 0, part, 0.0)
                total = part if total is None else total + part
            at = base + level.nyquist
            re, im = f_ref[at : at + 8, :LANES], f_ref[at : at + 8, LANES:]
            tail = jnp.where(sub == level.number + b, re * re + im * im, 0.0)
            sums.append(2.0 * total - head + tail)
    high, low = split(jnp.concatenate(sums, axis=0))
    return dot(jnp.concatenate([high, low], axis=1), jnp.concatenate([ones, ones], axis=0))


def scale_spectrum(level, f_ref, sums, spec_ref):
    sub = lax.broadcasted_iota(jnp.int32, (8, 2 * LANES), 0)
    lane = lax.broadcasted_iota(jnp.int32, (8, 2 * LANES), 1)
    dc = (sub == 0) & (lane % PATCH == 0)
    for tile in range(level.tiles):
        base = tile * level.rows
        at = base + level.nyquist
        nyq = f_ref[at : at + 8]
        scaled = jnp.zeros_like(nyq)
        for b in range(level.blocks):
            number = (tile * level.blocks + b) * 8
            scale = lax.rsqrt(all_rows(sums[number : number + 8]) * (1.0 / PATCH**4) + 1e-05)
            scale = jnp.concatenate([scale, scale], axis=1)
            for r in range(0, HALF, 16):
                at = base + level.first + b * HALF + r
                head = f_ref[at : at + 8]
                if r == 0:
                    head = jnp.where(dc, 0.0, head)
                both = jnp.concatenate([head * scale, f_ref[at + 8 : at + 16] * scale], axis=0)
                spec_ref[at : at + 16] = both.astype(bf16)
            scaled = jnp.where(sub == level.number + b, nyq * scale, scaled)
        at = base + level.nyquist
        spec_ref[at : at + 16] = jnp.concatenate([scaled, jnp.zeros_like(scaled)], axis=0).astype(bf16)


def transform(levels, x, row_ref, table_ref, tables_ready, scratch, specs):
    t_ref, *halves = scratch[:3]
    lefts, f_refs = (scratch[3:5], scratch[5:7]), scratch[7:9]
    transform_rows(x, row_ref, t_ref, halves)
    for level, left in zip(levels, lefts):
        gather_windows(level, halves, left)
    sums = []
    for level, left, f_ref, ready in zip(levels, lefts, f_refs, tables_ready):
        ready()
        f_ref[...] = dot3(left[0][...], left[1][...], table_ref, level.table)
        sums.append(spectrum_power(level, f_ref))
    for level, f_ref, total, spec_ref in zip(levels, f_refs, sums, specs):
        scale_spectrum(level, f_ref, total, spec_ref)


def correlate_pair(levels, own_specs, other_specs, masks, table_ref, shift_at, map_at, scratch, outs):
    high_ref, low_ref, y_ref, maps_ref, rows_ref = scratch[:5]
    stacks = scratch[5:]
    base = 0
    for level, own, other in zip(levels, own_specs, other_specs):
        for tile in range(level.tiles):
            quad, odd = divmod(tile, 2)
            for r in range(0, level.rows, 16):
                at = tile * level.rows + r
                a, b = own[at : at + 16].astype(f32), other[at : at + 16].astype(f32)
                ar, ai, br, bi = a[:, :LANES], a[:, LANES:], b[:, :LANES], b[:, LANES:]
                cross = jnp.concatenate([ar * br + ai * bi, ar * bi - ai * br], axis=1)
                to = base + quad * level.rows + r
                for ref, half in zip((high_ref, low_ref), split(cross)):
                    ref[to : to + 16, 2 * odd * LANES : 2 * (odd + 1) * LANES] = half
        base += level.quads * level.rows
    y_ref[...] = dot3(high_ref[...], low_ref[...], table_ref, shift_at)
    base = tile = 0
    starts = {}
    for index, level in enumerate(levels):
        for b in range(level.blocks):
            stack_ref = stacks[level.number + b]
            for quad in range(level.quads):
                row = base + quad * level.rows
                top, nyq = row + level.first + b * HALF, row + level.nyquist
                for at, value in (
                    (0, y_ref[top : top + HALF, :LANES]),
                    (HALF, y_ref[top : top + HALF, LANES:]),
                    (2 * HALF, y_ref[nyq : nyq + NYQ, :LANES]),
                ):
                    for half, part in enumerate(split(value)):
                        to = half * (2 * HALF + NYQ) + at
                        stack_ref[to : to + value.shape[0], quad * LANES : (quad + 1) * LANES] = part
            table = map_at + 2 * WINDOW * (level.number + b)
            depth, columns = stack_ref.shape
            both = dot(table_ref[table : table + 2 * WINDOW, :depth], stack_ref[...])
            maps = both[:WINDOW] + both[WINDOW:]
            for quad in range(level.quads):
                maps_ref[tile + quad] = maps[:, quad * LANES : (quad + 1) * LANES]
            starts[index, b] = tile
            tile += level.quads
        base += level.quads * level.rows
    kept = [jnp.transpose(mask) for mask in masks]
    lanes = lax.broadcasted_iota(jnp.int32, (tile, LANES), 1) // WINDOW
    for big in range(WINDOW // 4):
        rows = [maps_ref[:, 4 * big + r, :] for r in range(4)]
        for g in range(4):
            value = None
            for r in range(4):
                moved = rows[r] if r == g else pltpu.roll(rows[r], (WINDOW * (r - g)) % LANES, 1)
                value = moved if value is None else jnp.where(lanes == r, moved, value)
            rows_ref[big, pl.ds(g, tile, stride=4), :] = value
        for index, (level, out) in enumerate(zip(levels, outs)):
            for b in range(level.blocks):
                column = kept[index][: 4 * level.quads, b : b + 1]
                at = 4 * starts[index, b]
                out[b, :, big * LANES : (big + 1) * LANES] = rows_ref[big, at : at + 4 * level.quads] * column


def mask_tile(mask_ref, pad_ref):
    pad_ref[...] = jnp.zeros(pad_ref.shape, f32)
    pad_ref[: mask_ref.shape[1], : mask_ref.shape[2]] = mask_ref[0].astype(f32)
    return pad_ref[...]


def own_kernel(
    fine, coarse, places,
    own_hbm, rim, table_hbm,
    row_ref, table_ref, own_fine, own_coarse,
    own, *rest,
):
    *scratch, sems = rest
    fine_at, coarse_at, shift_at, map_at, end = places
    loads = [pltpu.make_async_copy(own_hbm, own, sems.at[0])]
    for i, (first, last) in enumerate(((fine_at, coarse_at), (coarse_at, shift_at), (shift_at, end))):
        piece = pl.ds(first, last - first)
        loads.append(pltpu.make_async_copy(table_hbm.at[piece], table_ref.at[piece], sems.at[1 + i]))
    for load in loads:
        load.start()
    write_row_table(row_ref, fine, coarse)
    levels = levels_of(fine, coarse, rim.shape[2], places)
    loads[0].wait()
    x = jnp.concatenate([own[0], rim[0]], axis=0)
    transform(levels, x, row_ref, table_ref, (loads[1].wait, loads[2].wait), scratch, (own_fine, own_coarse))
    loads[3].wait()


def other_maps(fine, coarse, places, other, row_ref, table_ref, own_specs, mask_hbms, outs, scratch, sems):
    mask, mask_coarse, pad, pad_coarse = scratch[:4]
    transform_scratch, specs, pair_scratch = scratch[4:13], scratch[13:15], scratch[15:]
    fine_at, coarse_at, shift_at, map_at, end = places
    loads = [
        pltpu.make_async_copy(source, target, sems.at[i])
        for i, (source, target) in enumerate(zip(mask_hbms, (mask, mask_coarse)))]
    for load in loads:
        load.start()
    levels = levels_of(fine, coarse, other.shape[2], places)
    x = jnp.concatenate([other[0], other[1]], axis=0)
    transform(levels, x, row_ref, table_ref, (lambda: None,) * 2, transform_scratch, specs)
    for load in loads:
        load.wait()
    correlate_pair(
        levels, own_specs, specs, (mask_tile(mask, pad), mask_tile(mask_coarse, pad_coarse)),
        table_ref, shift_at, map_at, pair_scratch, outs)


def near_kernel(
    fine, coarse, places,
    near, row_ref, table_ref, own_fine, own_coarse, mask_hbm, mask_coarse_hbm,
    map_fine, map_coarse,
    *rest,
):
    *scratch, sems = rest
    other_maps(
        fine, coarse, places, near, row_ref, table_ref, (own_fine, own_coarse), (mask_hbm, mask_coarse_hbm),
        (map_fine, map_coarse), scratch, sems)


def far_kernel(
    fine, coarse, places,
    far, row_ref, table_ref, own_fine, own_coarse, mask_hbm, mask_coarse_hbm, map_fine, map_coarse,
    out_fine, out_coarse,
    last_fine, last_coarse, *rest,
):
    *scratch, sems = rest
    stores = [
        pltpu.make_async_copy(map_fine, out_fine.at[0, 0], sems.at[2]),
        pltpu.make_async_copy(map_coarse, out_coarse.at[0, 0], sems.at[3]),
    ]
    for copy in stores:
        copy.start()
    other_maps(
        fine, coarse, places, far, row_ref, table_ref, (own_fine, own_coarse), (mask_hbm, mask_coarse_hbm),
        (last_fine, last_coarse), scratch, sems)
    last = [
        pltpu.make_async_copy(last_fine, out_fine.at[0, 1], sems.at[4]),
        pltpu.make_async_copy(last_coarse, out_coarse.at[0, 1], sems.at[5]),
    ]
    for copy in last:
        copy.start()
    for copy in stores + last:
        copy.wait()


def correlate(own, rim, near, far_of, mask_fine, mask_coarse):
    strip_rows, width = own.shape[1:]
    fine, coarse = mask_fine.shape[1], mask_coarse.shape[1]
    ext = strip_rows + PATCH
    table, places = all_tables(fine + coarse)
    levels = levels_of(fine, coarse, width, places)
    half_rows = (fine + coarse) * HALF + NYQ
    tiles = sum(level.blocks * level.quads for level in levels)
    spec_shapes = [(level.tiles * level.rows, 2 * LANES) for level in levels]
    left_shapes = [(level.tiles * level.rows, 2 * level.pool * LANES) for level in levels]
    map_shapes = [(level.blocks, 4 * level.quads, WINDOW * WINDOW) for level in levels]
    cross_rows = sum(level.quads * level.rows for level in levels)

    transform_scratch = [
        pltpu.VMEM((2 * half_rows, width), f32),
        pltpu.VMEM((2 * half_rows, width + LANES), bf16),
        pltpu.VMEM((2 * half_rows, width + LANES), bf16),
        *(pltpu.VMEM(shape, bf16) for shape in left_shapes for _ in range(2)),
        *(pltpu.VMEM(shape, f32) for shape in spec_shapes),
    ]
    other_scratch = [
        pltpu.VMEM(mask_fine.shape, jnp.int32),
        pltpu.VMEM(mask_coarse.shape, jnp.int32),
        pltpu.VMEM((8, LANES), f32),
        pltpu.VMEM((8, LANES), f32),
        *transform_scratch,
        *(pltpu.VMEM(shape, bf16) for shape in spec_shapes),
        pltpu.VMEM((cross_rows, 4 * LANES), bf16),
        pltpu.VMEM((cross_rows, 4 * LANES), bf16),
        pltpu.VMEM((cross_rows, 2 * LANES), f32),
        pltpu.VMEM((tiles, WINDOW, LANES), f32),
        pltpu.VMEM((WINDOW // 4, 4 * tiles, LANES), f32),
        *(pltpu.VMEM((4 * HALF + 2 * NYQ, level.quads * LANES), bf16) for level in levels for _ in range(level.blocks)),
        pltpu.SemaphoreType.DMA((6,)),
    ]
    hbm = pl.BlockSpec(memory_space=pltpu.HBM)
    vmem = pl.BlockSpec(memory_space=pltpu.VMEM)
    params = pltpu.CompilerParams(vmem_limit_bytes=24 * 1024 * 1024)

    def cost(flops):
        return pl.CostEstimate(flops=flops, bytes_accessed=4 * 10**6, transcendentals=0)

    own, table, mask_fine, mask_coarse = (
        pltpu.with_memory_space_constraint(value, pltpu.HBM)
        for value in (own, jnp.asarray(table), mask_fine, mask_coarse))
    handed = pl.pallas_call(
        functools.partial(own_kernel, fine, coarse, places),
        out_shape=(
            jax.ShapeDtypeStruct((2 * half_rows, 2 * ext), bf16),
            jax.ShapeDtypeStruct(table.shape, bf16),
            *(jax.ShapeDtypeStruct(shape, bf16) for shape in spec_shapes),
        ),
        in_specs=[hbm, vmem, hbm],
        out_specs=(vmem,) * 4,
        scratch_shapes=[pltpu.VMEM(own.shape, bf16), *transform_scratch, pltpu.SemaphoreType.DMA((4,))],
        compiler_params=params,
        cost_estimate=cost(2 * 10**9),
        name="own_spectra",
    )(own, rim, table)
    near, handed = lax.optimization_barrier((near, handed))
    far = far_of(near)
    maps = pl.pallas_call(
        functools.partial(near_kernel, fine, coarse, places),
        out_shape=tuple(jax.ShapeDtypeStruct(shape, f32) for shape in map_shapes),
        in_specs=[vmem] * 5 + [hbm, hbm],
        out_specs=(vmem, vmem),
        scratch_shapes=other_scratch,
        compiler_params=params,
        cost_estimate=cost(3 * 10**9),
        name="near_maps",
    )(near, *handed, mask_fine, mask_coarse)
    return pl.pallas_call(
        functools.partial(far_kernel, fine, coarse, places),
        out_shape=tuple(jax.ShapeDtypeStruct((1, 2) + shape, f32) for shape in map_shapes),
        in_specs=[vmem] * 5 + [hbm, hbm, vmem, vmem],
        out_specs=(hbm, hbm),
        scratch_shapes=[*(pltpu.VMEM(shape, f32) for shape in map_shapes), *other_scratch],
        compiler_params=params,
        cost_estimate=cost(3 * 10**9),
        name="far_maps",
    )(far, *handed, mask_fine, mask_coarse, *maps)


def local(sections, mask_fine, mask_coarse):
    rim = from_device(sections, 0, 1)
    near = jnp.concatenate([from_device(sections, 1, 0), from_device(sections, 1, 1)], axis=0)
    return correlate(sections, rim, near, lambda value: from_device(value, 1, 0), mask_fine, mask_coarse)


def solution(mesh):
    in_specs = (
        P("sec", "strip", "groups"),
        P("sec", "strip", "groups"),
        P("sec", "strip", "groups"),
    )
    out_specs = (P("sec", None, "strip", "groups", None), P("sec", None, "strip", "groups", None))
    return jax.shard_map(local, mesh=mesh, in_specs=in_specs, out_specs=out_specs, check_vma=False)
```

```python
import functools

import jax
import jax.numpy as jnp
import numpy as np
from jax import lax
from jax.experimental import pallas as pl
from jax.experimental.pallas import tpu as pltpu
from jax.sharding import PartitionSpec as P

PATCH = 64
STRIDE = 32
WINDOW = 32
HALF = PATCH // 2
LANES = 128
NYQ = 16

f32 = jnp.float32
bf16 = jnp.bfloat16


def from_device(value, sec_steps, strip_steps):
    secs, strips = lax.axis_size("sec"), lax.axis_size("strip")
    pairs = []
    for sec in range(secs - sec_steps):
        for strip in range(strips - strip_steps):
            pairs.append(((sec + sec_steps) * strips + strip + strip_steps, sec * strips + strip))
    return lax.ppermute(value, ("sec", "strip"), pairs)


def wave(phase):
    turns = np.arange(PATCH) * (2 * np.pi / PATCH)
    cos = np.round(np.cos(turns), 14)
    sin = np.round(np.sin(turns), 14)
    phase = np.mod(phase, PATCH)
    return cos[phase], sin[phase]


def split_table(table):
    high = table.astype(jnp.bfloat16)
    low = (table - high.astype(np.float64)).astype(jnp.bfloat16)
    return high, low


def stacked(table):
    return np.concatenate(split_table(table), axis=0)


def fine_table():
    c, s = wave(np.arange(PATCH)[:, None] * np.arange(PATCH)[None, :])
    table = np.zeros((2, 2, PATCH, 2, 2, PATCH))
    for p in range(2):
        table[0, p, :, 0, p] = c
        table[1, p, :, 0, p] = -s
        table[0, p, :, 1, p] = -s
        table[1, p, :, 1, p] = -c
    return stacked(table.reshape(4 * PATCH, 4 * PATCH))


def coarse_table():
    c, s = wave((np.arange(2 * PATCH) // 2)[:, None] * np.arange(PATCH)[None, :])
    table = np.zeros((2, 2, 2 * PATCH, 2, 2, PATCH))
    for p in range(2):
        table[p, 0, :, 0, p] = 0.5 * c
        table[p, 1, :, 0, p] = -0.5 * s
        table[p, 0, :, 1, p] = -0.5 * s
        table[p, 1, :, 1, p] = -0.5 * c
    return stacked(table.reshape(8 * PATCH, 4 * PATCH))


def shift_table():
    t = np.arange(WINDOW) - WINDOW // 2
    c, s = wave(np.arange(PATCH)[:, None] * t[None, :])
    table = np.zeros((2, 2, 2, PATCH, 2, 4, WINDOW))
    for odd in range(2):
        for p in range(2):
            table[odd, 0, p, :, 0, 2 * p + odd] = c
            table[odd, 1, p, :, 0, 2 * p + odd] = -s
            table[odd, 0, p, :, 1, 2 * p + odd] = s
            table[odd, 1, p, :, 1, 2 * p + odd] = c
    return stacked(table.reshape(8 * PATCH, 8 * WINDOW))


def map_table(blocks):
    shift = np.arange(WINDOW) - WINDOW // 2
    c, s = wave(shift[:, None] * np.arange(HALF)[None, :])
    weight = np.where(np.arange(HALF) == 0, 1.0, 2.0) / PATCH**3
    rows = []
    for block in range(blocks):
        nyquist = np.zeros((WINDOW, NYQ))
        nyquist[:, block] = wave(HALF * shift)[0] / PATCH**3
        high, low = split_table(np.concatenate([c * weight, -s * weight, nyquist], axis=1))
        rows += [np.concatenate([high, high], axis=1), np.concatenate([low, np.zeros_like(low)], axis=1)]
    return np.concatenate(rows)


def all_tables(blocks):
    tables = [fine_table(), coarse_table(), shift_table(), map_table(blocks)]
    width = max(table.shape[1] for table in tables)
    places = np.cumsum([0] + [table.shape[0] for table in tables])
    padded = [np.pad(table, ((0, 0), (0, width - table.shape[1]))) for table in tables]
    return np.concatenate(padded), [int(place) for place in places]


def split(value):
    high = value.astype(bf16)
    return high, (value - high.astype(f32)).astype(bf16)


def dot(left, right):
    return jnp.dot(left, right, preferred_element_type=f32)


def dot3(high, low, table_ref, at):
    depth = high.shape[1]
    table_high = table_ref[at : at + depth]
    table_low = table_ref[at + depth : at + 2 * depth]
    return dot(
        jnp.concatenate([high, low, high], axis=1),
        jnp.concatenate([table_high, table_high, table_low], axis=0))


def cosine(turns):
    turns = turns + PATCH // 4
    part = (turns & (HALF - 1)) - PATCH // 4
    angle = part.astype(f32) * (2 * np.pi / PATCH)
    square = angle * angle
    value = jnp.full(square.shape, 1.0 / 479001600, f32)
    for term in (-1.0 / 3628800, 1.0 / 40320, -1.0 / 720, 1.0 / 24, -0.5, 1.0):
        value = value * square + term
    return jnp.where((turns & HALF) == 0, value, -value)


def write_row_table(row_ref, fine, coarse):
    ext = row_ref.shape[1] // 2
    half_rows = row_ref.shape[0] // 2
    blocks = [(b * HALF, b * STRIDE, 0) for b in range(fine)]
    blocks += [(fine * HALF + NYQ + b * HALF, b * 2 * STRIDE, 1) for b in range(coarse)]

    def put(at, value):
        high, low = split(value)
        row_ref[at : at + value.shape[0], :ext] = high
        row_ref[at : at + value.shape[0], ext:] = low

    k = lax.broadcasted_iota(jnp.int32, (HALF, ext), 0)
    column = lax.broadcasted_iota(jnp.int32, (HALF, ext), 1)
    row = lax.broadcasted_iota(jnp.int32, (NYQ, ext), 0)
    nyquist = jnp.zeros((NYQ, ext), f32)
    for number, (at, first, pool) in enumerate(blocks):
        x = column - first
        kept = jnp.where((x >= 0) & (x < PATCH << pool), 1.0 / (1 << pool), 0.0)
        turns = k * (x >> pool)
        put(at, cosine(turns) * kept)
        put(half_rows + at, cosine(turns - PATCH // 4) * kept)
        wave_half = cosine((x[:NYQ] >> pool) * HALF) * kept[:NYQ]
        nyquist = jnp.where(row == number, wave_half, nyquist)
    put(fine * HALF, nyquist)
    put(half_rows + fine * HALF, jnp.zeros((NYQ, ext), f32))


def all_rows(value):
    for step in (4, 2, 1):
        value = value + pltpu.roll(value, step, 0)
    return value


class Level:
    def __init__(self, pool, blocks, quads, first, nyquist, number, start, table):
        self.pool = pool
        self.blocks, self.quads, self.tiles = blocks, quads, 2 * quads
        self.first, self.nyquist, self.number = first, nyquist, number
        self.rows = blocks * HALF + NYQ
        self.start = start
        self.table = table


def levels_of(fine, coarse, width, places):
    fine_at, coarse_at = places[0], places[1]
    return [
        Level(1, fine, width // STRIDE // 4, 0, fine * HALF, 0, 0, fine_at),
        Level(2, coarse, width // (2 * STRIDE) // 4, NYQ, 0, fine, fine * HALF, coarse_at),
    ]


def gather_windows(level, halves, left):
    half_rows = halves[0].shape[0] // 2
    rows, pool = level.rows, level.pool
    for source, target in zip(halves, left):
        for tile in range(level.tiles):
            for p in range(pool):
                at = pool * LANES * (tile // 2) + LANES * p + pool * STRIDE * (tile % 2)
                for half in range(2):
                    target[tile * rows : (tile + 1) * rows, (2 * p + half) * LANES : (2 * p + half + 1) * LANES] = (
                        source[half * half_rows + level.start : half * half_rows + level.start + rows, at : at + LANES])


def spectrum_power(level, f_ref):
    sub = lax.broadcasted_iota(jnp.int32, (8, LANES), 0)
    lane = lax.broadcasted_iota(jnp.int32, (8, LANES), 1)
    dc = (sub == 0) & (lane % PATCH == 0)
    group = lax.broadcasted_iota(jnp.int32, (LANES, LANES), 0) // PATCH
    same = group == lax.broadcasted_iota(jnp.int32, (LANES, LANES), 1) // PATCH
    ones = jnp.where(same, 1.0, 0.0).astype(bf16)
    sums = []
    for tile in range(level.tiles):
        base = tile * level.rows
        for b in range(level.blocks):
            total = None
            for r in range(0, HALF, 8):
                at = base + level.first + b * HALF + r
                re, im = f_ref[at : at + 8, :LANES], f_ref[at : at + 8, LANES:]
                part = re * re + im * im
                if r == 0:
                    part = jnp.where(dc, 0.0, part)
                    head = jnp.where(sub == 0, part, 0.0)
                total = part if total is None else total + part
            at = base + level.nyquist
            re, im = f_ref[at : at + 8, :LANES], f_ref[at : at + 8, LANES:]
            tail = jnp.where(sub == level.number + b, re * re + im * im, 0.0)
            sums.append(2.0 * total - head + tail)
    high, low = split(jnp.concatenate(sums, axis=0))
    return dot(jnp.concatenate([high, low], axis=1), jnp.concatenate([ones, ones], axis=0))


def scale_spectrum(level, f_ref, sums, spec_ref):
    sub = lax.broadcasted_iota(jnp.int32, (8, 2 * LANES), 0)
    lane = lax.broadcasted_iota(jnp.int32, (8, 2 * LANES), 1)
    dc = (sub == 0) & (lane % PATCH == 0)
    for tile in range(level.tiles):
        base = tile * level.rows
        at = base + level.nyquist
        nyq = f_ref[at : at + 8]
        scaled = jnp.zeros_like(nyq)
        for b in range(level.blocks):
            number = (tile * level.blocks + b) * 8
            scale = lax.rsqrt(all_rows(sums[number : number + 8]) * (1.0 / PATCH**4) + 1e-05)
            scale = jnp.concatenate([scale, scale], axis=1)
            for r in range(0, HALF, 16):
                at = base + level.first + b * HALF + r
                head = f_ref[at : at + 8]
                if r == 0:
                    head = jnp.where(dc, 0.0, head)
                both = jnp.concatenate([head * scale, f_ref[at + 8 : at + 16] * scale], axis=0)
                spec_ref[at : at + 16] = both.astype(bf16)
            scaled = jnp.where(sub == level.number + b, nyq * scale, scaled)
        at = base + level.nyquist
        spec_ref[at : at + 16] = jnp.concatenate([scaled, jnp.zeros_like(scaled)], axis=0).astype(bf16)


def transform(levels, strips, row_ref, table_ref, ready, scratch, specs):
    t_ref, *halves = scratch[:3]
    lefts, f_refs = (scratch[3:5], scratch[5:7]), scratch[7:9]
    ready[0]()
    x = jnp.concatenate([strip[0] for strip in strips], axis=0)
    t_ref[...] = dot(row_ref[...], jnp.concatenate([x, x], axis=0))
    yield
    width = x.shape[1]
    for r in range(0, t_ref.shape[0], 16):
        for ref, half in zip(halves, split(t_ref[r : r + 16])):
            ref[r : r + 16, :width] = half
            ref[r : r + 16, width:] = jnp.zeros((16, LANES), bf16)
    for level, left in zip(levels, lefts):
        gather_windows(level, halves, left)
        yield
    sums = []
    for level, left, f_ref, wait in zip(levels, lefts, f_refs, ready[1:]):
        wait()
        f_ref[...] = dot3(left[0][...], left[1][...], table_ref, level.table)
        yield
    for level, f_ref in zip(levels, f_refs):
        sums.append(spectrum_power(level, f_ref))
    yield
    for level, f_ref, total, spec_ref in zip(levels, f_refs, sums, specs):
        scale_spectrum(level, f_ref, total, spec_ref)
        yield


def correlate_pair(levels, own_specs, other_specs, masks, table_ref, shift_at, map_at, ready, scratch, outs):
    high_ref, low_ref, y_ref, maps_ref, rows_ref = scratch[:5]
    stacks = scratch[5:]
    base = 0
    for level, own, other in zip(levels, own_specs, other_specs):
        for tile in range(level.tiles):
            quad, odd = divmod(tile, 2)
            for r in range(0, level.rows, 16):
                at = tile * level.rows + r
                a, b = own[at : at + 16].astype(f32), other[at : at + 16].astype(f32)
                ar, ai, br, bi = a[:, :LANES], a[:, LANES:], b[:, :LANES], b[:, LANES:]
                cross = jnp.concatenate([ar * br + ai * bi, ar * bi - ai * br], axis=1)
                to = base + quad * level.rows + r
                for ref, half in zip((high_ref, low_ref), split(cross)):
                    ref[to : to + 16, 2 * odd * LANES : 2 * (odd + 1) * LANES] = half
        base += level.quads * level.rows
        yield
    ready()
    y_ref[...] = dot3(high_ref[...], low_ref[...], table_ref, shift_at)
    yield
    base = tile = 0
    starts = {}
    for index, level in enumerate(levels):
        for b in range(level.blocks):
            stack_ref = stacks[level.number + b]
            for quad in range(level.quads):
                row = base + quad * level.rows
                top, nyq = row + level.first + b * HALF, row + level.nyquist
                for at, value in (
                    (0, y_ref[top : top + HALF, :LANES]),
                    (HALF, y_ref[top : top + HALF, LANES:]),
                    (2 * HALF, y_ref[nyq : nyq + NYQ, :LANES]),
                ):
                    for half, part in enumerate(split(value)):
                        to = half * (2 * HALF + NYQ) + at
                        stack_ref[to : to + value.shape[0], quad * LANES : (quad + 1) * LANES] = part
            table = map_at + 2 * WINDOW * (level.number + b)
            depth, columns = stack_ref.shape
            both = dot(table_ref[table : table + 2 * WINDOW, :depth], stack_ref[...])
            maps = both[:WINDOW] + both[WINDOW:]
            for quad in range(level.quads):
                maps_ref[tile + quad] = maps[:, quad * LANES : (quad + 1) * LANES]
            starts[index, b] = tile
            tile += level.quads
            yield
        base += level.quads * level.rows
    kept = [jnp.transpose(mask()) for mask in masks]
    lanes = lax.broadcasted_iota(jnp.int32, (tile, LANES), 1) // WINDOW
    for big in range(WINDOW // 4):
        rows = [maps_ref[:, 4 * big + r, :] for r in range(4)]
        for g in range(4):
            value = None
            for r in range(4):
                moved = rows[r] if r == g else pltpu.roll(rows[r], (WINDOW * (r - g)) % LANES, 1)
                value = moved if value is None else jnp.where(lanes == r, moved, value)
            rows_ref[big, pl.ds(g, tile, stride=4), :] = value
        for index, (level, out) in enumerate(zip(levels, outs)):
            for b in range(level.blocks):
                column = kept[index][: 4 * level.quads, b : b + 1]
                at = 4 * starts[index, b]
                out[b, :, big * LANES : (big + 1) * LANES] = rows_ref[big, at : at + 4 * level.quads] * column


def mask_tile(mask_ref, pad_ref):
    pad_ref[...] = jnp.zeros(pad_ref.shape, f32)
    pad_ref[: mask_ref.shape[1], : mask_ref.shape[2]] = mask_ref[0].astype(f32)
    return pad_ref[...]


def run_staggered(tasks):
    done = set()
    waiting = list(tasks)
    active = []
    while waiting or active:
        for task in waiting:
            if task[2] <= done:
                active.append(task)
                waiting.remove(task)
                break
        for task in list(active):
            if next(task[1], done) is done:
                active.remove(task)
                done.add(task[0])


def maps_kernel(
    fine, coarse, places,
    own_hbm, near, far, rim, rim_near, rim_far, mask_hbm, mask_coarse_hbm, table_hbm,
    out_fine, out_coarse,
    own, mask, mask_coarse, pad, pad_coarse, row_ref, table_ref, *rest,
):
    *scratch, sems = rest
    fine_at, coarse_at, shift_at, map_at, end = places
    copies = {}

    def load(name, source, target):
        copies[name] = pltpu.make_async_copy(source, target, sems.at[len(copies)])
        copies[name].start()

    def table(name, first, last):
        load(name, table_hbm.at[pl.ds(first, last - first)], table_ref.at[pl.ds(first, last - first)])

    def once(name):
        def wait():
            copy = copies.pop(name, None)
            if copy is not None:
                copy.wait()

        return wait

    table("fine", fine_at, coarse_at)
    load("own", own_hbm, own)
    table("coarse", coarse_at, shift_at)
    table("shift", shift_at, end)
    load("mask", mask_hbm, mask)
    load("mask_coarse", mask_coarse_hbm, mask_coarse)
    waits = {name: once(name) for name in list(copies)}

    def mask_of(name, source, target):
        waits[name]()
        return mask_tile(source, target)

    write_row_table(row_ref, fine, coarse)
    levels = levels_of(fine, coarse, near.shape[2], places)
    sections = [scratch[i * 11 : (i + 1) * 11] for i in range(3)]
    rest = scratch[33:]
    half = len(rest) // 2
    pairs = [rest[:half], rest[half:]]
    specs = [section[9:] for section in sections]
    masks = (lambda: mask_of("mask", mask, pad), lambda: mask_of("mask_coarse", mask_coarse, pad_coarse))
    tables = (waits["fine"], waits["coarse"])

    def section(z, strips, first=lambda: None):
        return transform(levels, strips, row_ref, table_ref, (first,) + tables, sections[z][:9], specs[z])

    def pair(d):
        *pair_scratch, last_fine, last_coarse = pairs[d - 1]
        yield from correlate_pair(
            levels, specs[0], specs[d], masks, table_ref, shift_at, map_at, waits["shift"], pair_scratch,
            (last_fine, last_coarse))
        for i, (source, target) in enumerate(((last_fine, out_fine), (last_coarse, out_coarse))):
            store = pltpu.make_async_copy(source, target.at[0, d - 1], sems.at[6 + 2 * (d - 1) + i])
            store.start()
            stores.append(store)

    stores = []
    run_staggered([
        ("near", section(1, (near, rim_near)), set()),
        ("own", section(0, (own, rim), waits["own"]), set()),
        ("far", section(2, (far, rim_far)), set()),
        ("first", pair(1), {"near", "own"}),
        ("second", pair(2), {"far", "own"}),
    ])
    for store in stores:
        store.wait()


def correlate(own, near, far, rim, rim_near, rim_far, mask_fine, mask_coarse):
    strip_rows, width = own.shape[1:]
    fine, coarse = mask_fine.shape[1], mask_coarse.shape[1]
    ext = strip_rows + PATCH
    table, places = all_tables(fine + coarse)
    levels = levels_of(fine, coarse, width, places)
    half_rows = (fine + coarse) * HALF + NYQ
    tiles = sum(level.blocks * level.quads for level in levels)
    spec_shapes = [(level.tiles * level.rows, 2 * LANES) for level in levels]
    left_shapes = [(level.tiles * level.rows, 2 * level.pool * LANES) for level in levels]
    map_shapes = [(level.blocks, 4 * level.quads, WINDOW * WINDOW) for level in levels]
    cross_rows = sum(level.quads * level.rows for level in levels)

    section_scratch = [
        pltpu.VMEM((2 * half_rows, width), f32),
        pltpu.VMEM((2 * half_rows, width + LANES), bf16),
        pltpu.VMEM((2 * half_rows, width + LANES), bf16),
        *(pltpu.VMEM(shape, bf16) for shape in left_shapes for _ in range(2)),
        *(pltpu.VMEM(shape, f32) for shape in spec_shapes),
        *(pltpu.VMEM(shape, bf16) for shape in spec_shapes),
    ]
    pair_scratch = [
        pltpu.VMEM((cross_rows, 4 * LANES), bf16),
        pltpu.VMEM((cross_rows, 4 * LANES), bf16),
        pltpu.VMEM((cross_rows, 2 * LANES), f32),
        pltpu.VMEM((tiles, WINDOW, LANES), f32),
        pltpu.VMEM((WINDOW // 4, 4 * tiles, LANES), f32),
        *(pltpu.VMEM((4 * HALF + 2 * NYQ, level.quads * LANES), bf16) for level in levels for _ in range(level.blocks)),
        *(pltpu.VMEM(shape, f32) for shape in map_shapes),
    ]
    hbm = pl.BlockSpec(memory_space=pltpu.HBM)
    vmem = pl.BlockSpec(memory_space=pltpu.VMEM)
    own, table, mask_fine, mask_coarse = (
        pltpu.with_memory_space_constraint(value, pltpu.HBM)
        for value in (own, jnp.asarray(table), mask_fine, mask_coarse))
    return pl.pallas_call(
        functools.partial(maps_kernel, fine, coarse, places),
        out_shape=tuple(jax.ShapeDtypeStruct((1, 2) + shape, f32) for shape in map_shapes),
        in_specs=[hbm] + [vmem] * 5 + [hbm] * 3,
        out_specs=(hbm, hbm),
        scratch_shapes=[
            pltpu.VMEM(own.shape, bf16),
            pltpu.VMEM(mask_fine.shape, jnp.int32),
            pltpu.VMEM(mask_coarse.shape, jnp.int32),
            pltpu.VMEM((8, LANES), f32),
            pltpu.VMEM((8, LANES), f32),
            pltpu.VMEM((2 * half_rows, 2 * ext), bf16),
            pltpu.VMEM(table.shape, bf16),
            *section_scratch * 3,
            *pair_scratch * 2,
            pltpu.SemaphoreType.DMA((10,)),
        ],
        compiler_params=pltpu.CompilerParams(vmem_limit_bytes=36 * 1024 * 1024),
        name="maps",
    )(own, near, far, rim, rim_near, rim_far, mask_fine, mask_coarse, table)


def local(sections, mask_fine, mask_coarse):
    far = from_device(sections, 2, 0)
    near = from_device(sections, 1, 0)
    rims = [from_device(sections, z, 1) for z in range(3)]
    return correlate(sections, near, far, *rims, mask_fine, mask_coarse)


def solution(mesh):
    in_specs = (
        P("sec", "strip", "groups"),
        P("sec", "strip", "groups"),
        P("sec", "strip", "groups"),
    )
    out_specs = (P("sec", None, "strip", "groups", None), P("sec", None, "strip", "groups", None))
    return jax.shard_map(local, mesh=mesh, in_specs=in_specs, out_specs=out_specs, check_vma=False)
```

```python
import functools

import jax
import jax.numpy as jnp
import numpy as np
from jax import lax
from jax.experimental import pallas as pl
from jax.experimental.pallas import tpu as pltpu
from jax.sharding import PartitionSpec as P

PATCH = 64
STRIDE = 32
WINDOW = 32
HALF = PATCH // 2
LANES = 128
NYQ = 16

f32 = jnp.float32
bf16 = jnp.bfloat16


def from_device(value, sec_steps, strip_steps):
    secs, strips = lax.axis_size("sec"), lax.axis_size("strip")
    pairs = []
    for sec in range(secs - sec_steps):
        for strip in range(strips - strip_steps):
            pairs.append(((sec + sec_steps) * strips + strip + strip_steps, sec * strips + strip))
    return lax.ppermute(value, ("sec", "strip"), pairs)


def wave(phase):
    turns = np.arange(PATCH) * (2 * np.pi / PATCH)
    cos = np.round(np.cos(turns), 14)
    sin = np.round(np.sin(turns), 14)
    phase = np.mod(phase, PATCH)
    return cos[phase], sin[phase]


def split_table(table):
    high = table.astype(jnp.bfloat16)
    low = (table - high.astype(np.float64)).astype(jnp.bfloat16)
    return high, low


def stacked(table):
    return np.concatenate(split_table(table), axis=0)


def fine_table():
    c, s = wave(np.arange(PATCH)[:, None] * np.arange(PATCH)[None, :])
    table = np.zeros((2, 2, PATCH, 2, 2, PATCH))
    for p in range(2):
        table[0, p, :, 0, p] = c
        table[1, p, :, 0, p] = -s
        table[0, p, :, 1, p] = -s
        table[1, p, :, 1, p] = -c
    return stacked(table.reshape(4 * PATCH, 4 * PATCH))


def coarse_table():
    c, s = wave((np.arange(2 * PATCH) // 2)[:, None] * np.arange(PATCH)[None, :])
    table = np.zeros((2, 2, 2 * PATCH, 2, 2, PATCH))
    for p in range(2):
        table[p, 0, :, 0, p] = 0.5 * c
        table[p, 1, :, 0, p] = -0.5 * s
        table[p, 0, :, 1, p] = -0.5 * s
        table[p, 1, :, 1, p] = -0.5 * c
    return stacked(table.reshape(8 * PATCH, 4 * PATCH))


def shift_tables():
    spread = 1.869545
    t = np.arange(WINDOW) - WINDOW // 2
    c, s = wave(np.arange(PATCH)[:, None] * t[None, :])
    table = np.zeros((2, 2, 2, PATCH, 2, 4, WINDOW))
    for odd in range(2):
        for p in range(2):
            table[odd, 0, p, :, 0, 2 * p + odd] = c
            table[odd, 1, p, :, 0, 2 * p + odd] = -s
            table[odd, 0, p, :, 1, 2 * p + odd] = s
            table[odd, 1, p, :, 1, 2 * p + odd] = c
    along_t = (spread * table.reshape(8 * PATCH, 8 * WINDOW)).astype(jnp.bfloat16)
    c, s = wave(t[:, None] * np.arange(HALF)[None, :])
    weight = np.where(np.arange(HALF) == 0, 1.0, 2.0)
    nyquist = np.repeat(wave(HALF * t)[0][:, None], NYQ, axis=1)
    along_s = np.concatenate([c * weight, -s * weight, nyquist], axis=1) / (spread * PATCH**3)
    high, low = split_table(along_s)
    along_s = np.concatenate(
        [np.concatenate([high, high], axis=1), np.concatenate([low, np.zeros_like(low)], axis=1)], axis=0)
    return along_t, along_s


class Level:
    def __init__(self, pool, blocks, width, table):
        self.pool, self.first, self.blocks, self.table = pool, blocks[0], len(blocks), table
        self.quads = width // (4 * pool * STRIDE)
        self.tiles = 2 * self.quads
        self.body = self.blocks * HALF
        self.half = -(-self.quads * self.blocks // 8) * 8
        self.rows = self.tiles * self.body + 2 * self.half
        self.cross_body = self.quads * self.body
        self.cross_rows = self.cross_body + -(-self.half // 16) * 16

    def window(self, tile, p):
        quad, odd = divmod(tile, 2)
        return self.pool * LANES * quad + LANES * p + self.pool * STRIDE * odd

    def nyquist_row(self, tile, b):
        quad, odd = divmod(tile, 2)
        return odd * self.half + quad * self.blocks + b


def row_places(levels):
    at, places = 0, []
    for level in levels:
        places.append([at, at + level.body])
        at += level.body + 2 * level.half
    for level, place in zip(levels, places):
        place.append(at)
        at += level.body
    return places, at


def row_table(levels, ext):
    places, size = row_places(levels)
    table = np.zeros((size, ext))
    k = np.arange(HALF)[:, None]
    for level, (cos_at, nyquist_at, sin_at) in zip(levels, places):
        pool = level.pool
        x = np.arange(pool * PATCH) // pool
        c, s = wave(k * x[None, :])
        for b in range(level.blocks):
            first = (level.first + b) * pool * STRIDE
            columns = slice(first, first + x.size)
            table[cos_at + b * HALF : cos_at + (b + 1) * HALF, columns] = c / pool
            table[sin_at + b * HALF : sin_at + (b + 1) * HALF, columns] = s / pool
            for tile in range(level.tiles):
                table[nyquist_at + level.nyquist_row(tile, b), columns] = wave(HALF * x)[0] / pool
    return np.concatenate(split_table(table), axis=1)


def split(value):
    high = value.astype(bf16)
    return high, (value - high.astype(f32)).astype(bf16)


def dot(left, right):
    return jnp.dot(left, right, preferred_element_type=f32)


def dot3(high, low, table_ref, at):
    depth = high.shape[1]
    table_high = table_ref[at : at + depth]
    table_low = table_ref[at + depth : at + 2 * depth]
    return dot(
        jnp.concatenate([high, low, high], axis=1),
        jnp.concatenate([table_high, table_high, table_low], axis=0))


def cosine(turns):
    turns = turns + PATCH // 4
    part = (turns & (HALF - 1)) - PATCH // 4
    angle = part.astype(f32) * (2 * np.pi / PATCH)
    square = angle * angle
    value = jnp.full(square.shape, 1.0 / 479001600, f32)
    for term in (-1.0 / 3628800, 1.0 / 40320, -1.0 / 720, 1.0 / 24, -0.5, 1.0):
        value = value * square + term
    return jnp.where((turns & HALF) == 0, value, -value)


def write_row_table(row_ref, level):
    (cos_at, nyquist_at, sin_at), = row_places([level])[0]
    ext = row_ref.shape[1] // 2

    def put(at, value):
        high, low = split(value)
        row_ref[at : at + value.shape[0], :ext] = high
        row_ref[at : at + value.shape[0], ext:] = low

    def inside(x):
        return jnp.where((x >= 0) & (x < PATCH), 1.0, 0.0)

    k = lax.broadcasted_iota(jnp.int32, (HALF, ext), 0)
    for b in range(level.blocks):
        x = lax.broadcasted_iota(jnp.int32, (HALF, ext), 1) - (level.first + b) * STRIDE
        put(cos_at + b * HALF, cosine(k * x) * inside(x))
        put(sin_at + b * HALF, cosine(k * x - PATCH // 4) * inside(x))
    row = lax.broadcasted_iota(jnp.int32, (2 * level.half, ext), 0)
    x = lax.broadcasted_iota(jnp.int32, (2 * level.half, ext), 1)
    x = x - (level.first + lax.rem(lax.rem(row, level.half), level.blocks)) * STRIDE
    put(nyquist_at, cosine(x * HALF) * inside(x))


def all_rows(value):
    for step in (4, 2, 1):
        value = value + pltpu.roll(value, step, 0)
    return value


def gather_windows(level, place, t_ref, halves, left):
    cos_at, nyquist_at, sin_at = place
    body, end = level.body, level.tiles * level.body
    for p in range(level.pool):
        for source, target in zip(halves, left):
            for tile in range(level.tiles):
                at = level.window(tile, p)
                for half, start in enumerate((cos_at, sin_at)):
                    target[tile * body : (tile + 1) * body, (2 * p + half) * LANES : (2 * p + half + 1) * LANES] = (
                        source[start : start + body, at : at + LANES])
        row = lax.broadcasted_iota(jnp.int32, (2 * level.half, LANES), 0)
        nyquist = jnp.zeros((2 * level.half, LANES), f32)
        for tile in range(level.tiles):
            at, first = level.window(tile, p), level.nyquist_row(tile, 0)
            value = t_ref[nyquist_at : nyquist_at + 2 * level.half, at : at + LANES]
            nyquist = jnp.where((row >= first) & (row < first + level.blocks), value, nyquist)
        for target, part in zip(left, split(nyquist)):
            target[end:, 2 * p * LANES : (2 * p + 1) * LANES] = part
            target[end:, (2 * p + 1) * LANES : (2 * p + 2) * LANES] = jnp.zeros(part.shape, bf16)


def spectrum_power(level, f_ref):
    sub = lax.broadcasted_iota(jnp.int32, (8, LANES), 0)
    lane = lax.broadcasted_iota(jnp.int32, (8, LANES), 1)
    dc = (sub == 0) & (lane % PATCH == 0)
    group = lax.broadcasted_iota(jnp.int32, (LANES, LANES), 0) // PATCH
    same = group == lax.broadcasted_iota(jnp.int32, (LANES, LANES), 1) // PATCH
    ones = jnp.where(same, 1.0, 0.0).astype(bf16)

    def square(at):
        re, im = f_ref[at : at + 8, :LANES], f_ref[at : at + 8, LANES:]
        return re * re + im * im

    tails = [square(level.tiles * level.body + at) for at in range(0, 2 * level.half, 8)]
    sums = []
    for tile in range(level.tiles):
        for b in range(level.blocks):
            base = tile * level.body + b * HALF
            total = jnp.where(dc, 0.0, square(base))
            head = jnp.where(sub == 0, total, 0.0)
            for r in range(8, HALF, 8):
                total = total + square(base + r)
            row = level.nyquist_row(tile, b)
            sums.append(2.0 * total - head + jnp.where(sub == row % 8, tails[row // 8], 0.0))
    if len(sums) % 2:
        sums.append(jnp.zeros_like(sums[0]))
    high, low = split(jnp.concatenate(sums, axis=0))
    return dot(jnp.concatenate([high, low], axis=1), jnp.concatenate([ones, ones], axis=0))


def scale_spectrum(level, f_ref, sums, spec_ref):
    sub = lax.broadcasted_iota(jnp.int32, (8, 2 * LANES), 0)
    lane = lax.broadcasted_iota(jnp.int32, (8, 2 * LANES), 1)
    dc = (sub == 0) & (lane % PATCH == 0)
    end = level.tiles * level.body
    tails = [f_ref[end + at : end + at + 8] for at in range(0, 2 * level.half, 8)]
    scaled = [jnp.zeros_like(tail) for tail in tails]
    for tile in range(level.tiles):
        for b in range(level.blocks):
            number = (tile * level.blocks + b) * 8
            scale = lax.rsqrt(all_rows(sums[number : number + 8]) * (1.0 / PATCH**4) + 1e-05)
            scale = jnp.concatenate([scale, scale], axis=1)
            for r in range(0, HALF, 16):
                at = tile * level.body + b * HALF + r
                head = f_ref[at : at + 8]
                if r == 0:
                    head = jnp.where(dc, 0.0, head)
                both = jnp.concatenate([head * scale, f_ref[at + 8 : at + 16] * scale], axis=0)
                spec_ref[at : at + 16] = both.astype(bf16)
            row = level.nyquist_row(tile, b)
            scaled[row // 8] = jnp.where(sub == row % 8, tails[row // 8] * scale, scaled[row // 8])
    spec_ref[end:] = jnp.concatenate(scaled, axis=0).astype(bf16)


def transform(levels, strips, row_ref, table_ref, ready, scratch, specs):
    count = len(levels)
    t_ref, *halves = scratch[:3]
    lefts = [scratch[3 + 2 * i : 5 + 2 * i] for i in range(count)]
    f_refs = scratch[3 + 2 * count : 3 + 3 * count]
    places, size = row_places(levels)
    ready[0]()
    x = jnp.concatenate([strip[0] for strip in strips], axis=0)
    width = x.shape[1]
    t_ref[:, :width] = dot(row_ref[...], jnp.concatenate([x, x], axis=0))
    t_ref[:, width:] = jnp.zeros((size, LANES), f32)
    yield
    for level, place in zip(levels, places):
        for start in (place[0], place[2]):
            for r in range(start, start + level.body, 16):
                for ref, half in zip(halves, split(t_ref[r : r + 16])):
                    ref[r : r + 16] = half
    for level, place, left in zip(levels, places, lefts):
        gather_windows(level, place, t_ref, halves, left)
        yield
    for level, left, f_ref, wait in zip(levels, lefts, f_refs, ready[1:]):
        wait()
        f_ref[...] = dot3(left[0][...], left[1][...], table_ref, level.table)
        yield
    sums = []
    for level, f_ref in zip(levels, f_refs):
        sums.append(spectrum_power(level, f_ref))
        yield
    for level, f_ref, total, spec_ref in zip(levels, f_refs, sums, specs):
        scale_spectrum(level, f_ref, total, spec_ref)
        yield


def run_staggered(tasks):
    active, waiting = [], list(tasks)
    while waiting or active:
        if waiting:
            active.append(waiting.pop(0))
        for task in list(active):
            if next(task, True):
                active.remove(task)


def write_maps(levels, specs, masks, table_ref, shift_at, map_at, scratch, outs):
    cross_ref, y_ref, maps_ref, rows_ref, *stacks = scratch
    pairs = len(specs) - 1
    base = 0
    for index, level in enumerate(levels):
        for d in range(pairs):
            own, other = specs[0][index], specs[d + 1][index]

            def cross(at, rows):
                a, b = own[at : at + rows].astype(f32), other[at : at + rows].astype(f32)
                ar, ai, br, bi = a[:, :LANES], a[:, LANES:], b[:, :LANES], b[:, LANES:]
                return jnp.concatenate([ar * br + ai * bi, ar * bi - ai * br], axis=1)

            for tile in range(level.tiles):
                quad, odd = divmod(tile, 2)
                for r in range(0, level.body, 16):
                    to = base + quad * level.body + r
                    cross_ref[to : to + 16, 2 * odd * LANES : 2 * (odd + 1) * LANES] = (
                        cross(tile * level.body + r, 16).astype(bf16))
            nyquist = cross(level.tiles * level.body, 2 * level.half)
            nyquist = jnp.concatenate([nyquist[: level.half], nyquist[level.half :]], axis=1)
            to = base + level.cross_body
            spare = level.cross_rows - level.cross_body - level.half
            if spare:
                nyquist = jnp.concatenate([nyquist, jnp.zeros((spare, 4 * LANES), f32)], axis=0)
            cross_ref[to : base + level.cross_rows] = nyquist.astype(bf16)
            base += level.cross_rows
    y_ref[...] = dot(cross_ref[...], table_ref[shift_at : shift_at + 4 * LANES])
    base = tile = 0
    starts = {}
    row = lax.broadcasted_iota(jnp.int32, (NYQ, LANES), 0)
    for index, level in enumerate(levels):
        for b in range(level.blocks):
            stack_ref = stacks[index]
            for d in range(pairs):
                first = base + d * level.cross_rows
                nyq_at = first + level.cross_body
                nyquist = y_ref[nyq_at : nyq_at + NYQ, :LANES]
                for quad in range(level.quads):
                    top = first + quad * level.body + b * HALF
                    column = (d * level.quads + quad) * LANES
                    for at, value in (
                        (0, y_ref[top : top + HALF, :LANES]),
                        (HALF, y_ref[top : top + HALF, LANES:]),
                        (2 * HALF, jnp.where(row == quad * level.blocks + b, nyquist, 0.0)),
                    ):
                        for half, part in enumerate(split(value)):
                            to = half * (2 * HALF + NYQ) + at
                            stack_ref[to : to + value.shape[0], column : column + LANES] = part
            both = dot(table_ref[map_at : map_at + 2 * WINDOW, : stack_ref.shape[0]], stack_ref[...])
            maps = both[:WINDOW] + both[WINDOW:]
            for d in range(pairs):
                starts[index, d, b] = tile
                for quad in range(level.quads):
                    column = (d * level.quads + quad) * LANES
                    maps_ref[tile] = maps[:, column : column + LANES]
                    tile += 1
        base += pairs * level.cross_rows
    kept = [jnp.transpose(mask()) for mask in masks]
    lanes = lax.broadcasted_iota(jnp.int32, (tile, LANES), 1) // WINDOW
    for big in range(WINDOW // 4):
        rows = [maps_ref[:, 4 * big + r, :] for r in range(4)]
        for g in range(4):
            value = None
            for r in range(4):
                moved = rows[r] if r == g else pltpu.roll(rows[r], (WINDOW * (r - g)) % LANES, 1)
                value = moved if value is None else jnp.where(lanes == r, moved, value)
            rows_ref[big, pl.ds(g, tile, stride=4), :] = value
        for index, (level, out) in enumerate(zip(levels, outs)):
            for b in range(level.blocks):
                column = kept[index][: 4 * level.quads, level.first + b : level.first + b + 1]
                for d in range(pairs):
                    at = 4 * starts[index, d, b]
                    out[d, b, :, big * LANES : (big + 1) * LANES] = rows_ref[big, at : at + 4 * level.quads] * column


def mask_tile(mask_ref, pad_ref):
    pad_ref[...] = jnp.zeros(pad_ref.shape, f32)
    pad_ref[: mask_ref.shape[1], : mask_ref.shape[2]] = mask_ref[0].astype(f32)
    return pad_ref[...]


def section_scratch(levels, width):
    size = row_places(levels)[1]
    return [
        pltpu.VMEM((size, width + LANES), f32),
        pltpu.VMEM((size, width + LANES), bf16),
        pltpu.VMEM((size, width + LANES), bf16),
        *(pltpu.VMEM((level.rows, 2 * level.pool * LANES), bf16) for level in levels for _ in range(2)),
        *(pltpu.VMEM((level.rows, 2 * LANES), f32) for level in levels),
        *(pltpu.VMEM((level.rows, 2 * LANES), bf16) for level in levels),
    ]


def pair_scratch(levels):
    rows = sum(2 * level.cross_rows for level in levels)
    tiles = sum(2 * level.blocks * level.quads for level in levels)
    return [
        pltpu.VMEM((rows, 4 * LANES), bf16),
        pltpu.VMEM((rows, 2 * LANES), f32),
        pltpu.VMEM((tiles, WINDOW, LANES), f32),
        pltpu.VMEM((WINDOW // 4, 4 * tiles, LANES), f32),
        *(pltpu.VMEM((4 * HALF + 2 * NYQ, 2 * level.quads * LANES), bf16) for level in levels),
    ]


def all_maps(levels, strips, first_ready, row_ref, table_ref, tables_ready, shift_ready, places, masks, scratch, outs):
    size = 3 + 4 * len(levels)
    sections = [scratch[z * size : (z + 1) * size] for z in range(3)]
    specs = [section[size - len(levels) :] for section in sections]
    run_staggered([
        transform(
            levels, strips[z], row_ref, table_ref, (first_ready if z == 0 else lambda: None,) + tables_ready,
            sections[z], specs[z])
        for z in (1, 2, 0)])
    shift_ready()
    write_maps(levels, specs, masks, table_ref, *places, scratch[3 * size :], outs)


def copier(sems):
    used = []

    def start(source, target):
        copy = pltpu.make_async_copy(source, target, sems.at[len(used)])
        used.append(copy)
        copy.start()
        return copy.wait

    return start


def inner_kernel(
    levels, cuts,
    own_hbm, near, far, mask_hbm, table_hbm,
    maps, table_ref,
    own, mask, pad, row_ref, *rest,
):
    *scratch, sems = rest
    start = copier(sems)

    def table(first, last):
        piece = pl.ds(first, last - first)
        return start(table_hbm.at[piece], table_ref.at[piece])

    fine_at, shift_at, map_at, coarse_at, end = cuts
    fine_ready = table(fine_at, shift_at)
    own_ready = start(own_hbm, own)
    shift_ready = table(shift_at, coarse_at)
    mask_ready = start(mask_hbm, mask)
    coarse_ready = table(coarse_at, end)
    write_row_table(row_ref, levels[0])
    waited = []

    def fine_once():
        if not waited:
            fine_ready()
            waited.append(True)

    def mask_rows():
        mask_ready()
        return mask_tile(mask, pad)

    all_maps(
        levels, ((own,), (near,), (far,)), own_ready, row_ref, table_ref, (fine_once,), shift_ready,
        (shift_at, map_at), (mask_rows,), scratch, (maps,))
    coarse_ready()


def outer_kernel(
    levels, cuts, inner, row_at,
    own_hbm, near, far, rim, rim_near, rim_far, mask_hbm, mask_coarse_hbm, table_ref, inner_maps,
    out_fine, out_coarse,
    own, mask, mask_coarse, pad, pad_coarse, maps, maps_coarse, *rest,
):
    *scratch, sems = rest
    start = copier(sems)
    own_ready = start(own_hbm, own)
    mask_ready = start(mask_hbm, mask)
    mask_coarse_ready = start(mask_coarse_hbm, mask_coarse)
    stores = [start(inner_maps.at[d], out_fine.at[0, d, pl.ds(0, inner)]) for d in range(2)]

    def mask_rows():
        mask_ready()
        return mask_tile(mask, pad)

    def mask_coarse_rows():
        mask_coarse_ready()
        return mask_tile(mask_coarse, pad_coarse)

    fine_at, shift_at, map_at, coarse_at, end = cuts
    row_ref = table_ref.at[pl.ds(row_at, row_places(levels)[1])]
    all_maps(
        levels, ((own, rim), (near, rim_near), (far, rim_far)), own_ready, row_ref, table_ref,
        (lambda: None,) * 2, lambda: None, (shift_at, map_at), (mask_rows, mask_coarse_rows), scratch,
        (maps, maps_coarse))
    for d in range(2):
        stores.append(start(maps.at[d], out_fine.at[0, d, pl.ds(inner, levels[0].blocks)]))
        stores.append(start(maps_coarse.at[d], out_coarse.at[0, d]))
    for wait in stores:
        wait()


def correlate(own, near, far, rim, rim_near, rim_far, mask_fine, mask_coarse):
    strip_rows, width = own.shape[1:]
    fine, coarse = mask_fine.shape[1], mask_coarse.shape[1]
    inner = fine - 1
    shift, map_ = shift_tables()
    tables = [fine_table(), shift, map_, coarse_table()]
    cuts = [int(at) for at in np.cumsum([0] + [table.shape[0] for table in tables])]
    inner_levels = [Level(1, range(inner), width, cuts[0])]
    outer_levels = [Level(1, range(inner, fine), width, cuts[0]), Level(2, range(coarse), width, cuts[3])]
    row_at = cuts[4]
    tables.append(row_table(outer_levels, strip_rows + PATCH))
    columns = max(table.shape[1] for table in tables)
    table = np.concatenate([np.pad(table, ((0, 0), (0, columns - table.shape[1]))) for table in tables])
    cuts[4] = table.shape[0]

    shifts = WINDOW * WINDOW
    hbm = pl.BlockSpec(memory_space=pltpu.HBM)
    vmem = pl.BlockSpec(memory_space=pltpu.VMEM)
    params = pltpu.CompilerParams(vmem_limit_bytes=28 * 1024 * 1024)
    own, table, mask_fine, mask_coarse = (
        pltpu.with_memory_space_constraint(value, pltpu.HBM)
        for value in (own, jnp.asarray(table), mask_fine, mask_coarse))

    def cost(flops):
        return pl.CostEstimate(flops=flops, bytes_accessed=4 * 10**6, transcendentals=0)

    maps, handed = pl.pallas_call(
        functools.partial(inner_kernel, inner_levels, cuts),
        out_shape=(
            jax.ShapeDtypeStruct((2, inner, 4 * inner_levels[0].quads, shifts), f32),
            jax.ShapeDtypeStruct(table.shape, bf16),
        ),
        in_specs=[hbm, vmem, vmem, hbm, hbm],
        out_specs=(vmem, vmem),
        scratch_shapes=[
            pltpu.VMEM(own.shape, bf16),
            pltpu.VMEM(mask_fine.shape, jnp.int32),
            pltpu.VMEM((8, LANES), f32),
            pltpu.VMEM((row_places(inner_levels)[1], 2 * strip_rows), bf16),
            *section_scratch(inner_levels, width) * 3,
            *pair_scratch(inner_levels),
            pltpu.SemaphoreType.DMA((5,)),
        ],
        compiler_params=params,
        cost_estimate=cost(3 * 10**9),
        name="inner_blocks",
    )(own, near, far, mask_fine, table)
    return pl.pallas_call(
        functools.partial(outer_kernel, outer_levels, cuts, inner, row_at),
        out_shape=(
            jax.ShapeDtypeStruct((1, 2, fine, 4 * outer_levels[0].quads, shifts), f32),
            jax.ShapeDtypeStruct((1, 2, coarse, 4 * outer_levels[1].quads, shifts), f32),
        ),
        in_specs=[hbm] + [vmem] * 5 + [hbm] * 2 + [vmem] * 2,
        out_specs=(hbm, hbm),
        scratch_shapes=[
            pltpu.VMEM(own.shape, bf16),
            pltpu.VMEM(mask_fine.shape, jnp.int32),
            pltpu.VMEM(mask_coarse.shape, jnp.int32),
            pltpu.VMEM((8, LANES), f32),
            pltpu.VMEM((8, LANES), f32),
            *(pltpu.VMEM((2, level.blocks, 4 * level.quads, shifts), f32) for level in outer_levels),
            *section_scratch(outer_levels, width) * 3,
            *pair_scratch(outer_levels),
            pltpu.SemaphoreType.DMA((9,)),
        ],
        compiler_params=params,
        cost_estimate=cost(4 * 10**9),
        name="outer_blocks",
    )(own, near, far, rim, rim_near, rim_far, mask_fine, mask_coarse, handed, maps)


def local(sections, mask_fine, mask_coarse):
    far = from_device(sections, 2, 0)
    near = from_device(sections, 1, 0)
    rims = [from_device(sections, z, 1) for z in range(3)]
    return correlate(sections, near, far, *rims, mask_fine, mask_coarse)


def solution(mesh):
    in_specs = (
        P("sec", "strip", "groups"),
        P("sec", "strip", "groups"),
        P("sec", "strip", "groups"),
    )
    out_specs = (P("sec", None, "strip", "groups", None), P("sec", None, "strip", "groups", None))
    return jax.shard_map(local, mesh=mesh, in_specs=in_specs, out_specs=out_specs, check_vma=False)
```

```python
import functools

import jax
import jax.numpy as jnp
import numpy as np
from jax import lax
from jax.experimental import pallas as pl
from jax.experimental.pallas import tpu as pltpu
from jax.sharding import PartitionSpec as P

PATCH = 64
STRIDE = 32
WINDOW = 32
HALF = PATCH // 2
LANES = 128
NYQ = 16

f32 = jnp.float32
bf16 = jnp.bfloat16


def from_device(value, sec_steps, strip_steps):
    secs, strips = lax.axis_size("sec"), lax.axis_size("strip")
    pairs = []
    for sec in range(secs - sec_steps):
        for strip in range(strips - strip_steps):
            pairs.append(((sec + sec_steps) * strips + strip + strip_steps, sec * strips + strip))
    return lax.ppermute(value, ("sec", "strip"), pairs)


def wave(phase):
    turns = np.arange(PATCH) * (2 * np.pi / PATCH)
    cos = np.round(np.cos(turns), 14)
    sin = np.round(np.sin(turns), 14)
    phase = np.mod(phase, PATCH)
    return cos[phase], sin[phase]


def split_table(table):
    high = table.astype(jnp.bfloat16)
    low = (table - high.astype(np.float64)).astype(jnp.bfloat16)
    return high, low


def stacked(table):
    return np.concatenate(split_table(table), axis=0)


def fine_table():
    c, s = wave(np.arange(PATCH)[:, None] * np.arange(PATCH)[None, :])
    table = np.zeros((2, 2, PATCH, 2, 2, PATCH))
    for p in range(2):
        table[0, p, :, 0, p] = c
        table[1, p, :, 0, p] = -s
        table[0, p, :, 1, p] = -s
        table[1, p, :, 1, p] = -c
    return stacked(table.reshape(4 * PATCH, 4 * PATCH))


def coarse_table():
    c, s = wave((np.arange(2 * PATCH) // 2)[:, None] * np.arange(PATCH)[None, :])
    table = np.zeros((2, 2, 2 * PATCH, 2, 2, PATCH))
    for p in range(2):
        table[p, 0, :, 0, p] = 0.5 * c
        table[p, 1, :, 0, p] = -0.5 * s
        table[p, 0, :, 1, p] = -0.5 * s
        table[p, 1, :, 1, p] = -0.5 * c
    return stacked(table.reshape(8 * PATCH, 4 * PATCH))


def shift_tables():
    spread = 1.869545
    t = np.arange(WINDOW) - WINDOW // 2
    c, s = wave(np.arange(PATCH)[:, None] * t[None, :])
    table = np.zeros((2, 2, 2, PATCH, 2, 4, WINDOW))
    for odd in range(2):
        for p in range(2):
            table[odd, 0, p, :, 0, 2 * p + odd] = c
            table[odd, 1, p, :, 0, 2 * p + odd] = -s
            table[odd, 0, p, :, 1, 2 * p + odd] = s
            table[odd, 1, p, :, 1, 2 * p + odd] = c
    along_t = (spread * table.reshape(8 * PATCH, 8 * WINDOW)).astype(jnp.bfloat16)
    c, s = wave(t[:, None] * np.arange(HALF)[None, :])
    weight = np.where(np.arange(HALF) == 0, 1.0, 2.0)
    nyquist = np.repeat(wave(HALF * t)[0][:, None], NYQ, axis=1)
    along_s = np.concatenate([c * weight, -s * weight, nyquist], axis=1) / (spread * PATCH**3)
    high, low = split_table(along_s)
    along_s = np.concatenate(
        [np.concatenate([high, high], axis=1), np.concatenate([low, np.zeros_like(low)], axis=1)], axis=0)
    return along_t, along_s


class Level:
    def __init__(self, pool, blocks, width, table):
        self.pool, self.first, self.blocks, self.table = pool, blocks[0], len(blocks), table
        self.quads = width // (4 * pool * STRIDE)
        self.tiles = 2 * self.quads
        self.body = self.blocks * HALF
        self.half = -(-self.quads * self.blocks // 8) * 8
        self.rows = self.tiles * self.body + 2 * self.half
        self.cross_body = self.quads * self.body
        self.cross_rows = self.cross_body + -(-self.half // 16) * 16

    def window(self, tile, p):
        quad, odd = divmod(tile, 2)
        return self.pool * LANES * quad + LANES * p + self.pool * STRIDE * odd

    def nyquist_row(self, tile, b):
        quad, odd = divmod(tile, 2)
        return odd * self.half + quad * self.blocks + b


def row_places(levels):
    at, places = 0, []
    for level in levels:
        places.append([at, at + level.body])
        at += level.body + 2 * level.half
    for level, place in zip(levels, places):
        place.append(at)
        at += level.body
    return places, at


def row_table(levels, ext):
    places, size = row_places(levels)
    table = np.zeros((size, ext))
    k = np.arange(HALF)[:, None]
    for level, (cos_at, nyquist_at, sin_at) in zip(levels, places):
        pool = level.pool
        x = np.arange(pool * PATCH) // pool
        c, s = wave(k * x[None, :])
        for b in range(level.blocks):
            first = (level.first + b) * pool * STRIDE
            columns = slice(first, first + x.size)
            table[cos_at + b * HALF : cos_at + (b + 1) * HALF, columns] = c / pool
            table[sin_at + b * HALF : sin_at + (b + 1) * HALF, columns] = s / pool
            for tile in range(level.tiles):
                table[nyquist_at + level.nyquist_row(tile, b), columns] = wave(HALF * x)[0] / pool
    return np.concatenate(split_table(table), axis=1)


def split(value):
    high = value.astype(bf16)
    return high, (value - high.astype(f32)).astype(bf16)


def dot(left, right):
    return jnp.dot(left, right, preferred_element_type=f32)


def dot3(high, low, table_ref, at):
    depth = high.shape[1]
    table_high = table_ref[at : at + depth]
    table_low = table_ref[at + depth : at + 2 * depth]
    return dot(
        jnp.concatenate([high, low, high], axis=1),
        jnp.concatenate([table_high, table_high, table_low], axis=0))


def cosine(turns):
    turns = turns + PATCH // 4
    part = (turns & (HALF - 1)) - PATCH // 4
    angle = part.astype(f32) * (2 * np.pi / PATCH)
    square = angle * angle
    value = jnp.full(square.shape, 1.0 / 479001600, f32)
    for term in (-1.0 / 3628800, 1.0 / 40320, -1.0 / 720, 1.0 / 24, -0.5, 1.0):
        value = value * square + term
    return jnp.where((turns & HALF) == 0, value, -value)


def write_row_table(row_ref, level):
    (cos_at, nyquist_at, sin_at), = row_places([level])[0]
    ext = row_ref.shape[1] // 2

    def put(at, value):
        high, low = split(value)
        row_ref[at : at + value.shape[0], :ext] = high
        row_ref[at : at + value.shape[0], ext:] = low

    def inside(x):
        return jnp.where((x >= 0) & (x < PATCH), 1.0, 0.0)

    k = lax.broadcasted_iota(jnp.int32, (HALF, ext), 0)
    for b in range(level.blocks):
        x = lax.broadcasted_iota(jnp.int32, (HALF, ext), 1) - (level.first + b) * STRIDE
        put(cos_at + b * HALF, cosine(k * x) * inside(x))
        put(sin_at + b * HALF, cosine(k * x - PATCH // 4) * inside(x))
    row = lax.broadcasted_iota(jnp.int32, (2 * level.half, ext), 0)
    x = lax.broadcasted_iota(jnp.int32, (2 * level.half, ext), 1)
    x = x - (level.first + lax.rem(lax.rem(row, level.half), level.blocks)) * STRIDE
    put(nyquist_at, cosine(x * HALF) * inside(x))


def write_fine_table(table_ref, at):
    y = lax.broadcasted_iota(jnp.int32, (PATCH, LANES), 0)
    lane = lax.broadcasted_iota(jnp.int32, (PATCH, LANES), 1)
    frequency = lane & (PATCH - 1)
    c, s = cosine(y * frequency), cosine(y * frequency - PATCH // 4)
    depth = 4 * PATCH
    for p in range(2):
        mine = (lane >= PATCH) if p else (lane < PATCH)
        cos, minus_cos, minus_sin = (jnp.where(mine, value, 0.0) for value in (c, -c, -s))
        for number, pair in enumerate(((cos, minus_sin), (minus_sin, minus_cos))):
            to = at + (2 * number + p) * PATCH
            for half, value in enumerate(pair):
                for level, part in enumerate(split(value)):
                    table_ref[to + level * depth : to + level * depth + PATCH, half * LANES : (half + 1) * LANES] = part


def all_rows(value):
    for step in (4, 2, 1):
        value = value + pltpu.roll(value, step, 0)
    return value


def left_of(level, place, half_ref, odd_ref):
    cos_at, nyquist_at, sin_at = place
    pieces = []
    for tile in range(level.tiles):
        if tile % 2:
            pieces.append(odd_ref[tile // 2 * level.body : (tile // 2 + 1) * level.body])
        else:
            columns = []
            for p in range(level.pool):
                at = level.window(tile, p)
                columns += [half_ref[start : start + level.body, at : at + LANES] for start in (cos_at, sin_at)]
            pieces.append(jnp.concatenate(columns, axis=1))
    pieces.append(odd_ref[level.quads * level.body :])
    return jnp.concatenate(pieces, axis=0)


def gather_windows(level, place, t_ref, halves, odds):
    cos_at, nyquist_at, sin_at = place
    body, end = level.body, level.quads * level.body
    row = lax.broadcasted_iota(jnp.int32, (2 * level.half, LANES), 0)
    for p in range(level.pool):
        for source, target in zip(halves, odds):
            for tile in range(1, level.tiles, 2):
                at = level.window(tile, p)
                for half, start in enumerate((cos_at, sin_at)):
                    to = tile // 2 * body
                    target[to : to + body, (2 * p + half) * LANES : (2 * p + half + 1) * LANES] = (
                        source[start : start + body, at : at + LANES])
        nyquist = jnp.zeros((2 * level.half, LANES), f32)
        for tile in range(level.tiles):
            at, first = level.window(tile, p), level.nyquist_row(tile, 0)
            value = t_ref[nyquist_at : nyquist_at + 2 * level.half, at : at + LANES]
            nyquist = jnp.where((row >= first) & (row < first + level.blocks), value, nyquist)
        for target, part in zip(odds, split(nyquist)):
            target[end:, 2 * p * LANES : (2 * p + 1) * LANES] = part
            target[end:, (2 * p + 1) * LANES : (2 * p + 2) * LANES] = jnp.zeros(part.shape, bf16)


def spectrum_power(level, f_ref, sections):
    sub = lax.broadcasted_iota(jnp.int32, (8, LANES), 0)
    lane = lax.broadcasted_iota(jnp.int32, (8, LANES), 1)
    dc = (sub == 0) & (lane % PATCH == 0)
    group = lax.broadcasted_iota(jnp.int32, (LANES, LANES), 0) // PATCH
    same = group == lax.broadcasted_iota(jnp.int32, (LANES, LANES), 1) // PATCH
    ones = jnp.where(same, 1.0, 0.0).astype(bf16)

    def square(at):
        re, im = f_ref[at : at + 8, :LANES], f_ref[at : at + 8, LANES:]
        return re * re + im * im

    sums = []
    for z in sections:
        end = z * level.rows + level.tiles * level.body
        tails = [square(end + at) for at in range(0, 2 * level.half, 8)]
        for tile in range(level.tiles):
            for b in range(level.blocks):
                base = z * level.rows + tile * level.body + b * HALF
                total = jnp.where(dc, 0.0, square(base))
                head = jnp.where(sub == 0, total, 0.0)
                for r in range(8, HALF, 8):
                    total = total + square(base + r)
                row = level.nyquist_row(tile, b)
                sums.append(2.0 * total - head + jnp.where(sub == row % 8, tails[row // 8], 0.0))
    high, low = split(jnp.concatenate(sums, axis=0))
    return dot(jnp.concatenate([high, low], axis=1), jnp.concatenate([ones, ones], axis=0))


def scale_spectrum(level, f_ref, sections, sums, spec_ref):
    sub = lax.broadcasted_iota(jnp.int32, (8, 2 * LANES), 0)
    lane = lax.broadcasted_iota(jnp.int32, (8, 2 * LANES), 1)
    dc = (sub == 0) & (lane % PATCH == 0)
    number = 0
    for z in sections:
        start = z * level.rows
        end = start + level.tiles * level.body
        tails = [f_ref[end + at : end + at + 8] for at in range(0, 2 * level.half, 8)]
        scaled = [jnp.zeros_like(tail) for tail in tails]
        for tile in range(level.tiles):
            for b in range(level.blocks):
                scale = lax.rsqrt(all_rows(sums[number : number + 8]) * (1.0 / PATCH**4) + 1e-05)
                number += 8
                scale = jnp.concatenate([scale, scale], axis=1)
                for r in range(0, HALF, 16):
                    at = start + tile * level.body + b * HALF + r
                    head = f_ref[at : at + 8]
                    if r == 0:
                        head = jnp.where(dc, 0.0, head)
                    both = jnp.concatenate([head * scale, f_ref[at + 8 : at + 16] * scale], axis=0)
                    spec_ref[at : at + 16] = both.astype(bf16)
                row = level.nyquist_row(tile, b)
                scaled[row // 8] = jnp.where(sub == row % 8, tails[row // 8] * scale, scaled[row // 8])
        spec_ref[end : end + 2 * level.half] = jnp.concatenate(scaled, axis=0).astype(bf16)


def transform(levels, sections, strips, row_ref, table_ref, scratch):
    count = len(levels)
    t_ref, high_ref, low_ref = scratch[:3]
    odd_refs = scratch[3 : 3 + 2 * count]
    f_refs, spec_refs = scratch[3 + 2 * count : 3 + 3 * count], scratch[3 + 3 * count :]
    places, size = row_places(levels)
    for z in sections:
        x = jnp.concatenate([strip[0] for strip in strips[z]], axis=0)
        width = x.shape[1]
        x = jnp.concatenate([x, x], axis=0)
        for first in range(0, width, 2 * LANES):
            columns = slice(first, first + 2 * LANES)
            t = dot(row_ref[...], x[:, columns])
            for level, (cos_at, nyquist_at, sin_at) in zip(levels, places):
                for start in (cos_at, sin_at):
                    for ref, half in zip((high_ref, low_ref), split(t[start : start + level.body])):
                        ref[z, start : start + level.body, columns] = half
                rows = slice(nyquist_at, nyquist_at + 2 * level.half)
                t_ref[z, rows, columns] = t[rows]
        t_ref[z, :, width:] = jnp.zeros((size, LANES), f32)
        for ref in (high_ref, low_ref):
            ref[z, :, width:] = jnp.zeros((size, LANES), bf16)
    for index, (level, place) in enumerate(zip(levels, places)):
        odds = odd_refs[2 * index : 2 * index + 2]
        for z in sections:
            gather_windows(level, place, t_ref.at[z], (high_ref.at[z], low_ref.at[z]), [ref.at[z] for ref in odds])
    for index, (level, place) in enumerate(zip(levels, places)):
        lefts = [
            jnp.concatenate([left_of(level, place, ref.at[z], odd.at[z]) for z in sections], axis=0)
            for ref, odd in zip((high_ref, low_ref), odd_refs[2 * index : 2 * index + 2])]
        rows = slice(sections[0] * level.rows, (sections[-1] + 1) * level.rows)
        f_refs[index][rows] = dot3(*lefts, table_ref, level.table)
    for level, f_ref, spec_ref in zip(levels, f_refs, spec_refs):
        scale_spectrum(level, f_ref, sections, spectrum_power(level, f_ref, sections), spec_ref)


def write_maps(levels, specs, masks, table_ref, shift_at, map_at, scratch, outs):
    cross_ref, y_ref, maps_ref, rows_ref, *stacks = scratch
    pairs = 2
    base = 0
    for level, spec in zip(levels, specs):
        def cross(at, rows):
            a = spec[pairs * level.rows + at : pairs * level.rows + at + rows].astype(f32)
            ar, ai = a[:, :LANES], a[:, LANES:]
            for d in range(pairs):
                b = spec[d * level.rows + at : d * level.rows + at + rows].astype(f32)
                br, bi = b[:, :LANES], b[:, LANES:]
                yield base + d * level.cross_rows, jnp.concatenate([ar * br + ai * bi, ar * bi - ai * br], axis=1)

        for tile in range(level.tiles):
            quad, odd = divmod(tile, 2)
            for r in range(0, level.body, 16):
                for to, value in cross(tile * level.body + r, 16):
                    to += quad * level.body + r
                    cross_ref[to : to + 16, 2 * odd * LANES : 2 * (odd + 1) * LANES] = value.astype(bf16)
        for to, value in cross(level.tiles * level.body, 2 * level.half):
            value = jnp.concatenate([value[: level.half], value[level.half :]], axis=1)
            spare = level.cross_rows - level.cross_body - level.half
            if spare:
                value = jnp.concatenate([value, jnp.zeros((spare, 4 * LANES), f32)], axis=0)
            cross_ref[to + level.cross_body : to + level.cross_rows] = value.astype(bf16)
        base += pairs * level.cross_rows
    y_ref[...] = dot(cross_ref[...], table_ref[shift_at : shift_at + 4 * LANES])
    base = tile = 0
    starts = {}
    row = lax.broadcasted_iota(jnp.int32, (NYQ, LANES), 0)
    for index, level in enumerate(levels):
        for b in range(level.blocks):
            stack_ref = stacks[index]
            for d in range(pairs):
                first = base + d * level.cross_rows
                nyq_at = first + level.cross_body
                nyquist = y_ref[nyq_at : nyq_at + NYQ, :LANES]
                for quad in range(level.quads):
                    top = first + quad * level.body + b * HALF
                    column = (d * level.quads + quad) * LANES
                    for at, value in (
                        (0, y_ref[top : top + HALF, :LANES]),
                        (HALF, y_ref[top : top + HALF, LANES:]),
                        (2 * HALF, jnp.where(row == quad * level.blocks + b, nyquist, 0.0)),
                    ):
                        for half, part in enumerate(split(value)):
                            to = half * (2 * HALF + NYQ) + at
                            stack_ref[to : to + value.shape[0], column : column + LANES] = part
            both = dot(table_ref[map_at : map_at + 2 * WINDOW, : stack_ref.shape[0]], stack_ref[...])
            maps = both[:WINDOW] + both[WINDOW:]
            for d in range(pairs):
                starts[index, d, b] = tile
                for quad in range(level.quads):
                    column = (d * level.quads + quad) * LANES
                    maps_ref[tile] = maps[:, column : column + LANES]
                    tile += 1
        base += pairs * level.cross_rows
    kept = [jnp.transpose(mask()) for mask in masks]
    lane = lax.broadcasted_iota(jnp.int32, (tile, LANES), 1)

    def exchange(low, high, width):
        even = (lane & width) == 0
        return (
            jnp.where(even, low, pltpu.roll(high, width, 1)),
            jnp.where(even, pltpu.roll(low, LANES - width, 1), high))

    for big in range(WINDOW // 4):
        rows = [maps_ref[:, 4 * big + r, :] for r in range(4)]
        for step in (2, 1):
            for r in range(4):
                if not r & step:
                    rows[r], rows[r + step] = exchange(rows[r], rows[r + step], step * WINDOW)
        for g in range(4):
            rows_ref[big, pl.ds(g, tile, stride=4), :] = rows[g]
        for index, (level, out) in enumerate(zip(levels, outs)):
            for b in range(level.blocks):
                column = kept[index][: 4 * level.quads, level.first + b : level.first + b + 1]
                for d in range(pairs):
                    at = 4 * starts[index, d, b]
                    out[d, b, :, big * LANES : (big + 1) * LANES] = rows_ref[big, at : at + 4 * level.quads] * column


def mask_tile(mask_ref, pad_ref):
    pad_ref[...] = jnp.zeros(pad_ref.shape, f32)
    pad_ref[: mask_ref.shape[1], : mask_ref.shape[2]] = mask_ref[0].astype(f32)
    return pad_ref[...]


def section_scratch(levels, width):
    size = row_places(levels)[1]
    return [
        pltpu.VMEM((3, size, width + LANES), f32),
        pltpu.VMEM((3, size, width + LANES), bf16),
        pltpu.VMEM((3, size, width + LANES), bf16),
        *(pltpu.VMEM((3, level.quads * level.body + 2 * level.half, 2 * level.pool * LANES), bf16)
          for level in levels for _ in range(2)),
        *(pltpu.VMEM((3 * level.rows, 2 * LANES), f32) for level in levels),
        *(pltpu.VMEM((3 * level.rows, 2 * LANES), bf16) for level in levels),
    ]


def pair_scratch(levels):
    rows = sum(2 * level.cross_rows for level in levels)
    tiles = sum(2 * level.blocks * level.quads for level in levels)
    return [
        pltpu.VMEM((rows, 4 * LANES), bf16),
        pltpu.VMEM((rows, 2 * LANES), f32),
        pltpu.VMEM((tiles, WINDOW, LANES), f32),
        pltpu.VMEM((WINDOW // 4, 4 * tiles, LANES), f32),
        *(pltpu.VMEM((4 * HALF + 2 * NYQ, 2 * level.quads * LANES), bf16) for level in levels),
    ]


def copier(sems):
    used = []

    def start(source, target):
        copy = pltpu.make_async_copy(source, target, sems.at[len(used)])
        used.append(copy)
        copy.start()
        return copy.wait

    return start


def inner_kernel(
    levels, cuts,
    own_hbm, near, far, mask_hbm, table_hbm,
    maps, own, table_ref,
    mask, pad, row_ref, *rest,
):
    *scratch, sems = rest
    start = copier(sems)

    def table(first, last):
        piece = pl.ds(first, last - first)
        return start(table_hbm.at[piece], table_ref.at[piece])

    fine_at, shift_at, map_at, coarse_at, end = cuts
    own_ready = start(own_hbm, own)
    shift_ready = table(shift_at, coarse_at)
    mask_ready = start(mask_hbm, mask)
    coarse_ready = table(coarse_at, end)
    write_row_table(row_ref, levels[0])
    write_fine_table(table_ref, fine_at)
    size = 3 + 4 * len(levels)
    strips = ((near,), (far,), (own,))
    transform(levels, (0, 1), strips, row_ref, table_ref, scratch[:size])
    own_ready()
    transform(levels, (2,), strips, row_ref, table_ref, scratch[:size])
    shift_ready()
    mask_ready()
    write_maps(
        levels, scratch[size - len(levels) : size], (lambda: mask_tile(mask, pad),), table_ref, shift_at, map_at,
        scratch[size:], (maps,))
    coarse_ready()


def outer_kernel(
    levels, cuts, inner, row_at,
    own, near, far, rim, rim_near, rim_far, mask_hbm, mask_coarse_hbm, table_ref, inner_maps,
    out_fine, out_coarse,
    mask, mask_coarse, pad, pad_coarse, maps, maps_coarse, *rest,
):
    *scratch, sems = rest
    start = copier(sems)
    masks_ready = [start(mask_hbm, mask), start(mask_coarse_hbm, mask_coarse)]
    stores = [start(inner_maps.at[d], out_fine.at[0, d, pl.ds(0, inner)]) for d in range(2)]
    fine_at, shift_at, map_at, coarse_at, end = cuts
    row_ref = table_ref.at[pl.ds(row_at, row_places(levels)[1])]
    size = 3 + 4 * len(levels)
    strips = ((near, rim_near), (far, rim_far), (own, rim))
    transform(levels, (0, 1, 2), strips, row_ref, table_ref, scratch[:size])
    for wait in masks_ready:
        wait()
    write_maps(
        levels, scratch[size - len(levels) : size],
        (lambda: mask_tile(mask, pad), lambda: mask_tile(mask_coarse, pad_coarse)), table_ref, shift_at, map_at,
        scratch[size:], (maps, maps_coarse))
    for d in range(2):
        stores.append(start(maps.at[d], out_fine.at[0, d, pl.ds(inner, levels[0].blocks)]))
        stores.append(start(maps_coarse.at[d], out_coarse.at[0, d]))
    for wait in stores:
        wait()


def correlate(own, near, far, rim, rim_near, rim_far, mask_fine, mask_coarse):
    strip_rows, width = own.shape[1:]
    fine, coarse = mask_fine.shape[1], mask_coarse.shape[1]
    inner = fine - 1
    shift, map_ = shift_tables()
    tables = [fine_table(), shift, map_, coarse_table()]
    cuts = [int(at) for at in np.cumsum([0] + [table.shape[0] for table in tables])]
    inner_levels = [Level(1, range(inner), width, cuts[0])]
    outer_levels = [Level(1, range(inner, fine), width, cuts[0]), Level(2, range(coarse), width, cuts[3])]
    row_at = cuts[4]
    tables.append(row_table(outer_levels, strip_rows + PATCH))
    columns = max(table.shape[1] for table in tables)
    table = np.concatenate([np.pad(table, ((0, 0), (0, columns - table.shape[1]))) for table in tables])
    cuts[4] = table.shape[0]

    shifts = WINDOW * WINDOW
    hbm = pl.BlockSpec(memory_space=pltpu.HBM)
    vmem = pl.BlockSpec(memory_space=pltpu.VMEM)
    params = pltpu.CompilerParams(vmem_limit_bytes=28 * 1024 * 1024)
    own, table, mask_fine, mask_coarse = (
        pltpu.with_memory_space_constraint(value, pltpu.HBM)
        for value in (own, jnp.asarray(table), mask_fine, mask_coarse))

    def cost(flops):
        return pl.CostEstimate(flops=flops, bytes_accessed=4 * 10**6, transcendentals=0)

    maps, own_kept, handed = pl.pallas_call(
        functools.partial(inner_kernel, inner_levels, cuts),
        out_shape=(
            jax.ShapeDtypeStruct((2, inner, 4 * inner_levels[0].quads, shifts), f32),
            jax.ShapeDtypeStruct(own.shape, bf16),
            jax.ShapeDtypeStruct(table.shape, bf16),
        ),
        in_specs=[hbm, vmem, vmem, hbm, hbm],
        out_specs=(vmem,) * 3,
        scratch_shapes=[
            pltpu.VMEM(mask_fine.shape, jnp.int32),
            pltpu.VMEM((8, LANES), f32),
            pltpu.VMEM((row_places(inner_levels)[1], 2 * strip_rows), bf16),
            *section_scratch(inner_levels, width),
            *pair_scratch(inner_levels),
            pltpu.SemaphoreType.DMA((4,)),
        ],
        compiler_params=params,
        cost_estimate=cost(3 * 10**9),
        name="inner_blocks",
    )(own, near, far, mask_fine, table)
    return pl.pallas_call(
        functools.partial(outer_kernel, outer_levels, cuts, inner, row_at),
        out_shape=(
            jax.ShapeDtypeStruct((1, 2, fine, 4 * outer_levels[0].quads, shifts), f32),
            jax.ShapeDtypeStruct((1, 2, coarse, 4 * outer_levels[1].quads, shifts), f32),
        ),
        in_specs=[vmem] * 6 + [hbm] * 2 + [vmem] * 2,
        out_specs=(hbm, hbm),
        scratch_shapes=[
            pltpu.VMEM(mask_fine.shape, jnp.int32),
            pltpu.VMEM(mask_coarse.shape, jnp.int32),
            pltpu.VMEM((8, LANES), f32),
            pltpu.VMEM((8, LANES), f32),
            *(pltpu.VMEM((2, level.blocks, 4 * level.quads, shifts), f32) for level in outer_levels),
            *section_scratch(outer_levels, width),
            *pair_scratch(outer_levels),
            pltpu.SemaphoreType.DMA((8,)),
        ],
        compiler_params=params,
        cost_estimate=cost(4 * 10**9),
        name="outer_blocks",
    )(own_kept, near, far, rim, rim_near, rim_far, mask_fine, mask_coarse, handed, maps)


def local(sections, mask_fine, mask_coarse):
    far = from_device(sections, 2, 0)
    near = from_device(sections, 1, 0)
    rims = [from_device(sections, z, 1) for z in range(3)]
    return correlate(sections, near, far, *rims, mask_fine, mask_coarse)


def solution(mesh):
    in_specs = (
        P("sec", "strip", "groups"),
        P("sec", "strip", "groups"),
        P("sec", "strip", "groups"),
    )
    out_specs = (P("sec", None, "strip", "groups", None), P("sec", None, "strip", "groups", None))
    return jax.shard_map(local, mesh=mesh, in_specs=in_specs, out_specs=out_specs, check_vma=False)
```

```python
import functools

import jax
import jax.numpy as jnp
import numpy as np
from jax import lax
from jax.experimental import pallas as pl
from jax.experimental.pallas import tpu as pltpu
from jax.sharding import PartitionSpec as P

PATCH = 64
STRIDE = 32
WINDOW = 32
HALF = PATCH // 2
LANES = 128
NYQ = 16

f32 = jnp.float32
bf16 = jnp.bfloat16


def from_device(value, sec_steps, strip_steps):
    secs, strips = lax.axis_size("sec"), lax.axis_size("strip")
    pairs = []
    for sec in range(secs - sec_steps):
        for strip in range(strips - strip_steps):
            pairs.append(((sec + sec_steps) * strips + strip + strip_steps, sec * strips + strip))
    return lax.ppermute(value, ("sec", "strip"), pairs)


def wave(phase):
    turns = np.arange(PATCH) * (2 * np.pi / PATCH)
    cos = np.round(np.cos(turns), 14)
    sin = np.round(np.sin(turns), 14)
    phase = np.mod(phase, PATCH)
    return cos[phase], sin[phase]


def split_table(table):
    high = table.astype(jnp.bfloat16)
    low = (table - high.astype(np.float64)).astype(jnp.bfloat16)
    return high, low


def stacked(table):
    return np.concatenate(split_table(table), axis=0)


def fine_table():
    c, s = wave(np.arange(PATCH)[:, None] * np.arange(PATCH)[None, :])
    table = np.zeros((2, 2, PATCH, 2, 2, PATCH))
    for p in range(2):
        table[0, p, :, 0, p] = c
        table[1, p, :, 0, p] = -s
        table[0, p, :, 1, p] = -s
        table[1, p, :, 1, p] = -c
    return stacked(table.reshape(4 * PATCH, 4 * PATCH))


def coarse_table():
    c, s = wave((np.arange(2 * PATCH) // 2)[:, None] * np.arange(PATCH)[None, :])
    table = np.zeros((2, 2, 2 * PATCH, 2, 2, PATCH))
    for p in range(2):
        table[p, 0, :, 0, p] = 0.5 * c
        table[p, 1, :, 0, p] = -0.5 * s
        table[p, 0, :, 1, p] = -0.5 * s
        table[p, 1, :, 1, p] = -0.5 * c
    return stacked(table.reshape(8 * PATCH, 4 * PATCH))


def shift_tables():
    spread = 1.869545
    t = np.arange(WINDOW) - WINDOW // 2
    c, s = wave(np.arange(PATCH)[:, None] * t[None, :])
    table = np.zeros((2, 2, 2, PATCH, 2, 4, WINDOW))
    for odd in range(2):
        for p in range(2):
            table[odd, 0, p, :, 0, 2 * p + odd] = c
            table[odd, 1, p, :, 0, 2 * p + odd] = -s
            table[odd, 0, p, :, 1, 2 * p + odd] = s
            table[odd, 1, p, :, 1, 2 * p + odd] = c
    along_t = (spread * table.reshape(8 * PATCH, 8 * WINDOW)).astype(jnp.bfloat16)
    c, s = wave(t[:, None] * np.arange(HALF)[None, :])
    weight = np.where(np.arange(HALF) == 0, 1.0, 2.0)
    nyquist = np.repeat(wave(HALF * t)[0][:, None], NYQ, axis=1)
    along_s = np.concatenate([c * weight, -s * weight, nyquist], axis=1) / (spread * PATCH**3)
    high, low = split_table(along_s)
    along_s = np.concatenate(
        [np.concatenate([high, high], axis=1), np.concatenate([low, np.zeros_like(low)], axis=1)], axis=0)
    return along_t, along_s


class Level:
    def __init__(self, pool, blocks, width, table):
        self.pool, self.first, self.blocks, self.table = pool, blocks[0], len(blocks), table
        self.quads = width // (4 * pool * STRIDE)
        self.tiles = 2 * self.quads
        self.body = self.blocks * HALF
        self.half = -(-self.quads * self.blocks // 8) * 8
        self.rows = self.tiles * self.body + 2 * self.half
        self.cross_body = self.quads * self.body
        self.cross_rows = self.cross_body + -(-self.half // 16) * 16

    def window(self, tile, p):
        quad, odd = divmod(tile, 2)
        return self.pool * LANES * quad + LANES * p + self.pool * STRIDE * odd

    def nyquist_row(self, tile, b):
        quad, odd = divmod(tile, 2)
        return odd * self.half + quad * self.blocks + b


def row_places(levels):
    at, places = 0, []
    for level in levels:
        places.append([at, at + level.body])
        at += level.body + 2 * level.half
    for level, place in zip(levels, places):
        place.append(at)
        at += level.body
    return places, at


def row_table(levels, ext):
    places, size = row_places(levels)
    table = np.zeros((size, ext))
    k = np.arange(HALF)[:, None]
    for level, (cos_at, nyquist_at, sin_at) in zip(levels, places):
        pool = level.pool
        x = np.arange(pool * PATCH) // pool
        c, s = wave(k * x[None, :])
        for b in range(level.blocks):
            first = (level.first + b) * pool * STRIDE
            columns = slice(first, first + x.size)
            table[cos_at + b * HALF : cos_at + (b + 1) * HALF, columns] = c / pool
            table[sin_at + b * HALF : sin_at + (b + 1) * HALF, columns] = s / pool
            for tile in range(level.tiles):
                table[nyquist_at + level.nyquist_row(tile, b), columns] = wave(HALF * x)[0] / pool
    return np.concatenate(split_table(table), axis=1)


def split(value):
    high = value.astype(bf16)
    return high, (value - high.astype(f32)).astype(bf16)


def dot(left, right):
    return jnp.dot(left, right, preferred_element_type=f32)


def dot3(high, low, table_ref, at):
    depth = high.shape[1]
    table_high = table_ref[at : at + depth]
    table_low = table_ref[at + depth : at + 2 * depth]
    return dot(
        jnp.concatenate([high, low, high], axis=1),
        jnp.concatenate([table_high, table_high, table_low], axis=0))


def cosine(turns):
    turns = turns + PATCH // 4
    part = (turns & (HALF - 1)) - PATCH // 4
    angle = part.astype(f32) * (2 * np.pi / PATCH)
    square = angle * angle
    value = jnp.full(square.shape, 1.0 / 479001600, f32)
    for term in (-1.0 / 3628800, 1.0 / 40320, -1.0 / 720, 1.0 / 24, -0.5, 1.0):
        value = value * square + term
    return jnp.where((turns & HALF) == 0, value, -value)


def write_row_table(row_ref, level):
    (cos_at, nyquist_at, sin_at), = row_places([level])[0]
    ext = row_ref.shape[1] // 2

    def put(at, value):
        high, low = split(value)
        row_ref[at : at + value.shape[0], :ext] = high
        row_ref[at : at + value.shape[0], ext:] = low

    def inside(x):
        return jnp.where((x >= 0) & (x < PATCH), 1.0, 0.0)

    k = lax.broadcasted_iota(jnp.int32, (HALF, ext), 0)
    for b in range(level.blocks):
        x = lax.broadcasted_iota(jnp.int32, (HALF, ext), 1) - (level.first + b) * STRIDE
        put(cos_at + b * HALF, cosine(k * x) * inside(x))
        put(sin_at + b * HALF, cosine(k * x - PATCH // 4) * inside(x))
    row = lax.broadcasted_iota(jnp.int32, (2 * level.half, ext), 0)
    x = lax.broadcasted_iota(jnp.int32, (2 * level.half, ext), 1)
    x = x - (level.first + lax.rem(lax.rem(row, level.half), level.blocks)) * STRIDE
    put(nyquist_at, cosine(x * HALF) * inside(x))


def write_fine_table(table_ref, at):
    y = lax.broadcasted_iota(jnp.int32, (PATCH, LANES), 0)
    lane = lax.broadcasted_iota(jnp.int32, (PATCH, LANES), 1)
    frequency = lane & (PATCH - 1)
    c, s = cosine(y * frequency), cosine(y * frequency - PATCH // 4)
    depth = 4 * PATCH
    for p in range(2):
        mine = (lane >= PATCH) if p else (lane < PATCH)
        cos, minus_cos, minus_sin = (jnp.where(mine, value, 0.0) for value in (c, -c, -s))
        for number, pair in enumerate(((cos, minus_sin), (minus_sin, minus_cos))):
            to = at + (2 * number + p) * PATCH
            for half, value in enumerate(pair):
                for level, part in enumerate(split(value)):
                    table_ref[to + level * depth : to + level * depth + PATCH, half * LANES : (half + 1) * LANES] = part


def all_rows(value):
    for step in (4, 2, 1):
        value = value + pltpu.roll(value, step, 0)
    return value


def left_of(level, place, half_ref, odd_ref):
    cos_at, nyquist_at, sin_at = place
    pieces = []
    for tile in range(level.tiles):
        if tile % 2:
            pieces.append(odd_ref[tile // 2 * level.body : (tile // 2 + 1) * level.body])
        else:
            columns = []
            for p in range(level.pool):
                at = level.window(tile, p)
                columns += [half_ref[start : start + level.body, at : at + LANES] for start in (cos_at, sin_at)]
            pieces.append(jnp.concatenate(columns, axis=1))
    pieces.append(odd_ref[level.quads * level.body :])
    return jnp.concatenate(pieces, axis=0)


def gather_windows(level, place, t_ref, halves, odds):
    cos_at, nyquist_at, sin_at = place
    body, end = level.body, level.quads * level.body
    row = lax.broadcasted_iota(jnp.int32, (2 * level.half, LANES), 0)
    for p in range(level.pool):
        for source, target in zip(halves, odds):
            for tile in range(1, level.tiles, 2):
                at = level.window(tile, p)
                for half, start in enumerate((cos_at, sin_at)):
                    to = tile // 2 * body
                    target[to : to + body, (2 * p + half) * LANES : (2 * p + half + 1) * LANES] = (
                        source[start : start + body, at : at + LANES])
        nyquist = jnp.zeros((2 * level.half, LANES), f32)
        for tile in range(level.tiles):
            at, first = level.window(tile, p), level.nyquist_row(tile, 0)
            value = t_ref[nyquist_at : nyquist_at + 2 * level.half, at : at + LANES]
            nyquist = jnp.where((row >= first) & (row < first + level.blocks), value, nyquist)
        for target, part in zip(odds, split(nyquist)):
            target[end:, 2 * p * LANES : (2 * p + 1) * LANES] = part
            target[end:, (2 * p + 1) * LANES : (2 * p + 2) * LANES] = jnp.zeros(part.shape, bf16)


def spectrum_power(level, f_ref):
    sub = lax.broadcasted_iota(jnp.int32, (8, LANES), 0)
    lane = lax.broadcasted_iota(jnp.int32, (8, LANES), 1)
    dc = (sub == 0) & (lane % PATCH == 0)
    group = lax.broadcasted_iota(jnp.int32, (LANES, LANES), 0) // PATCH
    same = group == lax.broadcasted_iota(jnp.int32, (LANES, LANES), 1) // PATCH
    ones = jnp.where(same, 1.0, 0.0).astype(bf16)

    def square(at):
        re, im = f_ref[at : at + 8, :LANES], f_ref[at : at + 8, LANES:]
        return re * re + im * im

    sums = []
    tails = [square(level.tiles * level.body + at) for at in range(0, 2 * level.half, 8)]
    for tile in range(level.tiles):
        for b in range(level.blocks):
            base = tile * level.body + b * HALF
            total = jnp.where(dc, 0.0, square(base))
            head = jnp.where(sub == 0, total, 0.0)
            for r in range(8, HALF, 8):
                total = total + square(base + r)
            row = level.nyquist_row(tile, b)
            sums.append(2.0 * total - head + jnp.where(sub == row % 8, tails[row // 8], 0.0))
    high, low = split(jnp.concatenate(sums, axis=0))
    return dot(jnp.concatenate([high, low], axis=1), jnp.concatenate([ones, ones], axis=0))


def scale_spectrum(level, f_ref, sums, spec_ref):
    sub = lax.broadcasted_iota(jnp.int32, (8, 2 * LANES), 0)
    lane = lax.broadcasted_iota(jnp.int32, (8, 2 * LANES), 1)
    dc = (sub == 0) & (lane % PATCH == 0)
    end = level.tiles * level.body
    tails = [f_ref[end + at : end + at + 8] for at in range(0, 2 * level.half, 8)]
    scaled = [jnp.zeros_like(tail) for tail in tails]
    for tile in range(level.tiles):
        for b in range(level.blocks):
            number = 8 * (tile * level.blocks + b)
            scale = lax.rsqrt(all_rows(sums[number : number + 8]) * (1.0 / PATCH**4) + 1e-05)
            scale = jnp.concatenate([scale, scale], axis=1)
            for r in range(0, HALF, 16):
                at = tile * level.body + b * HALF + r
                head = f_ref[at : at + 8]
                if r == 0:
                    head = jnp.where(dc, 0.0, head)
                both = jnp.concatenate([head * scale, f_ref[at + 8 : at + 16] * scale], axis=0)
                spec_ref[at : at + 16] = both.astype(bf16)
            row = level.nyquist_row(tile, b)
            scaled[row // 8] = jnp.where(sub == row % 8, tails[row // 8] * scale, scaled[row // 8])
    spec_ref[end : end + 2 * level.half] = jnp.concatenate(scaled, axis=0).astype(bf16)


def transform(levels, z, x_ref, row_ref, table_ref, scratch):
    count = len(levels)
    t_ref, *halves = scratch[:3]
    odd_refs = scratch[3 : 3 + 2 * count]
    f_refs, spec_refs = scratch[3 + 2 * count : 3 + 3 * count], scratch[3 + 3 * count :]
    places, size = row_places(levels)
    x = x_ref[z]
    width = x.shape[1]
    x = jnp.concatenate([x, x], axis=0)
    for first in range(0, width, 2 * LANES):
        columns = slice(first, first + 2 * LANES)
        t = dot(row_ref[...], x[:, columns])
        for level, (cos_at, nyquist_at, sin_at) in zip(levels, places):
            for start in (cos_at, sin_at):
                for ref, half in zip(halves, split(t[start : start + level.body])):
                    ref[start : start + level.body, columns] = half
            rows = slice(nyquist_at, nyquist_at + 2 * level.half)
            t_ref[rows, columns] = t[rows]
    for index, (level, place) in enumerate(zip(levels, places)):
        gather_windows(level, place, t_ref, halves, odd_refs[2 * index : 2 * index + 2])
    for index, (level, place) in enumerate(zip(levels, places)):
        lefts = [left_of(level, place, ref, odd) for ref, odd in zip(halves, odd_refs[2 * index : 2 * index + 2])]
        f_refs[index][...] = dot3(*lefts, table_ref, level.table)
    for level, f_ref, spec_ref in zip(levels, f_refs, spec_refs):
        scale_spectrum(level, f_ref, spectrum_power(level, f_ref), spec_ref.at[z])


def transform_all(levels, x_ref, own_ready, row_ref, table_ref, scratch):
    t_ref, *halves = scratch[:3]
    width = x_ref.shape[2]
    for ref in (t_ref, *halves):
        ref[:, width:] = jnp.zeros((ref.shape[0], LANES), ref.dtype)

    def one_section(z, carry):
        if own_ready is not None:
            pl.when(z == 2)(own_ready)
        transform(levels, z, x_ref, row_ref, table_ref, scratch)
        return carry

    lax.fori_loop(0, 3, one_section, 0)


def write_maps(levels, specs, masks, table_ref, shift_at, map_at, scratch, outs):
    cross_ref, y_ref, maps_ref, rows_ref, *stacks = scratch
    pairs = 2
    base = 0
    for level, spec in zip(levels, specs):
        def cross(at, rows):
            a = spec[pairs, at : at + rows].astype(f32)
            ar, ai = a[:, :LANES], a[:, LANES:]
            for d in range(pairs):
                b = spec[d, at : at + rows].astype(f32)
                br, bi = b[:, :LANES], b[:, LANES:]
                yield base + d * level.cross_rows, jnp.concatenate([ar * br + ai * bi, ar * bi - ai * br], axis=1)

        for tile in range(level.tiles):
            quad, odd = divmod(tile, 2)
            for r in range(0, level.body, 16):
                for to, value in cross(tile * level.body + r, 16):
                    to += quad * level.body + r
                    cross_ref[to : to + 16, 2 * odd * LANES : 2 * (odd + 1) * LANES] = value.astype(bf16)
        for to, value in cross(level.tiles * level.body, 2 * level.half):
            value = jnp.concatenate([value[: level.half], value[level.half :]], axis=1)
            spare = level.cross_rows - level.cross_body - level.half
            if spare:
                value = jnp.concatenate([value, jnp.zeros((spare, 4 * LANES), f32)], axis=0)
            cross_ref[to + level.cross_body : to + level.cross_rows] = value.astype(bf16)
        base += pairs * level.cross_rows
    y_ref[...] = dot(cross_ref[...], table_ref[shift_at : shift_at + 4 * LANES])
    base = tile = 0
    starts = {}
    row = lax.broadcasted_iota(jnp.int32, (NYQ, LANES), 0)
    for index, level in enumerate(levels):
        for b in range(level.blocks):
            stack_ref = stacks[index]
            for d in range(pairs):
                first = base + d * level.cross_rows
                nyq_at = first + level.cross_body
                nyquist = y_ref[nyq_at : nyq_at + NYQ, :LANES]
                for quad in range(level.quads):
                    top = first + quad * level.body + b * HALF
                    column = (d * level.quads + quad) * LANES
                    for at, value in (
                        (0, y_ref[top : top + HALF, :LANES]),
                        (HALF, y_ref[top : top + HALF, LANES:]),
                        (2 * HALF, jnp.where(row == quad * level.blocks + b, nyquist, 0.0)),
                    ):
                        for half, part in enumerate(split(value)):
                            to = half * (2 * HALF + NYQ) + at
                            stack_ref[to : to + value.shape[0], column : column + LANES] = part
            both = dot(table_ref[map_at : map_at + 2 * WINDOW, : stack_ref.shape[0]], stack_ref[...])
            maps = both[:WINDOW] + both[WINDOW:]
            for d in range(pairs):
                starts[index, d, b] = tile
                for quad in range(level.quads):
                    column = (d * level.quads + quad) * LANES
                    maps_ref[tile] = maps[:, column : column + LANES]
                    tile += 1
        base += pairs * level.cross_rows
    kept = [jnp.transpose(mask()) for mask in masks]
    lane = lax.broadcasted_iota(jnp.int32, (tile, LANES), 1)

    def exchange(low, high, width):
        even = (lane & width) == 0
        return (
            jnp.where(even, low, pltpu.roll(high, width, 1)),
            jnp.where(even, pltpu.roll(low, LANES - width, 1), high))

    for big in range(WINDOW // 4):
        rows = [maps_ref[:, 4 * big + r, :] for r in range(4)]
        for step in (2, 1):
            for r in range(4):
                if not r & step:
                    rows[r], rows[r + step] = exchange(rows[r], rows[r + step], step * WINDOW)
        for g in range(4):
            rows_ref[big, pl.ds(g, tile, stride=4), :] = rows[g]
        for index, (level, out) in enumerate(zip(levels, outs)):
            for b in range(level.blocks):
                column = kept[index][: 4 * level.quads, level.first + b : level.first + b + 1]
                for d in range(pairs):
                    at = 4 * starts[index, d, b]
                    out[d, b, :, big * LANES : (big + 1) * LANES] = rows_ref[big, at : at + 4 * level.quads] * column


def mask_tile(mask_ref, pad_ref):
    pad_ref[...] = jnp.zeros(pad_ref.shape, f32)
    pad_ref[: mask_ref.shape[1], : mask_ref.shape[2]] = mask_ref[0].astype(f32)
    return pad_ref[...]


def section_scratch(levels, width):
    size = row_places(levels)[1]
    return [
        pltpu.VMEM((size, width + LANES), f32),
        pltpu.VMEM((size, width + LANES), bf16),
        pltpu.VMEM((size, width + LANES), bf16),
        *(pltpu.VMEM((level.quads * level.body + 2 * level.half, 2 * level.pool * LANES), bf16)
          for level in levels for _ in range(2)),
        *(pltpu.VMEM((level.rows, 2 * LANES), f32) for level in levels),
        *(pltpu.VMEM((3, level.rows, 2 * LANES), bf16) for level in levels),
    ]


def pair_scratch(levels):
    rows = sum(2 * level.cross_rows for level in levels)
    tiles = sum(2 * level.blocks * level.quads for level in levels)
    return [
        pltpu.VMEM((rows, 4 * LANES), bf16),
        pltpu.VMEM((rows, 2 * LANES), f32),
        pltpu.VMEM((tiles, WINDOW, LANES), f32),
        pltpu.VMEM((WINDOW // 4, 4 * tiles, LANES), f32),
        *(pltpu.VMEM((4 * HALF + 2 * NYQ, 2 * level.quads * LANES), bf16) for level in levels),
    ]


def copier(sems):
    used = []

    def start(source, target):
        copy = pltpu.make_async_copy(source, target, sems.at[len(used)])
        used.append(copy)
        copy.start()
        return copy.wait

    return start


def inner_kernel(
    levels, cuts,
    own_hbm, near, far, mask_hbm, table_hbm,
    maps, own, table_ref,
    mask, pad, row_ref, x_ref, *rest,
):
    *scratch, sems = rest
    start = copier(sems)

    def table(first, last):
        piece = pl.ds(first, last - first)
        return start(table_hbm.at[piece], table_ref.at[piece])

    fine_at, shift_at, map_at, coarse_at, end = cuts
    own_ready = start(own_hbm, own)
    shift_ready = table(shift_at, coarse_at)
    mask_ready = start(mask_hbm, mask)
    coarse_ready = table(coarse_at, end)
    write_row_table(row_ref, levels[0])
    write_fine_table(table_ref, fine_at)
    size = 3 + 4 * len(levels)
    x_ref[0], x_ref[1] = near[0], far[0]

    def take_own():
        own_ready()
        x_ref[2] = own[0]

    transform_all(levels, x_ref, take_own, row_ref, table_ref, scratch[:size])
    shift_ready()
    mask_ready()
    write_maps(
        levels, scratch[size - len(levels) : size], (lambda: mask_tile(mask, pad),), table_ref, shift_at, map_at,
        scratch[size:], (maps,))
    coarse_ready()


def outer_kernel(
    levels, cuts, inner, row_at,
    own, near, far, rim, rim_near, rim_far, mask_hbm, mask_coarse_hbm, table_ref, inner_maps,
    out_fine, out_coarse,
    mask, mask_coarse, pad, pad_coarse, maps, maps_coarse, x_ref, *rest,
):
    *scratch, sems = rest
    start = copier(sems)
    masks_ready = [start(mask_hbm, mask), start(mask_coarse_hbm, mask_coarse)]
    stores = [start(inner_maps.at[d], out_fine.at[0, d, pl.ds(0, inner)]) for d in range(2)]
    fine_at, shift_at, map_at, coarse_at, end = cuts
    row_ref = table_ref.at[pl.ds(row_at, row_places(levels)[1])]
    size = 3 + 4 * len(levels)
    rows = own.shape[1]
    for z, (strip, below) in enumerate(((near, rim_near), (far, rim_far), (own, rim))):
        x_ref[z, :rows] = strip[0]
        x_ref[z, rows:] = below[0]
    transform_all(levels, x_ref, None, row_ref, table_ref, scratch[:size])
    for wait in masks_ready:
        wait()
    write_maps(
        levels, scratch[size - len(levels) : size],
        (lambda: mask_tile(mask, pad), lambda: mask_tile(mask_coarse, pad_coarse)), table_ref, shift_at, map_at,
        scratch[size:], (maps, maps_coarse))
    for d in range(2):
        stores.append(start(maps.at[d], out_fine.at[0, d, pl.ds(inner, levels[0].blocks)]))
        stores.append(start(maps_coarse.at[d], out_coarse.at[0, d]))
    for wait in stores:
        wait()


def correlate(own, near, far, rim, rim_near, rim_far, mask_fine, mask_coarse):
    strip_rows, width = own.shape[1:]
    fine, coarse = mask_fine.shape[1], mask_coarse.shape[1]
    inner = fine - 1
    shift, map_ = shift_tables()
    tables = [fine_table(), shift, map_, coarse_table()]
    cuts = [int(at) for at in np.cumsum([0] + [table.shape[0] for table in tables])]
    inner_levels = [Level(1, range(inner), width, cuts[0])]
    outer_levels = [Level(1, range(inner, fine), width, cuts[0]), Level(2, range(coarse), width, cuts[3])]
    row_at = cuts[4]
    tables.append(row_table(outer_levels, strip_rows + PATCH))
    columns = max(table.shape[1] for table in tables)
    table = np.concatenate([np.pad(table, ((0, 0), (0, columns - table.shape[1]))) for table in tables])
    cuts[4] = table.shape[0]

    shifts = WINDOW * WINDOW
    hbm = pl.BlockSpec(memory_space=pltpu.HBM)
    vmem = pl.BlockSpec(memory_space=pltpu.VMEM)
    params = pltpu.CompilerParams(vmem_limit_bytes=28 * 1024 * 1024)
    own, table, mask_fine, mask_coarse = (
        pltpu.with_memory_space_constraint(value, pltpu.HBM)
        for value in (own, jnp.asarray(table), mask_fine, mask_coarse))

    def cost(flops):
        return pl.CostEstimate(flops=flops, bytes_accessed=4 * 10**6, transcendentals=0)

    maps, own_kept, handed = pl.pallas_call(
        functools.partial(inner_kernel, inner_levels, cuts),
        out_shape=(
            jax.ShapeDtypeStruct((2, inner, 4 * inner_levels[0].quads, shifts), f32),
            jax.ShapeDtypeStruct(own.shape, bf16),
            jax.ShapeDtypeStruct(table.shape, bf16),
        ),
        in_specs=[hbm, vmem, vmem, hbm, hbm],
        out_specs=(vmem,) * 3,
        scratch_shapes=[
            pltpu.VMEM(mask_fine.shape, jnp.int32),
            pltpu.VMEM((8, LANES), f32),
            pltpu.VMEM((row_places(inner_levels)[1], 2 * strip_rows), bf16),
            pltpu.VMEM((3, strip_rows, width), bf16),
            *section_scratch(inner_levels, width),
            *pair_scratch(inner_levels),
            pltpu.SemaphoreType.DMA((4,)),
        ],
        compiler_params=params,
        cost_estimate=cost(3 * 10**9),
        name="inner_blocks",
    )(own, near, far, mask_fine, table)
    return pl.pallas_call(
        functools.partial(outer_kernel, outer_levels, cuts, inner, row_at),
        out_shape=(
            jax.ShapeDtypeStruct((1, 2, fine, 4 * outer_levels[0].quads, shifts), f32),
            jax.ShapeDtypeStruct((1, 2, coarse, 4 * outer_levels[1].quads, shifts), f32),
        ),
        in_specs=[vmem] * 6 + [hbm] * 2 + [vmem] * 2,
        out_specs=(hbm, hbm),
        scratch_shapes=[
            pltpu.VMEM(mask_fine.shape, jnp.int32),
            pltpu.VMEM(mask_coarse.shape, jnp.int32),
            pltpu.VMEM((8, LANES), f32),
            pltpu.VMEM((8, LANES), f32),
            *(pltpu.VMEM((2, level.blocks, 4 * level.quads, shifts), f32) for level in outer_levels),
            pltpu.VMEM((3, strip_rows + PATCH, width), bf16),
            *section_scratch(outer_levels, width),
            *pair_scratch(outer_levels),
            pltpu.SemaphoreType.DMA((8,)),
        ],
        compiler_params=params,
        cost_estimate=cost(4 * 10**9),
        name="outer_blocks",
    )(own_kept, near, far, rim, rim_near, rim_far, mask_fine, mask_coarse, handed, maps)


def local(sections, mask_fine, mask_coarse):
    far = from_device(sections, 2, 0)
    near = from_device(sections, 1, 0)
    last, far = lax.optimization_barrier((sections, far))
    rims = [from_device(last if z == 0 else sections, z, 1) for z in range(3)]
    return correlate(sections, near, far, *rims, mask_fine, mask_coarse)


def solution(mesh):
    in_specs = (
        P("sec", "strip", "groups"),
        P("sec", "strip", "groups"),
        P("sec", "strip", "groups"),
    )
    out_specs = (P("sec", None, "strip", "groups", None), P("sec", None, "strip", "groups", None))
    return jax.shard_map(local, mesh=mesh, in_specs=in_specs, out_specs=out_specs, check_vma=False)
```

```python
import functools

import jax
import jax.numpy as jnp
import numpy as np
from jax import lax
from jax.experimental import pallas as pl
from jax.experimental.pallas import tpu as pltpu
from jax.sharding import PartitionSpec as P

PATCH = 64
STRIDE = 32
WINDOW = 32
HALF = PATCH // 2
LANES = 128
NYQ = 16

f32 = jnp.float32
bf16 = jnp.bfloat16


def from_device(value, sec_steps, strip_steps):
    secs, strips = lax.axis_size("sec"), lax.axis_size("strip")
    pairs = []
    for sec in range(secs - sec_steps):
        for strip in range(strips - strip_steps):
            pairs.append(((sec + sec_steps) * strips + strip + strip_steps, sec * strips + strip))
    return lax.ppermute(value, ("sec", "strip"), pairs)


def wave(phase):
    turns = np.arange(PATCH) * (2 * np.pi / PATCH)
    cos = np.round(np.cos(turns), 14)
    sin = np.round(np.sin(turns), 14)
    phase = np.mod(phase, PATCH)
    return cos[phase], sin[phase]


def split_table(table):
    high = table.astype(jnp.bfloat16)
    low = (table - high.astype(np.float64)).astype(jnp.bfloat16)
    return high, low


def stacked(table):
    return np.concatenate(split_table(table), axis=0)


def fine_table():
    c, s = wave(np.arange(PATCH)[:, None] * np.arange(PATCH)[None, :])
    table = np.zeros((2, 2, PATCH, 2, 2, PATCH))
    for p in range(2):
        table[0, p, :, 0, p] = c
        table[1, p, :, 0, p] = -s
        table[0, p, :, 1, p] = -s
        table[1, p, :, 1, p] = -c
    return stacked(table.reshape(4 * PATCH, 4 * PATCH))


def coarse_table():
    c, s = wave((np.arange(2 * PATCH) // 2)[:, None] * np.arange(PATCH)[None, :])
    table = np.zeros((2, 2, 2 * PATCH, 2, 2, PATCH))
    for p in range(2):
        table[p, 0, :, 0, p] = 0.5 * c
        table[p, 1, :, 0, p] = -0.5 * s
        table[p, 0, :, 1, p] = -0.5 * s
        table[p, 1, :, 1, p] = -0.5 * c
    return stacked(table.reshape(8 * PATCH, 4 * PATCH))


def shift_tables():
    spread = 1.869545
    t = np.arange(WINDOW) - WINDOW // 2
    c, s = wave(np.arange(PATCH)[:, None] * t[None, :])
    table = np.zeros((2, 2, 2, PATCH, 2, 4, WINDOW))
    for odd in range(2):
        for p in range(2):
            table[odd, 0, p, :, 0, 2 * p + odd] = c
            table[odd, 1, p, :, 0, 2 * p + odd] = -s
            table[odd, 0, p, :, 1, 2 * p + odd] = s
            table[odd, 1, p, :, 1, 2 * p + odd] = c
    along_t = (spread * table.reshape(8 * PATCH, 8 * WINDOW)).astype(jnp.bfloat16)
    c, s = wave(t[:, None] * np.arange(HALF)[None, :])
    weight = np.where(np.arange(HALF) == 0, 1.0, 2.0)
    nyquist = np.repeat(wave(HALF * t)[0][:, None], NYQ, axis=1)
    along_s = np.concatenate([c * weight, -s * weight, nyquist], axis=1) / (spread * PATCH**3)
    high, low = split_table(along_s)
    along_s = np.concatenate(
        [np.concatenate([high, high], axis=1), np.concatenate([low, np.zeros_like(low)], axis=1)], axis=0)
    return along_t, along_s


class Level:
    def __init__(self, pool, blocks, width, table):
        self.pool, self.first, self.blocks, self.table = pool, blocks[0], len(blocks), table
        self.quads = width // (4 * pool * STRIDE)
        self.tiles = 2 * self.quads
        self.body = self.blocks * HALF
        self.half = -(-self.quads * self.blocks // 8) * 8
        self.rows = self.tiles * self.body + 2 * self.half
        self.cross_body = self.quads * self.body
        self.cross_rows = self.cross_body + -(-self.half // 16) * 16

    def window(self, tile, p):
        quad, odd = divmod(tile, 2)
        return self.pool * LANES * quad + LANES * p + self.pool * STRIDE * odd

    def nyquist_row(self, tile, b):
        quad, odd = divmod(tile, 2)
        return odd * self.half + quad * self.blocks + b


def row_places(levels):
    at, places = 0, []
    for level in levels:
        places.append([at, at + level.body])
        at += level.body + 2 * level.half
    for level, place in zip(levels, places):
        place.append(at)
        at += level.body
    return places, at


def row_table(levels, ext):
    places, size = row_places(levels)
    table = np.zeros((size, ext))
    k = np.arange(HALF)[:, None]
    for level, (cos_at, nyquist_at, sin_at) in zip(levels, places):
        pool = level.pool
        x = np.arange(pool * PATCH) // pool
        c, s = wave(k * x[None, :])
        for b in range(level.blocks):
            first = (level.first + b) * pool * STRIDE
            columns = slice(first, first + x.size)
            table[cos_at + b * HALF : cos_at + (b + 1) * HALF, columns] = c / pool
            table[sin_at + b * HALF : sin_at + (b + 1) * HALF, columns] = s / pool
            for tile in range(level.tiles):
                table[nyquist_at + level.nyquist_row(tile, b), columns] = wave(HALF * x)[0] / pool
    return np.concatenate(split_table(table), axis=1)


def split(value):
    high = value.astype(bf16)
    return high, (value - high.astype(f32)).astype(bf16)


def dot(left, right):
    return jnp.dot(left, right, preferred_element_type=f32)


def dot3(high, low, table_ref, at):
    depth = high.shape[1]
    table_high = table_ref[at : at + depth]
    table_low = table_ref[at + depth : at + 2 * depth]
    return dot(
        jnp.concatenate([high, low, high], axis=1),
        jnp.concatenate([table_high, table_high, table_low], axis=0))


def cosine(turns):
    turns = turns + PATCH // 4
    part = (turns & (HALF - 1)) - PATCH // 4
    angle = part.astype(f32) * (2 * np.pi / PATCH)
    square = angle * angle
    value = jnp.full(square.shape, 1.0 / 479001600, f32)
    for term in (-1.0 / 3628800, 1.0 / 40320, -1.0 / 720, 1.0 / 24, -0.5, 1.0):
        value = value * square + term
    return jnp.where((turns & HALF) == 0, value, -value)


def write_row_table(row_ref, level):
    (cos_at, nyquist_at, sin_at), = row_places([level])[0]
    ext = row_ref.shape[1] // 2

    def put(at, value):
        high, low = split(value)
        row_ref[at : at + value.shape[0], :ext] = high
        row_ref[at : at + value.shape[0], ext:] = low

    def inside(x):
        return jnp.where((x >= 0) & (x < PATCH), 1.0, 0.0)

    k = lax.broadcasted_iota(jnp.int32, (HALF, ext), 0)
    for b in range(level.blocks):
        x = lax.broadcasted_iota(jnp.int32, (HALF, ext), 1) - (level.first + b) * STRIDE
        put(cos_at + b * HALF, cosine(k * x) * inside(x))
        put(sin_at + b * HALF, cosine(k * x - PATCH // 4) * inside(x))
    row = lax.broadcasted_iota(jnp.int32, (2 * level.half, ext), 0)
    x = lax.broadcasted_iota(jnp.int32, (2 * level.half, ext), 1)
    x = x - (level.first + lax.rem(lax.rem(row, level.half), level.blocks)) * STRIDE
    put(nyquist_at, cosine(x * HALF) * inside(x))


def write_fine_table(table_ref, at):
    y = lax.broadcasted_iota(jnp.int32, (PATCH, LANES), 0)
    lane = lax.broadcasted_iota(jnp.int32, (PATCH, LANES), 1)
    frequency = lane & (PATCH - 1)
    c, s = cosine(y * frequency), cosine(y * frequency - PATCH // 4)
    depth = 4 * PATCH
    for p in range(2):
        mine = (lane >= PATCH) if p else (lane < PATCH)
        cos, minus_cos, minus_sin = (jnp.where(mine, value, 0.0) for value in (c, -c, -s))
        for number, pair in enumerate(((cos, minus_sin), (minus_sin, minus_cos))):
            to = at + (2 * number + p) * PATCH
            for half, value in enumerate(pair):
                for level, part in enumerate(split(value)):
                    table_ref[to + level * depth : to + level * depth + PATCH, half * LANES : (half + 1) * LANES] = part


def all_rows(value):
    for step in (4, 2, 1):
        value = value + pltpu.roll(value, step, 0)
    return value


def left_of(level, place, half_ref, odd_ref):
    cos_at, nyquist_at, sin_at = place
    pieces = []
    for tile in range(level.tiles):
        if tile % 2:
            pieces.append(odd_ref[tile // 2 * level.body : (tile // 2 + 1) * level.body])
        else:
            columns = []
            for p in range(level.pool):
                at = level.window(tile, p)
                columns += [half_ref[start : start + level.body, at : at + LANES] for start in (cos_at, sin_at)]
            pieces.append(jnp.concatenate(columns, axis=1))
    pieces.append(odd_ref[level.quads * level.body :])
    return jnp.concatenate(pieces, axis=0)


def gather_windows(level, place, t_ref, halves, odds):
    cos_at, nyquist_at, sin_at = place
    body, end = level.body, level.quads * level.body
    row = lax.broadcasted_iota(jnp.int32, (2 * level.half, LANES), 0)
    for p in range(level.pool):
        for source, target in zip(halves, odds):
            for tile in range(1, level.tiles, 2):
                at = level.window(tile, p)
                for half, start in enumerate((cos_at, sin_at)):
                    to = tile // 2 * body
                    target[to : to + body, (2 * p + half) * LANES : (2 * p + half + 1) * LANES] = (
                        source[start : start + body, at : at + LANES])
        nyquist = jnp.zeros((2 * level.half, LANES), f32)
        for tile in range(level.tiles):
            at, first = level.window(tile, p), level.nyquist_row(tile, 0)
            value = t_ref[nyquist_at : nyquist_at + 2 * level.half, at : at + LANES]
            nyquist = jnp.where((row >= first) & (row < first + level.blocks), value, nyquist)
        for target, part in zip(odds, split(nyquist)):
            target[end:, 2 * p * LANES : (2 * p + 1) * LANES] = part
            target[end:, (2 * p + 1) * LANES : (2 * p + 2) * LANES] = jnp.zeros(part.shape, bf16)


def spectrum_power(level, f_ref, sections):
    sub = lax.broadcasted_iota(jnp.int32, (8, LANES), 0)
    lane = lax.broadcasted_iota(jnp.int32, (8, LANES), 1)
    dc = (sub == 0) & (lane % PATCH == 0)
    group = lax.broadcasted_iota(jnp.int32, (LANES, LANES), 0) // PATCH
    same = group == lax.broadcasted_iota(jnp.int32, (LANES, LANES), 1) // PATCH
    ones = jnp.where(same, 1.0, 0.0).astype(bf16)

    def square(at):
        re, im = f_ref[at : at + 8, :LANES], f_ref[at : at + 8, LANES:]
        return re * re + im * im

    sums = []
    for z in sections:
        end = z * level.rows + level.tiles * level.body
        tails = [square(end + at) for at in range(0, 2 * level.half, 8)]
        for tile in range(level.tiles):
            for b in range(level.blocks):
                base = z * level.rows + tile * level.body + b * HALF
                total = jnp.where(dc, 0.0, square(base))
                head = jnp.where(sub == 0, total, 0.0)
                for r in range(8, HALF, 8):
                    total = total + square(base + r)
                row = level.nyquist_row(tile, b)
                sums.append(2.0 * total - head + jnp.where(sub == row % 8, tails[row // 8], 0.0))
    high, low = split(jnp.concatenate(sums, axis=0))
    return dot(jnp.concatenate([high, low], axis=1), jnp.concatenate([ones, ones], axis=0))


def scale_spectrum(level, f_ref, sections, sums, spec_ref):
    sub = lax.broadcasted_iota(jnp.int32, (8, 2 * LANES), 0)
    lane = lax.broadcasted_iota(jnp.int32, (8, 2 * LANES), 1)
    dc = (sub == 0) & (lane % PATCH == 0)
    number = 0
    for z in sections:
        start = z * level.rows
        end = start + level.tiles * level.body
        tails = [f_ref[end + at : end + at + 8] for at in range(0, 2 * level.half, 8)]
        scaled = [jnp.zeros_like(tail) for tail in tails]
        for tile in range(level.tiles):
            for b in range(level.blocks):
                scale = lax.rsqrt(all_rows(sums[number : number + 8]) * (1.0 / PATCH**4) + 1e-05)
                number += 8
                scale = jnp.concatenate([scale, scale], axis=1)
                for r in range(0, HALF, 16):
                    at = start + tile * level.body + b * HALF + r
                    head = f_ref[at : at + 8]
                    if r == 0:
                        head = jnp.where(dc, 0.0, head)
                    both = jnp.concatenate([head * scale, f_ref[at + 8 : at + 16] * scale], axis=0)
                    spec_ref[at : at + 16] = both.astype(bf16)
                row = level.nyquist_row(tile, b)
                scaled[row // 8] = jnp.where(sub == row % 8, tails[row // 8] * scale, scaled[row // 8])
        spec_ref[end : end + 2 * level.half] = jnp.concatenate(scaled, axis=0).astype(bf16)


def transform(levels, sections, strips, row_ref, table_ref, scratch):
    count = len(levels)
    t_ref, high_ref, low_ref = scratch[:3]
    odd_refs = scratch[3 : 3 + 2 * count]
    f_refs, spec_refs = scratch[3 + 2 * count : 3 + 3 * count], scratch[3 + 3 * count :]
    places, size = row_places(levels)
    for z in sections:
        x = jnp.concatenate([strip[0] for strip in strips[z]], axis=0)
        width = x.shape[1]
        x = jnp.concatenate([x, x], axis=0)
        for first in range(0, width, 2 * LANES):
            columns = slice(first, first + 2 * LANES)
            t = dot(row_ref[...], x[:, columns])
            for level, (cos_at, nyquist_at, sin_at) in zip(levels, places):
                for start in (cos_at, sin_at):
                    for ref, half in zip((high_ref, low_ref), split(t[start : start + level.body])):
                        ref[z, start : start + level.body, columns] = half
                rows = slice(nyquist_at, nyquist_at + 2 * level.half)
                t_ref[z, rows, columns] = t[rows]
        t_ref[z, :, width:] = jnp.zeros((size, LANES), f32)
        for ref in (high_ref, low_ref):
            ref[z, :, width:] = jnp.zeros((size, LANES), bf16)
    for index, (level, place) in enumerate(zip(levels, places)):
        odds = odd_refs[2 * index : 2 * index + 2]
        for z in sections:
            gather_windows(level, place, t_ref.at[z], (high_ref.at[z], low_ref.at[z]), [ref.at[z] for ref in odds])
    for index, (level, place) in enumerate(zip(levels, places)):
        lefts = [
            jnp.concatenate([left_of(level, place, ref.at[z], odd.at[z]) for z in sections], axis=0)
            for ref, odd in zip((high_ref, low_ref), odd_refs[2 * index : 2 * index + 2])]
        rows = slice(sections[0] * level.rows, (sections[-1] + 1) * level.rows)
        f_refs[index][rows] = dot3(*lefts, table_ref, level.table)
    for level, f_ref, spec_ref in zip(levels, f_refs, spec_refs):
        scale_spectrum(level, f_ref, sections, spectrum_power(level, f_ref, sections), spec_ref)


def write_maps(levels, specs, masks, table_ref, shift_at, map_at, scratch, outs):
    cross_ref, y_ref, maps_ref, rows_ref, *stacks = scratch
    pairs = 2
    base = 0
    for level, spec in zip(levels, specs):
        def cross(at, rows):
            a = spec[pairs * level.rows + at : pairs * level.rows + at + rows].astype(f32)
            ar, ai = a[:, :LANES], a[:, LANES:]
            for d in range(pairs):
                b = spec[d * level.rows + at : d * level.rows + at + rows].astype(f32)
                br, bi = b[:, :LANES], b[:, LANES:]
                yield base + d * level.cross_rows, jnp.concatenate([ar * br + ai * bi, ar * bi - ai * br], axis=1)

        for tile in range(level.tiles):
            quad, odd = divmod(tile, 2)
            for r in range(0, level.body, 16):
                for to, value in cross(tile * level.body + r, 16):
                    to += quad * level.body + r
                    cross_ref[to : to + 16, 2 * odd * LANES : 2 * (odd + 1) * LANES] = value.astype(bf16)
        for to, value in cross(level.tiles * level.body, 2 * level.half):
            value = jnp.concatenate([value[: level.half], value[level.half :]], axis=1)
            spare = level.cross_rows - level.cross_body - level.half
            if spare:
                value = jnp.concatenate([value, jnp.zeros((spare, 4 * LANES), f32)], axis=0)
            cross_ref[to + level.cross_body : to + level.cross_rows] = value.astype(bf16)
        base += pairs * level.cross_rows
    y_ref[...] = dot(cross_ref[...], table_ref[shift_at : shift_at + 4 * LANES])
    base = tile = 0
    starts = {}
    row = lax.broadcasted_iota(jnp.int32, (NYQ, LANES), 0)
    for index, level in enumerate(levels):
        for b in range(level.blocks):
            stack_ref = stacks[index]
            for d in range(pairs):
                first = base + d * level.cross_rows
                nyq_at = first + level.cross_body
                nyquist = y_ref[nyq_at : nyq_at + NYQ, :LANES]
                for quad in range(level.quads):
                    top = first + quad * level.body + b * HALF
                    column = (d * level.quads + quad) * LANES
                    for at, value in (
                        (0, y_ref[top : top + HALF, :LANES]),
                        (HALF, y_ref[top : top + HALF, LANES:]),
                        (2 * HALF, jnp.where(row == quad * level.blocks + b, nyquist, 0.0)),
                    ):
                        for half, part in enumerate(split(value)):
                            to = half * (2 * HALF + NYQ) + at
                            stack_ref[to : to + value.shape[0], column : column + LANES] = part
            both = dot(table_ref[map_at : map_at + 2 * WINDOW, : stack_ref.shape[0]], stack_ref[...])
            maps = both[:WINDOW] + both[WINDOW:]
            for d in range(pairs):
                starts[index, d, b] = tile
                for quad in range(level.quads):
                    column = (d * level.quads + quad) * LANES
                    maps_ref[tile] = maps[:, column : column + LANES]
                    tile += 1
        base += pairs * level.cross_rows
    kept = [jnp.transpose(mask()) for mask in masks]
    lane = lax.broadcasted_iota(jnp.int32, (tile, LANES), 1)

    def exchange(low, high, width):
        even = (lane & width) == 0
        return (
            jnp.where(even, low, pltpu.roll(high, width, 1)),
            jnp.where(even, pltpu.roll(low, LANES - width, 1), high))

    for big in range(WINDOW // 4):
        rows = [maps_ref[:, 4 * big + r, :] for r in range(4)]
        for step in (2, 1):
            for r in range(4):
                if not r & step:
                    rows[r], rows[r + step] = exchange(rows[r], rows[r + step], step * WINDOW)
        for g in range(4):
            rows_ref[big, pl.ds(g, tile, stride=4), :] = rows[g]
        for index, (level, out) in enumerate(zip(levels, outs)):
            for b in range(level.blocks):
                column = kept[index][: 4 * level.quads, level.first + b : level.first + b + 1]
                for d in range(pairs):
                    at = 4 * starts[index, d, b]
                    out[d, b, :, big * LANES : (big + 1) * LANES] = rows_ref[big, at : at + 4 * level.quads] * column


def mask_tile(mask_ref, pad_ref):
    pad_ref[...] = jnp.zeros(pad_ref.shape, f32)
    pad_ref[: mask_ref.shape[1], : mask_ref.shape[2]] = mask_ref[0].astype(f32)
    return pad_ref[...]


def section_scratch(levels, width):
    size = row_places(levels)[1]
    return [
        pltpu.VMEM((3, size, width + LANES), f32),
        pltpu.VMEM((3, size, width + LANES), bf16),
        pltpu.VMEM((3, size, width + LANES), bf16),
        *(pltpu.VMEM((3, level.quads * level.body + 2 * level.half, 2 * level.pool * LANES), bf16)
          for level in levels for _ in range(2)),
        *(pltpu.VMEM((3 * level.rows, 2 * LANES), f32) for level in levels),
        *(pltpu.VMEM((3 * level.rows, 2 * LANES), bf16) for level in levels),
    ]


def pair_scratch(levels):
    rows = sum(2 * level.cross_rows for level in levels)
    tiles = sum(2 * level.blocks * level.quads for level in levels)
    return [
        pltpu.VMEM((rows, 4 * LANES), bf16),
        pltpu.VMEM((rows, 2 * LANES), f32),
        pltpu.VMEM((tiles, WINDOW, LANES), f32),
        pltpu.VMEM((WINDOW // 4, 4 * tiles, LANES), f32),
        *(pltpu.VMEM((4 * HALF + 2 * NYQ, 2 * level.quads * LANES), bf16) for level in levels),
    ]


def copier(sems):
    used = []

    def start(source, target):
        copy = pltpu.make_async_copy(source, target, sems.at[len(used)])
        used.append(copy)
        copy.start()
        return copy.wait

    return start


def inner_kernel(
    levels, cuts,
    own_hbm, others, mask_hbm, table_hbm,
    maps, own, table_ref,
    mask, pad, row_ref, *rest,
):
    *scratch, sems = rest
    start = copier(sems)

    def table(first, last):
        piece = pl.ds(first, last - first)
        return start(table_hbm.at[piece], table_ref.at[piece])

    fine_at, shift_at, map_at, coarse_at, end = cuts
    own_ready = start(own_hbm, own)
    shift_ready = table(shift_at, coarse_at)
    mask_ready = start(mask_hbm, mask)
    coarse_ready = table(coarse_at, end)
    write_row_table(row_ref, levels[0])
    write_fine_table(table_ref, fine_at)
    size = 3 + 4 * len(levels)
    strips = ((others.at[0:1],), (others.at[1:2],), (own,))
    transform(levels, (0, 1), strips, row_ref, table_ref, scratch[:size])
    own_ready()
    transform(levels, (2,), strips, row_ref, table_ref, scratch[:size])
    shift_ready()
    mask_ready()
    write_maps(
        levels, scratch[size - len(levels) : size], (lambda: mask_tile(mask, pad),), table_ref, shift_at, map_at,
        scratch[size:], (maps,))
    coarse_ready()


def outer_kernel(
    levels, cuts, inner, row_at,
    own, others, rim, rims, mask_hbm, mask_coarse_hbm, table_ref, inner_maps,
    out_fine, out_coarse,
    mask, mask_coarse, pad, pad_coarse, maps, maps_coarse, *rest,
):
    *scratch, sems = rest
    start = copier(sems)
    masks_ready = [start(mask_hbm, mask), start(mask_coarse_hbm, mask_coarse)]
    stores = [start(inner_maps.at[d], out_fine.at[0, d, pl.ds(0, inner)]) for d in range(2)]
    fine_at, shift_at, map_at, coarse_at, end = cuts
    row_ref = table_ref.at[pl.ds(row_at, row_places(levels)[1])]
    size = 3 + 4 * len(levels)
    strips = ((others.at[0:1], rims.at[0:1]), (others.at[1:2], rims.at[1:2]), (own, rim))
    transform(levels, (0, 1, 2), strips, row_ref, table_ref, scratch[:size])
    for wait in masks_ready:
        wait()
    write_maps(
        levels, scratch[size - len(levels) : size],
        (lambda: mask_tile(mask, pad), lambda: mask_tile(mask_coarse, pad_coarse)), table_ref, shift_at, map_at,
        scratch[size:], (maps, maps_coarse))
    for d in range(2):
        stores.append(start(maps.at[d], out_fine.at[0, d, pl.ds(inner, levels[0].blocks)]))
        stores.append(start(maps_coarse.at[d], out_coarse.at[0, d]))
    for wait in stores:
        wait()


def correlate(own, others, rim, rims, mask_fine, mask_coarse):
    strip_rows, width = own.shape[1:]
    fine, coarse = mask_fine.shape[1], mask_coarse.shape[1]
    inner = fine - 1
    shift, map_ = shift_tables()
    tables = [fine_table(), shift, map_, coarse_table()]
    cuts = [int(at) for at in np.cumsum([0] + [table.shape[0] for table in tables])]
    inner_levels = [Level(1, range(inner), width, cuts[0])]
    outer_levels = [Level(1, range(inner, fine), width, cuts[0]), Level(2, range(coarse), width, cuts[3])]
    row_at = cuts[4]
    tables.append(row_table(outer_levels, strip_rows + PATCH))
    columns = max(table.shape[1] for table in tables)
    table = np.concatenate([np.pad(table, ((0, 0), (0, columns - table.shape[1]))) for table in tables])
    cuts[4] = table.shape[0]

    shifts = WINDOW * WINDOW
    hbm = pl.BlockSpec(memory_space=pltpu.HBM)
    vmem = pl.BlockSpec(memory_space=pltpu.VMEM)
    params = pltpu.CompilerParams(vmem_limit_bytes=28 * 1024 * 1024)
    own, table, mask_fine, mask_coarse = (
        pltpu.with_memory_space_constraint(value, pltpu.HBM)
        for value in (own, jnp.asarray(table), mask_fine, mask_coarse))

    def cost(flops):
        return pl.CostEstimate(flops=flops, bytes_accessed=4 * 10**6, transcendentals=0)

    maps, own_kept, handed = pl.pallas_call(
        functools.partial(inner_kernel, inner_levels, cuts),
        out_shape=(
            jax.ShapeDtypeStruct((2, inner, 4 * inner_levels[0].quads, shifts), f32),
            jax.ShapeDtypeStruct(own.shape, bf16),
            jax.ShapeDtypeStruct(table.shape, bf16),
        ),
        in_specs=[hbm, vmem, hbm, hbm],
        out_specs=(vmem,) * 3,
        scratch_shapes=[
            pltpu.VMEM(mask_fine.shape, jnp.int32),
            pltpu.VMEM((8, LANES), f32),
            pltpu.VMEM((row_places(inner_levels)[1], 2 * strip_rows), bf16),
            *section_scratch(inner_levels, width),
            *pair_scratch(inner_levels),
            pltpu.SemaphoreType.DMA((4,)),
        ],
        compiler_params=params,
        cost_estimate=cost(3 * 10**9),
        name="inner_blocks",
    )(own, others, mask_fine, table)
    return pl.pallas_call(
        functools.partial(outer_kernel, outer_levels, cuts, inner, row_at),
        out_shape=(
            jax.ShapeDtypeStruct((1, 2, fine, 4 * outer_levels[0].quads, shifts), f32),
            jax.ShapeDtypeStruct((1, 2, coarse, 4 * outer_levels[1].quads, shifts), f32),
        ),
        in_specs=[vmem] * 4 + [hbm] * 2 + [vmem] * 2,
        out_specs=(hbm, hbm),
        scratch_shapes=[
            pltpu.VMEM(mask_fine.shape, jnp.int32),
            pltpu.VMEM(mask_coarse.shape, jnp.int32),
            pltpu.VMEM((8, LANES), f32),
            pltpu.VMEM((8, LANES), f32),
            *(pltpu.VMEM((2, level.blocks, 4 * level.quads, shifts), f32) for level in outer_levels),
            *section_scratch(outer_levels, width),
            *pair_scratch(outer_levels),
            pltpu.SemaphoreType.DMA((8,)),
        ],
        compiler_params=params,
        cost_estimate=cost(4 * 10**9),
        name="outer_blocks",
    )(own_kept, others, rim, rims, mask_fine, mask_coarse, handed, maps)


def local(sections, mask_fine, mask_coarse):
    far = from_device(sections, 2, 0)
    near = from_device(sections, 1, 0)
    rim = from_device(sections, 0, 1)
    others = jnp.concatenate([near, far], axis=0)
    rims = from_device(others, 0, 1)
    return correlate(sections, others, rim, rims, mask_fine, mask_coarse)


def solution(mesh):
    in_specs = (
        P("sec", "strip", "groups"),
        P("sec", "strip", "groups"),
        P("sec", "strip", "groups"),
    )
    out_specs = (P("sec", None, "strip", "groups", None), P("sec", None, "strip", "groups", None))
    return jax.shard_map(local, mesh=mesh, in_specs=in_specs, out_specs=out_specs, check_vma=False)
```

```python
import functools

import jax
import jax.numpy as jnp
import numpy as np
from jax import lax
from jax.experimental import pallas as pl
from jax.experimental.pallas import tpu as pltpu
from jax.sharding import PartitionSpec as P

PATCH = 64
STRIDE = 32
WINDOW = 32
HALF = PATCH // 2
LANES = 128
NYQ = 16

f32 = jnp.float32
bf16 = jnp.bfloat16


def from_device(value, sec_steps, strip_steps):
    secs, strips = lax.axis_size("sec"), lax.axis_size("strip")
    pairs = []
    for sec in range(secs - sec_steps):
        for strip in range(strips - strip_steps):
            pairs.append(((sec + sec_steps) * strips + strip + strip_steps, sec * strips + strip))
    return lax.ppermute(value, ("sec", "strip"), pairs)


def wave(phase):
    turns = np.arange(PATCH) * (2 * np.pi / PATCH)
    cos = np.round(np.cos(turns), 14)
    sin = np.round(np.sin(turns), 14)
    phase = np.mod(phase, PATCH)
    return cos[phase], sin[phase]


def split_table(table):
    high = table.astype(jnp.bfloat16)
    low = (table - high.astype(np.float64)).astype(jnp.bfloat16)
    return high, low


def stacked(table):
    return np.concatenate(split_table(table), axis=0)


def fine_table():
    c, s = wave(np.arange(PATCH)[:, None] * np.arange(PATCH)[None, :])
    table = np.zeros((2, 2, PATCH, 2, 2, PATCH))
    for p in range(2):
        table[0, p, :, 0, p] = c
        table[1, p, :, 0, p] = -s
        table[0, p, :, 1, p] = -s
        table[1, p, :, 1, p] = -c
    return stacked(table.reshape(4 * PATCH, 4 * PATCH))


def coarse_table():
    c, s = wave((np.arange(2 * PATCH) // 2)[:, None] * np.arange(PATCH)[None, :])
    table = np.zeros((2, 2, 2 * PATCH, 2, 2, PATCH))
    for p in range(2):
        table[p, 0, :, 0, p] = 0.5 * c
        table[p, 1, :, 0, p] = -0.5 * s
        table[p, 0, :, 1, p] = -0.5 * s
        table[p, 1, :, 1, p] = -0.5 * c
    return stacked(table.reshape(8 * PATCH, 4 * PATCH))


def shift_tables():
    spread = 1.869545
    t = np.arange(WINDOW) - WINDOW // 2
    c, s = wave(np.arange(PATCH)[:, None] * t[None, :])
    table = np.zeros((2, 2, 2, PATCH, 2, 4, WINDOW))
    for odd in range(2):
        for p in range(2):
            table[odd, 0, p, :, 0, 2 * p + odd] = c
            table[odd, 1, p, :, 0, 2 * p + odd] = -s
            table[odd, 0, p, :, 1, 2 * p + odd] = s
            table[odd, 1, p, :, 1, 2 * p + odd] = c
    along_t = (spread * table.reshape(8 * PATCH, 8 * WINDOW)).astype(jnp.bfloat16)
    c, s = wave(t[:, None] * np.arange(HALF)[None, :])
    weight = np.where(np.arange(HALF) == 0, 1.0, 2.0)
    nyquist = np.repeat(wave(HALF * t)[0][:, None], NYQ, axis=1)
    along_s = np.concatenate([c * weight, -s * weight, nyquist], axis=1) / (spread * PATCH**3)
    high, low = split_table(along_s)
    along_s = np.concatenate(
        [np.concatenate([high, high], axis=1), np.concatenate([low, np.zeros_like(low)], axis=1)], axis=0)
    return along_t, along_s


class Level:
    def __init__(self, pool, blocks, width, table):
        self.pool, self.first, self.blocks, self.table = pool, blocks[0], len(blocks), table
        self.quads = width // (4 * pool * STRIDE)
        self.tiles = 2 * self.quads
        self.body = self.blocks * HALF
        self.half = -(-self.quads * self.blocks // 8) * 8
        self.rows = self.tiles * self.body + 2 * self.half
        self.cross_body = self.quads * self.body
        self.cross_rows = self.cross_body + -(-self.half // 16) * 16

    def window(self, tile, p):
        quad, odd = divmod(tile, 2)
        return self.pool * LANES * quad + LANES * p + self.pool * STRIDE * odd

    def nyquist_row(self, tile, b):
        quad, odd = divmod(tile, 2)
        return odd * self.half + quad * self.blocks + b


def row_places(levels):
    at, places = 0, []
    for level in levels:
        places.append([at, at + level.body])
        at += level.body + 2 * level.half
    for level, place in zip(levels, places):
        place.append(at)
        at += level.body
    return places, at


def row_table(levels, ext):
    places, size = row_places(levels)
    table = np.zeros((size, ext))
    k = np.arange(HALF)[:, None]
    for level, (cos_at, nyquist_at, sin_at) in zip(levels, places):
        pool = level.pool
        x = np.arange(pool * PATCH) // pool
        c, s = wave(k * x[None, :])
        for b in range(level.blocks):
            first = (level.first + b) * pool * STRIDE
            columns = slice(first, first + x.size)
            table[cos_at + b * HALF : cos_at + (b + 1) * HALF, columns] = c / pool
            table[sin_at + b * HALF : sin_at + (b + 1) * HALF, columns] = s / pool
            for tile in range(level.tiles):
                table[nyquist_at + level.nyquist_row(tile, b), columns] = wave(HALF * x)[0] / pool
    return np.concatenate(split_table(table), axis=1)


def split(value):
    high = value.astype(bf16)
    return high, (value - high.astype(f32)).astype(bf16)


def dot(left, right):
    return jnp.dot(left, right, preferred_element_type=f32)


def dot3(high, low, table_ref, at):
    depth = high.shape[1]
    table_high = table_ref[at : at + depth]
    table_low = table_ref[at + depth : at + 2 * depth]
    return dot(
        jnp.concatenate([high, low, high], axis=1),
        jnp.concatenate([table_high, table_high, table_low], axis=0))


def cosine(turns):
    turns = turns + PATCH // 4
    part = (turns & (HALF - 1)) - PATCH // 4
    angle = part.astype(f32) * (2 * np.pi / PATCH)
    square = angle * angle
    value = jnp.full(square.shape, 1.0 / 479001600, f32)
    for term in (-1.0 / 3628800, 1.0 / 40320, -1.0 / 720, 1.0 / 24, -0.5, 1.0):
        value = value * square + term
    return jnp.where((turns & HALF) == 0, value, -value)


def write_row_table(row_ref, level):
    (cos_at, nyquist_at, sin_at), = row_places([level])[0]
    ext = row_ref.shape[1] // 2

    def put(at, value):
        high, low = split(value)
        row_ref[at : at + value.shape[0], :ext] = high
        row_ref[at : at + value.shape[0], ext:] = low

    def inside(x):
        return jnp.where((x >= 0) & (x < PATCH), 1.0, 0.0)

    k = lax.broadcasted_iota(jnp.int32, (HALF, ext), 0)
    for b in range(level.blocks):
        x = lax.broadcasted_iota(jnp.int32, (HALF, ext), 1) - (level.first + b) * STRIDE
        put(cos_at + b * HALF, cosine(k * x) * inside(x))
        put(sin_at + b * HALF, cosine(k * x - PATCH // 4) * inside(x))
    row = lax.broadcasted_iota(jnp.int32, (2 * level.half, ext), 0)
    x = lax.broadcasted_iota(jnp.int32, (2 * level.half, ext), 1)
    x = x - (level.first + lax.rem(lax.rem(row, level.half), level.blocks)) * STRIDE
    put(nyquist_at, cosine(x * HALF) * inside(x))


def write_fine_table(table_ref, at):
    y = lax.broadcasted_iota(jnp.int32, (PATCH, LANES), 0)
    lane = lax.broadcasted_iota(jnp.int32, (PATCH, LANES), 1)
    frequency = lane & (PATCH - 1)
    c, s = cosine(y * frequency), cosine(y * frequency - PATCH // 4)
    depth = 4 * PATCH
    for p in range(2):
        mine = (lane >= PATCH) if p else (lane < PATCH)
        cos, minus_cos, minus_sin = (jnp.where(mine, value, 0.0) for value in (c, -c, -s))
        for number, pair in enumerate(((cos, minus_sin), (minus_sin, minus_cos))):
            to = at + (2 * number + p) * PATCH
            for half, value in enumerate(pair):
                for level, part in enumerate(split(value)):
                    table_ref[to + level * depth : to + level * depth + PATCH, half * LANES : (half + 1) * LANES] = part


def all_rows(value):
    for step in (4, 2, 1):
        value = value + pltpu.roll(value, step, 0)
    return value


def left_of(level, place, half_ref, odd_ref):
    cos_at, nyquist_at, sin_at = place
    pieces = []
    for tile in range(level.tiles):
        if tile % 2:
            pieces.append(odd_ref[tile // 2 * level.body : (tile // 2 + 1) * level.body])
        else:
            columns = []
            for p in range(level.pool):
                at = level.window(tile, p)
                columns += [half_ref[start : start + level.body, at : at + LANES] for start in (cos_at, sin_at)]
            pieces.append(jnp.concatenate(columns, axis=1))
    pieces.append(odd_ref[level.quads * level.body :])
    return jnp.concatenate(pieces, axis=0)


def gather_windows(level, place, t_ref, halves, odds):
    cos_at, nyquist_at, sin_at = place
    body, end = level.body, level.quads * level.body
    row = lax.broadcasted_iota(jnp.int32, (2 * level.half, LANES), 0)
    for p in range(level.pool):
        for source, target in zip(halves, odds):
            for tile in range(1, level.tiles, 2):
                at = level.window(tile, p)
                for half, start in enumerate((cos_at, sin_at)):
                    to = tile // 2 * body
                    target[to : to + body, (2 * p + half) * LANES : (2 * p + half + 1) * LANES] = (
                        source[start : start + body, at : at + LANES])
        nyquist = jnp.zeros((2 * level.half, LANES), f32)
        for tile in range(level.tiles):
            at, first = level.window(tile, p), level.nyquist_row(tile, 0)
            value = t_ref[nyquist_at : nyquist_at + 2 * level.half, at : at + LANES]
            nyquist = jnp.where((row >= first) & (row < first + level.blocks), value, nyquist)
        for target, part in zip(odds, split(nyquist)):
            target[end:, 2 * p * LANES : (2 * p + 1) * LANES] = part
            target[end:, (2 * p + 1) * LANES : (2 * p + 2) * LANES] = jnp.zeros(part.shape, bf16)


def spectrum_power(level, f_ref, sections):
    sub = lax.broadcasted_iota(jnp.int32, (8, LANES), 0)
    lane = lax.broadcasted_iota(jnp.int32, (8, LANES), 1)
    dc = (sub == 0) & (lane % PATCH == 0)
    group = lax.broadcasted_iota(jnp.int32, (LANES, LANES), 0) // PATCH
    same = group == lax.broadcasted_iota(jnp.int32, (LANES, LANES), 1) // PATCH
    ones = jnp.where(same, 1.0, 0.0).astype(bf16)

    def square(at):
        re, im = f_ref[at : at + 8, :LANES], f_ref[at : at + 8, LANES:]
        return re * re + im * im

    sums = []
    for z in sections:
        end = z * level.rows + level.tiles * level.body
        tails = [square(end + at) for at in range(0, 2 * level.half, 8)]
        for tile in range(level.tiles):
            for b in range(level.blocks):
                base = z * level.rows + tile * level.body + b * HALF
                total = jnp.where(dc, 0.0, square(base))
                head = jnp.where(sub == 0, total, 0.0)
                for r in range(8, HALF, 8):
                    total = total + square(base + r)
                row = level.nyquist_row(tile, b)
                sums.append(2.0 * total - head + jnp.where(sub == row % 8, tails[row // 8], 0.0))
    high, low = split(jnp.concatenate(sums, axis=0))
    return dot(jnp.concatenate([high, low], axis=1), jnp.concatenate([ones, ones], axis=0))


def scale_spectrum(level, f_ref, sections, sums, spec_ref):
    sub = lax.broadcasted_iota(jnp.int32, (8, 2 * LANES), 0)
    lane = lax.broadcasted_iota(jnp.int32, (8, 2 * LANES), 1)
    dc = (sub == 0) & (lane % PATCH == 0)
    number = 0
    for z in sections:
        start = z * level.rows
        end = start + level.tiles * level.body
        tails = [f_ref[end + at : end + at + 8] for at in range(0, 2 * level.half, 8)]
        scaled = [jnp.zeros_like(tail) for tail in tails]
        for tile in range(level.tiles):
            for b in range(level.blocks):
                scale = lax.rsqrt(all_rows(sums[number : number + 8]) * (1.0 / PATCH**4) + 1e-05)
                number += 8
                scale = jnp.concatenate([scale, scale], axis=1)
                for r in range(0, HALF, 16):
                    at = start + tile * level.body + b * HALF + r
                    head = f_ref[at : at + 8]
                    if r == 0:
                        head = jnp.where(dc, 0.0, head)
                    both = jnp.concatenate([head * scale, f_ref[at + 8 : at + 16] * scale], axis=0)
                    spec_ref[at : at + 16] = both.astype(bf16)
                row = level.nyquist_row(tile, b)
                scaled[row // 8] = jnp.where(sub == row % 8, tails[row // 8] * scale, scaled[row // 8])
        spec_ref[end : end + 2 * level.half] = jnp.concatenate(scaled, axis=0).astype(bf16)


def transform(levels, sections, strips, row_ref, table_ref, scratch, spec_refs):
    count = len(levels)
    t_ref, high_ref, low_ref = scratch[:3]
    odd_refs = scratch[3 : 3 + 2 * count]
    f_refs = scratch[3 + 2 * count :]
    places, size = row_places(levels)
    for z in sections:
        x = jnp.concatenate([strip[0] for strip in strips[z]], axis=0)
        width = x.shape[1]
        x = jnp.concatenate([x, x], axis=0)
        for first in range(0, width, 2 * LANES):
            columns = slice(first, first + 2 * LANES)
            t = dot(row_ref[...], x[:, columns])
            for level, (cos_at, nyquist_at, sin_at) in zip(levels, places):
                for start in (cos_at, sin_at):
                    for ref, half in zip((high_ref, low_ref), split(t[start : start + level.body])):
                        ref[z, start : start + level.body, columns] = half
                rows = slice(nyquist_at, nyquist_at + 2 * level.half)
                t_ref[z, rows, columns] = t[rows]
        t_ref[z, :, width:] = jnp.zeros((size, LANES), f32)
        for ref in (high_ref, low_ref):
            ref[z, :, width:] = jnp.zeros((size, LANES), bf16)
    for index, (level, place) in enumerate(zip(levels, places)):
        odds = odd_refs[2 * index : 2 * index + 2]
        for z in sections:
            gather_windows(level, place, t_ref.at[z], (high_ref.at[z], low_ref.at[z]), [ref.at[z] for ref in odds])
    for index, (level, place) in enumerate(zip(levels, places)):
        lefts = [
            jnp.concatenate([left_of(level, place, ref.at[z], odd.at[z]) for z in sections], axis=0)
            for ref, odd in zip((high_ref, low_ref), odd_refs[2 * index : 2 * index + 2])]
        rows = slice(sections[0] * level.rows, (sections[-1] + 1) * level.rows)
        f_refs[index][rows] = dot3(*lefts, table_ref, level.table)
    for level, f_ref, spec_ref in zip(levels, f_refs, spec_refs):
        scale_spectrum(level, f_ref, sections, spectrum_power(level, f_ref, sections), spec_ref)


def write_maps(levels, own_specs, specs, masks, table_ref, shift_at, map_at, scratch, outs):
    cross_ref, y_ref, maps_ref, rows_ref, *stacks = scratch
    pairs = 2
    base = 0
    for level, own, spec in zip(levels, own_specs, specs):
        def cross(at, rows):
            a = own[at : at + rows].astype(f32)
            ar, ai = a[:, :LANES], a[:, LANES:]
            for d in range(pairs):
                b = spec[d * level.rows + at : d * level.rows + at + rows].astype(f32)
                br, bi = b[:, :LANES], b[:, LANES:]
                yield base + d * level.cross_rows, jnp.concatenate([ar * br + ai * bi, ar * bi - ai * br], axis=1)

        for tile in range(level.tiles):
            quad, odd = divmod(tile, 2)
            for r in range(0, level.body, 16):
                for to, value in cross(tile * level.body + r, 16):
                    to += quad * level.body + r
                    cross_ref[to : to + 16, 2 * odd * LANES : 2 * (odd + 1) * LANES] = value.astype(bf16)
        for to, value in cross(level.tiles * level.body, 2 * level.half):
            value = jnp.concatenate([value[: level.half], value[level.half :]], axis=1)
            spare = level.cross_rows - level.cross_body - level.half
            if spare:
                value = jnp.concatenate([value, jnp.zeros((spare, 4 * LANES), f32)], axis=0)
            cross_ref[to + level.cross_body : to + level.cross_rows] = value.astype(bf16)
        base += pairs * level.cross_rows
    y_ref[...] = dot(cross_ref[...], table_ref[shift_at : shift_at + 4 * LANES])
    base = tile = 0
    starts = {}
    row = lax.broadcasted_iota(jnp.int32, (NYQ, LANES), 0)
    for index, level in enumerate(levels):
        for b in range(level.blocks):
            stack_ref = stacks[index]
            for d in range(pairs):
                first = base + d * level.cross_rows
                nyq_at = first + level.cross_body
                nyquist = y_ref[nyq_at : nyq_at + NYQ, :LANES]
                for quad in range(level.quads):
                    top = first + quad * level.body + b * HALF
                    column = (d * level.quads + quad) * LANES
                    for at, value in (
                        (0, y_ref[top : top + HALF, :LANES]),
                        (HALF, y_ref[top : top + HALF, LANES:]),
                        (2 * HALF, jnp.where(row == quad * level.blocks + b, nyquist, 0.0)),
                    ):
                        for half, part in enumerate(split(value)):
                            to = half * (2 * HALF + NYQ) + at
                            stack_ref[to : to + value.shape[0], column : column + LANES] = part
            both = dot(table_ref[map_at : map_at + 2 * WINDOW, : stack_ref.shape[0]], stack_ref[...])
            maps = both[:WINDOW] + both[WINDOW:]
            for d in range(pairs):
                starts[index, d, b] = tile
                for quad in range(level.quads):
                    column = (d * level.quads + quad) * LANES
                    maps_ref[tile] = maps[:, column : column + LANES]
                    tile += 1
        base += pairs * level.cross_rows
    kept = [jnp.transpose(mask()) for mask in masks]
    lane = lax.broadcasted_iota(jnp.int32, (tile, LANES), 1)

    def exchange(low, high, width):
        even = (lane & width) == 0
        return (
            jnp.where(even, low, pltpu.roll(high, width, 1)),
            jnp.where(even, pltpu.roll(low, LANES - width, 1), high))

    for big in range(WINDOW // 4):
        rows = [maps_ref[:, 4 * big + r, :] for r in range(4)]
        for step in (2, 1):
            for r in range(4):
                if not r & step:
                    rows[r], rows[r + step] = exchange(rows[r], rows[r + step], step * WINDOW)
        for g in range(4):
            rows_ref[big, pl.ds(g, tile, stride=4), :] = rows[g]
        for index, (level, out) in enumerate(zip(levels, outs)):
            for b in range(level.blocks):
                column = kept[index][: 4 * level.quads, level.first + b : level.first + b + 1]
                for d in range(pairs):
                    at = 4 * starts[index, d, b]
                    out[d, b, :, big * LANES : (big + 1) * LANES] = rows_ref[big, at : at + 4 * level.quads] * column


def mask_tile(mask_ref, pad_ref):
    pad_ref[...] = jnp.zeros(pad_ref.shape, f32)
    pad_ref[: mask_ref.shape[1], : mask_ref.shape[2]] = mask_ref[0].astype(f32)
    return pad_ref[...]


def section_scratch(levels, width, count):
    size = row_places(levels)[1]
    return [
        pltpu.VMEM((count, size, width + LANES), f32),
        pltpu.VMEM((count, size, width + LANES), bf16),
        pltpu.VMEM((count, size, width + LANES), bf16),
        *(pltpu.VMEM((count, level.quads * level.body + 2 * level.half, 2 * level.pool * LANES), bf16)
          for level in levels for _ in range(2)),
        *(pltpu.VMEM((count * level.rows, 2 * LANES), f32) for level in levels),
    ]


def spec_scratch(levels, count):
    return [pltpu.VMEM((count * level.rows, 2 * LANES), bf16) for level in levels]


def pair_scratch(levels):
    rows = sum(2 * level.cross_rows for level in levels)
    tiles = sum(2 * level.blocks * level.quads for level in levels)
    return [
        pltpu.VMEM((rows, 4 * LANES), bf16),
        pltpu.VMEM((rows, 2 * LANES), f32),
        pltpu.VMEM((tiles, WINDOW, LANES), f32),
        pltpu.VMEM((WINDOW // 4, 4 * tiles, LANES), f32),
        *(pltpu.VMEM((4 * HALF + 2 * NYQ, 2 * level.quads * LANES), bf16) for level in levels),
    ]


def copier(sems):
    used = []

    def start(source, target):
        copy = pltpu.make_async_copy(source, target, sems.at[len(used)])
        used.append(copy)
        copy.start()
        return copy.wait

    return start


def inner_kernel(
    levels, cuts,
    own_hbm, near, far, mask_hbm, table_hbm,
    maps, own, table_ref,
    mask, pad, row_ref, *rest,
):
    *scratch, sems = rest
    start = copier(sems)

    def table(first, last):
        piece = pl.ds(first, last - first)
        return start(table_hbm.at[piece], table_ref.at[piece])

    fine_at, shift_at, map_at, coarse_at, end = cuts
    own_ready = start(own_hbm, own)
    shift_ready = table(shift_at, coarse_at)
    mask_ready = start(mask_hbm, mask)
    coarse_ready = table(coarse_at, end)
    write_row_table(row_ref, levels[0])
    write_fine_table(table_ref, fine_at)
    size = 3 + 3 * len(levels)
    sections, spec_refs, rest = scratch[:size], scratch[size : size + 1], scratch[size + 1 :]
    strips = ((near,), (far,), (own,))
    transform(levels, (0, 1), strips, row_ref, table_ref, sections, spec_refs)
    own_ready()
    transform(levels, (2,), strips, row_ref, table_ref, sections, spec_refs)
    shift_ready()
    mask_ready()
    rows = levels[0].rows
    write_maps(
        levels, [spec_refs[0].at[pl.ds(2 * rows, rows)]], spec_refs, (lambda: mask_tile(mask, pad),), table_ref,
        shift_at, map_at, rest, (maps,))
    coarse_ready()


def own_kernel(levels, row_at, own, rim, table_ref, *rest):
    spec_refs, sections = rest[: len(levels)], rest[len(levels) :]
    row_ref = table_ref.at[pl.ds(row_at, row_places(levels)[1])]
    transform(levels, (0,), ((own, rim),), row_ref, table_ref, sections, spec_refs)


def outer_kernel(
    levels, cuts, inner, row_at,
    near, far, rim_near, rim_far, mask_hbm, mask_coarse_hbm, table_ref, own_fine, own_coarse, inner_maps,
    out_fine, out_coarse,
    mask, mask_coarse, pad, pad_coarse, maps, maps_coarse, *rest,
):
    *scratch, sems = rest
    start = copier(sems)
    masks_ready = [start(mask_hbm, mask), start(mask_coarse_hbm, mask_coarse)]
    stores = [start(inner_maps.at[d], out_fine.at[0, d, pl.ds(0, inner)]) for d in range(2)]
    fine_at, shift_at, map_at, coarse_at, end = cuts
    row_ref = table_ref.at[pl.ds(row_at, row_places(levels)[1])]
    size, count = 3 + 3 * len(levels), len(levels)
    sections, spec_refs, rest = scratch[:size], scratch[size : size + count], scratch[size + count :]
    strips = ((near, rim_near), (far, rim_far))
    transform(levels, (0, 1), strips, row_ref, table_ref, sections, spec_refs)
    for wait in masks_ready:
        wait()
    write_maps(
        levels, (own_fine, own_coarse), spec_refs,
        (lambda: mask_tile(mask, pad), lambda: mask_tile(mask_coarse, pad_coarse)), table_ref, shift_at, map_at,
        rest, (maps, maps_coarse))
    for d in range(2):
        stores.append(start(maps.at[d], out_fine.at[0, d, pl.ds(inner, levels[0].blocks)]))
        stores.append(start(maps_coarse.at[d], out_coarse.at[0, d]))
    for wait in stores:
        wait()


def correlate(own, near, far, rim, rim_near, rim_far, mask_fine, mask_coarse):
    strip_rows, width = own.shape[1:]
    fine, coarse = mask_fine.shape[1], mask_coarse.shape[1]
    inner = fine - 1
    shift, map_ = shift_tables()
    tables = [fine_table(), shift, map_, coarse_table()]
    cuts = [int(at) for at in np.cumsum([0] + [table.shape[0] for table in tables])]
    inner_levels = [Level(1, range(inner), width, cuts[0])]
    outer_levels = [Level(1, range(inner, fine), width, cuts[0]), Level(2, range(coarse), width, cuts[3])]
    row_at = cuts[4]
    tables.append(row_table(outer_levels, strip_rows + PATCH))
    columns = max(table.shape[1] for table in tables)
    table = np.concatenate([np.pad(table, ((0, 0), (0, columns - table.shape[1]))) for table in tables])
    cuts[4] = table.shape[0]

    shifts = WINDOW * WINDOW
    hbm = pl.BlockSpec(memory_space=pltpu.HBM)
    vmem = pl.BlockSpec(memory_space=pltpu.VMEM)
    params = pltpu.CompilerParams(vmem_limit_bytes=28 * 1024 * 1024)
    own, table, mask_fine, mask_coarse = (
        pltpu.with_memory_space_constraint(value, pltpu.HBM)
        for value in (own, jnp.asarray(table), mask_fine, mask_coarse))

    def cost(flops):
        return pl.CostEstimate(flops=flops, bytes_accessed=4 * 10**6, transcendentals=0)

    maps, own_kept, handed = pl.pallas_call(
        functools.partial(inner_kernel, inner_levels, cuts),
        out_shape=(
            jax.ShapeDtypeStruct((2, inner, 4 * inner_levels[0].quads, shifts), f32),
            jax.ShapeDtypeStruct(own.shape, bf16),
            jax.ShapeDtypeStruct(table.shape, bf16),
        ),
        in_specs=[hbm, vmem, vmem, hbm, hbm],
        out_specs=(vmem,) * 3,
        scratch_shapes=[
            pltpu.VMEM(mask_fine.shape, jnp.int32),
            pltpu.VMEM((8, LANES), f32),
            pltpu.VMEM((row_places(inner_levels)[1], 2 * strip_rows), bf16),
            *section_scratch(inner_levels, width, 3),
            *spec_scratch(inner_levels, 3),
            *pair_scratch(inner_levels),
            pltpu.SemaphoreType.DMA((4,)),
        ],
        compiler_params=params,
        cost_estimate=cost(3 * 10**9),
        name="inner_blocks",
    )(own, near, far, mask_fine, table)
    own_specs = pl.pallas_call(
        functools.partial(own_kernel, outer_levels, row_at),
        out_shape=tuple(jax.ShapeDtypeStruct((level.rows, 2 * LANES), bf16) for level in outer_levels),
        in_specs=[vmem] * 3,
        out_specs=(vmem,) * 2,
        scratch_shapes=section_scratch(outer_levels, width, 1),
        compiler_params=params,
        cost_estimate=cost(2 * 10**9),
        name="own_outer_blocks",
    )(own_kept, rim, handed)
    return pl.pallas_call(
        functools.partial(outer_kernel, outer_levels, cuts, inner, row_at),
        out_shape=(
            jax.ShapeDtypeStruct((1, 2, fine, 4 * outer_levels[0].quads, shifts), f32),
            jax.ShapeDtypeStruct((1, 2, coarse, 4 * outer_levels[1].quads, shifts), f32),
        ),
        in_specs=[vmem] * 4 + [hbm] * 2 + [vmem] * 4,
        out_specs=(hbm, hbm),
        scratch_shapes=[
            pltpu.VMEM(mask_fine.shape, jnp.int32),
            pltpu.VMEM(mask_coarse.shape, jnp.int32),
            pltpu.VMEM((8, LANES), f32),
            pltpu.VMEM((8, LANES), f32),
            *(pltpu.VMEM((2, level.blocks, 4 * level.quads, shifts), f32) for level in outer_levels),
            *section_scratch(outer_levels, width, 2),
            *spec_scratch(outer_levels, 2),
            *pair_scratch(outer_levels),
            pltpu.SemaphoreType.DMA((8,)),
        ],
        compiler_params=params,
        cost_estimate=cost(4 * 10**9),
        name="outer_blocks",
    )(near, far, rim_near, rim_far, mask_fine, mask_coarse, handed, *own_specs, maps)


def local(sections, mask_fine, mask_coarse):
    far = from_device(sections, 2, 0)
    near = from_device(sections, 1, 0)
    rims = [from_device(sections, z, 1) for z in range(3)]
    return correlate(sections, near, far, *rims, mask_fine, mask_coarse)


def solution(mesh):
    in_specs = (
        P("sec", "strip", "groups"),
        P("sec", "strip", "groups"),
        P("sec", "strip", "groups"),
    )
    out_specs = (P("sec", None, "strip", "groups", None), P("sec", None, "strip", "groups", None))
    return jax.shard_map(local, mesh=mesh, in_specs=in_specs, out_specs=out_specs, check_vma=False)
```

```python
import functools

import jax
import jax.numpy as jnp
import numpy as np
from jax import lax
from jax.experimental import pallas as pl
from jax.experimental.pallas import tpu as pltpu
from jax.sharding import PartitionSpec as P

PATCH = 64
STRIDE = 32
WINDOW = 32
HALF = PATCH // 2
LANES = 128
NYQ = 16

f32 = jnp.float32
bf16 = jnp.bfloat16


def from_device(value, sec_steps, strip_steps):
    secs, strips = lax.axis_size("sec"), lax.axis_size("strip")
    pairs = []
    for sec in range(secs - sec_steps):
        for strip in range(strips - strip_steps):
            pairs.append(((sec + sec_steps) * strips + strip + strip_steps, sec * strips + strip))
    return lax.ppermute(value, ("sec", "strip"), pairs)


def wave(phase):
    turns = np.arange(PATCH) * (2 * np.pi / PATCH)
    cos = np.round(np.cos(turns), 14)
    sin = np.round(np.sin(turns), 14)
    phase = np.mod(phase, PATCH)
    return cos[phase], sin[phase]


def split_table(table):
    high = table.astype(jnp.bfloat16)
    low = (table - high.astype(np.float64)).astype(jnp.bfloat16)
    return high, low


def stacked(table):
    return np.concatenate(split_table(table), axis=0)


def fine_table():
    c, s = wave(np.arange(PATCH)[:, None] * np.arange(PATCH)[None, :])
    table = np.zeros((2, 2, PATCH, 2, 2, PATCH))
    for p in range(2):
        table[0, p, :, 0, p] = c
        table[1, p, :, 0, p] = -s
        table[0, p, :, 1, p] = -s
        table[1, p, :, 1, p] = -c
    return stacked(table.reshape(4 * PATCH, 4 * PATCH))


def coarse_table():
    c, s = wave((np.arange(2 * PATCH) // 2)[:, None] * np.arange(PATCH)[None, :])
    table = np.zeros((2, 2, 2 * PATCH, 2, 2, PATCH))
    for p in range(2):
        table[p, 0, :, 0, p] = 0.5 * c
        table[p, 1, :, 0, p] = -0.5 * s
        table[p, 0, :, 1, p] = -0.5 * s
        table[p, 1, :, 1, p] = -0.5 * c
    return stacked(table.reshape(8 * PATCH, 4 * PATCH))


def shift_tables():
    spread = 1.869545
    t = np.arange(WINDOW) - WINDOW // 2
    c, s = wave(np.arange(PATCH)[:, None] * t[None, :])
    table = np.zeros((2, 2, 2, PATCH, 2, 4, WINDOW))
    for odd in range(2):
        for p in range(2):
            table[odd, 0, p, :, 0, 2 * p + odd] = c
            table[odd, 1, p, :, 0, 2 * p + odd] = -s
            table[odd, 0, p, :, 1, 2 * p + odd] = s
            table[odd, 1, p, :, 1, 2 * p + odd] = c
    along_t = (spread * table.reshape(8 * PATCH, 8 * WINDOW)).astype(jnp.bfloat16)
    c, s = wave(t[:, None] * np.arange(HALF)[None, :])
    weight = np.where(np.arange(HALF) == 0, 1.0, 2.0)
    nyquist = np.repeat(wave(HALF * t)[0][:, None], NYQ, axis=1)
    along_s = np.concatenate([c * weight, -s * weight, nyquist], axis=1) / (spread * PATCH**3)
    high, low = split_table(along_s)
    along_s = np.concatenate(
        [np.concatenate([high, high], axis=1), np.concatenate([low, np.zeros_like(low)], axis=1)], axis=0)
    return along_t, along_s


class Level:
    def __init__(self, pool, blocks, width, table):
        self.pool, self.first, self.blocks, self.table = pool, blocks[0], len(blocks), table
        self.quads = width // (4 * pool * STRIDE)
        self.tiles = 2 * self.quads
        self.body = self.blocks * HALF
        self.half = -(-self.quads * self.blocks // 8) * 8
        self.rows = self.tiles * self.body + 2 * self.half
        self.cross_body = self.quads * self.body
        self.cross_rows = self.cross_body + -(-self.half // 16) * 16

    def window(self, tile, p):
        quad, odd = divmod(tile, 2)
        return self.pool * LANES * quad + LANES * p + self.pool * STRIDE * odd

    def nyquist_row(self, tile, b):
        quad, odd = divmod(tile, 2)
        return odd * self.half + quad * self.blocks + b


def row_places(levels):
    at, places = 0, []
    for level in levels:
        places.append([at, at + level.body])
        at += level.body + 2 * level.half
    for level, place in zip(levels, places):
        place.append(at)
        at += level.body
    return places, at


def row_table(levels, ext):
    places, size = row_places(levels)
    table = np.zeros((size, ext))
    k = np.arange(HALF)[:, None]
    for level, (cos_at, nyquist_at, sin_at) in zip(levels, places):
        pool = level.pool
        x = np.arange(pool * PATCH) // pool
        c, s = wave(k * x[None, :])
        for b in range(level.blocks):
            first = (level.first + b) * pool * STRIDE
            columns = slice(first, first + x.size)
            table[cos_at + b * HALF : cos_at + (b + 1) * HALF, columns] = c / pool
            table[sin_at + b * HALF : sin_at + (b + 1) * HALF, columns] = s / pool
            for tile in range(level.tiles):
                table[nyquist_at + level.nyquist_row(tile, b), columns] = wave(HALF * x)[0] / pool
    return np.concatenate(split_table(table), axis=1)


def split(value):
    high = value.astype(bf16)
    return high, (value - high.astype(f32)).astype(bf16)


def dot(left, right):
    return jnp.dot(left, right, preferred_element_type=f32)


def dot3(high, low, table_ref, at):
    depth = high.shape[1]
    table_high = table_ref[at : at + depth]
    table_low = table_ref[at + depth : at + 2 * depth]
    return dot(
        jnp.concatenate([high, low, high], axis=1),
        jnp.concatenate([table_high, table_high, table_low], axis=0))


def cosine(turns):
    turns = turns + PATCH // 4
    part = (turns & (HALF - 1)) - PATCH // 4
    angle = part.astype(f32) * (2 * np.pi / PATCH)
    square = angle * angle
    value = jnp.full(square.shape, 1.0 / 479001600, f32)
    for term in (-1.0 / 3628800, 1.0 / 40320, -1.0 / 720, 1.0 / 24, -0.5, 1.0):
        value = value * square + term
    return jnp.where((turns & HALF) == 0, value, -value)


def write_row_table(row_ref, level):
    (cos_at, nyquist_at, sin_at), = row_places([level])[0]
    ext = row_ref.shape[1] // 2

    def put(at, value):
        high, low = split(value)
        row_ref[at : at + value.shape[0], :ext] = high
        row_ref[at : at + value.shape[0], ext:] = low

    def inside(x):
        return jnp.where((x >= 0) & (x < PATCH), 1.0, 0.0)

    k = lax.broadcasted_iota(jnp.int32, (HALF, ext), 0)
    for b in range(level.blocks):
        x = lax.broadcasted_iota(jnp.int32, (HALF, ext), 1) - (level.first + b) * STRIDE
        put(cos_at + b * HALF, cosine(k * x) * inside(x))
        put(sin_at + b * HALF, cosine(k * x - PATCH // 4) * inside(x))
    row = lax.broadcasted_iota(jnp.int32, (2 * level.half, ext), 0)
    x = lax.broadcasted_iota(jnp.int32, (2 * level.half, ext), 1)
    x = x - (level.first + lax.rem(lax.rem(row, level.half), level.blocks)) * STRIDE
    put(nyquist_at, cosine(x * HALF) * inside(x))


def write_fine_table(table_ref, at):
    y = lax.broadcasted_iota(jnp.int32, (PATCH, LANES), 0)
    lane = lax.broadcasted_iota(jnp.int32, (PATCH, LANES), 1)
    frequency = lane & (PATCH - 1)
    c, s = cosine(y * frequency), cosine(y * frequency - PATCH // 4)
    depth = 4 * PATCH
    for p in range(2):
        mine = (lane >= PATCH) if p else (lane < PATCH)
        cos, minus_cos, minus_sin = (jnp.where(mine, value, 0.0) for value in (c, -c, -s))
        for number, pair in enumerate(((cos, minus_sin), (minus_sin, minus_cos))):
            to = at + (2 * number + p) * PATCH
            for half, value in enumerate(pair):
                for level, part in enumerate(split(value)):
                    table_ref[to + level * depth : to + level * depth + PATCH, half * LANES : (half + 1) * LANES] = part


def all_rows(value):
    for step in (4, 2, 1):
        value = value + pltpu.roll(value, step, 0)
    return value


def left_of(level, place, half_ref, odd_ref):
    cos_at, nyquist_at, sin_at = place
    pieces = []
    for tile in range(level.tiles):
        if tile % 2:
            pieces.append(odd_ref[tile // 2 * level.body : (tile // 2 + 1) * level.body])
        else:
            columns = []
            for p in range(level.pool):
                at = level.window(tile, p)
                columns += [half_ref[start : start + level.body, at : at + LANES] for start in (cos_at, sin_at)]
            pieces.append(jnp.concatenate(columns, axis=1))
    pieces.append(odd_ref[level.quads * level.body :])
    return jnp.concatenate(pieces, axis=0)


def gather_windows(level, place, t_ref, halves, odds):
    cos_at, nyquist_at, sin_at = place
    body, end = level.body, level.quads * level.body
    row = lax.broadcasted_iota(jnp.int32, (2 * level.half, LANES), 0)
    for p in range(level.pool):
        for source, target in zip(halves, odds):
            for tile in range(1, level.tiles, 2):
                at = level.window(tile, p)
                for half, start in enumerate((cos_at, sin_at)):
                    to = tile // 2 * body
                    target[to : to + body, (2 * p + half) * LANES : (2 * p + half + 1) * LANES] = (
                        source[start : start + body, at : at + LANES])
        nyquist = jnp.zeros((2 * level.half, LANES), f32)
        for tile in range(level.tiles):
            at, first = level.window(tile, p), level.nyquist_row(tile, 0)
            value = t_ref[nyquist_at : nyquist_at + 2 * level.half, at : at + LANES]
            nyquist = jnp.where((row >= first) & (row < first + level.blocks), value, nyquist)
        for target, part in zip(odds, split(nyquist)):
            target[end:, 2 * p * LANES : (2 * p + 1) * LANES] = part
            target[end:, (2 * p + 1) * LANES : (2 * p + 2) * LANES] = jnp.zeros(part.shape, bf16)


def spectrum_power(level, f_ref, sections):
    sub = lax.broadcasted_iota(jnp.int32, (8, LANES), 0)
    lane = lax.broadcasted_iota(jnp.int32, (8, LANES), 1)
    dc = (sub == 0) & (lane % PATCH == 0)
    group = lax.broadcasted_iota(jnp.int32, (LANES, LANES), 0) // PATCH
    same = group == lax.broadcasted_iota(jnp.int32, (LANES, LANES), 1) // PATCH
    ones = jnp.where(same, 1.0, 0.0).astype(bf16)

    def square(at):
        re, im = f_ref[at : at + 8, :LANES], f_ref[at : at + 8, LANES:]
        return re * re + im * im

    sums = []
    for z in sections:
        end = z * level.rows + level.tiles * level.body
        tails = [square(end + at) for at in range(0, 2 * level.half, 8)]
        for tile in range(level.tiles):
            for b in range(level.blocks):
                base = z * level.rows + tile * level.body + b * HALF
                total = jnp.where(dc, 0.0, square(base))
                head = jnp.where(sub == 0, total, 0.0)
                for r in range(8, HALF, 8):
                    total = total + square(base + r)
                row = level.nyquist_row(tile, b)
                sums.append(2.0 * total - head + jnp.where(sub == row % 8, tails[row // 8], 0.0))
    high, low = split(jnp.concatenate(sums, axis=0))
    return dot(jnp.concatenate([high, low], axis=1), jnp.concatenate([ones, ones], axis=0))


def scale_spectrum(level, f_ref, sections, sums, spec_ref):
    sub = lax.broadcasted_iota(jnp.int32, (8, 2 * LANES), 0)
    lane = lax.broadcasted_iota(jnp.int32, (8, 2 * LANES), 1)
    dc = (sub == 0) & (lane % PATCH == 0)
    number = 0
    for z in sections:
        start = z * level.rows
        end = start + level.tiles * level.body
        tails = [f_ref[end + at : end + at + 8] for at in range(0, 2 * level.half, 8)]
        scaled = [jnp.zeros_like(tail) for tail in tails]
        for tile in range(level.tiles):
            for b in range(level.blocks):
                scale = lax.rsqrt(all_rows(sums[number : number + 8]) * (1.0 / PATCH**4) + 1e-05)
                number += 8
                scale = jnp.concatenate([scale, scale], axis=1)
                for r in range(0, HALF, 16):
                    at = start + tile * level.body + b * HALF + r
                    head = f_ref[at : at + 8]
                    if r == 0:
                        head = jnp.where(dc, 0.0, head)
                    both = jnp.concatenate([head * scale, f_ref[at + 8 : at + 16] * scale], axis=0)
                    spec_ref[at : at + 16] = both.astype(bf16)
                row = level.nyquist_row(tile, b)
                scaled[row // 8] = jnp.where(sub == row % 8, tails[row // 8] * scale, scaled[row // 8])
        spec_ref[end : end + 2 * level.half] = jnp.concatenate(scaled, axis=0).astype(bf16)


def transform_rows(levels, sections, strips, row_ref, scratch):
    t_ref, high_ref, low_ref = scratch[:3]
    odd_refs = scratch[3 : 3 + 2 * len(levels)]
    places, size = row_places(levels)
    for z in sections:
        x = jnp.concatenate([strip[0] for strip in strips[z]], axis=0)
        width = x.shape[1]
        x = jnp.concatenate([x, x], axis=0)
        for first in range(0, width, 2 * LANES):
            columns = slice(first, first + 2 * LANES)
            t = dot(row_ref[...], x[:, columns])
            for level, (cos_at, nyquist_at, sin_at) in zip(levels, places):
                for start in (cos_at, sin_at):
                    for ref, half in zip((high_ref, low_ref), split(t[start : start + level.body])):
                        ref[z, start : start + level.body, columns] = half
                rows = slice(nyquist_at, nyquist_at + 2 * level.half)
                t_ref[z, rows, columns] = t[rows]
        t_ref[z, :, width:] = jnp.zeros((size, LANES), f32)
        for ref in (high_ref, low_ref):
            ref[z, :, width:] = jnp.zeros((size, LANES), bf16)
    for index, (level, place) in enumerate(zip(levels, places)):
        odds = odd_refs[2 * index : 2 * index + 2]
        for z in sections:
            gather_windows(level, place, t_ref.at[z], (high_ref.at[z], low_ref.at[z]), [ref.at[z] for ref in odds])


def transform_columns(levels, sections, table_ref, scratch, spec_refs):
    high_ref, low_ref = scratch[1:3]
    odd_refs, f_refs = scratch[3 : 3 + 2 * len(levels)], scratch[3 + 2 * len(levels) :]
    places, size = row_places(levels)
    for index, (level, place) in enumerate(zip(levels, places)):
        lefts = [
            jnp.concatenate([left_of(level, place, ref.at[z], odd.at[z]) for z in sections], axis=0)
            for ref, odd in zip((high_ref, low_ref), odd_refs[2 * index : 2 * index + 2])]
        rows = slice(sections[0] * level.rows, (sections[-1] + 1) * level.rows)
        f_refs[index][rows] = dot3(*lefts, table_ref, level.table)
    for level, f_ref, spec_ref in zip(levels, f_refs, spec_refs):
        scale_spectrum(level, f_ref, sections, spectrum_power(level, f_ref, sections), spec_ref)


def write_maps(levels, pairs, own_specs, specs, kept, table_ref, shift_at, map_at, scratch, outs):
    cross_ref, y_ref, maps_ref, rows_ref, *stacks = scratch
    base = 0
    for level, own, spec in zip(levels, own_specs, specs):
        def cross(at, rows):
            a = own[at : at + rows].astype(f32)
            ar, ai = a[:, :LANES], a[:, LANES:]
            for d in range(pairs):
                b = spec[d * level.rows + at : d * level.rows + at + rows].astype(f32)
                br, bi = b[:, :LANES], b[:, LANES:]
                yield base + d * level.cross_rows, jnp.concatenate([ar * br + ai * bi, ar * bi - ai * br], axis=1)

        for tile in range(level.tiles):
            quad, odd = divmod(tile, 2)
            for r in range(0, level.body, 16):
                for to, value in cross(tile * level.body + r, 16):
                    to += quad * level.body + r
                    cross_ref[to : to + 16, 2 * odd * LANES : 2 * (odd + 1) * LANES] = value.astype(bf16)
        for to, value in cross(level.tiles * level.body, 2 * level.half):
            value = jnp.concatenate([value[: level.half], value[level.half :]], axis=1)
            spare = level.cross_rows - level.cross_body - level.half
            if spare:
                value = jnp.concatenate([value, jnp.zeros((spare, 4 * LANES), f32)], axis=0)
            cross_ref[to + level.cross_body : to + level.cross_rows] = value.astype(bf16)
        base += pairs * level.cross_rows
    y_ref[:base] = dot(cross_ref[:base], table_ref[shift_at : shift_at + 4 * LANES])
    base = tile = 0
    starts = {}
    row = lax.broadcasted_iota(jnp.int32, (NYQ, LANES), 0)
    for index, level in enumerate(levels):
        for b in range(level.blocks):
            stack_ref = stacks[index]
            for d in range(pairs):
                first = base + d * level.cross_rows
                nyq_at = first + level.cross_body
                nyquist = y_ref[nyq_at : nyq_at + NYQ, :LANES]
                for quad in range(level.quads):
                    top = first + quad * level.body + b * HALF
                    column = (d * level.quads + quad) * LANES
                    for at, value in (
                        (0, y_ref[top : top + HALF, :LANES]),
                        (HALF, y_ref[top : top + HALF, LANES:]),
                        (2 * HALF, jnp.where(row == quad * level.blocks + b, nyquist, 0.0)),
                    ):
                        for half, part in enumerate(split(value)):
                            to = half * (2 * HALF + NYQ) + at
                            stack_ref[to : to + value.shape[0], column : column + LANES] = part
            columns = pairs * level.quads * LANES
            both = dot(table_ref[map_at : map_at + 2 * WINDOW, : stack_ref.shape[0]], stack_ref[:, :columns])
            maps = both[:WINDOW] + both[WINDOW:]
            for d in range(pairs):
                starts[index, d, b] = tile
                for quad in range(level.quads):
                    column = (d * level.quads + quad) * LANES
                    maps_ref[tile] = maps[:, column : column + LANES]
                    tile += 1
        base += pairs * level.cross_rows
    lane = lax.broadcasted_iota(jnp.int32, (tile, LANES), 1)

    def exchange(low, high, width):
        even = (lane & width) == 0
        return (
            jnp.where(even, low, pltpu.roll(high, width, 1)),
            jnp.where(even, pltpu.roll(low, LANES - width, 1), high))

    for big in range(WINDOW // 4):
        rows = [maps_ref[:tile, 4 * big + r, :] for r in range(4)]
        for step in (2, 1):
            for r in range(4):
                if not r & step:
                    rows[r], rows[r + step] = exchange(rows[r], rows[r + step], step * WINDOW)
        for g in range(4):
            rows_ref[big, pl.ds(g, tile, stride=4), :] = rows[g]
        for index, (level, out) in enumerate(zip(levels, outs)):
            for b in range(level.blocks):
                column = kept[index][: 4 * level.quads, level.first + b : level.first + b + 1]
                for d in range(pairs):
                    at = 4 * starts[index, d, b]
                    out[d, b, :, big * LANES : (big + 1) * LANES] = rows_ref[big, at : at + 4 * level.quads] * column


def write_mask_columns(mask_ref, pad_ref, kept_ref):
    pad_ref[...] = jnp.zeros(pad_ref.shape, f32)
    pad_ref[: mask_ref.shape[1], : mask_ref.shape[2]] = mask_ref[0].astype(f32)
    kept_ref[...] = jnp.transpose(pad_ref[...])


def sections_ahead():
    return lax.axis_size("sec") - 1 - lax.axis_index("sec")


def for_pairs(run):
    ahead = sections_ahead()
    pl.when(ahead >= 2)(lambda: run(2))
    pl.when(ahead == 1)(lambda: run(1))
    pl.when(ahead < 1)(lambda: run(0))


def clear_maps(pairs, outs):
    for out in outs:
        if pairs < 2:
            out[pairs:] = jnp.zeros((2 - pairs,) + out.shape[1:], f32)


def section_scratch(levels, width, count):
    size = row_places(levels)[1]
    return [
        pltpu.VMEM((count, size, width + LANES), f32),
        pltpu.VMEM((count, size, width + LANES), bf16),
        pltpu.VMEM((count, size, width + LANES), bf16),
        *(pltpu.VMEM((count, level.quads * level.body + 2 * level.half, 2 * level.pool * LANES), bf16)
          for level in levels for _ in range(2)),
        *(pltpu.VMEM((count * level.rows, 2 * LANES), f32) for level in levels),
    ]


def spec_scratch(levels, count):
    return [pltpu.VMEM((count * level.rows, 2 * LANES), bf16) for level in levels]


def pair_scratch(levels):
    rows = sum(2 * level.cross_rows for level in levels)
    tiles = sum(2 * level.blocks * level.quads for level in levels)
    return [
        pltpu.VMEM((rows, 4 * LANES), bf16),
        pltpu.VMEM((rows, 2 * LANES), f32),
        pltpu.VMEM((tiles, WINDOW, LANES), f32),
        pltpu.VMEM((WINDOW // 4, 4 * tiles, LANES), f32),
        *(pltpu.VMEM((4 * HALF + 2 * NYQ, 2 * level.quads * LANES), bf16) for level in levels),
    ]


def copier(sems):
    used = []

    def start(source, target):
        copy = pltpu.make_async_copy(source, target, sems.at[len(used)])
        used.append(copy)
        copy.start()
        return copy.wait

    return start


def inner_kernel(
    levels, cuts,
    own_hbm, near, far, mask_hbm, mask_coarse_hbm, table_hbm,
    maps, own, table_ref, kept, kept_coarse,
    mask, mask_coarse, pad, row_ref, *rest,
):
    *scratch, sems = rest
    start = copier(sems)

    def table(first, last):
        piece = pl.ds(first, last - first)
        return start(table_hbm.at[piece], table_ref.at[piece])

    fine_at, shift_at, map_at, coarse_at, end = cuts
    copies = [
        start(own_hbm, own), table(shift_at, coarse_at), start(mask_hbm, mask), start(mask_coarse_hbm, mask_coarse),
        table(coarse_at, end)]
    size = 3 + 3 * len(levels)
    sections, spec_refs, rest = scratch[:size], scratch[size : size + 1], scratch[size + 1 :]
    strips = ((own,), (near,), (far,))
    rows = levels[0].rows

    def run(pairs):
        others = range(1, pairs + 1)
        if pairs:
            write_row_table(row_ref, levels[0])
            write_fine_table(table_ref, fine_at)
            transform_rows(levels, others, strips, row_ref, sections)
        for wait in copies:
            wait()
        if pairs:
            write_mask_columns(mask, pad, kept)
            write_mask_columns(mask_coarse, pad, kept_coarse)
            transform_rows(levels, (0,), strips, row_ref, sections)
            transform_columns(levels, range(pairs + 1), table_ref, sections, spec_refs)
            write_maps(
                levels, pairs, [spec_refs[0].at[pl.ds(0, rows)]], [spec_refs[0].at[pl.ds(rows, pairs * rows)]],
                (kept,), table_ref, shift_at, map_at, rest, (maps,))
        clear_maps(pairs, (maps,))

    for_pairs(run)


def own_kernel(levels, row_at, own, rim, table_ref, *rest):
    spec_refs, sections = rest[: len(levels)], rest[len(levels) :]
    row_ref = table_ref.at[pl.ds(row_at, row_places(levels)[1])]

    @pl.when(sections_ahead() >= 1)
    def _():
        transform_rows(levels, (0,), ((own, rim),), row_ref, sections)
        transform_columns(levels, (0,), table_ref, sections, spec_refs)


def outer_kernel(
    levels, cuts, inner, row_at,
    near, far, rim_near, rim_far, table_ref, own_fine, own_coarse, kept, kept_coarse, inner_maps,
    out_fine, out_coarse,
    maps, maps_coarse, *rest,
):
    *scratch, sems = rest
    start = copier(sems)
    stores = [start(inner_maps.at[d], out_fine.at[0, d, pl.ds(0, inner)]) for d in range(2)]
    fine_at, shift_at, map_at, coarse_at, end = cuts
    row_ref = table_ref.at[pl.ds(row_at, row_places(levels)[1])]
    size, count = 3 + 3 * len(levels), len(levels)
    sections, spec_refs, rest = scratch[:size], scratch[size : size + count], scratch[size + count :]
    strips = ((near, rim_near), (far, rim_far))

    def run(pairs):
        if pairs:
            transform_rows(levels, range(pairs), strips, row_ref, sections)
            transform_columns(levels, range(pairs), table_ref, sections, spec_refs)
            write_maps(
                levels, pairs, (own_fine, own_coarse), spec_refs, (kept, kept_coarse), table_ref, shift_at, map_at,
                rest, (maps, maps_coarse))
        clear_maps(pairs, (maps, maps_coarse))

    for_pairs(run)
    for d in range(2):
        stores.append(start(maps.at[d], out_fine.at[0, d, pl.ds(inner, levels[0].blocks)]))
        stores.append(start(maps_coarse.at[d], out_coarse.at[0, d]))
    for wait in stores:
        wait()


def correlate(own, near, far, rim, rim_near, rim_far, mask_fine, mask_coarse):
    strip_rows, width = own.shape[1:]
    fine, coarse = mask_fine.shape[1], mask_coarse.shape[1]
    inner = fine - 1
    shift, map_ = shift_tables()
    tables = [fine_table(), shift, map_, coarse_table()]
    cuts = [int(at) for at in np.cumsum([0] + [table.shape[0] for table in tables])]
    inner_levels = [Level(1, range(inner), width, cuts[0])]
    outer_levels = [Level(1, range(inner, fine), width, cuts[0]), Level(2, range(coarse), width, cuts[3])]
    row_at = cuts[4]
    tables.append(row_table(outer_levels, strip_rows + PATCH))
    columns = max(table.shape[1] for table in tables)
    table = np.concatenate([np.pad(table, ((0, 0), (0, columns - table.shape[1]))) for table in tables])
    cuts[4] = table.shape[0]

    shifts = WINDOW * WINDOW
    hbm = pl.BlockSpec(memory_space=pltpu.HBM)
    vmem = pl.BlockSpec(memory_space=pltpu.VMEM)
    params = pltpu.CompilerParams(vmem_limit_bytes=28 * 1024 * 1024)
    own, table, mask_fine, mask_coarse = (
        pltpu.with_memory_space_constraint(value, pltpu.HBM)
        for value in (own, jnp.asarray(table), mask_fine, mask_coarse))

    def cost(flops):
        return pl.CostEstimate(flops=flops, bytes_accessed=4 * 10**6, transcendentals=0)

    maps, own_kept, handed, *kept = pl.pallas_call(
        functools.partial(inner_kernel, inner_levels, cuts),
        out_shape=(
            jax.ShapeDtypeStruct((2, inner, 4 * inner_levels[0].quads, shifts), f32),
            jax.ShapeDtypeStruct(own.shape, bf16),
            jax.ShapeDtypeStruct(table.shape, bf16),
            *(jax.ShapeDtypeStruct((LANES, 8), f32) for _ in range(2)),
        ),
        in_specs=[hbm, vmem, vmem, hbm, hbm, hbm],
        out_specs=(vmem,) * 5,
        scratch_shapes=[
            pltpu.VMEM(mask_fine.shape, jnp.int32),
            pltpu.VMEM(mask_coarse.shape, jnp.int32),
            pltpu.VMEM((8, LANES), f32),
            pltpu.VMEM((row_places(inner_levels)[1], 2 * strip_rows), bf16),
            *section_scratch(inner_levels, width, 3),
            *spec_scratch(inner_levels, 3),
            *pair_scratch(inner_levels),
            pltpu.SemaphoreType.DMA((5,)),
        ],
        compiler_params=params,
        cost_estimate=cost(3 * 10**9),
        name="inner_blocks",
    )(own, near, far, mask_fine, mask_coarse, table)
    own_specs = pl.pallas_call(
        functools.partial(own_kernel, outer_levels, row_at),
        out_shape=tuple(jax.ShapeDtypeStruct((level.rows, 2 * LANES), bf16) for level in outer_levels),
        in_specs=[vmem] * 3,
        out_specs=(vmem,) * 2,
        scratch_shapes=section_scratch(outer_levels, width, 1),
        compiler_params=params,
        cost_estimate=cost(2 * 10**9),
        name="own_outer_blocks",
    )(own_kept, rim, handed)
    return pl.pallas_call(
        functools.partial(outer_kernel, outer_levels, cuts, inner, row_at),
        out_shape=(
            jax.ShapeDtypeStruct((1, 2, fine, 4 * outer_levels[0].quads, shifts), f32),
            jax.ShapeDtypeStruct((1, 2, coarse, 4 * outer_levels[1].quads, shifts), f32),
        ),
        in_specs=[vmem] * 10,
        out_specs=(hbm, hbm),
        scratch_shapes=[
            *(pltpu.VMEM((2, level.blocks, 4 * level.quads, shifts), f32) for level in outer_levels),
            *section_scratch(outer_levels, width, 2),
            *spec_scratch(outer_levels, 2),
            *pair_scratch(outer_levels),
            pltpu.SemaphoreType.DMA((6,)),
        ],
        compiler_params=params,
        cost_estimate=cost(4 * 10**9),
        name="outer_blocks",
    )(near, far, rim_near, rim_far, handed, *own_specs, *kept, maps)


def local(sections, mask_fine, mask_coarse):
    far = from_device(sections, 2, 0)
    near = from_device(sections, 1, 0)
    rims = [from_device(sections, z, 1) for z in range(3)]
    return correlate(sections, near, far, *rims, mask_fine, mask_coarse)


def solution(mesh):
    in_specs = (
        P("sec", "strip", "groups"),
        P("sec", "strip", "groups"),
        P("sec", "strip", "groups"),
    )
    out_specs = (P("sec", None, "strip", "groups", None), P("sec", None, "strip", "groups", None))
    return jax.shard_map(local, mesh=mesh, in_specs=in_specs, out_specs=out_specs, check_vma=False)
```

```python
import functools

import jax
import jax.numpy as jnp
import numpy as np
from jax import lax
from jax.experimental import pallas as pl
from jax.experimental.pallas import tpu as pltpu
from jax.sharding import PartitionSpec as P

PATCH = 64
STRIDE = 32
WINDOW = 32
HALF = PATCH // 2
LANES = 128
NYQ = 16

f32 = jnp.float32
bf16 = jnp.bfloat16


def from_device(value, sec_steps, strip_steps):
    secs, strips = lax.axis_size("sec"), lax.axis_size("strip")
    pairs = []
    for sec in range(secs - sec_steps):
        for strip in range(strips - strip_steps):
            pairs.append(((sec + sec_steps) * strips + strip + strip_steps, sec * strips + strip))
    return lax.ppermute(value, ("sec", "strip"), pairs)


def wave(phase):
    turns = np.arange(PATCH) * (2 * np.pi / PATCH)
    cos = np.round(np.cos(turns), 14)
    sin = np.round(np.sin(turns), 14)
    phase = np.mod(phase, PATCH)
    return cos[phase], sin[phase]


def split_table(table):
    high = table.astype(jnp.bfloat16)
    low = (table - high.astype(np.float64)).astype(jnp.bfloat16)
    return high, low


def stacked(table):
    return np.concatenate(split_table(table), axis=0)


def fine_table():
    c, s = wave(np.arange(PATCH)[:, None] * np.arange(PATCH)[None, :])
    table = np.zeros((2, 2, PATCH, 2, 2, PATCH))
    for p in range(2):
        table[0, p, :, 0, p] = c
        table[1, p, :, 0, p] = -s
        table[0, p, :, 1, p] = -s
        table[1, p, :, 1, p] = -c
    return stacked(table.reshape(4 * PATCH, 4 * PATCH))


def coarse_table():
    c, s = wave((np.arange(2 * PATCH) // 2)[:, None] * np.arange(PATCH)[None, :])
    table = np.zeros((2, 2, 2 * PATCH, 2, 2, PATCH))
    for p in range(2):
        table[p, 0, :, 0, p] = 0.5 * c
        table[p, 1, :, 0, p] = -0.5 * s
        table[p, 0, :, 1, p] = -0.5 * s
        table[p, 1, :, 1, p] = -0.5 * c
    return stacked(table.reshape(8 * PATCH, 4 * PATCH))


def shift_tables():
    spread = 1.869545
    t = np.arange(WINDOW) - WINDOW // 2
    c, s = wave(np.arange(PATCH)[:, None] * t[None, :])
    table = np.zeros((2, 2, 2, PATCH, 2, 4, WINDOW))
    for odd in range(2):
        for p in range(2):
            table[odd, 0, p, :, 0, 2 * p + odd] = c
            table[odd, 1, p, :, 0, 2 * p + odd] = -s
            table[odd, 0, p, :, 1, 2 * p + odd] = s
            table[odd, 1, p, :, 1, 2 * p + odd] = c
    along_t = (spread * table.reshape(8 * PATCH, 8 * WINDOW)).astype(jnp.bfloat16)
    c, s = wave(t[:, None] * np.arange(HALF)[None, :])
    weight = np.where(np.arange(HALF) == 0, 1.0, 2.0)
    nyquist = np.repeat(wave(HALF * t)[0][:, None], NYQ, axis=1)
    along_s = np.concatenate([c * weight, -s * weight, nyquist], axis=1) / (spread * PATCH**3)
    high, low = split_table(along_s)
    along_s = np.concatenate(
        [np.concatenate([high, high], axis=1), np.concatenate([low, np.zeros_like(low)], axis=1)], axis=0)
    return along_t, along_s


class Level:
    def __init__(self, pool, blocks, width, table):
        self.pool, self.first, self.blocks, self.table = pool, blocks[0], len(blocks), table
        self.quads = width // (4 * pool * STRIDE)
        self.tiles = 2 * self.quads
        self.body = self.blocks * HALF
        self.half = -(-self.quads * self.blocks // 8) * 8
        self.rows = self.tiles * self.body + 2 * self.half
        self.cross_body = self.quads * self.body
        self.cross_rows = self.cross_body + -(-self.half // 16) * 16

    def window(self, tile, p):
        quad, odd = divmod(tile, 2)
        return self.pool * LANES * quad + LANES * p + self.pool * STRIDE * odd

    def nyquist_row(self, tile, b):
        quad, odd = divmod(tile, 2)
        return odd * self.half + quad * self.blocks + b


def row_places(levels):
    at, places = 0, []
    for level in levels:
        places.append([at, at + level.body])
        at += level.body + 2 * level.half
    for level, place in zip(levels, places):
        place.append(at)
        at += level.body
    return places, at


def row_table(levels, ext):
    places, size = row_places(levels)
    table = np.zeros((size, ext))
    k = np.arange(HALF)[:, None]
    for level, (cos_at, nyquist_at, sin_at) in zip(levels, places):
        pool = level.pool
        x = np.arange(pool * PATCH) // pool
        c, s = wave(k * x[None, :])
        for b in range(level.blocks):
            first = (level.first + b) * pool * STRIDE
            columns = slice(first, first + x.size)
            table[cos_at + b * HALF : cos_at + (b + 1) * HALF, columns] = c / pool
            table[sin_at + b * HALF : sin_at + (b + 1) * HALF, columns] = s / pool
            for tile in range(level.tiles):
                table[nyquist_at + level.nyquist_row(tile, b), columns] = wave(HALF * x)[0] / pool
    return np.concatenate(split_table(table), axis=1)


def split(value):
    high = value.astype(bf16)
    return high, (value - high.astype(f32)).astype(bf16)


def dot(left, right):
    return jnp.dot(left, right, preferred_element_type=f32)


def dot3(high, low, table_ref, at):
    depth = high.shape[1]
    table_high = table_ref[at : at + depth]
    table_low = table_ref[at + depth : at + 2 * depth]
    return dot(
        jnp.concatenate([high, low, high], axis=1),
        jnp.concatenate([table_high, table_high, table_low], axis=0))


def cosine(turns):
    turns = turns + PATCH // 4
    part = (turns & (HALF - 1)) - PATCH // 4
    angle = part.astype(f32) * (2 * np.pi / PATCH)
    square = angle * angle
    value = jnp.full(square.shape, 1.0 / 479001600, f32)
    for term in (-1.0 / 3628800, 1.0 / 40320, -1.0 / 720, 1.0 / 24, -0.5, 1.0):
        value = value * square + term
    return jnp.where((turns & HALF) == 0, value, -value)


def write_row_table(row_ref, level):
    (cos_at, nyquist_at, sin_at), = row_places([level])[0]
    ext = row_ref.shape[1] // 2

    def put(at, value):
        high, low = split(value)
        row_ref[at : at + value.shape[0], :ext] = high
        row_ref[at : at + value.shape[0], ext:] = low

    def inside(x):
        return jnp.where((x >= 0) & (x < PATCH), 1.0, 0.0)

    k = lax.broadcasted_iota(jnp.int32, (HALF, ext), 0)
    for b in range(level.blocks):
        x = lax.broadcasted_iota(jnp.int32, (HALF, ext), 1) - (level.first + b) * STRIDE
        put(cos_at + b * HALF, cosine(k * x) * inside(x))
        put(sin_at + b * HALF, cosine(k * x - PATCH // 4) * inside(x))
    row = lax.broadcasted_iota(jnp.int32, (2 * level.half, ext), 0)
    x = lax.broadcasted_iota(jnp.int32, (2 * level.half, ext), 1)
    x = x - (level.first + lax.rem(lax.rem(row, level.half), level.blocks)) * STRIDE
    put(nyquist_at, cosine(x * HALF) * inside(x))


def write_fine_table(table_ref, at):
    y = lax.broadcasted_iota(jnp.int32, (PATCH, LANES), 0)
    lane = lax.broadcasted_iota(jnp.int32, (PATCH, LANES), 1)
    frequency = lane & (PATCH - 1)
    c, s = cosine(y * frequency), cosine(y * frequency - PATCH // 4)
    depth = 4 * PATCH
    for p in range(2):
        mine = (lane >= PATCH) if p else (lane < PATCH)
        cos, minus_cos, minus_sin = (jnp.where(mine, value, 0.0) for value in (c, -c, -s))
        for number, pair in enumerate(((cos, minus_sin), (minus_sin, minus_cos))):
            to = at + (2 * number + p) * PATCH
            for half, value in enumerate(pair):
                for level, part in enumerate(split(value)):
                    table_ref[to + level * depth : to + level * depth + PATCH, half * LANES : (half + 1) * LANES] = part


def all_rows(value):
    for step in (4, 2, 1):
        value = value + pltpu.roll(value, step, 0)
    return value


def left_of(level, place, half_ref, odd_ref):
    cos_at, nyquist_at, sin_at = place
    pieces = []
    for tile in range(level.tiles):
        if tile % 2:
            pieces.append(odd_ref[tile // 2 * level.body : (tile // 2 + 1) * level.body])
        else:
            columns = []
            for p in range(level.pool):
                at = level.window(tile, p)
                columns += [half_ref[start : start + level.body, at : at + LANES] for start in (cos_at, sin_at)]
            pieces.append(jnp.concatenate(columns, axis=1))
    pieces.append(odd_ref[level.quads * level.body :])
    return jnp.concatenate(pieces, axis=0)


def gather_windows(level, place, t_ref, halves, odds):
    cos_at, nyquist_at, sin_at = place
    body, end = level.body, level.quads * level.body
    row = lax.broadcasted_iota(jnp.int32, (2 * level.half, LANES), 0)
    for p in range(level.pool):
        for source, target in zip(halves, odds):
            for tile in range(1, level.tiles, 2):
                at = level.window(tile, p)
                for half, start in enumerate((cos_at, sin_at)):
                    to = tile // 2 * body
                    target[to : to + body, (2 * p + half) * LANES : (2 * p + half + 1) * LANES] = (
                        source[start : start + body, at : at + LANES])
        nyquist = jnp.zeros((2 * level.half, LANES), f32)
        for tile in range(level.tiles):
            at, first = level.window(tile, p), level.nyquist_row(tile, 0)
            value = t_ref[nyquist_at : nyquist_at + 2 * level.half, at : at + LANES]
            nyquist = jnp.where((row >= first) & (row < first + level.blocks), value, nyquist)
        for target, part in zip(odds, split(nyquist)):
            target[end:, 2 * p * LANES : (2 * p + 1) * LANES] = part
            target[end:, (2 * p + 1) * LANES : (2 * p + 2) * LANES] = jnp.zeros(part.shape, bf16)


def spectrum_power(level, f_ref, sections):
    sub = lax.broadcasted_iota(jnp.int32, (8, LANES), 0)
    lane = lax.broadcasted_iota(jnp.int32, (8, LANES), 1)
    dc = (sub == 0) & (lane % PATCH == 0)
    group = lax.broadcasted_iota(jnp.int32, (LANES, LANES), 0) // PATCH
    same = group == lax.broadcasted_iota(jnp.int32, (LANES, LANES), 1) // PATCH
    ones = jnp.where(same, 1.0, 0.0).astype(bf16)

    def square(at):
        re, im = f_ref[at : at + 8, :LANES], f_ref[at : at + 8, LANES:]
        return re * re + im * im

    sums = []
    for z in sections:
        end = z * level.rows + level.tiles * level.body
        tails = [square(end + at) for at in range(0, 2 * level.half, 8)]
        for tile in range(level.tiles):
            for b in range(level.blocks):
                base = z * level.rows + tile * level.body + b * HALF
                total = jnp.where(dc, 0.0, square(base))
                head = jnp.where(sub == 0, total, 0.0)
                for r in range(8, HALF, 8):
                    total = total + square(base + r)
                row = level.nyquist_row(tile, b)
                sums.append(2.0 * total - head + jnp.where(sub == row % 8, tails[row // 8], 0.0))
    high, low = split(jnp.concatenate(sums, axis=0))
    return dot(jnp.concatenate([high, low], axis=1), jnp.concatenate([ones, ones], axis=0))


def scale_spectrum(level, f_ref, sections, sums, spec_ref):
    sub = lax.broadcasted_iota(jnp.int32, (8, 2 * LANES), 0)
    lane = lax.broadcasted_iota(jnp.int32, (8, 2 * LANES), 1)
    dc = (sub == 0) & (lane % PATCH == 0)
    number = 0
    for z in sections:
        start = z * level.rows
        end = start + level.tiles * level.body
        tails = [f_ref[end + at : end + at + 8] for at in range(0, 2 * level.half, 8)]
        scaled = [jnp.zeros_like(tail) for tail in tails]
        for tile in range(level.tiles):
            for b in range(level.blocks):
                scale = lax.rsqrt(all_rows(sums[number : number + 8]) * (1.0 / PATCH**4) + 1e-05)
                number += 8
                scale = jnp.concatenate([scale, scale], axis=1)
                for r in range(0, HALF, 16):
                    at = start + tile * level.body + b * HALF + r
                    head = f_ref[at : at + 8]
                    if r == 0:
                        head = jnp.where(dc, 0.0, head)
                    both = jnp.concatenate([head * scale, f_ref[at + 8 : at + 16] * scale], axis=0)
                    spec_ref[at : at + 16] = both.astype(bf16)
                row = level.nyquist_row(tile, b)
                scaled[row // 8] = jnp.where(sub == row % 8, tails[row // 8] * scale, scaled[row // 8])
        spec_ref[end : end + 2 * level.half] = jnp.concatenate(scaled, axis=0).astype(bf16)


def transform_rows(levels, sections, strips, row_ref, scratch):
    t_ref, high_ref, low_ref = scratch[:3]
    odd_refs = scratch[3 : 3 + 2 * len(levels)]
    places, size = row_places(levels)
    for z in sections:
        x = jnp.concatenate([strip[0] for strip in strips[z]], axis=0)
        width = x.shape[1]
        x = jnp.concatenate([x, x], axis=0)
        for first in range(0, width, 2 * LANES):
            columns = slice(first, first + 2 * LANES)
            t = dot(row_ref[...], x[:, columns])
            for level, (cos_at, nyquist_at, sin_at) in zip(levels, places):
                for start in (cos_at, sin_at):
                    for ref, half in zip((high_ref, low_ref), split(t[start : start + level.body])):
                        ref[z, start : start + level.body, columns] = half
                rows = slice(nyquist_at, nyquist_at + 2 * level.half)
                t_ref[z, rows, columns] = t[rows]
        t_ref[z, :, width:] = jnp.zeros((size, LANES), f32)
        for ref in (high_ref, low_ref):
            ref[z, :, width:] = jnp.zeros((size, LANES), bf16)
    for index, (level, place) in enumerate(zip(levels, places)):
        odds = odd_refs[2 * index : 2 * index + 2]
        for z in sections:
            gather_windows(level, place, t_ref.at[z], (high_ref.at[z], low_ref.at[z]), [ref.at[z] for ref in odds])


def transform_columns(levels, sections, table_ref, scratch, spec_refs):
    high_ref, low_ref = scratch[1:3]
    odd_refs, f_refs = scratch[3 : 3 + 2 * len(levels)], scratch[3 + 2 * len(levels) :]
    places, size = row_places(levels)
    for index, (level, place) in enumerate(zip(levels, places)):
        lefts = [
            jnp.concatenate([left_of(level, place, ref.at[z], odd.at[z]) for z in sections], axis=0)
            for ref, odd in zip((high_ref, low_ref), odd_refs[2 * index : 2 * index + 2])]
        rows = slice(sections[0] * level.rows, (sections[-1] + 1) * level.rows)
        f_refs[index][rows] = dot3(*lefts, table_ref, level.table)
    for level, f_ref, spec_ref in zip(levels, f_refs, spec_refs):
        scale_spectrum(level, f_ref, sections, spectrum_power(level, f_ref, sections), spec_ref)


def write_maps(levels, pairs, own_specs, specs, kept, table_ref, shift_at, map_at, scratch, outs):
    cross_ref, y_ref, maps_ref, rows_ref, *stacks = scratch
    base = 0
    for level, own, spec in zip(levels, own_specs, specs):
        def cross(at, rows):
            a = own[at : at + rows].astype(f32)
            ar, ai = a[:, :LANES], a[:, LANES:]
            for d in range(pairs):
                b = spec[d * level.rows + at : d * level.rows + at + rows].astype(f32)
                br, bi = b[:, :LANES], b[:, LANES:]
                yield base + d * level.cross_rows, jnp.concatenate([ar * br + ai * bi, ar * bi - ai * br], axis=1)

        for tile in range(level.tiles):
            quad, odd = divmod(tile, 2)
            for r in range(0, level.body, 16):
                for to, value in cross(tile * level.body + r, 16):
                    to += quad * level.body + r
                    cross_ref[to : to + 16, 2 * odd * LANES : 2 * (odd + 1) * LANES] = value.astype(bf16)
        for to, value in cross(level.tiles * level.body, 2 * level.half):
            value = jnp.concatenate([value[: level.half], value[level.half :]], axis=1)
            spare = level.cross_rows - level.cross_body - level.half
            if spare:
                value = jnp.concatenate([value, jnp.zeros((spare, 4 * LANES), f32)], axis=0)
            cross_ref[to + level.cross_body : to + level.cross_rows] = value.astype(bf16)
        base += pairs * level.cross_rows
    y_ref[:base] = dot(cross_ref[:base], table_ref[shift_at : shift_at + 4 * LANES])
    base = tile = 0
    starts = {}
    row = lax.broadcasted_iota(jnp.int32, (NYQ, LANES), 0)
    for index, level in enumerate(levels):
        for b in range(level.blocks):
            stack_ref = stacks[index]
            for d in range(pairs):
                first = base + d * level.cross_rows
                nyq_at = first + level.cross_body
                nyquist = y_ref[nyq_at : nyq_at + NYQ, :LANES]
                for quad in range(level.quads):
                    top = first + quad * level.body + b * HALF
                    column = (d * level.quads + quad) * LANES
                    for at, value in (
                        (0, y_ref[top : top + HALF, :LANES]),
                        (HALF, y_ref[top : top + HALF, LANES:]),
                        (2 * HALF, jnp.where(row == quad * level.blocks + b, nyquist, 0.0)),
                    ):
                        for half, part in enumerate(split(value)):
                            to = half * (2 * HALF + NYQ) + at
                            stack_ref[to : to + value.shape[0], column : column + LANES] = part
            columns = pairs * level.quads * LANES
            both = dot(table_ref[map_at : map_at + 2 * WINDOW, : stack_ref.shape[0]], stack_ref[:, :columns])
            maps = both[:WINDOW] + both[WINDOW:]
            for d in range(pairs):
                starts[index, d, b] = tile
                for quad in range(level.quads):
                    column = (d * level.quads + quad) * LANES
                    maps_ref[tile] = maps[:, column : column + LANES]
                    tile += 1
        base += pairs * level.cross_rows
    lane = lax.broadcasted_iota(jnp.int32, (tile, LANES), 1)

    def exchange(low, high, width):
        even = (lane & width) == 0
        return (
            jnp.where(even, low, pltpu.roll(high, width, 1)),
            jnp.where(even, pltpu.roll(low, LANES - width, 1), high))

    for big in range(WINDOW // 4):
        rows = [maps_ref[:tile, 4 * big + r, :] for r in range(4)]
        for step in (2, 1):
            for r in range(4):
                if not r & step:
                    rows[r], rows[r + step] = exchange(rows[r], rows[r + step], step * WINDOW)
        for g in range(4):
            rows_ref[big, pl.ds(g, tile, stride=4), :] = rows[g]
        for index, (level, out) in enumerate(zip(levels, outs)):
            for b in range(level.blocks):
                column = kept[index][: 4 * level.quads, level.first + b : level.first + b + 1]
                for d in range(pairs):
                    at = 4 * starts[index, d, b]
                    out[d, b, :, big * LANES : (big + 1) * LANES] = rows_ref[big, at : at + 4 * level.quads] * column


def write_mask_columns(mask_ref, pad_ref, kept_ref):
    pad_ref[...] = jnp.zeros(pad_ref.shape, f32)
    pad_ref[: mask_ref.shape[1], : mask_ref.shape[2]] = mask_ref[0].astype(f32)
    kept_ref[...] = jnp.transpose(pad_ref[...])


def sections_ahead():
    return lax.axis_size("sec") - 1 - lax.axis_index("sec")


def for_pairs(run):
    ahead = sections_ahead()
    pl.when(ahead >= 2)(lambda: run(2))
    pl.when(ahead == 1)(lambda: run(1))
    pl.when(ahead < 1)(lambda: run(0))


def clear_maps(pairs, outs):
    for out in outs:
        if pairs < 2:
            out[pairs:] = jnp.zeros((2 - pairs,) + out.shape[1:], f32)


def section_scratch(levels, width, count):
    size = row_places(levels)[1]
    return [
        pltpu.VMEM((count, size, width + LANES), f32),
        pltpu.VMEM((count, size, width + LANES), bf16),
        pltpu.VMEM((count, size, width + LANES), bf16),
        *(pltpu.VMEM((count, level.quads * level.body + 2 * level.half, 2 * level.pool * LANES), bf16)
          for level in levels for _ in range(2)),
        *(pltpu.VMEM((count * level.rows, 2 * LANES), f32) for level in levels),
    ]


def spec_scratch(levels, count):
    return [pltpu.VMEM((count * level.rows, 2 * LANES), bf16) for level in levels]


def pair_scratch(levels):
    rows = sum(2 * level.cross_rows for level in levels)
    tiles = sum(2 * level.blocks * level.quads for level in levels)
    return [
        pltpu.VMEM((rows, 4 * LANES), bf16),
        pltpu.VMEM((rows, 2 * LANES), f32),
        pltpu.VMEM((tiles, WINDOW, LANES), f32),
        pltpu.VMEM((WINDOW // 4, 4 * tiles, LANES), f32),
        *(pltpu.VMEM((4 * HALF + 2 * NYQ, 2 * level.quads * LANES), bf16) for level in levels),
    ]


def copier(sems):
    used = []

    def start(source, target):
        copy = pltpu.make_async_copy(source, target, sems.at[len(used)])
        used.append(copy)
        copy.start()
        return copy.wait

    return start


def inner_kernel(
    levels, cuts,
    own_hbm, near, far, mask_hbm, mask_coarse_hbm, table_hbm,
    maps, own, table_ref, kept, kept_coarse,
    mask, mask_coarse, pad, row_ref, *rest,
):
    *scratch, sems = rest
    start = copier(sems)

    def table(first, last):
        piece = pl.ds(first, last - first)
        return start(table_hbm.at[piece], table_ref.at[piece])

    fine_at, shift_at, map_at, coarse_at, end = cuts
    copies = [
        start(own_hbm, own), table(shift_at, coarse_at), start(mask_hbm, mask), start(mask_coarse_hbm, mask_coarse),
        table(coarse_at, end)]
    size = 3 + 3 * len(levels)
    sections, spec_refs, rest = scratch[:size], scratch[size : size + 1], scratch[size + 1 :]
    strips = ((own,), (near,), (far,))
    rows = levels[0].rows

    def run(pairs):
        others = range(1, pairs + 1)
        if pairs:
            write_row_table(row_ref, levels[0])
            write_fine_table(table_ref, fine_at)
            transform_rows(levels, others, strips, row_ref, sections)
        for wait in copies:
            wait()
        if pairs:
            write_mask_columns(mask, pad, kept)
            write_mask_columns(mask_coarse, pad, kept_coarse)
            transform_rows(levels, (0,), strips, row_ref, sections)
            transform_columns(levels, range(pairs + 1), table_ref, sections, spec_refs)
            write_maps(
                levels, pairs, [spec_refs[0].at[pl.ds(0, rows)]], [spec_refs[0].at[pl.ds(rows, pairs * rows)]],
                (kept,), table_ref, shift_at, map_at, rest, (maps,))
        clear_maps(pairs, (maps,))

    for_pairs(run)


def outer_kernel(
    levels, cuts, inner, row_at,
    own, near, far, gathered_hbm, table_ref, kept, kept_coarse, inner_maps,
    out_fine, out_coarse,
    rims, maps, maps_coarse, *rest,
):
    *scratch, sems = rest
    start = copier(sems)
    secs, strip_count = lax.axis_size("sec"), lax.axis_size("strip")
    sec, strip = lax.axis_index("sec"), lax.axis_index("strip")
    below = jnp.minimum(strip + 1, strip_count - 1)
    loads = [
        start(gathered_hbm.at[jnp.minimum(sec + z, secs - 1) * strip_count + below], rims.at[z]) for z in range(3)]
    stores = [start(inner_maps.at[d], out_fine.at[0, d, pl.ds(0, inner)]) for d in range(2)]
    fine_at, shift_at, map_at, coarse_at, end = cuts
    row_ref = table_ref.at[pl.ds(row_at, row_places(levels)[1])]
    size, count = 3 + 3 * len(levels), len(levels)
    sections, spec_refs, rest = scratch[:size], scratch[size : size + count], scratch[size + count :]
    strips = ((own, rims.at[0]), (near, rims.at[1]), (far, rims.at[2]))
    for wait in loads:
        wait()

    @pl.when(strip == strip_count - 1)
    def _():
        rims[...] = jnp.zeros(rims.shape, bf16)

    def run(pairs):
        if pairs:
            transform_rows(levels, range(pairs + 1), strips, row_ref, sections)
            transform_columns(levels, range(pairs + 1), table_ref, sections, spec_refs)
            write_maps(
                levels, pairs,
                [spec.at[pl.ds(0, level.rows)] for level, spec in zip(levels, spec_refs)],
                [spec.at[pl.ds(level.rows, pairs * level.rows)] for level, spec in zip(levels, spec_refs)],
                (kept, kept_coarse), table_ref, shift_at, map_at, rest, (maps, maps_coarse))
        clear_maps(pairs, (maps, maps_coarse))

    for_pairs(run)
    for d in range(2):
        stores.append(start(maps.at[d], out_fine.at[0, d, pl.ds(inner, levels[0].blocks)]))
        stores.append(start(maps_coarse.at[d], out_coarse.at[0, d]))
    for wait in stores:
        wait()


def correlate(own, near, far, gathered, mask_fine, mask_coarse):
    strip_rows, width = own.shape[1:]
    fine, coarse = mask_fine.shape[1], mask_coarse.shape[1]
    inner = fine - 1
    shift, map_ = shift_tables()
    tables = [fine_table(), shift, map_, coarse_table()]
    cuts = [int(at) for at in np.cumsum([0] + [table.shape[0] for table in tables])]
    inner_levels = [Level(1, range(inner), width, cuts[0])]
    outer_levels = [Level(1, range(inner, fine), width, cuts[0]), Level(2, range(coarse), width, cuts[3])]
    row_at = cuts[4]
    tables.append(row_table(outer_levels, strip_rows + PATCH))
    columns = max(table.shape[1] for table in tables)
    table = np.concatenate([np.pad(table, ((0, 0), (0, columns - table.shape[1]))) for table in tables])
    cuts[4] = table.shape[0]

    shifts = WINDOW * WINDOW
    hbm = pl.BlockSpec(memory_space=pltpu.HBM)
    vmem = pl.BlockSpec(memory_space=pltpu.VMEM)
    params = pltpu.CompilerParams(vmem_limit_bytes=28 * 1024 * 1024)
    own, gathered, table, mask_fine, mask_coarse = (
        pltpu.with_memory_space_constraint(value, pltpu.HBM)
        for value in (own, gathered, jnp.asarray(table), mask_fine, mask_coarse))

    def cost(flops):
        return pl.CostEstimate(flops=flops, bytes_accessed=4 * 10**6, transcendentals=0)

    maps, own_kept, handed, *kept = pl.pallas_call(
        functools.partial(inner_kernel, inner_levels, cuts),
        out_shape=(
            jax.ShapeDtypeStruct((2, inner, 4 * inner_levels[0].quads, shifts), f32),
            jax.ShapeDtypeStruct(own.shape, bf16),
            jax.ShapeDtypeStruct(table.shape, bf16),
            *(jax.ShapeDtypeStruct((LANES, 8), f32) for _ in range(2)),
        ),
        in_specs=[hbm, vmem, vmem, hbm, hbm, hbm],
        out_specs=(vmem,) * 5,
        scratch_shapes=[
            pltpu.VMEM(mask_fine.shape, jnp.int32),
            pltpu.VMEM(mask_coarse.shape, jnp.int32),
            pltpu.VMEM((8, LANES), f32),
            pltpu.VMEM((row_places(inner_levels)[1], 2 * strip_rows), bf16),
            *section_scratch(inner_levels, width, 3),
            *spec_scratch(inner_levels, 3),
            *pair_scratch(inner_levels),
            pltpu.SemaphoreType.DMA((5,)),
        ],
        compiler_params=params,
        cost_estimate=cost(3 * 10**9),
        name="inner_blocks",
    )(own, near, far, mask_fine, mask_coarse, table)
    return pl.pallas_call(
        functools.partial(outer_kernel, outer_levels, cuts, inner, row_at),
        out_shape=(
            jax.ShapeDtypeStruct((1, 2, fine, 4 * outer_levels[0].quads, shifts), f32),
            jax.ShapeDtypeStruct((1, 2, coarse, 4 * outer_levels[1].quads, shifts), f32),
        ),
        in_specs=[vmem] * 3 + [hbm] + [vmem] * 4,
        out_specs=(hbm, hbm),
        scratch_shapes=[
            pltpu.VMEM((3,) + own.shape, bf16),
            *(pltpu.VMEM((2, level.blocks, 4 * level.quads, shifts), f32) for level in outer_levels),
            *section_scratch(outer_levels, width, 3),
            *spec_scratch(outer_levels, 3),
            *pair_scratch(outer_levels),
            pltpu.SemaphoreType.DMA((9,)),
        ],
        compiler_params=params,
        cost_estimate=cost(4 * 10**9),
        name="outer_blocks",
    )(own_kept, near, far, gathered, handed, *kept, maps)


def local(sections, mask_fine, mask_coarse):
    far = from_device(sections, 2, 0)
    near = from_device(sections, 1, 0)
    gathered = lax.all_gather(sections, ("sec", "strip"))
    return correlate(sections, near, far, gathered, mask_fine, mask_coarse)


def solution(mesh):
    in_specs = (
        P("sec", "strip", "groups"),
        P("sec", "strip", "groups"),
        P("sec", "strip", "groups"),
    )
    out_specs = (P("sec", None, "strip", "groups", None), P("sec", None, "strip", "groups", None))
    return jax.shard_map(local, mesh=mesh, in_specs=in_specs, out_specs=out_specs, check_vma=False)
```

```python
import functools

import jax
import jax.numpy as jnp
import numpy as np
from jax import lax
from jax.experimental import pallas as pl
from jax.experimental.pallas import tpu as pltpu
from jax.sharding import PartitionSpec as P

PATCH = 64
STRIDE = 32
WINDOW = 32
HALF = PATCH // 2
LANES = 128
NYQ = 16

f32 = jnp.float32
bf16 = jnp.bfloat16


def from_device(value, sec_steps, strip_steps):
    secs, strips = lax.axis_size("sec"), lax.axis_size("strip")
    pairs = []
    for sec in range(secs - sec_steps):
        for strip in range(strips - strip_steps):
            pairs.append(((sec + sec_steps) * strips + strip + strip_steps, sec * strips + strip))
    return lax.ppermute(value, ("sec", "strip"), pairs)


def wave(phase):
    turns = np.arange(PATCH) * (2 * np.pi / PATCH)
    cos = np.round(np.cos(turns), 14)
    sin = np.round(np.sin(turns), 14)
    phase = np.mod(phase, PATCH)
    return cos[phase], sin[phase]


def split_table(table):
    high = table.astype(jnp.bfloat16)
    low = (table - high.astype(np.float64)).astype(jnp.bfloat16)
    return high, low


def stacked(table):
    return np.concatenate(split_table(table), axis=0)


def fine_table():
    c, s = wave(np.arange(PATCH)[:, None] * np.arange(PATCH)[None, :])
    table = np.zeros((2, 2, PATCH, 2, 2, PATCH))
    for p in range(2):
        table[0, p, :, 0, p] = c
        table[1, p, :, 0, p] = -s
        table[0, p, :, 1, p] = -s
        table[1, p, :, 1, p] = -c
    return stacked(table.reshape(4 * PATCH, 4 * PATCH))


def coarse_table():
    c, s = wave((np.arange(2 * PATCH) // 2)[:, None] * np.arange(PATCH)[None, :])
    table = np.zeros((2, 2, 2 * PATCH, 2, 2, PATCH))
    for p in range(2):
        table[p, 0, :, 0, p] = 0.5 * c
        table[p, 1, :, 0, p] = -0.5 * s
        table[p, 0, :, 1, p] = -0.5 * s
        table[p, 1, :, 1, p] = -0.5 * c
    return stacked(table.reshape(8 * PATCH, 4 * PATCH))


def shift_tables():
    spread = 1.869545
    t = np.arange(WINDOW) - WINDOW // 2
    c, s = wave(np.arange(PATCH)[:, None] * t[None, :])
    table = np.zeros((2, 2, 2, PATCH, 2, 4, WINDOW))
    for odd in range(2):
        for p in range(2):
            table[odd, 0, p, :, 0, 2 * p + odd] = c
            table[odd, 1, p, :, 0, 2 * p + odd] = -s
            table[odd, 0, p, :, 1, 2 * p + odd] = s
            table[odd, 1, p, :, 1, 2 * p + odd] = c
    along_t = (spread * table.reshape(8 * PATCH, 8 * WINDOW)).astype(jnp.bfloat16)
    c, s = wave(t[:, None] * np.arange(HALF)[None, :])
    weight = np.where(np.arange(HALF) == 0, 1.0, 2.0)
    nyquist = np.repeat(wave(HALF * t)[0][:, None], NYQ, axis=1)
    along_s = np.concatenate([c * weight, -s * weight, nyquist], axis=1) / (spread * PATCH**3)
    high, low = split_table(along_s)
    along_s = np.concatenate(
        [np.concatenate([high, high], axis=1), np.concatenate([low, np.zeros_like(low)], axis=1)], axis=0)
    return along_t, along_s


class Level:
    def __init__(self, pool, blocks, width, table):
        self.pool, self.first, self.blocks, self.table = pool, blocks[0], len(blocks), table
        self.quads = width // (4 * pool * STRIDE)
        self.tiles = 2 * self.quads
        self.body = self.blocks * HALF
        self.half = -(-self.quads * self.blocks // 8) * 8
        self.rows = self.tiles * self.body + 2 * self.half
        self.cross_body = self.quads * self.body
        self.cross_rows = self.cross_body + -(-self.half // 16) * 16

    def window(self, tile, p):
        quad, odd = divmod(tile, 2)
        return self.pool * LANES * quad + LANES * p + self.pool * STRIDE * odd

    def nyquist_row(self, tile, b):
        quad, odd = divmod(tile, 2)
        return odd * self.half + quad * self.blocks + b


def row_places(levels):
    at, places = 0, []
    for level in levels:
        places.append([at, at + level.body])
        at += level.body + 2 * level.half
    for level, place in zip(levels, places):
        place.append(at)
        at += level.body
    return places, at


def row_table(levels, ext):
    places, size = row_places(levels)
    table = np.zeros((size, ext))
    k = np.arange(HALF)[:, None]
    for level, (cos_at, nyquist_at, sin_at) in zip(levels, places):
        pool = level.pool
        x = np.arange(pool * PATCH) // pool
        c, s = wave(k * x[None, :])
        for b in range(level.blocks):
            first = (level.first + b) * pool * STRIDE
            columns = slice(first, first + x.size)
            table[cos_at + b * HALF : cos_at + (b + 1) * HALF, columns] = c / pool
            table[sin_at + b * HALF : sin_at + (b + 1) * HALF, columns] = s / pool
            for tile in range(level.tiles):
                table[nyquist_at + level.nyquist_row(tile, b), columns] = wave(HALF * x)[0] / pool
    return np.concatenate(split_table(table), axis=1)


def split(value):
    high = value.astype(bf16)
    return high, (value - high.astype(f32)).astype(bf16)


def dot(left, right):
    return jnp.dot(left, right, preferred_element_type=f32)


def dot3(high, low, table_ref, at):
    depth = high.shape[1]
    table_high = table_ref[at : at + depth]
    table_low = table_ref[at + depth : at + 2 * depth]
    return dot(
        jnp.concatenate([high, low, high], axis=1),
        jnp.concatenate([table_high, table_high, table_low], axis=0))


def cosine(turns):
    turns = turns + PATCH // 4
    part = (turns & (HALF - 1)) - PATCH // 4
    angle = part.astype(f32) * (2 * np.pi / PATCH)
    square = angle * angle
    value = jnp.full(square.shape, 1.0 / 479001600, f32)
    for term in (-1.0 / 3628800, 1.0 / 40320, -1.0 / 720, 1.0 / 24, -0.5, 1.0):
        value = value * square + term
    return jnp.where((turns & HALF) == 0, value, -value)


def write_row_table(row_ref, level):
    (cos_at, nyquist_at, sin_at), = row_places([level])[0]
    ext = row_ref.shape[1] // 2

    def put(at, value):
        high, low = split(value)
        row_ref[at : at + value.shape[0], :ext] = high
        row_ref[at : at + value.shape[0], ext:] = low

    def inside(x):
        return jnp.where((x >= 0) & (x < PATCH), 1.0, 0.0)

    k = lax.broadcasted_iota(jnp.int32, (HALF, ext), 0)
    for b in range(level.blocks):
        x = lax.broadcasted_iota(jnp.int32, (HALF, ext), 1) - (level.first + b) * STRIDE
        put(cos_at + b * HALF, cosine(k * x) * inside(x))
        put(sin_at + b * HALF, cosine(k * x - PATCH // 4) * inside(x))
    row = lax.broadcasted_iota(jnp.int32, (2 * level.half, ext), 0)
    x = lax.broadcasted_iota(jnp.int32, (2 * level.half, ext), 1)
    x = x - (level.first + lax.rem(lax.rem(row, level.half), level.blocks)) * STRIDE
    put(nyquist_at, cosine(x * HALF) * inside(x))


def write_fine_table(table_ref, at):
    y = lax.broadcasted_iota(jnp.int32, (PATCH, LANES), 0)
    lane = lax.broadcasted_iota(jnp.int32, (PATCH, LANES), 1)
    frequency = lane & (PATCH - 1)
    c, s = cosine(y * frequency), cosine(y * frequency - PATCH // 4)
    depth = 4 * PATCH
    for p in range(2):
        mine = (lane >= PATCH) if p else (lane < PATCH)
        cos, minus_cos, minus_sin = (jnp.where(mine, value, 0.0) for value in (c, -c, -s))
        for number, pair in enumerate(((cos, minus_sin), (minus_sin, minus_cos))):
            to = at + (2 * number + p) * PATCH
            for half, value in enumerate(pair):
                for level, part in enumerate(split(value)):
                    table_ref[to + level * depth : to + level * depth + PATCH, half * LANES : (half + 1) * LANES] = part


def all_rows(value):
    for step in (4, 2, 1):
        value = value + pltpu.roll(value, step, 0)
    return value


def left_of(level, place, half_ref, odd_ref):
    cos_at, nyquist_at, sin_at = place
    pieces = []
    for tile in range(level.tiles):
        if tile % 2:
            pieces.append(odd_ref[tile // 2 * level.body : (tile // 2 + 1) * level.body])
        else:
            columns = []
            for p in range(level.pool):
                at = level.window(tile, p)
                columns += [half_ref[start : start + level.body, at : at + LANES] for start in (cos_at, sin_at)]
            pieces.append(jnp.concatenate(columns, axis=1))
    pieces.append(odd_ref[level.quads * level.body :])
    return jnp.concatenate(pieces, axis=0)


def gather_windows(level, place, t_ref, halves, odds):
    cos_at, nyquist_at, sin_at = place
    body, end = level.body, level.quads * level.body
    row = lax.broadcasted_iota(jnp.int32, (2 * level.half, LANES), 0)
    for p in range(level.pool):
        for source, target in zip(halves, odds):
            for tile in range(1, level.tiles, 2):
                at = level.window(tile, p)
                for half, start in enumerate((cos_at, sin_at)):
                    to = tile // 2 * body
                    target[to : to + body, (2 * p + half) * LANES : (2 * p + half + 1) * LANES] = (
                        source[start : start + body, at : at + LANES])
        nyquist = jnp.zeros((2 * level.half, LANES), f32)
        for tile in range(level.tiles):
            at, first = level.window(tile, p), level.nyquist_row(tile, 0)
            value = t_ref[nyquist_at : nyquist_at + 2 * level.half, at : at + LANES]
            nyquist = jnp.where((row >= first) & (row < first + level.blocks), value, nyquist)
        for target, part in zip(odds, split(nyquist)):
            target[end:, 2 * p * LANES : (2 * p + 1) * LANES] = part
            target[end:, (2 * p + 1) * LANES : (2 * p + 2) * LANES] = jnp.zeros(part.shape, bf16)


def spectrum_power(level, f_ref, sections):
    sub = lax.broadcasted_iota(jnp.int32, (8, LANES), 0)
    lane = lax.broadcasted_iota(jnp.int32, (8, LANES), 1)
    dc = (sub == 0) & (lane % PATCH == 0)
    group = lax.broadcasted_iota(jnp.int32, (LANES, LANES), 0) // PATCH
    same = group == lax.broadcasted_iota(jnp.int32, (LANES, LANES), 1) // PATCH
    ones = jnp.where(same, 1.0, 0.0).astype(bf16)

    def square(at):
        re, im = f_ref[at : at + 8, :LANES], f_ref[at : at + 8, LANES:]
        return re * re + im * im

    sums = []
    for z in sections:
        end = z * level.rows + level.tiles * level.body
        tails = [square(end + at) for at in range(0, 2 * level.half, 8)]
        for tile in range(level.tiles):
            for b in range(level.blocks):
                base = z * level.rows + tile * level.body + b * HALF
                total = jnp.where(dc, 0.0, square(base))
                head = jnp.where(sub == 0, total, 0.0)
                for r in range(8, HALF, 8):
                    total = total + square(base + r)
                row = level.nyquist_row(tile, b)
                sums.append(2.0 * total - head + jnp.where(sub == row % 8, tails[row // 8], 0.0))
    high, low = split(jnp.concatenate(sums, axis=0))
    return dot(jnp.concatenate([high, low], axis=1), jnp.concatenate([ones, ones], axis=0))


def scale_spectrum(level, f_ref, sections, sums, spec_ref):
    sub = lax.broadcasted_iota(jnp.int32, (8, 2 * LANES), 0)
    lane = lax.broadcasted_iota(jnp.int32, (8, 2 * LANES), 1)
    dc = (sub == 0) & (lane % PATCH == 0)
    number = 0
    for z in sections:
        start = z * level.rows
        end = start + level.tiles * level.body
        tails = [f_ref[end + at : end + at + 8] for at in range(0, 2 * level.half, 8)]
        scaled = [jnp.zeros_like(tail) for tail in tails]
        for tile in range(level.tiles):
            for b in range(level.blocks):
                scale = lax.rsqrt(all_rows(sums[number : number + 8]) * (1.0 / PATCH**4) + 1e-05)
                number += 8
                scale = jnp.concatenate([scale, scale], axis=1)
                for r in range(0, HALF, 16):
                    at = start + tile * level.body + b * HALF + r
                    head = f_ref[at : at + 8]
                    if r == 0:
                        head = jnp.where(dc, 0.0, head)
                    both = jnp.concatenate([head * scale, f_ref[at + 8 : at + 16] * scale], axis=0)
                    spec_ref[at : at + 16] = both.astype(bf16)
                row = level.nyquist_row(tile, b)
                scaled[row // 8] = jnp.where(sub == row % 8, tails[row // 8] * scale, scaled[row // 8])
        spec_ref[end : end + 2 * level.half] = jnp.concatenate(scaled, axis=0).astype(bf16)


def transform_rows(levels, sections, strips, row_ref, scratch):
    t_ref, high_ref, low_ref = scratch[:3]
    odd_refs = scratch[3 : 3 + 2 * len(levels)]
    places, size = row_places(levels)
    for z in sections:
        x = jnp.concatenate([strip[0] for strip in strips[z]], axis=0)
        width = x.shape[1]
        x = jnp.concatenate([x, x], axis=0)
        for first in range(0, width, 2 * LANES):
            columns = slice(first, first + 2 * LANES)
            t = dot(row_ref[...], x[:, columns])
            for level, (cos_at, nyquist_at, sin_at) in zip(levels, places):
                for start in (cos_at, sin_at):
                    for ref, half in zip((high_ref, low_ref), split(t[start : start + level.body])):
                        ref[z, start : start + level.body, columns] = half
                rows = slice(nyquist_at, nyquist_at + 2 * level.half)
                t_ref[z, rows, columns] = t[rows]
        t_ref[z, :, width:] = jnp.zeros((size, LANES), f32)
        for ref in (high_ref, low_ref):
            ref[z, :, width:] = jnp.zeros((size, LANES), bf16)
    for index, (level, place) in enumerate(zip(levels, places)):
        odds = odd_refs[2 * index : 2 * index + 2]
        for z in sections:
            gather_windows(level, place, t_ref.at[z], (high_ref.at[z], low_ref.at[z]), [ref.at[z] for ref in odds])


def transform_columns(levels, sections, table_ref, scratch, spec_refs):
    high_ref, low_ref = scratch[1:3]
    odd_refs, f_refs = scratch[3 : 3 + 2 * len(levels)], scratch[3 + 2 * len(levels) :]
    places, size = row_places(levels)
    for index, (level, place) in enumerate(zip(levels, places)):
        lefts = [
            jnp.concatenate([left_of(level, place, ref.at[z], odd.at[z]) for z in sections], axis=0)
            for ref, odd in zip((high_ref, low_ref), odd_refs[2 * index : 2 * index + 2])]
        rows = slice(sections[0] * level.rows, (sections[-1] + 1) * level.rows)
        f_refs[index][rows] = dot3(*lefts, table_ref, level.table)
    for level, f_ref, spec_ref in zip(levels, f_refs, spec_refs):
        scale_spectrum(level, f_ref, sections, spectrum_power(level, f_ref, sections), spec_ref)


def write_maps(levels, pairs, own_specs, specs, kept, table_ref, shift_at, map_at, scratch, outs):
    count = len(levels)
    cross_refs, y_refs, maps_refs, rows_refs, stacks = (scratch[i * count : (i + 1) * count] for i in range(5))
    for level, own, spec, cross_ref, y_ref in zip(levels, own_specs, specs, cross_refs, y_refs):
        def cross(at, rows):
            a = own[at : at + rows].astype(f32)
            ar, ai = a[:, :LANES], a[:, LANES:]
            for d in range(pairs):
                b = spec[d * level.rows + at : d * level.rows + at + rows].astype(f32)
                br, bi = b[:, :LANES], b[:, LANES:]
                yield d * level.cross_rows, jnp.concatenate([ar * br + ai * bi, ar * bi - ai * br], axis=1)

        for tile in range(level.tiles):
            quad, odd = divmod(tile, 2)
            for r in range(0, level.body, 16):
                for to, value in cross(tile * level.body + r, 16):
                    to += quad * level.body + r
                    cross_ref[to : to + 16, 2 * odd * LANES : 2 * (odd + 1) * LANES] = value.astype(bf16)
        for to, value in cross(level.tiles * level.body, 2 * level.half):
            value = jnp.concatenate([value[: level.half], value[level.half :]], axis=1)
            spare = level.cross_rows - level.cross_body - level.half
            if spare:
                value = jnp.concatenate([value, jnp.zeros((spare, 4 * LANES), f32)], axis=0)
            cross_ref[to + level.cross_body : to + level.cross_rows] = value.astype(bf16)
        rows = pairs * level.cross_rows
        y_ref[:rows] = dot(cross_ref[:rows], table_ref[shift_at : shift_at + 4 * LANES])
    row = lax.broadcasted_iota(jnp.int32, (NYQ, LANES), 0)
    for level, y_ref, stack_ref, maps_ref in zip(levels, y_refs, stacks, maps_refs):
        for b in range(level.blocks):
            for d in range(pairs):
                first = d * level.cross_rows
                nyq_at = first + level.cross_body
                nyquist = y_ref[nyq_at : nyq_at + NYQ, :LANES]
                for quad in range(level.quads):
                    top = first + quad * level.body + b * HALF
                    column = (d * level.quads + quad) * LANES
                    for at, value in (
                        (0, y_ref[top : top + HALF, :LANES]),
                        (HALF, y_ref[top : top + HALF, LANES:]),
                        (2 * HALF, jnp.where(row == quad * level.blocks + b, nyquist, 0.0)),
                    ):
                        for half, part in enumerate(split(value)):
                            to = half * (2 * HALF + NYQ) + at
                            stack_ref[to : to + value.shape[0], column : column + LANES] = part
            columns = pairs * level.quads * LANES
            both = dot(table_ref[map_at : map_at + 2 * WINDOW, : stack_ref.shape[0]], stack_ref[:, :columns])
            maps = both[:WINDOW] + both[WINDOW:]
            for tile in range(pairs * level.quads):
                maps_ref[b * pairs * level.quads + tile] = maps[:, tile * LANES : (tile + 1) * LANES]

    def exchange(low, high, width):
        even = (lax.broadcasted_iota(jnp.int32, low.shape, 1) & width) == 0
        return (
            jnp.where(even, low, pltpu.roll(high, width, 1)),
            jnp.where(even, pltpu.roll(low, LANES - width, 1), high))

    for index, (level, maps_ref, rows_ref, out) in enumerate(zip(levels, maps_refs, rows_refs, outs)):
        tiles = level.blocks * pairs * level.quads
        for big in range(WINDOW // 4):
            rows = [maps_ref[:tiles, 4 * big + r, :] for r in range(4)]
            for step in (2, 1):
                for r in range(4):
                    if not r & step:
                        rows[r], rows[r + step] = exchange(rows[r], rows[r + step], step * WINDOW)
            for g in range(4):
                rows_ref[big, pl.ds(g, tiles, stride=4), :] = rows[g]
            for b in range(level.blocks):
                column = kept[index][: 4 * level.quads, level.first + b : level.first + b + 1]
                for d in range(pairs):
                    at = 4 * (b * pairs + d) * level.quads
                    out[d, b, :, big * LANES : (big + 1) * LANES] = rows_ref[big, at : at + 4 * level.quads] * column


def write_mask_columns(mask_ref, pad_ref, kept_ref):
    pad_ref[...] = jnp.zeros(pad_ref.shape, f32)
    pad_ref[: mask_ref.shape[1], : mask_ref.shape[2]] = mask_ref[0].astype(f32)
    kept_ref[...] = jnp.transpose(pad_ref[...])


def sections_ahead():
    return lax.axis_size("sec") - 1 - lax.axis_index("sec")


def for_pairs(run):
    ahead = sections_ahead()
    pl.when(ahead >= 2)(lambda: run(2))
    pl.when(ahead == 1)(lambda: run(1))
    pl.when(ahead < 1)(lambda: run(0))


def clear_maps(pairs, outs):
    for out in outs:
        if pairs < 2:
            out[pairs:] = jnp.zeros((2 - pairs,) + out.shape[1:], f32)


def section_scratch(levels, width, count):
    size = row_places(levels)[1]
    return [
        pltpu.VMEM((count, size, width + LANES), f32),
        pltpu.VMEM((count, size, width + LANES), bf16),
        pltpu.VMEM((count, size, width + LANES), bf16),
        *(pltpu.VMEM((count, level.quads * level.body + 2 * level.half, 2 * level.pool * LANES), bf16)
          for level in levels for _ in range(2)),
        *(pltpu.VMEM((count * level.rows, 2 * LANES), f32) for level in levels),
    ]


def spec_scratch(levels, count):
    return [pltpu.VMEM((count * level.rows, 2 * LANES), bf16) for level in levels]


def pair_scratch(levels):
    def each(shape, dtype):
        return [pltpu.VMEM(shape(level), dtype) for level in levels]

    return [
        *each(lambda level: (2 * level.cross_rows, 4 * LANES), bf16),
        *each(lambda level: (2 * level.cross_rows, 2 * LANES), f32),
        *each(lambda level: (2 * level.blocks * level.quads, WINDOW, LANES), f32),
        *each(lambda level: (WINDOW // 4, 8 * level.blocks * level.quads, LANES), f32),
        *each(lambda level: (4 * HALF + 2 * NYQ, 2 * level.quads * LANES), bf16),
    ]


def copier(sems):
    used = []

    def start(source, target):
        copy = pltpu.make_async_copy(source, target, sems.at[len(used)])
        used.append(copy)
        copy.start()
        return copy.wait

    return start


def inner_kernel(
    levels, cuts,
    own_hbm, near, far, mask_hbm, mask_coarse_hbm, table_hbm,
    spec, own, table_ref, kept, kept_coarse,
    mask, mask_coarse, pad, pad_coarse, row_ref, *rest,
):
    *sections, sems = rest
    start = copier(sems)

    def table(first, last):
        piece = pl.ds(first, last - first)
        return start(table_hbm.at[piece], table_ref.at[piece])

    fine_at, shift_at, map_at, coarse_at, end = cuts
    copies = [start(own_hbm, own), start(mask_hbm, mask), start(mask_coarse_hbm, mask_coarse)]
    tables = [table(shift_at, coarse_at), table(coarse_at, end)]
    strips = ((own,), (near,), (far,))

    def run(pairs):
        if pairs:
            write_row_table(row_ref, levels[0])
            write_fine_table(table_ref, fine_at)
            transform_rows(levels, range(1, pairs + 1), strips, row_ref, sections)
        for wait in copies:
            wait()
        if pairs:
            write_mask_columns(mask, pad, kept)
            write_mask_columns(mask_coarse, pad_coarse, kept_coarse)
            transform_rows(levels, (0,), strips, row_ref, sections)
            transform_columns(levels, range(pairs + 1), table_ref, sections, [spec])
        for wait in tables:
            wait()

    for_pairs(run)


def middle_kernel(
    inner_levels, levels, cuts, row_at,
    own, rim, table_ref, spec, kept,
    own_fine, own_coarse, maps,
    *rest,
):
    size = 3 + 3 * len(levels)
    sections, pair = rest[:size], rest[size:]
    fine_at, shift_at, map_at, coarse_at, end = cuts
    row_ref = table_ref.at[pl.ds(row_at, row_places(levels)[1])]
    rows = inner_levels[0].rows

    def run(pairs):
        if pairs:
            transform_rows(levels, (0,), ((own, rim),), row_ref, sections)
            transform_columns(levels, (0,), table_ref, sections, (own_fine, own_coarse))
            write_maps(
                inner_levels, pairs, [spec.at[pl.ds(0, rows)]], [spec.at[pl.ds(rows, pairs * rows)]], (kept,),
                table_ref, shift_at, map_at, pair, (maps,))
        clear_maps(pairs, (maps,))

    for_pairs(run)


def outer_kernel(
    levels, cuts, inner, row_at,
    near, far, rim_near, rim_far, table_ref, own_fine, own_coarse, kept, kept_coarse, inner_maps,
    out_fine, out_coarse,
    maps, maps_coarse, *rest,
):
    *scratch, sems = rest
    start = copier(sems)
    stores = [start(inner_maps, out_fine.at[0, :, pl.ds(0, inner)])]
    fine_at, shift_at, map_at, coarse_at, end = cuts
    row_ref = table_ref.at[pl.ds(row_at, row_places(levels)[1])]
    size, count = 3 + 3 * len(levels), len(levels)
    sections, spec_refs, rest = scratch[:size], scratch[size : size + count], scratch[size + count :]
    strips = ((near, rim_near), (far, rim_far))

    def run(pairs):
        if pairs:
            transform_rows(levels, range(pairs), strips, row_ref, sections)
            transform_columns(levels, range(pairs), table_ref, sections, spec_refs)
            write_maps(
                levels, pairs, (own_fine, own_coarse), spec_refs, (kept, kept_coarse), table_ref, shift_at, map_at,
                rest, (maps, maps_coarse))
        clear_maps(pairs, (maps, maps_coarse))

    for_pairs(run)
    stores.append(start(maps, out_fine.at[0, :, pl.ds(inner, levels[0].blocks)]))
    stores.append(start(maps_coarse, out_coarse.at[0]))
    for wait in stores:
        wait()


def correlate(own, near, far, rim, rim_near, rim_far, mask_fine, mask_coarse):
    strip_rows, width = own.shape[1:]
    fine, coarse = mask_fine.shape[1], mask_coarse.shape[1]
    inner = fine - 1
    shift, map_ = shift_tables()
    tables = [fine_table(), shift, map_, coarse_table()]
    cuts = [int(at) for at in np.cumsum([0] + [table.shape[0] for table in tables])]
    inner_levels = [Level(1, range(inner), width, cuts[0])]
    outer_levels = [Level(1, range(inner, fine), width, cuts[0]), Level(2, range(coarse), width, cuts[3])]
    row_at = cuts[4]
    tables.append(row_table(outer_levels, strip_rows + PATCH))
    columns = max(table.shape[1] for table in tables)
    table = np.concatenate([np.pad(table, ((0, 0), (0, columns - table.shape[1]))) for table in tables])
    cuts[4] = table.shape[0]

    shifts = WINDOW * WINDOW
    hbm = pl.BlockSpec(memory_space=pltpu.HBM)
    vmem = pl.BlockSpec(memory_space=pltpu.VMEM)
    params = pltpu.CompilerParams(vmem_limit_bytes=28 * 1024 * 1024)
    own, table, mask_fine, mask_coarse = (
        pltpu.with_memory_space_constraint(value, pltpu.HBM)
        for value in (own, jnp.asarray(table), mask_fine, mask_coarse))

    def cost(flops):
        return pl.CostEstimate(flops=flops, bytes_accessed=4 * 10**6, transcendentals=0)

    spec, own_kept, handed, *kept = pl.pallas_call(
        functools.partial(inner_kernel, inner_levels, cuts),
        out_shape=(
            jax.ShapeDtypeStruct((3 * inner_levels[0].rows, 2 * LANES), bf16),
            jax.ShapeDtypeStruct(own.shape, bf16),
            jax.ShapeDtypeStruct(table.shape, bf16),
            *(jax.ShapeDtypeStruct((LANES, 8), f32) for _ in range(2)),
        ),
        in_specs=[hbm, vmem, vmem, hbm, hbm, hbm],
        out_specs=(vmem,) * 5,
        scratch_shapes=[
            pltpu.VMEM(mask_fine.shape, jnp.int32),
            pltpu.VMEM(mask_coarse.shape, jnp.int32),
            pltpu.VMEM((8, LANES), f32),
            pltpu.VMEM((8, LANES), f32),
            pltpu.VMEM((row_places(inner_levels)[1], 2 * strip_rows), bf16),
            *section_scratch(inner_levels, width, 3),
            pltpu.SemaphoreType.DMA((5,)),
        ],
        compiler_params=params,
        cost_estimate=cost(2 * 10**9),
        name="inner_spectra",
    )(own, near, far, mask_fine, mask_coarse, table)
    *own_specs, maps = pl.pallas_call(
        functools.partial(middle_kernel, inner_levels, outer_levels, cuts, row_at),
        out_shape=(
            *(jax.ShapeDtypeStruct((level.rows, 2 * LANES), bf16) for level in outer_levels),
            jax.ShapeDtypeStruct((2, inner, 4 * inner_levels[0].quads, shifts), f32),
        ),
        in_specs=[vmem] * 5,
        out_specs=(vmem,) * 3,
        scratch_shapes=[*section_scratch(outer_levels, width, 1), *pair_scratch(inner_levels)],
        compiler_params=params,
        cost_estimate=cost(2 * 10**9),
        name="inner_maps",
    )(own_kept, rim, handed, spec, kept[0])
    return pl.pallas_call(
        functools.partial(outer_kernel, outer_levels, cuts, inner, row_at),
        out_shape=(
            jax.ShapeDtypeStruct((1, 2, fine, 4 * outer_levels[0].quads, shifts), f32),
            jax.ShapeDtypeStruct((1, 2, coarse, 4 * outer_levels[1].quads, shifts), f32),
        ),
        in_specs=[vmem] * 10,
        out_specs=(hbm, hbm),
        scratch_shapes=[
            *(pltpu.VMEM((2, level.blocks, 4 * level.quads, shifts), f32) for level in outer_levels),
            *section_scratch(outer_levels, width, 2),
            *spec_scratch(outer_levels, 2),
            *pair_scratch(outer_levels),
            pltpu.SemaphoreType.DMA((3,)),
        ],
        compiler_params=params,
        cost_estimate=cost(4 * 10**9),
        name="outer_blocks",
    )(near, far, rim_near, rim_far, handed, *own_specs, *kept, maps)


def local(sections, mask_fine, mask_coarse):
    far = from_device(sections, 2, 0)
    near = from_device(sections, 1, 0)
    rims = [from_device(sections, z, 1) for z in range(3)]
    return correlate(sections, near, far, *rims, mask_fine, mask_coarse)


def solution(mesh):
    in_specs = (
        P("sec", "strip", "groups"),
        P("sec", "strip", "groups"),
        P("sec", "strip", "groups"),
    )
    out_specs = (P("sec", None, "strip", "groups", None), P("sec", None, "strip", "groups", None))
    return jax.shard_map(local, mesh=mesh, in_specs=in_specs, out_specs=out_specs, check_vma=False)
```

```python
import functools

import jax
import jax.numpy as jnp
import numpy as np
from jax import lax
from jax.experimental import pallas as pl
from jax.experimental.pallas import tpu as pltpu
from jax.sharding import PartitionSpec as P

PATCH = 64
STRIDE = 32
WINDOW = 32
HALF = PATCH // 2
LANES = 128
NYQ = 16

f32 = jnp.float32
bf16 = jnp.bfloat16


def from_device(value, sec_steps, strip_steps):
    secs, strips = lax.axis_size("sec"), lax.axis_size("strip")
    pairs = []
    for sec in range(secs - sec_steps):
        for strip in range(strips - strip_steps):
            pairs.append(((sec + sec_steps) * strips + strip + strip_steps, sec * strips + strip))
    return lax.ppermute(value, ("sec", "strip"), pairs)


def wave(phase):
    turns = np.arange(PATCH) * (2 * np.pi / PATCH)
    cos = np.round(np.cos(turns), 14)
    sin = np.round(np.sin(turns), 14)
    phase = np.mod(phase, PATCH)
    return cos[phase], sin[phase]


def split_table(table):
    high = table.astype(jnp.bfloat16)
    low = (table - high.astype(np.float64)).astype(jnp.bfloat16)
    return high, low


def stacked(table):
    return np.concatenate(split_table(table), axis=0)


def fine_table():
    c, s = wave(np.arange(PATCH)[:, None] * np.arange(PATCH)[None, :])
    table = np.zeros((2, 2, PATCH, 2, 2, PATCH))
    for p in range(2):
        table[0, p, :, 0, p] = c
        table[1, p, :, 0, p] = -s
        table[0, p, :, 1, p] = -s
        table[1, p, :, 1, p] = -c
    return stacked(table.reshape(4 * PATCH, 4 * PATCH))


def coarse_table():
    c, s = wave((np.arange(2 * PATCH) // 2)[:, None] * np.arange(PATCH)[None, :])
    table = np.zeros((2, 2, 2 * PATCH, 2, 2, PATCH))
    for p in range(2):
        table[p, 0, :, 0, p] = 0.5 * c
        table[p, 1, :, 0, p] = -0.5 * s
        table[p, 0, :, 1, p] = -0.5 * s
        table[p, 1, :, 1, p] = -0.5 * c
    return stacked(table.reshape(8 * PATCH, 4 * PATCH))


def shift_tables():
    spread = 1.869545
    t = np.arange(WINDOW) - WINDOW // 2
    c, s = wave(np.arange(PATCH)[:, None] * t[None, :])
    table = np.zeros((2, 2, 2, PATCH, 2, 4, WINDOW))
    for odd in range(2):
        for p in range(2):
            table[odd, 0, p, :, 0, 2 * p + odd] = c
            table[odd, 1, p, :, 0, 2 * p + odd] = -s
            table[odd, 0, p, :, 1, 2 * p + odd] = s
            table[odd, 1, p, :, 1, 2 * p + odd] = c
    along_t = (spread * table.reshape(8 * PATCH, 8 * WINDOW)).astype(jnp.bfloat16)
    c, s = wave(t[:, None] * np.arange(HALF)[None, :])
    weight = np.where(np.arange(HALF) == 0, 1.0, 2.0)
    nyquist = np.repeat(wave(HALF * t)[0][:, None], NYQ, axis=1)
    along_s = np.concatenate([c * weight, -s * weight, nyquist], axis=1) / (spread * PATCH**3)
    high, low = split_table(along_s)
    along_s = np.concatenate(
        [np.concatenate([high, high], axis=1), np.concatenate([low, np.zeros_like(low)], axis=1)], axis=0)
    return along_t, along_s


class Level:
    def __init__(self, pool, blocks, width, table):
        self.pool, self.first, self.blocks, self.table = pool, blocks[0], len(blocks), table
        self.quads = width // (4 * pool * STRIDE)
        self.tiles = 2 * self.quads
        self.body = self.blocks * HALF
        self.half = -(-self.quads * self.blocks // 8) * 8
        self.rows = self.tiles * self.body + 2 * self.half
        self.cross_body = self.quads * self.body
        self.cross_rows = self.cross_body + -(-self.half // 16) * 16

    def window(self, tile, p):
        quad, odd = divmod(tile, 2)
        return self.pool * LANES * quad + LANES * p + self.pool * STRIDE * odd

    def nyquist_row(self, tile, b):
        quad, odd = divmod(tile, 2)
        return odd * self.half + quad * self.blocks + b


def row_places(levels):
    at, places = 0, []
    for level in levels:
        places.append([at, at + level.body])
        at += level.body + 2 * level.half
    for level, place in zip(levels, places):
        place.append(at)
        at += level.body
    return places, at


def row_table(levels, ext):
    places, size = row_places(levels)
    table = np.zeros((size, ext))
    k = np.arange(HALF)[:, None]
    for level, (cos_at, nyquist_at, sin_at) in zip(levels, places):
        pool = level.pool
        x = np.arange(pool * PATCH) // pool
        c, s = wave(k * x[None, :])
        for b in range(level.blocks):
            first = (level.first + b) * pool * STRIDE
            columns = slice(first, first + x.size)
            table[cos_at + b * HALF : cos_at + (b + 1) * HALF, columns] = c / pool
            table[sin_at + b * HALF : sin_at + (b + 1) * HALF, columns] = s / pool
            for tile in range(level.tiles):
                table[nyquist_at + level.nyquist_row(tile, b), columns] = wave(HALF * x)[0] / pool
    return np.concatenate(split_table(table), axis=1)


def split(value):
    high = value.astype(bf16)
    return high, (value - high.astype(f32)).astype(bf16)


def dot(left, right):
    return jnp.dot(left, right, preferred_element_type=f32)


def dot3(high, low, table_ref, at):
    depth = high.shape[1]
    table_high = table_ref[at : at + depth]
    table_low = table_ref[at + depth : at + 2 * depth]
    return dot(
        jnp.concatenate([high, low, high], axis=1),
        jnp.concatenate([table_high, table_high, table_low], axis=0))


def cosine(turns):
    turns = turns + PATCH // 4
    part = (turns & (HALF - 1)) - PATCH // 4
    angle = part.astype(f32) * (2 * np.pi / PATCH)
    square = angle * angle
    value = jnp.full(square.shape, 1.0 / 479001600, f32)
    for term in (-1.0 / 3628800, 1.0 / 40320, -1.0 / 720, 1.0 / 24, -0.5, 1.0):
        value = value * square + term
    return jnp.where((turns & HALF) == 0, value, -value)


def write_row_table(row_ref, level):
    (cos_at, nyquist_at, sin_at), = row_places([level])[0]
    ext = row_ref.shape[1] // 2

    def put(at, value):
        high, low = split(value)
        row_ref[at : at + value.shape[0], :ext] = high
        row_ref[at : at + value.shape[0], ext:] = low

    def inside(x):
        return jnp.where((x >= 0) & (x < PATCH), 1.0, 0.0)

    k = lax.broadcasted_iota(jnp.int32, (HALF, ext), 0)
    for b in range(level.blocks):
        x = lax.broadcasted_iota(jnp.int32, (HALF, ext), 1) - (level.first + b) * STRIDE
        put(cos_at + b * HALF, cosine(k * x) * inside(x))
        put(sin_at + b * HALF, cosine(k * x - PATCH // 4) * inside(x))
    row = lax.broadcasted_iota(jnp.int32, (2 * level.half, ext), 0)
    x = lax.broadcasted_iota(jnp.int32, (2 * level.half, ext), 1)
    x = x - (level.first + lax.rem(lax.rem(row, level.half), level.blocks)) * STRIDE
    put(nyquist_at, cosine(x * HALF) * inside(x))


def write_fine_table(table_ref, at):
    y = lax.broadcasted_iota(jnp.int32, (PATCH, LANES), 0)
    lane = lax.broadcasted_iota(jnp.int32, (PATCH, LANES), 1)
    frequency = lane & (PATCH - 1)
    c, s = cosine(y * frequency), cosine(y * frequency - PATCH // 4)
    depth = 4 * PATCH
    for p in range(2):
        mine = (lane >= PATCH) if p else (lane < PATCH)
        cos, minus_cos, minus_sin = (jnp.where(mine, value, 0.0) for value in (c, -c, -s))
        for number, pair in enumerate(((cos, minus_sin), (minus_sin, minus_cos))):
            to = at + (2 * number + p) * PATCH
            for half, value in enumerate(pair):
                for level, part in enumerate(split(value)):
                    table_ref[to + level * depth : to + level * depth + PATCH, half * LANES : (half + 1) * LANES] = part


def all_rows(value):
    for step in (4, 2, 1):
        value = value + pltpu.roll(value, step, 0)
    return value


def left_of(level, place, half_ref, odd_ref):
    cos_at, nyquist_at, sin_at = place
    pieces = []
    for tile in range(level.tiles):
        if tile % 2:
            pieces.append(odd_ref[tile // 2 * level.body : (tile // 2 + 1) * level.body])
        else:
            columns = []
            for p in range(level.pool):
                at = level.window(tile, p)
                columns += [half_ref[start : start + level.body, at : at + LANES] for start in (cos_at, sin_at)]
            pieces.append(jnp.concatenate(columns, axis=1))
    pieces.append(odd_ref[level.quads * level.body :])
    return jnp.concatenate(pieces, axis=0)


def gather_windows(level, place, t_ref, halves, odds):
    cos_at, nyquist_at, sin_at = place
    body, end = level.body, level.quads * level.body
    row = lax.broadcasted_iota(jnp.int32, (2 * level.half, LANES), 0)
    for p in range(level.pool):
        for source, target in zip(halves, odds):
            for tile in range(1, level.tiles, 2):
                at = level.window(tile, p)
                for half, start in enumerate((cos_at, sin_at)):
                    to = tile // 2 * body
                    target[to : to + body, (2 * p + half) * LANES : (2 * p + half + 1) * LANES] = (
                        source[start : start + body, at : at + LANES])
        nyquist = jnp.zeros((2 * level.half, LANES), f32)
        for tile in range(level.tiles):
            at, first = level.window(tile, p), level.nyquist_row(tile, 0)
            value = t_ref[nyquist_at : nyquist_at + 2 * level.half, at : at + LANES]
            nyquist = jnp.where((row >= first) & (row < first + level.blocks), value, nyquist)
        for target, part in zip(odds, split(nyquist)):
            target[end:, 2 * p * LANES : (2 * p + 1) * LANES] = part
            target[end:, (2 * p + 1) * LANES : (2 * p + 2) * LANES] = jnp.zeros(part.shape, bf16)


def spectrum_power(level, f_ref, sections):
    sub = lax.broadcasted_iota(jnp.int32, (8, LANES), 0)
    lane = lax.broadcasted_iota(jnp.int32, (8, LANES), 1)
    dc = (sub == 0) & (lane % PATCH == 0)
    group = lax.broadcasted_iota(jnp.int32, (LANES, LANES), 0) // PATCH
    same = group == lax.broadcasted_iota(jnp.int32, (LANES, LANES), 1) // PATCH
    ones = jnp.where(same, 1.0, 0.0).astype(bf16)

    def square(at):
        re, im = f_ref[at : at + 8, :LANES], f_ref[at : at + 8, LANES:]
        return re * re + im * im

    sums = []
    for z in sections:
        end = z * level.rows + level.tiles * level.body
        tails = [square(end + at) for at in range(0, 2 * level.half, 8)]
        for tile in range(level.tiles):
            for b in range(level.blocks):
                base = z * level.rows + tile * level.body + b * HALF
                total = jnp.where(dc, 0.0, square(base))
                head = jnp.where(sub == 0, total, 0.0)
                for r in range(8, HALF, 8):
                    total = total + square(base + r)
                row = level.nyquist_row(tile, b)
                sums.append(2.0 * total - head + jnp.where(sub == row % 8, tails[row // 8], 0.0))
    high, low = split(jnp.concatenate(sums, axis=0))
    return dot(jnp.concatenate([high, low], axis=1), jnp.concatenate([ones, ones], axis=0))


def scale_spectrum(level, f_ref, sections, sums, spec_ref):
    sub = lax.broadcasted_iota(jnp.int32, (8, 2 * LANES), 0)
    lane = lax.broadcasted_iota(jnp.int32, (8, 2 * LANES), 1)
    dc = (sub == 0) & (lane % PATCH == 0)
    number = 0
    for z in sections:
        start = z * level.rows
        end = start + level.tiles * level.body
        tails = [f_ref[end + at : end + at + 8] for at in range(0, 2 * level.half, 8)]
        scaled = [jnp.zeros_like(tail) for tail in tails]
        for tile in range(level.tiles):
            for b in range(level.blocks):
                scale = lax.rsqrt(all_rows(sums[number : number + 8]) * (1.0 / PATCH**4) + 1e-05)
                number += 8
                scale = jnp.concatenate([scale, scale], axis=1)
                for r in range(0, HALF, 16):
                    at = start + tile * level.body + b * HALF + r
                    head = f_ref[at : at + 8]
                    if r == 0:
                        head = jnp.where(dc, 0.0, head)
                    both = jnp.concatenate([head * scale, f_ref[at + 8 : at + 16] * scale], axis=0)
                    spec_ref[at : at + 16] = both.astype(bf16)
                row = level.nyquist_row(tile, b)
                scaled[row // 8] = jnp.where(sub == row % 8, tails[row // 8] * scale, scaled[row // 8])
        spec_ref[end : end + 2 * level.half] = jnp.concatenate(scaled, axis=0).astype(bf16)


def transform_rows(levels, sections, strips, row_ref, scratch):
    t_ref, high_ref, low_ref = scratch[:3]
    odd_refs = scratch[3 : 3 + 2 * len(levels)]
    places, size = row_places(levels)
    for z in sections:
        x = jnp.concatenate([strip[0] for strip in strips[z]], axis=0)
        width = x.shape[1]
        x = jnp.concatenate([x, x], axis=0)
        for first in range(0, width, 2 * LANES):
            columns = slice(first, first + 2 * LANES)
            t = dot(row_ref[...], x[:, columns])
            for level, (cos_at, nyquist_at, sin_at) in zip(levels, places):
                for start in (cos_at, sin_at):
                    for ref, half in zip((high_ref, low_ref), split(t[start : start + level.body])):
                        ref[z, start : start + level.body, columns] = half
                rows = slice(nyquist_at, nyquist_at + 2 * level.half)
                t_ref[z, rows, columns] = t[rows]
        t_ref[z, :, width:] = jnp.zeros((size, LANES), f32)
        for ref in (high_ref, low_ref):
            ref[z, :, width:] = jnp.zeros((size, LANES), bf16)
    for index, (level, place) in enumerate(zip(levels, places)):
        odds = odd_refs[2 * index : 2 * index + 2]
        for z in sections:
            gather_windows(level, place, t_ref.at[z], (high_ref.at[z], low_ref.at[z]), [ref.at[z] for ref in odds])


def transform_columns(levels, sections, table_ref, scratch, spec_refs):
    high_ref, low_ref = scratch[1:3]
    odd_refs, f_refs = scratch[3 : 3 + 2 * len(levels)], scratch[3 + 2 * len(levels) :]
    places, size = row_places(levels)
    for index, (level, place) in enumerate(zip(levels, places)):
        lefts = [
            jnp.concatenate([left_of(level, place, ref.at[z], odd.at[z]) for z in sections], axis=0)
            for ref, odd in zip((high_ref, low_ref), odd_refs[2 * index : 2 * index + 2])]
        rows = slice(sections[0] * level.rows, (sections[-1] + 1) * level.rows)
        f_refs[index][rows] = dot3(*lefts, table_ref, level.table)
    for level, f_ref, spec_ref in zip(levels, f_refs, spec_refs):
        scale_spectrum(level, f_ref, sections, spectrum_power(level, f_ref, sections), spec_ref)


def write_maps(levels, pairs, own_specs, specs, kept, table_ref, shift_at, map_at, scratch, outs, finished=()):
    count = len(levels)
    cross_refs, y_refs, maps_refs, rows_refs, stacks = (scratch[i * count : (i + 1) * count] for i in range(5))
    for level, own, spec, cross_ref, y_ref in zip(levels, own_specs, specs, cross_refs, y_refs):
        def cross(at, rows):
            a = own[at : at + rows].astype(f32)
            ar, ai = a[:, :LANES], a[:, LANES:]
            for d in range(pairs):
                b = spec[d * level.rows + at : d * level.rows + at + rows].astype(f32)
                br, bi = b[:, :LANES], b[:, LANES:]
                yield d * level.cross_rows, jnp.concatenate([ar * br + ai * bi, ar * bi - ai * br], axis=1)

        for tile in range(level.tiles):
            quad, odd = divmod(tile, 2)
            for r in range(0, level.body, 16):
                for to, value in cross(tile * level.body + r, 16):
                    to += quad * level.body + r
                    cross_ref[to : to + 16, 2 * odd * LANES : 2 * (odd + 1) * LANES] = value.astype(bf16)
        for to, value in cross(level.tiles * level.body, 2 * level.half):
            value = jnp.concatenate([value[: level.half], value[level.half :]], axis=1)
            spare = level.cross_rows - level.cross_body - level.half
            if spare:
                value = jnp.concatenate([value, jnp.zeros((spare, 4 * LANES), f32)], axis=0)
            cross_ref[to + level.cross_body : to + level.cross_rows] = value.astype(bf16)
        rows = pairs * level.cross_rows
        y_ref[:rows] = dot(cross_ref[:rows], table_ref[shift_at : shift_at + 4 * LANES])
    row = lax.broadcasted_iota(jnp.int32, (NYQ, LANES), 0)
    for level, y_ref, stack_ref, maps_ref in zip(levels, y_refs, stacks, maps_refs):
        for b in range(level.blocks):
            for d in range(pairs):
                first = d * level.cross_rows
                nyq_at = first + level.cross_body
                nyquist = y_ref[nyq_at : nyq_at + NYQ, :LANES]
                for quad in range(level.quads):
                    top = first + quad * level.body + b * HALF
                    column = (d * level.quads + quad) * LANES
                    for at, value in (
                        (0, y_ref[top : top + HALF, :LANES]),
                        (HALF, y_ref[top : top + HALF, LANES:]),
                        (2 * HALF, jnp.where(row == quad * level.blocks + b, nyquist, 0.0)),
                    ):
                        for half, part in enumerate(split(value)):
                            to = half * (2 * HALF + NYQ) + at
                            stack_ref[to : to + value.shape[0], column : column + LANES] = part
            columns = pairs * level.quads * LANES
            both = dot(table_ref[map_at : map_at + 2 * WINDOW, : stack_ref.shape[0]], stack_ref[:, :columns])
            maps = both[:WINDOW] + both[WINDOW:]
            for tile in range(pairs * level.quads):
                maps_ref[b * pairs * level.quads + tile] = maps[:, tile * LANES : (tile + 1) * LANES]

    def exchange(low, high, width):
        even = (lax.broadcasted_iota(jnp.int32, low.shape, 1) & width) == 0
        return (
            jnp.where(even, low, pltpu.roll(high, width, 1)),
            jnp.where(even, pltpu.roll(low, LANES - width, 1), high))

    for index, (level, maps_ref, rows_ref, out) in enumerate(zip(levels, maps_refs, rows_refs, outs)):
        tiles = level.blocks * pairs * level.quads
        for big in range(WINDOW // 4):
            rows = [maps_ref[:tiles, 4 * big + r, :] for r in range(4)]
            for step in (2, 1):
                for r in range(4):
                    if not r & step:
                        rows[r], rows[r + step] = exchange(rows[r], rows[r + step], step * WINDOW)
            for g in range(4):
                rows_ref[big, pl.ds(g, tiles, stride=4), :] = rows[g]
            for b in range(level.blocks):
                column = kept[index][: 4 * level.quads, level.first + b : level.first + b + 1]
                for d in range(pairs):
                    at = 4 * (b * pairs + d) * level.quads
                    out[d, b, :, big * LANES : (big + 1) * LANES] = rows_ref[big, at : at + 4 * level.quads] * column
        if finished:
            finished[index]()


def write_mask_columns(mask_ref, pad_ref, kept_ref):
    pad_ref[...] = jnp.zeros(pad_ref.shape, f32)
    pad_ref[: mask_ref.shape[1], : mask_ref.shape[2]] = mask_ref[0].astype(f32)
    kept_ref[...] = jnp.transpose(pad_ref[...])


def sections_ahead():
    return lax.axis_size("sec") - 1 - lax.axis_index("sec")


def for_pairs(run):
    ahead = sections_ahead()
    pl.when(ahead >= 2)(lambda: run(2))
    pl.when(ahead == 1)(lambda: run(1))
    pl.when(ahead < 1)(lambda: run(0))


def clear_maps(pairs, outs):
    for out in outs:
        if pairs < 2:
            out[pairs:] = jnp.zeros((2 - pairs,) + out.shape[1:], f32)


def section_scratch(levels, width, count):
    size = row_places(levels)[1]
    return [
        pltpu.VMEM((count, size, width + LANES), f32),
        pltpu.VMEM((count, size, width + LANES), bf16),
        pltpu.VMEM((count, size, width + LANES), bf16),
        *(pltpu.VMEM((count, level.quads * level.body + 2 * level.half, 2 * level.pool * LANES), bf16)
          for level in levels for _ in range(2)),
        *(pltpu.VMEM((count * level.rows, 2 * LANES), f32) for level in levels),
    ]


def spec_scratch(levels, count):
    return [pltpu.VMEM((count * level.rows, 2 * LANES), bf16) for level in levels]


def pair_scratch(levels):
    def each(shape, dtype):
        return [pltpu.VMEM(shape(level), dtype) for level in levels]

    return [
        *each(lambda level: (2 * level.cross_rows, 4 * LANES), bf16),
        *each(lambda level: (2 * level.cross_rows, 2 * LANES), f32),
        *each(lambda level: (2 * level.blocks * level.quads, WINDOW, LANES), f32),
        *each(lambda level: (WINDOW // 4, 8 * level.blocks * level.quads, LANES), f32),
        *each(lambda level: (4 * HALF + 2 * NYQ, 2 * level.quads * LANES), bf16),
    ]


def copier(sems):
    used = []

    def start(source, target):
        copy = pltpu.make_async_copy(source, target, sems.at[len(used)])
        used.append(copy)
        copy.start()
        return copy.wait

    return start


def inner_kernel(
    levels, cuts,
    own_hbm, near, far, mask_hbm, mask_coarse_hbm, table_hbm,
    spec, own, table_ref, kept, kept_coarse,
    mask, mask_coarse, pad, pad_coarse, row_ref, *rest,
):
    *sections, sems = rest
    start = copier(sems)

    def table(first, last):
        piece = pl.ds(first, last - first)
        return start(table_hbm.at[piece], table_ref.at[piece])

    fine_at, shift_at, map_at, coarse_at, end = cuts
    copies = [start(own_hbm, own), start(mask_hbm, mask), start(mask_coarse_hbm, mask_coarse)]
    tables = [table(shift_at, coarse_at), table(coarse_at, end)]
    strips = ((own,), (near,), (far,))

    def run(pairs):
        if pairs:
            write_row_table(row_ref, levels[0])
            write_fine_table(table_ref, fine_at)
            transform_rows(levels, range(1, pairs + 1), strips, row_ref, sections)
        for wait in copies:
            wait()
        if pairs:
            write_mask_columns(mask, pad, kept)
            write_mask_columns(mask_coarse, pad_coarse, kept_coarse)
            transform_rows(levels, (0,), strips, row_ref, sections)
            transform_columns(levels, range(pairs + 1), table_ref, sections, [spec])
        for wait in tables:
            wait()

    for_pairs(run)


def middle_kernel(
    inner_levels, levels, cuts, row_at,
    own, rim, table_ref, spec, kept,
    own_fine, own_coarse, maps,
    *rest,
):
    size = 3 + 3 * len(levels)
    sections, pair = rest[:size], rest[size:]
    fine_at, shift_at, map_at, coarse_at, end = cuts
    row_ref = table_ref.at[pl.ds(row_at, row_places(levels)[1])]
    rows = inner_levels[0].rows

    def run(pairs):
        if pairs:
            transform_rows(levels, (0,), ((own, rim),), row_ref, sections)
            transform_columns(levels, (0,), table_ref, sections, (own_fine, own_coarse))
            write_maps(
                inner_levels, pairs, [spec.at[pl.ds(0, rows)]], [spec.at[pl.ds(rows, pairs * rows)]], (kept,),
                table_ref, shift_at, map_at, pair, (maps,))
        clear_maps(pairs, (maps,))

    for_pairs(run)


def outer_kernel(
    levels, cuts, inner, row_at,
    near, far, rim_near, rim_far, table_ref, own_fine, own_coarse, kept, kept_coarse, inner_maps,
    out_fine, out_coarse,
    maps, maps_coarse, *rest,
):
    *scratch, sems = rest
    inner_stored = copier(sems)(inner_maps, out_fine.at[0, :, pl.ds(0, inner)])
    fine_at, shift_at, map_at, coarse_at, end = cuts
    row_ref = table_ref.at[pl.ds(row_at, row_places(levels)[1])]
    size, count = 3 + 3 * len(levels), len(levels)
    sections, spec_refs, rest = scratch[:size], scratch[size : size + count], scratch[size + count :]
    strips = ((near, rim_near), (far, rim_far))

    def run(pairs):
        stores = [
            pltpu.make_async_copy(maps, out_fine.at[0, :, pl.ds(inner, levels[0].blocks)], sems.at[1]),
            pltpu.make_async_copy(maps_coarse, out_coarse.at[0], sems.at[2])]
        clear_maps(pairs, (maps, maps_coarse))
        if pairs:
            transform_rows(levels, range(pairs), strips, row_ref, sections)
            transform_columns(levels, range(pairs), table_ref, sections, spec_refs)
            write_maps(
                levels, pairs, (own_fine, own_coarse), spec_refs, (kept, kept_coarse), table_ref, shift_at, map_at,
                rest, (maps, maps_coarse), [store.start for store in stores])
        else:
            for store in stores:
                store.start()
        for store in stores:
            store.wait()

    for_pairs(run)
    inner_stored()


def correlate(own, near, far, rim, rim_near, rim_far, mask_fine, mask_coarse):
    strip_rows, width = own.shape[1:]
    fine, coarse = mask_fine.shape[1], mask_coarse.shape[1]
    inner = fine - 1
    shift, map_ = shift_tables()
    tables = [fine_table(), shift, map_, coarse_table()]
    cuts = [int(at) for at in np.cumsum([0] + [table.shape[0] for table in tables])]
    inner_levels = [Level(1, range(inner), width, cuts[0])]
    outer_levels = [Level(1, range(inner, fine), width, cuts[0]), Level(2, range(coarse), width, cuts[3])]
    row_at = cuts[4]
    tables.append(row_table(outer_levels, strip_rows + PATCH))
    columns = max(table.shape[1] for table in tables)
    table = np.concatenate([np.pad(table, ((0, 0), (0, columns - table.shape[1]))) for table in tables])
    cuts[4] = table.shape[0]

    shifts = WINDOW * WINDOW
    hbm = pl.BlockSpec(memory_space=pltpu.HBM)
    vmem = pl.BlockSpec(memory_space=pltpu.VMEM)
    params = pltpu.CompilerParams(vmem_limit_bytes=28 * 1024 * 1024)
    own, table, mask_fine, mask_coarse = (
        pltpu.with_memory_space_constraint(value, pltpu.HBM)
        for value in (own, jnp.asarray(table), mask_fine, mask_coarse))

    def cost(flops):
        return pl.CostEstimate(flops=flops, bytes_accessed=4 * 10**6, transcendentals=0)

    spec, own_kept, handed, *kept = pl.pallas_call(
        functools.partial(inner_kernel, inner_levels, cuts),
        out_shape=(
            jax.ShapeDtypeStruct((3 * inner_levels[0].rows, 2 * LANES), bf16),
            jax.ShapeDtypeStruct(own.shape, bf16),
            jax.ShapeDtypeStruct(table.shape, bf16),
            *(jax.ShapeDtypeStruct((LANES, 8), f32) for _ in range(2)),
        ),
        in_specs=[hbm, vmem, vmem, hbm, hbm, hbm],
        out_specs=(vmem,) * 5,
        scratch_shapes=[
            pltpu.VMEM(mask_fine.shape, jnp.int32),
            pltpu.VMEM(mask_coarse.shape, jnp.int32),
            pltpu.VMEM((8, LANES), f32),
            pltpu.VMEM((8, LANES), f32),
            pltpu.VMEM((row_places(inner_levels)[1], 2 * strip_rows), bf16),
            *section_scratch(inner_levels, width, 3),
            pltpu.SemaphoreType.DMA((5,)),
        ],
        compiler_params=params,
        cost_estimate=cost(3 * 10**9),
        name="inner_spectra",
    )(own, near, far, mask_fine, mask_coarse, table)
    *own_specs, maps = pl.pallas_call(
        functools.partial(middle_kernel, inner_levels, outer_levels, cuts, row_at),
        out_shape=(
            *(jax.ShapeDtypeStruct((level.rows, 2 * LANES), bf16) for level in outer_levels),
            jax.ShapeDtypeStruct((2, inner, 4 * inner_levels[0].quads, shifts), f32),
        ),
        in_specs=[vmem] * 5,
        out_specs=(vmem,) * 3,
        scratch_shapes=[*section_scratch(outer_levels, width, 1), *pair_scratch(inner_levels)],
        compiler_params=params,
        cost_estimate=cost(2 * 10**9),
        name="inner_maps",
    )(own_kept, rim, handed, spec, kept[0])
    return pl.pallas_call(
        functools.partial(outer_kernel, outer_levels, cuts, inner, row_at),
        out_shape=(
            jax.ShapeDtypeStruct((1, 2, fine, 4 * outer_levels[0].quads, shifts), f32),
            jax.ShapeDtypeStruct((1, 2, coarse, 4 * outer_levels[1].quads, shifts), f32),
        ),
        in_specs=[vmem] * 10,
        out_specs=(hbm, hbm),
        scratch_shapes=[
            *(pltpu.VMEM((2, level.blocks, 4 * level.quads, shifts), f32) for level in outer_levels),
            *section_scratch(outer_levels, width, 2),
            *spec_scratch(outer_levels, 2),
            *pair_scratch(outer_levels),
            pltpu.SemaphoreType.DMA((3,)),
        ],
        compiler_params=params,
        cost_estimate=cost(4 * 10**9),
        name="outer_blocks",
    )(near, far, rim_near, rim_far, handed, *own_specs, *kept, maps)


def local(sections, mask_fine, mask_coarse):
    far = from_device(sections, 2, 0)
    near = from_device(sections, 1, 0)
    rims = [from_device(sections, z, 1) for z in range(3)]
    return correlate(sections, near, far, *rims, mask_fine, mask_coarse)


def solution(mesh):
    in_specs = (
        P("sec", "strip", "groups"),
        P("sec", "strip", "groups"),
        P("sec", "strip", "groups"),
    )
    out_specs = (P("sec", None, "strip", "groups", None), P("sec", None, "strip", "groups", None))
    return jax.shard_map(local, mesh=mesh, in_specs=in_specs, out_specs=out_specs, check_vma=False)
```

```python
import functools

import jax
import jax.numpy as jnp
import numpy as np
from jax import lax
from jax.experimental import pallas as pl
from jax.experimental.pallas import tpu as pltpu
from jax.sharding import PartitionSpec as P

PATCH = 64
STRIDE = 32
WINDOW = 32
HALF = PATCH // 2
LANES = 128
NYQ = 16

f32 = jnp.float32
bf16 = jnp.bfloat16


def from_device(value, sec_steps, strip_steps):
    secs, strips = lax.axis_size("sec"), lax.axis_size("strip")
    pairs = []
    for sec in range(secs - sec_steps):
        for strip in range(strips - strip_steps):
            pairs.append(((sec + sec_steps) * strips + strip + strip_steps, sec * strips + strip))
    return lax.ppermute(value, ("sec", "strip"), pairs)


def wave(phase):
    turns = np.arange(PATCH) * (2 * np.pi / PATCH)
    cos = np.round(np.cos(turns), 14)
    sin = np.round(np.sin(turns), 14)
    phase = np.mod(phase, PATCH)
    return cos[phase], sin[phase]


def split_table(table):
    high = table.astype(jnp.bfloat16)
    low = (table - high.astype(np.float64)).astype(jnp.bfloat16)
    return high, low


def stacked(table):
    return np.concatenate(split_table(table), axis=0)


def fine_table():
    c, s = wave(np.arange(PATCH)[:, None] * np.arange(PATCH)[None, :])
    table = np.zeros((2, 2, PATCH, 2, 2, PATCH))
    for p in range(2):
        table[0, p, :, 0, p] = c
        table[1, p, :, 0, p] = -s
        table[0, p, :, 1, p] = -s
        table[1, p, :, 1, p] = -c
    return stacked(table.reshape(4 * PATCH, 4 * PATCH))


def coarse_table():
    c, s = wave((np.arange(2 * PATCH) // 2)[:, None] * np.arange(PATCH)[None, :])
    table = np.zeros((2, 2, 2 * PATCH, 2, 2, PATCH))
    for p in range(2):
        table[p, 0, :, 0, p] = 0.5 * c
        table[p, 1, :, 0, p] = -0.5 * s
        table[p, 0, :, 1, p] = -0.5 * s
        table[p, 1, :, 1, p] = -0.5 * c
    return stacked(table.reshape(8 * PATCH, 4 * PATCH))


def shift_tables():
    spread = 1.869545
    t = np.arange(WINDOW) - WINDOW // 2
    c, s = wave(np.arange(PATCH)[:, None] * t[None, :])
    table = np.zeros((2, 2, 2, PATCH, 2, 4, WINDOW))
    for odd in range(2):
        for p in range(2):
            table[odd, 0, p, :, 0, 2 * p + odd] = c
            table[odd, 1, p, :, 0, 2 * p + odd] = -s
            table[odd, 0, p, :, 1, 2 * p + odd] = s
            table[odd, 1, p, :, 1, 2 * p + odd] = c
    along_t = (spread * table.reshape(8 * PATCH, 8 * WINDOW)).astype(jnp.bfloat16)
    c, s = wave(t[:, None] * np.arange(HALF)[None, :])
    weight = np.where(np.arange(HALF) == 0, 1.0, 2.0)
    nyquist = np.repeat(wave(HALF * t)[0][:, None], NYQ, axis=1)
    along_s = np.concatenate([c * weight, -s * weight, nyquist], axis=1) / (spread * PATCH**3)
    high, low = split_table(along_s)
    along_s = np.concatenate(
        [np.concatenate([high, high], axis=1), np.concatenate([low, np.zeros_like(low)], axis=1)], axis=0)
    return along_t, along_s


class Level:
    def __init__(self, pool, blocks, width, table):
        self.pool, self.first, self.blocks, self.table = pool, blocks[0], len(blocks), table
        self.quads = width // (4 * pool * STRIDE)
        self.tiles = 2 * self.quads
        self.body = self.blocks * HALF
        self.half = -(-self.quads * self.blocks // 8) * 8
        self.rows = self.tiles * self.body + 2 * self.half
        self.cross_body = self.quads * self.body
        self.cross_rows = self.cross_body + -(-self.half // 16) * 16

    def window(self, tile, p):
        quad, odd = divmod(tile, 2)
        return self.pool * LANES * quad + LANES * p + self.pool * STRIDE * odd

    def nyquist_row(self, tile, b):
        quad, odd = divmod(tile, 2)
        return odd * self.half + quad * self.blocks + b


def row_places(levels):
    at, places = 0, []
    for level in levels:
        places.append([at, at + level.body])
        at += level.body + 2 * level.half
    for level, place in zip(levels, places):
        place.append(at)
        at += level.body
    return places, at


def row_table(levels, ext):
    places, size = row_places(levels)
    table = np.zeros((size, ext))
    k = np.arange(HALF)[:, None]
    for level, (cos_at, nyquist_at, sin_at) in zip(levels, places):
        pool = level.pool
        x = np.arange(pool * PATCH) // pool
        c, s = wave(k * x[None, :])
        for b in range(level.blocks):
            first = (level.first + b) * pool * STRIDE
            columns = slice(first, first + x.size)
            table[cos_at + b * HALF : cos_at + (b + 1) * HALF, columns] = c / pool
            table[sin_at + b * HALF : sin_at + (b + 1) * HALF, columns] = s / pool
            for tile in range(level.tiles):
                table[nyquist_at + level.nyquist_row(tile, b), columns] = wave(HALF * x)[0] / pool
    return np.concatenate(split_table(table), axis=1)


def split(value):
    high = value.astype(bf16)
    return high, (value - high.astype(f32)).astype(bf16)


def dot(left, right):
    return jnp.dot(left, right, preferred_element_type=f32)


def dot3(high, low, table_ref, at):
    depth = high.shape[1]
    table_high = table_ref[at : at + depth]
    table_low = table_ref[at + depth : at + 2 * depth]
    return dot(
        jnp.concatenate([high, low, high], axis=1),
        jnp.concatenate([table_high, table_high, table_low], axis=0))


def all_rows(value):
    for step in (4, 2, 1):
        value = value + pltpu.roll(value, step, 0)
    return value


def left_of(level, place, half_ref, odd_ref):
    cos_at, nyquist_at, sin_at = place
    pieces = []
    for tile in range(level.tiles):
        if tile % 2:
            pieces.append(odd_ref[tile // 2 * level.body : (tile // 2 + 1) * level.body])
        else:
            columns = []
            for p in range(level.pool):
                at = level.window(tile, p)
                columns += [half_ref[start : start + level.body, at : at + LANES] for start in (cos_at, sin_at)]
            pieces.append(jnp.concatenate(columns, axis=1))
    pieces.append(odd_ref[level.quads * level.body :])
    return jnp.concatenate(pieces, axis=0)


def gather_windows(level, place, t_ref, halves, odds):
    cos_at, nyquist_at, sin_at = place
    body, end = level.body, level.quads * level.body
    row = lax.broadcasted_iota(jnp.int32, (2 * level.half, LANES), 0)
    for p in range(level.pool):
        for source, target in zip(halves, odds):
            for tile in range(1, level.tiles, 2):
                at = level.window(tile, p)
                for half, start in enumerate((cos_at, sin_at)):
                    to = tile // 2 * body
                    target[to : to + body, (2 * p + half) * LANES : (2 * p + half + 1) * LANES] = (
                        source[start : start + body, at : at + LANES])
        nyquist = jnp.zeros((2 * level.half, LANES), f32)
        for tile in range(level.tiles):
            at, first = level.window(tile, p), level.nyquist_row(tile, 0)
            value = t_ref[nyquist_at : nyquist_at + 2 * level.half, at : at + LANES]
            nyquist = jnp.where((row >= first) & (row < first + level.blocks), value, nyquist)
        for target, part in zip(odds, split(nyquist)):
            target[end:, 2 * p * LANES : (2 * p + 1) * LANES] = part
            target[end:, (2 * p + 1) * LANES : (2 * p + 2) * LANES] = jnp.zeros(part.shape, bf16)


def spectrum_power(level, f_ref, sections):
    sub = lax.broadcasted_iota(jnp.int32, (8, LANES), 0)
    lane = lax.broadcasted_iota(jnp.int32, (8, LANES), 1)
    dc = (sub == 0) & (lane % PATCH == 0)
    group = lax.broadcasted_iota(jnp.int32, (LANES, LANES), 0) // PATCH
    same = group == lax.broadcasted_iota(jnp.int32, (LANES, LANES), 1) // PATCH
    ones = jnp.where(same, 1.0, 0.0).astype(bf16)

    def square(at):
        re, im = f_ref[at : at + 8, :LANES], f_ref[at : at + 8, LANES:]
        return re * re + im * im

    sums = []
    for z in sections:
        end = z * level.rows + level.tiles * level.body
        tails = [square(end + at) for at in range(0, 2 * level.half, 8)]
        for tile in range(level.tiles):
            for b in range(level.blocks):
                base = z * level.rows + tile * level.body + b * HALF
                total = jnp.where(dc, 0.0, square(base))
                head = jnp.where(sub == 0, total, 0.0)
                for r in range(8, HALF, 8):
                    total = total + square(base + r)
                row = level.nyquist_row(tile, b)
                sums.append(2.0 * total - head + jnp.where(sub == row % 8, tails[row // 8], 0.0))
    high, low = split(jnp.concatenate(sums, axis=0))
    return dot(jnp.concatenate([high, low], axis=1), jnp.concatenate([ones, ones], axis=0))


def scale_spectrum(level, f_ref, sections, sums, spec_ref):
    sub = lax.broadcasted_iota(jnp.int32, (8, 2 * LANES), 0)
    lane = lax.broadcasted_iota(jnp.int32, (8, 2 * LANES), 1)
    dc = (sub == 0) & (lane % PATCH == 0)
    number = 0
    for z in sections:
        start = z * level.rows
        end = start + level.tiles * level.body
        tails = [f_ref[end + at : end + at + 8] for at in range(0, 2 * level.half, 8)]
        scaled = [jnp.zeros_like(tail) for tail in tails]
        for tile in range(level.tiles):
            for b in range(level.blocks):
                scale = lax.rsqrt(all_rows(sums[number : number + 8]) * (1.0 / PATCH**4) + 1e-05)
                number += 8
                scale = jnp.concatenate([scale, scale], axis=1)
                for r in range(0, HALF, 16):
                    at = start + tile * level.body + b * HALF + r
                    head = f_ref[at : at + 8]
                    if r == 0:
                        head = jnp.where(dc, 0.0, head)
                    both = jnp.concatenate([head * scale, f_ref[at + 8 : at + 16] * scale], axis=0)
                    spec_ref[at : at + 16] = both.astype(bf16)
                row = level.nyquist_row(tile, b)
                scaled[row // 8] = jnp.where(sub == row % 8, tails[row // 8] * scale, scaled[row // 8])
        spec_ref[end : end + 2 * level.half] = jnp.concatenate(scaled, axis=0).astype(bf16)


def transform_rows(levels, sections, strips, row_ref, scratch):
    t_ref, high_ref, low_ref = scratch[:3]
    odd_refs = scratch[3 : 3 + 2 * len(levels)]
    places, size = row_places(levels)
    for z in sections:
        x = jnp.concatenate([strip[0] for strip in strips[z]], axis=0)
        width = x.shape[1]
        x = jnp.concatenate([x, x], axis=0)
        for first in range(0, width, 2 * LANES):
            columns = slice(first, first + 2 * LANES)
            t = dot(row_ref[...], x[:, columns])
            for level, (cos_at, nyquist_at, sin_at) in zip(levels, places):
                for start in (cos_at, sin_at):
                    for ref, half in zip((high_ref, low_ref), split(t[start : start + level.body])):
                        ref[z, start : start + level.body, columns] = half
                rows = slice(nyquist_at, nyquist_at + 2 * level.half)
                t_ref[z, rows, columns] = t[rows]
        t_ref[z, :, width:] = jnp.zeros((size, LANES), f32)
        for ref in (high_ref, low_ref):
            ref[z, :, width:] = jnp.zeros((size, LANES), bf16)
    for index, (level, place) in enumerate(zip(levels, places)):
        odds = odd_refs[2 * index : 2 * index + 2]
        for z in sections:
            gather_windows(level, place, t_ref.at[z], (high_ref.at[z], low_ref.at[z]), [ref.at[z] for ref in odds])


def transform_columns(levels, sections, table_ref, scratch, spec_refs):
    high_ref, low_ref = scratch[1:3]
    odd_refs, f_refs = scratch[3 : 3 + 2 * len(levels)], scratch[3 + 2 * len(levels) :]
    places, size = row_places(levels)
    for index, (level, place) in enumerate(zip(levels, places)):
        lefts = [
            jnp.concatenate([left_of(level, place, ref.at[z], odd.at[z]) for z in sections], axis=0)
            for ref, odd in zip((high_ref, low_ref), odd_refs[2 * index : 2 * index + 2])]
        rows = slice(sections[0] * level.rows, (sections[-1] + 1) * level.rows)
        f_refs[index][rows] = dot3(*lefts, table_ref, level.table)
    for level, f_ref, spec_ref in zip(levels, f_refs, spec_refs):
        scale_spectrum(level, f_ref, sections, spectrum_power(level, f_ref, sections), spec_ref)


def write_maps(levels, pairs, own_specs, specs, kept, table_ref, shift_at, map_at, scratch, outs, finished=()):
    count = len(levels)
    cross_refs, y_refs, maps_refs, rows_refs, stacks = (scratch[i * count : (i + 1) * count] for i in range(5))
    for level, own, spec, cross_ref, y_ref in zip(levels, own_specs, specs, cross_refs, y_refs):
        def cross(at, rows):
            a = own[at : at + rows].astype(f32)
            ar, ai = a[:, :LANES], a[:, LANES:]
            for d in range(pairs):
                b = spec[d * level.rows + at : d * level.rows + at + rows].astype(f32)
                br, bi = b[:, :LANES], b[:, LANES:]
                yield d * level.cross_rows, jnp.concatenate([ar * br + ai * bi, ar * bi - ai * br], axis=1)

        for tile in range(level.tiles):
            quad, odd = divmod(tile, 2)
            for r in range(0, level.body, 16):
                for to, value in cross(tile * level.body + r, 16):
                    to += quad * level.body + r
                    cross_ref[to : to + 16, 2 * odd * LANES : 2 * (odd + 1) * LANES] = value.astype(bf16)
        for to, value in cross(level.tiles * level.body, 2 * level.half):
            value = jnp.concatenate([value[: level.half], value[level.half :]], axis=1)
            spare = level.cross_rows - level.cross_body - level.half
            if spare:
                value = jnp.concatenate([value, jnp.zeros((spare, 4 * LANES), f32)], axis=0)
            cross_ref[to + level.cross_body : to + level.cross_rows] = value.astype(bf16)
        rows = pairs * level.cross_rows
        y_ref[:rows] = dot(cross_ref[:rows], table_ref[shift_at : shift_at + 4 * LANES])
    row = lax.broadcasted_iota(jnp.int32, (NYQ, LANES), 0)
    for level, y_ref, stack_ref, maps_ref in zip(levels, y_refs, stacks, maps_refs):
        for b in range(level.blocks):
            for d in range(pairs):
                first = d * level.cross_rows
                nyq_at = first + level.cross_body
                nyquist = y_ref[nyq_at : nyq_at + NYQ, :LANES]
                for quad in range(level.quads):
                    top = first + quad * level.body + b * HALF
                    column = (d * level.quads + quad) * LANES
                    for at, value in (
                        (0, y_ref[top : top + HALF, :LANES]),
                        (HALF, y_ref[top : top + HALF, LANES:]),
                        (2 * HALF, jnp.where(row == quad * level.blocks + b, nyquist, 0.0)),
                    ):
                        for half, part in enumerate(split(value)):
                            to = half * (2 * HALF + NYQ) + at
                            stack_ref[to : to + value.shape[0], column : column + LANES] = part
            columns = pairs * level.quads * LANES
            both = dot(table_ref[map_at : map_at + 2 * WINDOW, : stack_ref.shape[0]], stack_ref[:, :columns])
            maps = both[:WINDOW] + both[WINDOW:]
            for tile in range(pairs * level.quads):
                maps_ref[b * pairs * level.quads + tile] = maps[:, tile * LANES : (tile + 1) * LANES]

    def exchange(low, high, width):
        even = (lax.broadcasted_iota(jnp.int32, low.shape, 1) & width) == 0
        return (
            jnp.where(even, low, pltpu.roll(high, width, 1)),
            jnp.where(even, pltpu.roll(low, LANES - width, 1), high))

    for index, (level, maps_ref, rows_ref, out) in enumerate(zip(levels, maps_refs, rows_refs, outs)):
        tiles = level.blocks * pairs * level.quads
        for big in range(WINDOW // 4):
            rows = [maps_ref[:tiles, 4 * big + r, :] for r in range(4)]
            for step in (2, 1):
                for r in range(4):
                    if not r & step:
                        rows[r], rows[r + step] = exchange(rows[r], rows[r + step], step * WINDOW)
            for g in range(4):
                rows_ref[big, pl.ds(g, tiles, stride=4), :] = rows[g]
            for b in range(level.blocks):
                column = kept[index][: 4 * level.quads, level.first + b : level.first + b + 1]
                for d in range(pairs):
                    at = 4 * (b * pairs + d) * level.quads
                    out[d, b, :, big * LANES : (big + 1) * LANES] = rows_ref[big, at : at + 4 * level.quads] * column
        if finished:
            finished[index]()


def write_mask_columns(mask_ref, pad_ref, kept_ref):
    pad_ref[...] = jnp.zeros(pad_ref.shape, f32)
    pad_ref[: mask_ref.shape[1], : mask_ref.shape[2]] = mask_ref[0].astype(f32)
    kept_ref[...] = jnp.transpose(pad_ref[...])


def sections_ahead():
    return lax.axis_size("sec") - 1 - lax.axis_index("sec")


def for_pairs(run):
    ahead = sections_ahead()
    pl.when(ahead >= 2)(lambda: run(2))
    pl.when(ahead == 1)(lambda: run(1))
    pl.when(ahead < 1)(lambda: run(0))


def clear_maps(pairs, outs):
    for out in outs:
        if pairs < 2:
            out[pairs:] = jnp.zeros((2 - pairs,) + out.shape[1:], f32)


def section_scratch(levels, width, count):
    size = row_places(levels)[1]
    return [
        pltpu.VMEM((count, size, width + LANES), f32),
        pltpu.VMEM((count, size, width + LANES), bf16),
        pltpu.VMEM((count, size, width + LANES), bf16),
        *(pltpu.VMEM((count, level.quads * level.body + 2 * level.half, 2 * level.pool * LANES), bf16)
          for level in levels for _ in range(2)),
        *(pltpu.VMEM((count * level.rows, 2 * LANES), f32) for level in levels),
    ]


def spec_scratch(levels, count):
    return [pltpu.VMEM((count * level.rows, 2 * LANES), bf16) for level in levels]


def pair_scratch(levels):
    def each(shape, dtype):
        return [pltpu.VMEM(shape(level), dtype) for level in levels]

    return [
        *each(lambda level: (2 * level.cross_rows, 4 * LANES), bf16),
        *each(lambda level: (2 * level.cross_rows, 2 * LANES), f32),
        *each(lambda level: (2 * level.blocks * level.quads, WINDOW, LANES), f32),
        *each(lambda level: (WINDOW // 4, 8 * level.blocks * level.quads, LANES), f32),
        *each(lambda level: (4 * HALF + 2 * NYQ, 2 * level.quads * LANES), bf16),
    ]


def pieces(rows, count=6):
    cuts = [rows * i // count // 16 * 16 for i in range(count)] + [rows]
    return list(zip(cuts[:-1], cuts[1:]))


def copier(sems):
    used = []

    def start(source, target):
        copy = pltpu.make_async_copy(source, target, sems.at[len(used)])
        used.append(copy)
        copy.start()
        return copy.wait

    return start


def load_kernel(
    own_hbm, mask_hbm, mask_coarse_hbm, table_hbm,
    own, table_ref, kept, kept_coarse,
    mask, mask_coarse, pad, pad_coarse, sems,
):
    start = copier(sems)
    waits = [start(own_hbm, own), start(mask_hbm, mask), start(mask_coarse_hbm, mask_coarse)]
    for first, last in pieces(table_hbm.shape[0]):
        piece = pl.ds(first, last - first)
        waits.append(start(table_hbm.at[piece], table_ref.at[piece]))
    for wait in waits:
        wait()
    write_mask_columns(mask, pad, kept)
    write_mask_columns(mask_coarse, pad_coarse, kept_coarse)


def inner_kernel(levels, row_at, own, far, near, table_ref, spec, *sections):
    strips = ((own,), (near,), (far,))
    row_ref = table_ref.at[pl.ds(row_at, row_places(levels)[1]), pl.ds(0, 2 * own.shape[1])]

    def run(pairs):
        if pairs:
            transform_rows(levels, range(pairs + 1), strips, row_ref, sections)
            transform_columns(levels, range(pairs + 1), table_ref, sections, [spec])

    for_pairs(run)


def middle_kernel(
    inner_levels, levels, cuts, row_at,
    own, rim, table_ref, spec, kept,
    own_fine, own_coarse, maps,
    *rest,
):
    size = 3 + 3 * len(levels)
    sections, pair = rest[:size], rest[size:]
    fine_at, shift_at, map_at, coarse_at, end = cuts
    row_ref = table_ref.at[pl.ds(row_at, row_places(levels)[1])]
    rows = inner_levels[0].rows

    def run(pairs):
        if pairs:
            transform_rows(levels, (0,), ((own, rim),), row_ref, sections)
            transform_columns(levels, (0,), table_ref, sections, (own_fine, own_coarse))
            write_maps(
                inner_levels, pairs, [spec.at[pl.ds(0, rows)]], [spec.at[pl.ds(rows, pairs * rows)]], (kept,),
                table_ref, shift_at, map_at, pair, (maps,))
        clear_maps(pairs, (maps,))

    for_pairs(run)


def outer_kernel(
    levels, cuts, inner, row_at,
    far, near, rim_far, rim_near, table_ref, own_fine, own_coarse, kept, kept_coarse, inner_maps,
    out_fine, out_coarse,
    maps, maps_coarse, *rest,
):
    *scratch, sems = rest
    inner_stored = copier(sems)(inner_maps, out_fine.at[0, :, pl.ds(0, inner)])
    fine_at, shift_at, map_at, coarse_at, end = cuts
    row_ref = table_ref.at[pl.ds(row_at, row_places(levels)[1])]
    size, count = 3 + 3 * len(levels), len(levels)
    sections, spec_refs, rest = scratch[:size], scratch[size : size + count], scratch[size + count :]
    strips = ((near, rim_near), (far, rim_far))

    def run(pairs):
        stores = [
            pltpu.make_async_copy(maps, out_fine.at[0, :, pl.ds(inner, levels[0].blocks)], sems.at[1]),
            pltpu.make_async_copy(maps_coarse, out_coarse.at[0], sems.at[2])]
        clear_maps(pairs, (maps, maps_coarse))
        if pairs:
            transform_rows(levels, range(pairs), strips, row_ref, sections)
            transform_columns(levels, range(pairs), table_ref, sections, spec_refs)
            write_maps(
                levels, pairs, (own_fine, own_coarse), spec_refs, (kept, kept_coarse), table_ref, shift_at, map_at,
                rest, (maps, maps_coarse), [store.start for store in stores])
        else:
            for store in stores:
                store.start()
        for store in stores:
            store.wait()

    for_pairs(run)
    inner_stored()


def correlate(own, near, far, rim_of, rim_near, rim_far, mask_fine, mask_coarse):
    strip_rows, width = own.shape[1:]
    fine, coarse = mask_fine.shape[1], mask_coarse.shape[1]
    inner = fine - 1
    shift, map_ = shift_tables()
    tables = [fine_table(), shift, map_, coarse_table()]
    cuts = [int(at) for at in np.cumsum([0] + [table.shape[0] for table in tables])]
    inner_levels = [Level(1, range(inner), width, cuts[0])]
    outer_levels = [Level(1, range(inner, fine), width, cuts[0]), Level(2, range(coarse), width, cuts[3])]
    row_at = cuts[4]
    tables.append(row_table(outer_levels, strip_rows + PATCH))
    row_inner_at = row_at + tables[-1].shape[0]
    tables.append(row_table(inner_levels, strip_rows))
    columns = max(table.shape[1] for table in tables)
    table = np.concatenate([np.pad(table, ((0, 0), (0, columns - table.shape[1]))) for table in tables])
    cuts[4] = table.shape[0]

    shifts = WINDOW * WINDOW
    hbm = pl.BlockSpec(memory_space=pltpu.HBM)
    vmem = pl.BlockSpec(memory_space=pltpu.VMEM)
    params = pltpu.CompilerParams(vmem_limit_bytes=28 * 1024 * 1024)
    own, table, mask_fine, mask_coarse = (
        pltpu.with_memory_space_constraint(value, pltpu.HBM)
        for value in (own, jnp.asarray(table), mask_fine, mask_coarse))

    def cost(flops):
        return pl.CostEstimate(flops=flops, bytes_accessed=4 * 10**6, transcendentals=0)

    kept_own, handed, *kept = pl.pallas_call(
        load_kernel,
        out_shape=(
            jax.ShapeDtypeStruct(own.shape, bf16),
            jax.ShapeDtypeStruct(table.shape, bf16),
            *(jax.ShapeDtypeStruct((LANES, 8), f32) for _ in range(2)),
        ),
        in_specs=[hbm] * 4,
        out_specs=(vmem,) * 4,
        scratch_shapes=[
            pltpu.VMEM(mask_fine.shape, jnp.int32),
            pltpu.VMEM(mask_coarse.shape, jnp.int32),
            pltpu.VMEM((8, LANES), f32),
            pltpu.VMEM((8, LANES), f32),
            pltpu.SemaphoreType.DMA((3 + len(pieces(table.shape[0])),)),
        ],
        compiler_params=params,
        cost_estimate=cost(10**9),
        name="load",
    )(own, mask_fine, mask_coarse, table)
    rim = rim_of(kept_own)
    spec = pl.pallas_call(
        functools.partial(inner_kernel, inner_levels, row_inner_at),
        out_shape=jax.ShapeDtypeStruct((3 * inner_levels[0].rows, 2 * LANES), bf16),
        in_specs=[vmem] * 4,
        out_specs=vmem,
        scratch_shapes=section_scratch(inner_levels, width, 3),
        compiler_params=params,
        cost_estimate=cost(3 * 10**9),
        name="inner_spectra",
    )(kept_own, far, near, handed)
    *own_specs, maps = pl.pallas_call(
        functools.partial(middle_kernel, inner_levels, outer_levels, cuts, row_at),
        out_shape=(
            *(jax.ShapeDtypeStruct((level.rows, 2 * LANES), bf16) for level in outer_levels),
            jax.ShapeDtypeStruct((2, inner, 4 * inner_levels[0].quads, shifts), f32),
        ),
        in_specs=[vmem] * 5,
        out_specs=(vmem,) * 3,
        scratch_shapes=[*section_scratch(outer_levels, width, 1), *pair_scratch(inner_levels)],
        compiler_params=params,
        cost_estimate=cost(2 * 10**9),
        name="inner_maps",
    )(kept_own, rim, handed, spec, kept[0])
    return pl.pallas_call(
        functools.partial(outer_kernel, outer_levels, cuts, inner, row_at),
        out_shape=(
            jax.ShapeDtypeStruct((1, 2, fine, 4 * outer_levels[0].quads, shifts), f32),
            jax.ShapeDtypeStruct((1, 2, coarse, 4 * outer_levels[1].quads, shifts), f32),
        ),
        in_specs=[vmem] * 10,
        out_specs=(hbm, hbm),
        scratch_shapes=[
            *(pltpu.VMEM((2, level.blocks, 4 * level.quads, shifts), f32) for level in outer_levels),
            *section_scratch(outer_levels, width, 2),
            *spec_scratch(outer_levels, 2),
            *pair_scratch(outer_levels),
            pltpu.SemaphoreType.DMA((3,)),
        ],
        compiler_params=params,
        cost_estimate=cost(4 * 10**9),
        name="outer_blocks",
    )(far, near, rim_far, rim_near, handed, *own_specs, *kept, maps)


def local(sections, mask_fine, mask_coarse):
    far = from_device(sections, 2, 0)
    near = from_device(sections, 1, 0)
    rim_near, rim_far = from_device(sections, 1, 1), from_device(sections, 2, 1)
    return correlate(
        sections, near, far, lambda own: from_device(own, 0, 1), rim_near, rim_far, mask_fine, mask_coarse)


def solution(mesh):
    in_specs = (
        P("sec", "strip", "groups"),
        P("sec", "strip", "groups"),
        P("sec", "strip", "groups"),
    )
    out_specs = (P("sec", None, "strip", "groups", None), P("sec", None, "strip", "groups", None))
    return jax.shard_map(local, mesh=mesh, in_specs=in_specs, out_specs=out_specs, check_vma=False)
```

```python
import functools

import jax
import jax.numpy as jnp
import numpy as np
from jax import lax
from jax.experimental import pallas as pl
from jax.experimental.pallas import tpu as pltpu
from jax.sharding import PartitionSpec as P

PATCH = 64
STRIDE = 32
WINDOW = 32
HALF = PATCH // 2
LANES = 128
NYQ = 16

f32 = jnp.float32
bf16 = jnp.bfloat16


def from_device(value, sec_steps, strip_steps):
    secs, strips = lax.axis_size("sec"), lax.axis_size("strip")
    pairs = []
    for sec in range(secs - sec_steps):
        for strip in range(strips - strip_steps):
            pairs.append(((sec + sec_steps) * strips + strip + strip_steps, sec * strips + strip))
    return lax.ppermute(value, ("sec", "strip"), pairs)


def wave(phase):
    turns = np.arange(PATCH) * (2 * np.pi / PATCH)
    cos = np.round(np.cos(turns), 14)
    sin = np.round(np.sin(turns), 14)
    phase = np.mod(phase, PATCH)
    return cos[phase], sin[phase]


def split_table(table):
    high = table.astype(jnp.bfloat16)
    low = (table - high.astype(np.float64)).astype(jnp.bfloat16)
    return high, low


def stacked(table):
    return np.concatenate(split_table(table), axis=0)


def fine_table():
    c, s = wave(np.arange(PATCH)[:, None] * np.arange(PATCH)[None, :])
    table = np.zeros((2, 2, PATCH, 2, 2, PATCH))
    for p in range(2):
        table[0, p, :, 0, p] = c
        table[1, p, :, 0, p] = -s
        table[0, p, :, 1, p] = -s
        table[1, p, :, 1, p] = -c
    return stacked(table.reshape(4 * PATCH, 4 * PATCH))


def coarse_table():
    c, s = wave((np.arange(2 * PATCH) // 2)[:, None] * np.arange(PATCH)[None, :])
    table = np.zeros((2, 2, 2 * PATCH, 2, 2, PATCH))
    for p in range(2):
        table[p, 0, :, 0, p] = 0.5 * c
        table[p, 1, :, 0, p] = -0.5 * s
        table[p, 0, :, 1, p] = -0.5 * s
        table[p, 1, :, 1, p] = -0.5 * c
    return stacked(table.reshape(8 * PATCH, 4 * PATCH))


def shift_tables():
    spread = 1.869545
    t = np.arange(WINDOW) - WINDOW // 2
    c, s = wave(np.arange(PATCH)[:, None] * t[None, :])
    table = np.zeros((2, 2, 2, PATCH, 2, 4, WINDOW))
    for odd in range(2):
        for p in range(2):
            table[odd, 0, p, :, 0, 2 * p + odd] = c
            table[odd, 1, p, :, 0, 2 * p + odd] = -s
            table[odd, 0, p, :, 1, 2 * p + odd] = s
            table[odd, 1, p, :, 1, 2 * p + odd] = c
    along_t = (spread * table.reshape(8 * PATCH, 8 * WINDOW)).astype(jnp.bfloat16)
    c, s = wave(t[:, None] * np.arange(HALF)[None, :])
    weight = np.where(np.arange(HALF) == 0, 1.0, 2.0)
    nyquist = np.repeat(wave(HALF * t)[0][:, None], NYQ, axis=1)
    along_s = np.concatenate([c * weight, -s * weight, nyquist], axis=1) / (spread * PATCH**3)
    high, low = split_table(along_s)
    along_s = np.concatenate(
        [np.concatenate([high, high], axis=1), np.concatenate([low, np.zeros_like(low)], axis=1)], axis=0)
    return along_t, along_s


class Level:
    def __init__(self, pool, blocks, width, table):
        self.pool, self.first, self.blocks, self.table = pool, blocks[0], len(blocks), table
        self.quads = width // (4 * pool * STRIDE)
        self.tiles = 2 * self.quads
        self.body = self.blocks * HALF
        self.half = -(-self.quads * self.blocks // 8) * 8
        self.rows = self.tiles * self.body + 2 * self.half
        self.cross_body = self.quads * self.body
        self.cross_rows = self.cross_body + -(-self.half // 16) * 16

    def window(self, tile, p):
        quad, odd = divmod(tile, 2)
        return self.pool * LANES * quad + LANES * p + self.pool * STRIDE * odd

    def nyquist_row(self, tile, b):
        quad, odd = divmod(tile, 2)
        return odd * self.half + quad * self.blocks + b


def row_places(levels):
    at, places = 0, []
    for level in levels:
        places.append([at, at + level.body])
        at += level.body + 2 * level.half
    for level, place in zip(levels, places):
        place.append(at)
        at += level.body
    return places, at


def row_table(levels, ext):
    places, size = row_places(levels)
    table = np.zeros((size, ext))
    k = np.arange(HALF)[:, None]
    for level, (cos_at, nyquist_at, sin_at) in zip(levels, places):
        pool = level.pool
        x = np.arange(pool * PATCH) // pool
        c, s = wave(k * x[None, :])
        for b in range(level.blocks):
            first = (level.first + b) * pool * STRIDE
            columns = slice(first, first + x.size)
            table[cos_at + b * HALF : cos_at + (b + 1) * HALF, columns] = c / pool
            table[sin_at + b * HALF : sin_at + (b + 1) * HALF, columns] = s / pool
            for tile in range(level.tiles):
                table[nyquist_at + level.nyquist_row(tile, b), columns] = wave(HALF * x)[0] / pool
    return np.concatenate(split_table(table), axis=1)


def split(value):
    high = value.astype(bf16)
    return high, (value - high.astype(f32)).astype(bf16)


def dot(left, right):
    return jnp.dot(left, right, preferred_element_type=f32)


def dot3(high, low, table_ref, at):
    depth = high.shape[1]
    table_high = table_ref[at : at + depth]
    table_low = table_ref[at + depth : at + 2 * depth]
    return dot(
        jnp.concatenate([high, low, high], axis=1),
        jnp.concatenate([table_high, table_high, table_low], axis=0))


def cosine(turns):
    turns = turns + PATCH // 4
    part = (turns & (HALF - 1)) - PATCH // 4
    angle = part.astype(f32) * (2 * np.pi / PATCH)
    square = angle * angle
    value = jnp.full(square.shape, 1.0 / 479001600, f32)
    for term in (-1.0 / 3628800, 1.0 / 40320, -1.0 / 720, 1.0 / 24, -0.5, 1.0):
        value = value * square + term
    return jnp.where((turns & HALF) == 0, value, -value)


def write_row_table(row_ref, level):
    (cos_at, nyquist_at, sin_at), = row_places([level])[0]
    ext = row_ref.shape[1] // 2

    def put(at, value):
        high, low = split(value)
        row_ref[at : at + value.shape[0], :ext] = high
        row_ref[at : at + value.shape[0], ext:] = low

    def inside(x):
        return jnp.where((x >= 0) & (x < PATCH), 1.0, 0.0)

    k = lax.broadcasted_iota(jnp.int32, (HALF, ext), 0)
    for b in range(level.blocks):
        x = lax.broadcasted_iota(jnp.int32, (HALF, ext), 1) - (level.first + b) * STRIDE
        put(cos_at + b * HALF, cosine(k * x) * inside(x))
        put(sin_at + b * HALF, cosine(k * x - PATCH // 4) * inside(x))
    row = lax.broadcasted_iota(jnp.int32, (2 * level.half, ext), 0)
    x = lax.broadcasted_iota(jnp.int32, (2 * level.half, ext), 1)
    x = x - (level.first + lax.rem(lax.rem(row, level.half), level.blocks)) * STRIDE
    put(nyquist_at, cosine(x * HALF) * inside(x))


def write_fine_table(table_ref, at):
    y = lax.broadcasted_iota(jnp.int32, (PATCH, LANES), 0)
    lane = lax.broadcasted_iota(jnp.int32, (PATCH, LANES), 1)
    frequency = lane & (PATCH - 1)
    c, s = cosine(y * frequency), cosine(y * frequency - PATCH // 4)
    depth = 4 * PATCH
    for p in range(2):
        mine = (lane >= PATCH) if p else (lane < PATCH)
        cos, minus_cos, minus_sin = (jnp.where(mine, value, 0.0) for value in (c, -c, -s))
        for number, pair in enumerate(((cos, minus_sin), (minus_sin, minus_cos))):
            to = at + (2 * number + p) * PATCH
            for half, value in enumerate(pair):
                for level, part in enumerate(split(value)):
                    table_ref[to + level * depth : to + level * depth + PATCH, half * LANES : (half + 1) * LANES] = part


def all_rows(value):
    for step in (4, 2, 1):
        value = value + pltpu.roll(value, step, 0)
    return value


def left_of(level, place, half_ref, odd_ref):
    cos_at, nyquist_at, sin_at = place
    pieces = []
    for tile in range(level.tiles):
        if tile % 2:
            pieces.append(odd_ref[tile // 2 * level.body : (tile // 2 + 1) * level.body])
        else:
            columns = []
            for p in range(level.pool):
                at = level.window(tile, p)
                columns += [half_ref[start : start + level.body, at : at + LANES] for start in (cos_at, sin_at)]
            pieces.append(jnp.concatenate(columns, axis=1))
    pieces.append(odd_ref[level.quads * level.body :])
    return jnp.concatenate(pieces, axis=0)


def gather_windows(level, place, t_ref, halves, odds):
    cos_at, nyquist_at, sin_at = place
    body, end = level.body, level.quads * level.body
    row = lax.broadcasted_iota(jnp.int32, (2 * level.half, LANES), 0)
    for p in range(level.pool):
        for source, target in zip(halves, odds):
            for tile in range(1, level.tiles, 2):
                at = level.window(tile, p)
                for half, start in enumerate((cos_at, sin_at)):
                    to = tile // 2 * body
                    target[to : to + body, (2 * p + half) * LANES : (2 * p + half + 1) * LANES] = (
                        source[start : start + body, at : at + LANES])
        nyquist = jnp.zeros((2 * level.half, LANES), f32)
        for tile in range(level.tiles):
            at, first = level.window(tile, p), level.nyquist_row(tile, 0)
            value = t_ref[nyquist_at : nyquist_at + 2 * level.half, at : at + LANES]
            nyquist = jnp.where((row >= first) & (row < first + level.blocks), value, nyquist)
        for target, part in zip(odds, split(nyquist)):
            target[end:, 2 * p * LANES : (2 * p + 1) * LANES] = part
            target[end:, (2 * p + 1) * LANES : (2 * p + 2) * LANES] = jnp.zeros(part.shape, bf16)


def spectrum_power(level, f_ref, sections):
    sub = lax.broadcasted_iota(jnp.int32, (8, LANES), 0)
    lane = lax.broadcasted_iota(jnp.int32, (8, LANES), 1)
    dc = (sub == 0) & (lane % PATCH == 0)
    group = lax.broadcasted_iota(jnp.int32, (LANES, LANES), 0) // PATCH
    same = group == lax.broadcasted_iota(jnp.int32, (LANES, LANES), 1) // PATCH
    ones = jnp.where(same, 1.0, 0.0).astype(bf16)

    def square(at):
        re, im = f_ref[at : at + 8, :LANES], f_ref[at : at + 8, LANES:]
        return re * re + im * im

    sums = []
    for z in sections:
        end = z * level.rows + level.tiles * level.body
        tails = [square(end + at) for at in range(0, 2 * level.half, 8)]
        for tile in range(level.tiles):
            for b in range(level.blocks):
                base = z * level.rows + tile * level.body + b * HALF
                total = jnp.where(dc, 0.0, square(base))
                head = jnp.where(sub == 0, total, 0.0)
                for r in range(8, HALF, 8):
                    total = total + square(base + r)
                row = level.nyquist_row(tile, b)
                sums.append(2.0 * total - head + jnp.where(sub == row % 8, tails[row // 8], 0.0))
    high, low = split(jnp.concatenate(sums, axis=0))
    return dot(jnp.concatenate([high, low], axis=1), jnp.concatenate([ones, ones], axis=0))


def scale_spectrum(level, f_ref, sections, sums, spec_ref):
    sub = lax.broadcasted_iota(jnp.int32, (8, 2 * LANES), 0)
    lane = lax.broadcasted_iota(jnp.int32, (8, 2 * LANES), 1)
    dc = (sub == 0) & (lane % PATCH == 0)
    number = 0
    for z in sections:
        start = z * level.rows
        end = start + level.tiles * level.body
        tails = [f_ref[end + at : end + at + 8] for at in range(0, 2 * level.half, 8)]
        scaled = [jnp.zeros_like(tail) for tail in tails]
        for tile in range(level.tiles):
            for b in range(level.blocks):
                scale = lax.rsqrt(all_rows(sums[number : number + 8]) * (1.0 / PATCH**4) + 1e-05)
                number += 8
                scale = jnp.concatenate([scale, scale], axis=1)
                for r in range(0, HALF, 16):
                    at = start + tile * level.body + b * HALF + r
                    head = f_ref[at : at + 8]
                    if r == 0:
                        head = jnp.where(dc, 0.0, head)
                    both = jnp.concatenate([head * scale, f_ref[at + 8 : at + 16] * scale], axis=0)
                    spec_ref[at : at + 16] = both.astype(bf16)
                row = level.nyquist_row(tile, b)
                scaled[row // 8] = jnp.where(sub == row % 8, tails[row // 8] * scale, scaled[row // 8])
        spec_ref[end : end + 2 * level.half] = jnp.concatenate(scaled, axis=0).astype(bf16)


def transform_rows(levels, sections, strips, row_ref, scratch):
    t_ref, high_ref, low_ref = scratch[:3]
    odd_refs = scratch[3 : 3 + 2 * len(levels)]
    places, size = row_places(levels)
    for z in sections:
        x = jnp.concatenate([strip[0] for strip in strips[z]], axis=0)
        width = x.shape[1]
        x = jnp.concatenate([x, x], axis=0)
        for first in range(0, width, 2 * LANES):
            columns = slice(first, first + 2 * LANES)
            t = dot(row_ref[...], x[:, columns])
            for level, (cos_at, nyquist_at, sin_at) in zip(levels, places):
                for start in (cos_at, sin_at):
                    for ref, half in zip((high_ref, low_ref), split(t[start : start + level.body])):
                        ref[z, start : start + level.body, columns] = half
                rows = slice(nyquist_at, nyquist_at + 2 * level.half)
                t_ref[z, rows, columns] = t[rows]
        t_ref[z, :, width:] = jnp.zeros((size, LANES), f32)
        for ref in (high_ref, low_ref):
            ref[z, :, width:] = jnp.zeros((size, LANES), bf16)
    for index, (level, place) in enumerate(zip(levels, places)):
        odds = odd_refs[2 * index : 2 * index + 2]
        for z in sections:
            gather_windows(level, place, t_ref.at[z], (high_ref.at[z], low_ref.at[z]), [ref.at[z] for ref in odds])


def transform_columns(levels, sections, table_ref, scratch, spec_refs):
    high_ref, low_ref = scratch[1:3]
    odd_refs, f_refs = scratch[3 : 3 + 2 * len(levels)], scratch[3 + 2 * len(levels) :]
    places, size = row_places(levels)
    for index, (level, place) in enumerate(zip(levels, places)):
        lefts = [
            jnp.concatenate([left_of(level, place, ref.at[z], odd.at[z]) for z in sections], axis=0)
            for ref, odd in zip((high_ref, low_ref), odd_refs[2 * index : 2 * index + 2])]
        rows = slice(sections[0] * level.rows, (sections[-1] + 1) * level.rows)
        f_refs[index][rows] = dot3(*lefts, table_ref, level.table)
    for level, f_ref, spec_ref in zip(levels, f_refs, spec_refs):
        scale_spectrum(level, f_ref, sections, spectrum_power(level, f_ref, sections), spec_ref)


def write_maps(levels, pairs, own_specs, specs, kept, table_ref, shift_at, map_at, scratch, outs, finished=()):
    count = len(levels)
    cross_refs, y_refs, maps_refs, rows_refs, stacks = (scratch[i * count : (i + 1) * count] for i in range(5))
    for level, own, spec, cross_ref, y_ref in zip(levels, own_specs, specs, cross_refs, y_refs):
        def cross(at, rows):
            a = own[at : at + rows].astype(f32)
            ar, ai = a[:, :LANES], a[:, LANES:]
            for d in range(pairs):
                b = spec[d * level.rows + at : d * level.rows + at + rows].astype(f32)
                br, bi = b[:, :LANES], b[:, LANES:]
                yield d * level.cross_rows, jnp.concatenate([ar * br + ai * bi, ar * bi - ai * br], axis=1)

        for tile in range(level.tiles):
            quad, odd = divmod(tile, 2)
            for r in range(0, level.body, 16):
                for to, value in cross(tile * level.body + r, 16):
                    to += quad * level.body + r
                    cross_ref[to : to + 16, 2 * odd * LANES : 2 * (odd + 1) * LANES] = value.astype(bf16)
        for to, value in cross(level.tiles * level.body, 2 * level.half):
            value = jnp.concatenate([value[: level.half], value[level.half :]], axis=1)
            spare = level.cross_rows - level.cross_body - level.half
            if spare:
                value = jnp.concatenate([value, jnp.zeros((spare, 4 * LANES), f32)], axis=0)
            cross_ref[to + level.cross_body : to + level.cross_rows] = value.astype(bf16)
        rows = pairs * level.cross_rows
        y_ref[:rows] = dot(cross_ref[:rows], table_ref[shift_at : shift_at + 4 * LANES])
    row = lax.broadcasted_iota(jnp.int32, (NYQ, LANES), 0)
    for level, y_ref, stack_ref, maps_ref in zip(levels, y_refs, stacks, maps_refs):
        for b in range(level.blocks):
            for d in range(pairs):
                first = d * level.cross_rows
                nyq_at = first + level.cross_body
                nyquist = y_ref[nyq_at : nyq_at + NYQ, :LANES]
                for quad in range(level.quads):
                    top = first + quad * level.body + b * HALF
                    column = (d * level.quads + quad) * LANES
                    for at, value in (
                        (0, y_ref[top : top + HALF, :LANES]),
                        (HALF, y_ref[top : top + HALF, LANES:]),
                        (2 * HALF, jnp.where(row == quad * level.blocks + b, nyquist, 0.0)),
                    ):
                        for half, part in enumerate(split(value)):
                            to = half * (2 * HALF + NYQ) + at
                            stack_ref[to : to + value.shape[0], column : column + LANES] = part
            columns = pairs * level.quads * LANES
            both = dot(table_ref[map_at : map_at + 2 * WINDOW, : stack_ref.shape[0]], stack_ref[:, :columns])
            maps = both[:WINDOW] + both[WINDOW:]
            for tile in range(pairs * level.quads):
                maps_ref[b * pairs * level.quads + tile] = maps[:, tile * LANES : (tile + 1) * LANES]

    def exchange(low, high, width):
        even = (lax.broadcasted_iota(jnp.int32, low.shape, 1) & width) == 0
        return (
            jnp.where(even, low, pltpu.roll(high, width, 1)),
            jnp.where(even, pltpu.roll(low, LANES - width, 1), high))

    for index, (level, maps_ref, rows_ref, out) in enumerate(zip(levels, maps_refs, rows_refs, outs)):
        tiles = level.blocks * pairs * level.quads
        for big in range(WINDOW // 4):
            rows = [maps_ref[:tiles, 4 * big + r, :] for r in range(4)]
            for step in (2, 1):
                for r in range(4):
                    if not r & step:
                        rows[r], rows[r + step] = exchange(rows[r], rows[r + step], step * WINDOW)
            for g in range(4):
                rows_ref[big, pl.ds(g, tiles, stride=4), :] = rows[g]
            for b in range(level.blocks):
                column = kept[index][: 4 * level.quads, level.first + b : level.first + b + 1]
                for d in range(pairs):
                    at = 4 * (b * pairs + d) * level.quads
                    out[d, b, :, big * LANES : (big + 1) * LANES] = rows_ref[big, at : at + 4 * level.quads] * column
        if finished:
            finished[index]()


def write_mask_columns(mask_ref, pad_ref, kept_ref):
    pad_ref[...] = jnp.zeros(pad_ref.shape, f32)
    pad_ref[: mask_ref.shape[1], : mask_ref.shape[2]] = mask_ref[0].astype(f32)
    kept_ref[...] = jnp.transpose(pad_ref[...])


def sections_ahead():
    return lax.axis_size("sec") - 1 - lax.axis_index("sec")


def for_pairs(run):
    ahead = sections_ahead()
    pl.when(ahead >= 2)(lambda: run(2))
    pl.when(ahead == 1)(lambda: run(1))
    pl.when(ahead < 1)(lambda: run(0))


def clear_maps(pairs, outs):
    for out in outs:
        if pairs < 2:
            out[pairs:] = jnp.zeros((2 - pairs,) + out.shape[1:], f32)


def section_scratch(levels, width, count):
    size = row_places(levels)[1]
    return [
        pltpu.VMEM((count, size, width + LANES), f32),
        pltpu.VMEM((count, size, width + LANES), bf16),
        pltpu.VMEM((count, size, width + LANES), bf16),
        *(pltpu.VMEM((count, level.quads * level.body + 2 * level.half, 2 * level.pool * LANES), bf16)
          for level in levels for _ in range(2)),
        *(pltpu.VMEM((count * level.rows, 2 * LANES), f32) for level in levels),
    ]


def spec_scratch(levels, count):
    return [pltpu.VMEM((count * level.rows, 2 * LANES), bf16) for level in levels]


def pair_scratch(levels):
    def each(shape, dtype):
        return [pltpu.VMEM(shape(level), dtype) for level in levels]

    return [
        *each(lambda level: (2 * level.cross_rows, 4 * LANES), bf16),
        *each(lambda level: (2 * level.cross_rows, 2 * LANES), f32),
        *each(lambda level: (2 * level.blocks * level.quads, WINDOW, LANES), f32),
        *each(lambda level: (WINDOW // 4, 8 * level.blocks * level.quads, LANES), f32),
        *each(lambda level: (4 * HALF + 2 * NYQ, 2 * level.quads * LANES), bf16),
    ]


def copier(sems):
    used = []

    def start(source, target):
        copy = pltpu.make_async_copy(source, target, sems.at[len(used)])
        used.append(copy)
        copy.start()
        return copy.wait

    return start


def copy_kernel(own_hbm, own, sem):
    copy = pltpu.make_async_copy(own_hbm, own, sem)
    copy.start()
    copy.wait()


def inner_kernel(
    levels, cuts,
    own, far, near, mask_hbm, mask_coarse_hbm, table_hbm,
    maps, table_ref, kept, kept_coarse,
    mask, mask_coarse, pad, pad_coarse, row_ref, *rest,
):
    *scratch, sems = rest
    start = copier(sems)

    def table(first, last):
        piece = pl.ds(first, last - first)
        return start(table_hbm.at[piece], table_ref.at[piece])

    fine_at, shift_at, map_at, coarse_at, end = cuts
    copies = [table(shift_at, coarse_at), start(mask_hbm, mask), start(mask_coarse_hbm, mask_coarse)]
    outer_ready = table(coarse_at, end)
    size = 3 + 3 * len(levels)
    sections, spec_refs, rest = scratch[:size], scratch[size : size + 1], scratch[size + 1 :]
    strips = ((own,), (near,), (far,))
    rows = levels[0].rows

    def run(pairs):
        if pairs:
            write_row_table(row_ref, levels[0])
            write_fine_table(table_ref, fine_at)
            transform_rows(levels, range(pairs + 1), strips, row_ref, sections)
            transform_columns(levels, range(pairs + 1), table_ref, sections, spec_refs)
        for wait in copies:
            wait()
        if pairs:
            write_mask_columns(mask, pad, kept)
            write_mask_columns(mask_coarse, pad_coarse, kept_coarse)
            write_maps(
                levels, pairs, [spec_refs[0].at[pl.ds(0, rows)]], [spec_refs[0].at[pl.ds(rows, pairs * rows)]],
                (kept,), table_ref, shift_at, map_at, rest, (maps,))
        clear_maps(pairs, (maps,))
        outer_ready()

    for_pairs(run)


def outer_kernel(
    levels, cuts, inner, row_at,
    own, far, near, rim_far, rim_near, rim, table_ref, kept, kept_coarse, inner_maps,
    out_fine, out_coarse,
    maps, maps_coarse, *rest,
):
    *scratch, sems = rest
    inner_stored = copier(sems)(inner_maps, out_fine.at[0, :, pl.ds(0, inner)])
    fine_at, shift_at, map_at, coarse_at, end = cuts
    row_ref = table_ref.at[pl.ds(row_at, row_places(levels)[1])]
    size, count = 3 + 3 * len(levels), len(levels)
    sections, spec_refs, rest = scratch[:size], scratch[size : size + count], scratch[size + count :]
    strips = ((own, rim), (near, rim_near), (far, rim_far))
    own_specs = [spec.at[pl.ds(0, level.rows)] for level, spec in zip(levels, spec_refs)]

    def run(pairs):
        stores = [
            pltpu.make_async_copy(maps, out_fine.at[0, :, pl.ds(inner, levels[0].blocks)], sems.at[1]),
            pltpu.make_async_copy(maps_coarse, out_coarse.at[0], sems.at[2])]
        clear_maps(pairs, (maps, maps_coarse))
        if pairs:
            transform_rows(levels, range(pairs + 1), strips, row_ref, sections)
            transform_columns(levels, range(pairs + 1), table_ref, sections, spec_refs)
            other_specs = [
                spec.at[pl.ds(level.rows, pairs * level.rows)] for level, spec in zip(levels, spec_refs)]
            write_maps(
                levels, pairs, own_specs, other_specs, (kept, kept_coarse), table_ref, shift_at, map_at,
                rest, (maps, maps_coarse), [store.start for store in stores])
        else:
            for store in stores:
                store.start()
        for store in stores:
            store.wait()

    for_pairs(run)
    inner_stored()


def correlate(own, near, far, rim_of, rim_near, rim_far, mask_fine, mask_coarse):
    strip_rows, width = own.shape[1:]
    fine, coarse = mask_fine.shape[1], mask_coarse.shape[1]
    inner = fine - 1
    shift, map_ = shift_tables()
    tables = [fine_table(), shift, map_, coarse_table()]
    cuts = [int(at) for at in np.cumsum([0] + [table.shape[0] for table in tables])]
    inner_levels = [Level(1, range(inner), width, cuts[0])]
    outer_levels = [Level(1, range(inner, fine), width, cuts[0]), Level(2, range(coarse), width, cuts[3])]
    row_at = cuts[4]
    tables.append(row_table(outer_levels, strip_rows + PATCH))
    columns = max(table.shape[1] for table in tables)
    table = np.concatenate([np.pad(table, ((0, 0), (0, columns - table.shape[1]))) for table in tables])
    cuts[4] = table.shape[0]

    shifts = WINDOW * WINDOW
    hbm = pl.BlockSpec(memory_space=pltpu.HBM)
    vmem = pl.BlockSpec(memory_space=pltpu.VMEM)
    params = pltpu.CompilerParams(vmem_limit_bytes=28 * 1024 * 1024)
    own, table, mask_fine, mask_coarse = (
        pltpu.with_memory_space_constraint(value, pltpu.HBM)
        for value in (own, jnp.asarray(table), mask_fine, mask_coarse))

    def cost(flops):
        return pl.CostEstimate(flops=flops, bytes_accessed=4 * 10**6, transcendentals=0)

    kept_own = pl.pallas_call(
        copy_kernel,
        out_shape=jax.ShapeDtypeStruct(own.shape, bf16),
        in_specs=[hbm],
        out_specs=vmem,
        scratch_shapes=[pltpu.SemaphoreType.DMA],
        cost_estimate=cost(10**9),
        name="own_pixels",
    )(own)
    rim = rim_of(kept_own)
    maps, handed, *kept = pl.pallas_call(
        functools.partial(inner_kernel, inner_levels, cuts),
        out_shape=(
            jax.ShapeDtypeStruct((2, inner, 4 * inner_levels[0].quads, shifts), f32),
            jax.ShapeDtypeStruct(table.shape, bf16),
            *(jax.ShapeDtypeStruct((LANES, 8), f32) for _ in range(2)),
        ),
        in_specs=[vmem] * 3 + [hbm] * 3,
        out_specs=(vmem,) * 4,
        scratch_shapes=[
            pltpu.VMEM(mask_fine.shape, jnp.int32),
            pltpu.VMEM(mask_coarse.shape, jnp.int32),
            pltpu.VMEM((8, LANES), f32),
            pltpu.VMEM((8, LANES), f32),
            pltpu.VMEM((row_places(inner_levels)[1], 2 * strip_rows), bf16),
            *section_scratch(inner_levels, width, 3),
            *spec_scratch(inner_levels, 3),
            *pair_scratch(inner_levels),
            pltpu.SemaphoreType.DMA((4,)),
        ],
        compiler_params=params,
        cost_estimate=cost(3 * 10**9),
        name="inner_blocks",
    )(kept_own, far, near, mask_fine, mask_coarse, table)
    return pl.pallas_call(
        functools.partial(outer_kernel, outer_levels, cuts, inner, row_at),
        out_shape=(
            jax.ShapeDtypeStruct((1, 2, fine, 4 * outer_levels[0].quads, shifts), f32),
            jax.ShapeDtypeStruct((1, 2, coarse, 4 * outer_levels[1].quads, shifts), f32),
        ),
        in_specs=[vmem] * 10,
        out_specs=(hbm, hbm),
        scratch_shapes=[
            *(pltpu.VMEM((2, level.blocks, 4 * level.quads, shifts), f32) for level in outer_levels),
            *section_scratch(outer_levels, width, 3),
            *spec_scratch(outer_levels, 3),
            *pair_scratch(outer_levels),
            pltpu.SemaphoreType.DMA((3,)),
        ],
        compiler_params=params,
        cost_estimate=cost(4 * 10**9),
        name="outer_blocks",
    )(kept_own, far, near, rim_far, rim_near, rim, handed, *kept, maps)


def local(sections, mask_fine, mask_coarse):
    far = from_device(sections, 2, 0)
    near = from_device(sections, 1, 0)
    rim_near, rim_far = from_device(sections, 1, 1), from_device(sections, 2, 1)
    return correlate(
        sections, near, far, lambda own: from_device(own, 0, 1), rim_near, rim_far, mask_fine, mask_coarse)


def solution(mesh):
    in_specs = (
        P("sec", "strip", "groups"),
        P("sec", "strip", "groups"),
        P("sec", "strip", "groups"),
    )
    out_specs = (P("sec", None, "strip", "groups", None), P("sec", None, "strip", "groups", None))
    return jax.shard_map(local, mesh=mesh, in_specs=in_specs, out_specs=out_specs, check_vma=False)
```

```python
import functools

import jax
import jax.numpy as jnp
import numpy as np
from jax import lax
from jax.experimental import pallas as pl
from jax.experimental.pallas import tpu as pltpu
from jax.sharding import PartitionSpec as P

PATCH = 64
STRIDE = 32
WINDOW = 32
HALF = PATCH // 2
LANES = 128
NYQ = 16

f32 = jnp.float32
bf16 = jnp.bfloat16


def from_device(value, sec_steps, strip_steps):
    secs, strips = lax.axis_size("sec"), lax.axis_size("strip")
    pairs = []
    for sec in range(secs - sec_steps):
        for strip in range(strips - strip_steps):
            pairs.append(((sec + sec_steps) * strips + strip + strip_steps, sec * strips + strip))
    return lax.ppermute(value, ("sec", "strip"), pairs)


def wave(phase):
    turns = np.arange(PATCH) * (2 * np.pi / PATCH)
    cos = np.round(np.cos(turns), 14)
    sin = np.round(np.sin(turns), 14)
    phase = np.mod(phase, PATCH)
    return cos[phase], sin[phase]


def split_table(table):
    high = table.astype(jnp.bfloat16)
    low = (table - high.astype(np.float64)).astype(jnp.bfloat16)
    return high, low


def stacked(table):
    return np.concatenate(split_table(table), axis=0)


def fine_table():
    c, s = wave(np.arange(PATCH)[:, None] * np.arange(PATCH)[None, :])
    table = np.zeros((2, 2, PATCH, 2, 2, PATCH))
    for p in range(2):
        table[0, p, :, 0, p] = c
        table[1, p, :, 0, p] = -s
        table[0, p, :, 1, p] = -s
        table[1, p, :, 1, p] = -c
    return stacked(table.reshape(4 * PATCH, 4 * PATCH))


def coarse_table():
    c, s = wave((np.arange(2 * PATCH) // 2)[:, None] * np.arange(PATCH)[None, :])
    table = np.zeros((2, 2, 2 * PATCH, 2, 2, PATCH))
    for p in range(2):
        table[p, 0, :, 0, p] = 0.5 * c
        table[p, 1, :, 0, p] = -0.5 * s
        table[p, 0, :, 1, p] = -0.5 * s
        table[p, 1, :, 1, p] = -0.5 * c
    return stacked(table.reshape(8 * PATCH, 4 * PATCH))


def shift_tables():
    spread = 1.869545
    t = np.arange(WINDOW) - WINDOW // 2
    c, s = wave(np.arange(PATCH)[:, None] * t[None, :])
    table = np.zeros((2, 2, 2, PATCH, 2, 4, WINDOW))
    for odd in range(2):
        for p in range(2):
            table[odd, 0, p, :, 0, 2 * p + odd] = c
            table[odd, 1, p, :, 0, 2 * p + odd] = -s
            table[odd, 0, p, :, 1, 2 * p + odd] = s
            table[odd, 1, p, :, 1, 2 * p + odd] = c
    along_t = (spread * table.reshape(8 * PATCH, 8 * WINDOW)).astype(jnp.bfloat16)
    c, s = wave(t[:, None] * np.arange(HALF)[None, :])
    weight = np.where(np.arange(HALF) == 0, 1.0, 2.0)
    nyquist = np.repeat(wave(HALF * t)[0][:, None], NYQ, axis=1)
    along_s = np.concatenate([c * weight, -s * weight, nyquist], axis=1) / (spread * PATCH**3)
    high, low = split_table(along_s)
    along_s = np.concatenate(
        [np.concatenate([high, high], axis=1), np.concatenate([low, np.zeros_like(low)], axis=1)], axis=0)
    return along_t, along_s


class Level:
    def __init__(self, pool, blocks, width, table):
        self.pool, self.first, self.blocks, self.table = pool, blocks[0], len(blocks), table
        self.quads = width // (4 * pool * STRIDE)
        self.tiles = 2 * self.quads
        self.body = self.blocks * HALF
        self.half = -(-self.quads * self.blocks // 8) * 8
        self.rows = self.tiles * self.body + 2 * self.half
        self.cross_body = self.quads * self.body
        self.cross_rows = self.cross_body + -(-self.half // 16) * 16

    def window(self, tile, p):
        quad, odd = divmod(tile, 2)
        return self.pool * LANES * quad + LANES * p + self.pool * STRIDE * odd

    def nyquist_row(self, tile, b):
        quad, odd = divmod(tile, 2)
        return odd * self.half + quad * self.blocks + b


def row_places(levels):
    at, places = 0, []
    for level in levels:
        places.append([at, at + level.body])
        at += level.body + 2 * level.half
    for level, place in zip(levels, places):
        place.append(at)
        at += level.body
    return places, at


def row_table(levels, ext):
    places, size = row_places(levels)
    table = np.zeros((size, ext))
    k = np.arange(HALF)[:, None]
    for level, (cos_at, nyquist_at, sin_at) in zip(levels, places):
        pool = level.pool
        x = np.arange(pool * PATCH) // pool
        c, s = wave(k * x[None, :])
        for b in range(level.blocks):
            first = (level.first + b) * pool * STRIDE
            columns = slice(first, first + x.size)
            table[cos_at + b * HALF : cos_at + (b + 1) * HALF, columns] = c / pool
            table[sin_at + b * HALF : sin_at + (b + 1) * HALF, columns] = s / pool
            for tile in range(level.tiles):
                table[nyquist_at + level.nyquist_row(tile, b), columns] = wave(HALF * x)[0] / pool
    return np.concatenate(split_table(table), axis=1)


def split(value):
    high = value.astype(bf16)
    return high, (value - high.astype(f32)).astype(bf16)


def dot(left, right):
    return jnp.dot(left, right, preferred_element_type=f32)


def dot3(high, low, table_ref, at):
    depth = high.shape[1]
    table_high = table_ref[at : at + depth]
    table_low = table_ref[at + depth : at + 2 * depth]
    return dot(
        jnp.concatenate([high, low, high], axis=1),
        jnp.concatenate([table_high, table_high, table_low], axis=0))


def cosine(turns):
    turns = turns + PATCH // 4
    part = (turns & (HALF - 1)) - PATCH // 4
    angle = part.astype(f32) * (2 * np.pi / PATCH)
    square = angle * angle
    value = jnp.full(square.shape, 1.0 / 479001600, f32)
    for term in (-1.0 / 3628800, 1.0 / 40320, -1.0 / 720, 1.0 / 24, -0.5, 1.0):
        value = value * square + term
    return jnp.where((turns & HALF) == 0, value, -value)


def write_row_table(row_ref, level):
    (cos_at, nyquist_at, sin_at), = row_places([level])[0]
    ext = row_ref.shape[1] // 2

    def put(at, value):
        high, low = split(value)
        row_ref[at : at + value.shape[0], :ext] = high
        row_ref[at : at + value.shape[0], ext:] = low

    def inside(x):
        return jnp.where((x >= 0) & (x < PATCH), 1.0, 0.0)

    k = lax.broadcasted_iota(jnp.int32, (HALF, ext), 0)
    for b in range(level.blocks):
        x = lax.broadcasted_iota(jnp.int32, (HALF, ext), 1) - (level.first + b) * STRIDE
        put(cos_at + b * HALF, cosine(k * x) * inside(x))
        put(sin_at + b * HALF, cosine(k * x - PATCH // 4) * inside(x))
    row = lax.broadcasted_iota(jnp.int32, (2 * level.half, ext), 0)
    x = lax.broadcasted_iota(jnp.int32, (2 * level.half, ext), 1)
    x = x - (level.first + lax.rem(lax.rem(row, level.half), level.blocks)) * STRIDE
    put(nyquist_at, cosine(x * HALF) * inside(x))


def write_fine_table(table_ref, at):
    y = lax.broadcasted_iota(jnp.int32, (PATCH, LANES), 0)
    lane = lax.broadcasted_iota(jnp.int32, (PATCH, LANES), 1)
    frequency = lane & (PATCH - 1)
    c, s = cosine(y * frequency), cosine(y * frequency - PATCH // 4)
    depth = 4 * PATCH
    for p in range(2):
        mine = (lane >= PATCH) if p else (lane < PATCH)
        cos, minus_cos, minus_sin = (jnp.where(mine, value, 0.0) for value in (c, -c, -s))
        for number, pair in enumerate(((cos, minus_sin), (minus_sin, minus_cos))):
            to = at + (2 * number + p) * PATCH
            for half, value in enumerate(pair):
                for level, part in enumerate(split(value)):
                    table_ref[to + level * depth : to + level * depth + PATCH, half * LANES : (half + 1) * LANES] = part


def all_rows(value):
    for step in (4, 2, 1):
        value = value + pltpu.roll(value, step, 0)
    return value


def left_of(level, place, half_ref, odd_ref):
    cos_at, nyquist_at, sin_at = place
    pieces = []
    for tile in range(level.tiles):
        if tile % 2:
            pieces.append(odd_ref[tile // 2 * level.body : (tile // 2 + 1) * level.body])
        else:
            columns = []
            for p in range(level.pool):
                at = level.window(tile, p)
                columns += [half_ref[start : start + level.body, at : at + LANES] for start in (cos_at, sin_at)]
            pieces.append(jnp.concatenate(columns, axis=1))
    pieces.append(odd_ref[level.quads * level.body :])
    return jnp.concatenate(pieces, axis=0)


def gather_windows(level, place, t_ref, halves, odds):
    cos_at, nyquist_at, sin_at = place
    body, end = level.body, level.quads * level.body
    row = lax.broadcasted_iota(jnp.int32, (2 * level.half, LANES), 0)
    for p in range(level.pool):
        for source, target in zip(halves, odds):
            for tile in range(1, level.tiles, 2):
                at = level.window(tile, p)
                for half, start in enumerate((cos_at, sin_at)):
                    to = tile // 2 * body
                    target[to : to + body, (2 * p + half) * LANES : (2 * p + half + 1) * LANES] = (
                        source[start : start + body, at : at + LANES])
        nyquist = jnp.zeros((2 * level.half, LANES), f32)
        for tile in range(level.tiles):
            at, first = level.window(tile, p), level.nyquist_row(tile, 0)
            value = t_ref[nyquist_at : nyquist_at + 2 * level.half, at : at + LANES]
            nyquist = jnp.where((row >= first) & (row < first + level.blocks), value, nyquist)
        for target, part in zip(odds, split(nyquist)):
            target[end:, 2 * p * LANES : (2 * p + 1) * LANES] = part
            target[end:, (2 * p + 1) * LANES : (2 * p + 2) * LANES] = jnp.zeros(part.shape, bf16)


def spectrum_power(level, f_ref, sections):
    sub = lax.broadcasted_iota(jnp.int32, (8, LANES), 0)
    lane = lax.broadcasted_iota(jnp.int32, (8, LANES), 1)
    dc = (sub == 0) & (lane % PATCH == 0)
    group = lax.broadcasted_iota(jnp.int32, (LANES, LANES), 0) // PATCH
    same = group == lax.broadcasted_iota(jnp.int32, (LANES, LANES), 1) // PATCH
    ones = jnp.where(same, 1.0, 0.0).astype(bf16)

    def square(at):
        re, im = f_ref[at : at + 8, :LANES], f_ref[at : at + 8, LANES:]
        return re * re + im * im

    sums = []
    for z in sections:
        end = z * level.rows + level.tiles * level.body
        tails = [square(end + at) for at in range(0, 2 * level.half, 8)]
        for tile in range(level.tiles):
            for b in range(level.blocks):
                base = z * level.rows + tile * level.body + b * HALF
                total = jnp.where(dc, 0.0, square(base))
                head = jnp.where(sub == 0, total, 0.0)
                for r in range(8, HALF, 8):
                    total = total + square(base + r)
                row = level.nyquist_row(tile, b)
                sums.append(2.0 * total - head + jnp.where(sub == row % 8, tails[row // 8], 0.0))
    high, low = split(jnp.concatenate(sums, axis=0))
    return dot(jnp.concatenate([high, low], axis=1), jnp.concatenate([ones, ones], axis=0))


def scale_spectrum(level, f_ref, sections, sums, spec_ref):
    sub = lax.broadcasted_iota(jnp.int32, (8, 2 * LANES), 0)
    lane = lax.broadcasted_iota(jnp.int32, (8, 2 * LANES), 1)
    dc = (sub == 0) & (lane % PATCH == 0)
    number = 0
    for z in sections:
        start = z * level.rows
        end = start + level.tiles * level.body
        tails = [f_ref[end + at : end + at + 8] for at in range(0, 2 * level.half, 8)]
        scaled = [jnp.zeros_like(tail) for tail in tails]
        for tile in range(level.tiles):
            for b in range(level.blocks):
                scale = lax.rsqrt(all_rows(sums[number : number + 8]) * (1.0 / PATCH**4) + 1e-05)
                number += 8
                scale = jnp.concatenate([scale, scale], axis=1)
                for r in range(0, HALF, 16):
                    at = start + tile * level.body + b * HALF + r
                    head = f_ref[at : at + 8]
                    if r == 0:
                        head = jnp.where(dc, 0.0, head)
                    both = jnp.concatenate([head * scale, f_ref[at + 8 : at + 16] * scale], axis=0)
                    spec_ref[at : at + 16] = both.astype(bf16)
                row = level.nyquist_row(tile, b)
                scaled[row // 8] = jnp.where(sub == row % 8, tails[row // 8] * scale, scaled[row // 8])
        spec_ref[end : end + 2 * level.half] = jnp.concatenate(scaled, axis=0).astype(bf16)


def transform_rows(levels, sections, strips, row_ref, scratch):
    t_ref, high_ref, low_ref = scratch[:3]
    odd_refs = scratch[3 : 3 + 2 * len(levels)]
    places, size = row_places(levels)
    for z in sections:
        x = jnp.concatenate([strip[0] for strip in strips[z]], axis=0)
        width = x.shape[1]
        x = jnp.concatenate([x, x], axis=0)
        for first in range(0, width, 2 * LANES):
            columns = slice(first, first + 2 * LANES)
            t = dot(row_ref[...], x[:, columns])
            for level, (cos_at, nyquist_at, sin_at) in zip(levels, places):
                for start in (cos_at, sin_at):
                    for ref, half in zip((high_ref, low_ref), split(t[start : start + level.body])):
                        ref[z, start : start + level.body, columns] = half
                rows = slice(nyquist_at, nyquist_at + 2 * level.half)
                t_ref[z, rows, columns] = t[rows]
        t_ref[z, :, width:] = jnp.zeros((size, LANES), f32)
        for ref in (high_ref, low_ref):
            ref[z, :, width:] = jnp.zeros((size, LANES), bf16)
    for index, (level, place) in enumerate(zip(levels, places)):
        odds = odd_refs[2 * index : 2 * index + 2]
        for z in sections:
            gather_windows(level, place, t_ref.at[z], (high_ref.at[z], low_ref.at[z]), [ref.at[z] for ref in odds])


def transform_columns(levels, sections, table_ref, scratch, spec_refs):
    high_ref, low_ref = scratch[1:3]
    odd_refs, f_refs = scratch[3 : 3 + 2 * len(levels)], scratch[3 + 2 * len(levels) :]
    places, size = row_places(levels)
    for index, (level, place) in enumerate(zip(levels, places)):
        lefts = [
            jnp.concatenate([left_of(level, place, ref.at[z], odd.at[z]) for z in sections], axis=0)
            for ref, odd in zip((high_ref, low_ref), odd_refs[2 * index : 2 * index + 2])]
        rows = slice(sections[0] * level.rows, (sections[-1] + 1) * level.rows)
        f_refs[index][rows] = dot3(*lefts, table_ref, level.table)
    for level, f_ref, spec_ref in zip(levels, f_refs, spec_refs):
        scale_spectrum(level, f_ref, sections, spectrum_power(level, f_ref, sections), spec_ref)


def write_maps(levels, pairs, own_specs, specs, kept, table_ref, shift_at, map_at, scratch, outs, finished=()):
    count = len(levels)
    cross_refs, y_refs, maps_refs, rows_refs, stacks = (scratch[i * count : (i + 1) * count] for i in range(5))
    for level, own, spec, cross_ref, y_ref in zip(levels, own_specs, specs, cross_refs, y_refs):
        def cross(at, rows):
            a = own[at : at + rows].astype(f32)
            ar, ai = a[:, :LANES], a[:, LANES:]
            for d in range(pairs):
                b = spec[d * level.rows + at : d * level.rows + at + rows].astype(f32)
                br, bi = b[:, :LANES], b[:, LANES:]
                yield d * level.cross_rows, jnp.concatenate([ar * br + ai * bi, ar * bi - ai * br], axis=1)

        for tile in range(level.tiles):
            quad, odd = divmod(tile, 2)
            for r in range(0, level.body, 16):
                for to, value in cross(tile * level.body + r, 16):
                    to += quad * level.body + r
                    cross_ref[to : to + 16, 2 * odd * LANES : 2 * (odd + 1) * LANES] = value.astype(bf16)
        for to, value in cross(level.tiles * level.body, 2 * level.half):
            value = jnp.concatenate([value[: level.half], value[level.half :]], axis=1)
            spare = level.cross_rows - level.cross_body - level.half
            if spare:
                value = jnp.concatenate([value, jnp.zeros((spare, 4 * LANES), f32)], axis=0)
            cross_ref[to + level.cross_body : to + level.cross_rows] = value.astype(bf16)
        rows = pairs * level.cross_rows
        y_ref[:rows] = dot(cross_ref[:rows], table_ref[shift_at : shift_at + 4 * LANES])
    row = lax.broadcasted_iota(jnp.int32, (NYQ, LANES), 0)
    for level, y_ref, stack_ref, maps_ref in zip(levels, y_refs, stacks, maps_refs):
        for b in range(level.blocks):
            for d in range(pairs):
                first = d * level.cross_rows
                nyq_at = first + level.cross_body
                nyquist = y_ref[nyq_at : nyq_at + NYQ, :LANES]
                for quad in range(level.quads):
                    top = first + quad * level.body + b * HALF
                    column = (d * level.quads + quad) * LANES
                    for at, value in (
                        (0, y_ref[top : top + HALF, :LANES]),
                        (HALF, y_ref[top : top + HALF, LANES:]),
                        (2 * HALF, jnp.where(row == quad * level.blocks + b, nyquist, 0.0)),
                    ):
                        for half, part in enumerate(split(value)):
                            to = half * (2 * HALF + NYQ) + at
                            stack_ref[to : to + value.shape[0], column : column + LANES] = part
            columns = pairs * level.quads * LANES
            both = dot(table_ref[map_at : map_at + 2 * WINDOW, : stack_ref.shape[0]], stack_ref[:, :columns])
            maps = both[:WINDOW] + both[WINDOW:]
            for tile in range(pairs * level.quads):
                maps_ref[b * pairs * level.quads + tile] = maps[:, tile * LANES : (tile + 1) * LANES]

    def exchange(low, high, width):
        even = (lax.broadcasted_iota(jnp.int32, low.shape, 1) & width) == 0
        return (
            jnp.where(even, low, pltpu.roll(high, width, 1)),
            jnp.where(even, pltpu.roll(low, LANES - width, 1), high))

    for index, (level, maps_ref, rows_ref, out) in enumerate(zip(levels, maps_refs, rows_refs, outs)):
        tiles = level.blocks * pairs * level.quads
        for big in range(WINDOW // 4):
            rows = [maps_ref[:tiles, 4 * big + r, :] for r in range(4)]
            for step in (2, 1):
                for r in range(4):
                    if not r & step:
                        rows[r], rows[r + step] = exchange(rows[r], rows[r + step], step * WINDOW)
            for g in range(4):
                rows_ref[big, pl.ds(g, tiles, stride=4), :] = rows[g]
            for b in range(level.blocks):
                column = kept[index][: 4 * level.quads, level.first + b : level.first + b + 1]
                for d in range(pairs):
                    at = 4 * (b * pairs + d) * level.quads
                    out[d, b, :, big * LANES : (big + 1) * LANES] = rows_ref[big, at : at + 4 * level.quads] * column
        if finished:
            finished[index]()


def write_mask_columns(mask_ref, pad_ref, kept_ref):
    pad_ref[...] = jnp.zeros(pad_ref.shape, f32)
    pad_ref[: mask_ref.shape[1], : mask_ref.shape[2]] = mask_ref[0].astype(f32)
    kept_ref[...] = jnp.transpose(pad_ref[...])


def sections_ahead():
    return lax.axis_size("sec") - 1 - lax.axis_index("sec")


def for_pairs(run):
    ahead = sections_ahead()
    pl.when(ahead >= 2)(lambda: run(2))
    pl.when(ahead == 1)(lambda: run(1))
    pl.when(ahead < 1)(lambda: run(0))


def clear_maps(pairs, outs):
    for out in outs:
        if pairs < 2:
            out[pairs:] = jnp.zeros((2 - pairs,) + out.shape[1:], f32)


def section_scratch(levels, width, count):
    size = row_places(levels)[1]
    return [
        pltpu.VMEM((count, size, width + LANES), f32),
        pltpu.VMEM((count, size, width + LANES), bf16),
        pltpu.VMEM((count, size, width + LANES), bf16),
        *(pltpu.VMEM((count, level.quads * level.body + 2 * level.half, 2 * level.pool * LANES), bf16)
          for level in levels for _ in range(2)),
        *(pltpu.VMEM((count * level.rows, 2 * LANES), f32) for level in levels),
    ]


def spec_scratch(levels, count):
    return [pltpu.VMEM((count * level.rows, 2 * LANES), bf16) for level in levels]


def pair_scratch(levels):
    def each(shape, dtype):
        return [pltpu.VMEM(shape(level), dtype) for level in levels]

    return [
        *each(lambda level: (2 * level.cross_rows, 4 * LANES), bf16),
        *each(lambda level: (2 * level.cross_rows, 2 * LANES), f32),
        *each(lambda level: (2 * level.blocks * level.quads, WINDOW, LANES), f32),
        *each(lambda level: (WINDOW // 4, 8 * level.blocks * level.quads, LANES), f32),
        *each(lambda level: (4 * HALF + 2 * NYQ, 2 * level.quads * LANES), bf16),
    ]


def copier(sems):
    used = []

    def start(source, target):
        copy = pltpu.make_async_copy(source, target, sems.at[len(used)])
        used.append(copy)
        copy.start()
        return copy.wait

    return start


def inner_kernel(
    levels, cuts,
    own_hbm, near, far, mask_hbm, mask_coarse_hbm, table_hbm,
    maps, own, table_ref, kept, kept_coarse,
    mask, mask_coarse, pad, pad_coarse, row_ref, *rest,
):
    *scratch, sems = rest
    start = copier(sems)

    def table(first, last):
        piece = pl.ds(first, last - first)
        return start(table_hbm.at[piece], table_ref.at[piece])

    fine_at, shift_at, map_at, coarse_at, end = cuts
    own_ready = start(own_hbm, own)
    copies = [table(shift_at, coarse_at), start(mask_hbm, mask), start(mask_coarse_hbm, mask_coarse)]
    outer_ready = table(coarse_at, end)
    size = 3 + 3 * len(levels)
    sections, spec_refs, rest = scratch[:size], scratch[size : size + 1], scratch[size + 1 :]
    strips = ((own,), (near,), (far,))
    rows = levels[0].rows

    def run(pairs):
        if pairs:
            write_row_table(row_ref, levels[0])
            write_fine_table(table_ref, fine_at)
            transform_rows(levels, range(1, pairs + 1), strips, row_ref, sections)
        own_ready()
        if pairs:
            transform_rows(levels, (0,), strips, row_ref, sections)
            transform_columns(levels, range(pairs + 1), table_ref, sections, spec_refs)
        for wait in copies:
            wait()
        if pairs:
            write_mask_columns(mask, pad, kept)
            write_mask_columns(mask_coarse, pad_coarse, kept_coarse)
            write_maps(
                levels, pairs, [spec_refs[0].at[pl.ds(0, rows)]], [spec_refs[0].at[pl.ds(rows, pairs * rows)]],
                (kept,), table_ref, shift_at, map_at, rest, (maps,))
        clear_maps(pairs, (maps,))
        outer_ready()

    for_pairs(run)


def own_kernel(levels, row_at, own, rim, table_ref, *rest):
    spec_refs, sections = rest[: len(levels)], rest[len(levels) :]
    row_ref = table_ref.at[pl.ds(row_at, row_places(levels)[1])]

    @pl.when(sections_ahead() >= 1)
    def _():
        transform_rows(levels, (0,), ((own, rim),), row_ref, sections)
        transform_columns(levels, (0,), table_ref, sections, spec_refs)


def outer_kernel(
    levels, cuts, inner, row_at,
    near, far, rim_near, rim_far, table_ref, own_fine, own_coarse, kept, kept_coarse, inner_maps,
    out_fine, out_coarse,
    maps, maps_coarse, *rest,
):
    *scratch, sems = rest
    inner_stored = copier(sems)(inner_maps, out_fine.at[0, :, pl.ds(0, inner)])
    fine_at, shift_at, map_at, coarse_at, end = cuts
    row_ref = table_ref.at[pl.ds(row_at, row_places(levels)[1])]
    size, count = 3 + 3 * len(levels), len(levels)
    sections, spec_refs, rest = scratch[:size], scratch[size : size + count], scratch[size + count :]
    strips = ((near, rim_near), (far, rim_far))

    def run(pairs):
        stores = [
            pltpu.make_async_copy(maps, out_fine.at[0, :, pl.ds(inner, levels[0].blocks)], sems.at[1]),
            pltpu.make_async_copy(maps_coarse, out_coarse.at[0], sems.at[2])]
        clear_maps(pairs, (maps, maps_coarse))
        if pairs:
            transform_rows(levels, range(pairs), strips, row_ref, sections)
            transform_columns(levels, range(pairs), table_ref, sections, spec_refs)
            write_maps(
                levels, pairs, (own_fine, own_coarse), spec_refs, (kept, kept_coarse), table_ref, shift_at, map_at,
                rest, (maps, maps_coarse), [store.start for store in stores])
        else:
            for store in stores:
                store.start()
        for store in stores:
            store.wait()

    for_pairs(run)
    inner_stored()


def correlate(own, near, far, rim, rim_near, rim_far, mask_fine, mask_coarse):
    strip_rows, width = own.shape[1:]
    fine, coarse = mask_fine.shape[1], mask_coarse.shape[1]
    inner = fine - 1
    shift, map_ = shift_tables()
    tables = [fine_table(), shift, map_, coarse_table()]
    cuts = [int(at) for at in np.cumsum([0] + [table.shape[0] for table in tables])]
    inner_levels = [Level(1, range(inner), width, cuts[0])]
    outer_levels = [Level(1, range(inner, fine), width, cuts[0]), Level(2, range(coarse), width, cuts[3])]
    row_at = cuts[4]
    tables.append(row_table(outer_levels, strip_rows + PATCH))
    columns = max(table.shape[1] for table in tables)
    table = np.concatenate([np.pad(table, ((0, 0), (0, columns - table.shape[1]))) for table in tables])
    cuts[4] = table.shape[0]

    shifts = WINDOW * WINDOW
    hbm = pl.BlockSpec(memory_space=pltpu.HBM)
    vmem = pl.BlockSpec(memory_space=pltpu.VMEM)
    params = pltpu.CompilerParams(vmem_limit_bytes=28 * 1024 * 1024)
    own, table, mask_fine, mask_coarse = (
        pltpu.with_memory_space_constraint(value, pltpu.HBM)
        for value in (own, jnp.asarray(table), mask_fine, mask_coarse))

    def cost(flops):
        return pl.CostEstimate(flops=flops, bytes_accessed=4 * 10**6, transcendentals=0)

    maps, own_kept, handed, *kept = pl.pallas_call(
        functools.partial(inner_kernel, inner_levels, cuts),
        out_shape=(
            jax.ShapeDtypeStruct((2, inner, 4 * inner_levels[0].quads, shifts), f32),
            jax.ShapeDtypeStruct(own.shape, bf16),
            jax.ShapeDtypeStruct(table.shape, bf16),
            *(jax.ShapeDtypeStruct((LANES, 8), f32) for _ in range(2)),
        ),
        in_specs=[hbm, vmem, vmem, hbm, hbm, hbm],
        out_specs=(vmem,) * 5,
        scratch_shapes=[
            pltpu.VMEM(mask_fine.shape, jnp.int32),
            pltpu.VMEM(mask_coarse.shape, jnp.int32),
            pltpu.VMEM((8, LANES), f32),
            pltpu.VMEM((8, LANES), f32),
            pltpu.VMEM((row_places(inner_levels)[1], 2 * strip_rows), bf16),
            *section_scratch(inner_levels, width, 3),
            *spec_scratch(inner_levels, 3),
            *pair_scratch(inner_levels),
            pltpu.SemaphoreType.DMA((5,)),
        ],
        compiler_params=params,
        cost_estimate=cost(3 * 10**9),
        name="inner_blocks",
    )(own, near, far, mask_fine, mask_coarse, table)
    own_specs = pl.pallas_call(
        functools.partial(own_kernel, outer_levels, row_at),
        out_shape=tuple(jax.ShapeDtypeStruct((level.rows, 2 * LANES), bf16) for level in outer_levels),
        in_specs=[vmem] * 3,
        out_specs=(vmem,) * 2,
        scratch_shapes=section_scratch(outer_levels, width, 1),
        compiler_params=params,
        cost_estimate=cost(2 * 10**9),
        name="own_outer_blocks",
    )(own_kept, rim, handed)
    return pl.pallas_call(
        functools.partial(outer_kernel, outer_levels, cuts, inner, row_at),
        out_shape=(
            jax.ShapeDtypeStruct((1, 2, fine, 4 * outer_levels[0].quads, shifts), f32),
            jax.ShapeDtypeStruct((1, 2, coarse, 4 * outer_levels[1].quads, shifts), f32),
        ),
        in_specs=[vmem] * 10,
        out_specs=(hbm, hbm),
        scratch_shapes=[
            *(pltpu.VMEM((2, level.blocks, 4 * level.quads, shifts), f32) for level in outer_levels),
            *section_scratch(outer_levels, width, 2),
            *spec_scratch(outer_levels, 2),
            *pair_scratch(outer_levels),
            pltpu.SemaphoreType.DMA((3,)),
        ],
        compiler_params=params,
        cost_estimate=cost(4 * 10**9),
        name="outer_blocks",
    )(near, far, rim_near, rim_far, handed, *own_specs, *kept, maps)


def local(sections, mask_fine, mask_coarse):
    far = from_device(sections, 2, 0)
    near = from_device(sections, 1, 0)
    rims = [from_device(sections, z, 1) for z in range(3)]
    return correlate(sections, near, far, *rims, mask_fine, mask_coarse)


def solution(mesh):
    in_specs = (
        P("sec", "strip", "groups"),
        P("sec", "strip", "groups"),
        P("sec", "strip", "groups"),
    )
    out_specs = (P("sec", None, "strip", "groups", None), P("sec", None, "strip", "groups", None))
    return jax.shard_map(local, mesh=mesh, in_specs=in_specs, out_specs=out_specs, check_vma=False)
```

```python
import functools

import jax
import jax.numpy as jnp
import numpy as np
from jax import lax
from jax.experimental import pallas as pl
from jax.experimental.pallas import tpu as pltpu
from jax.sharding import PartitionSpec as P

PATCH = 64
STRIDE = 32
WINDOW = 32
HALF = PATCH // 2
LANES = 128
NYQ = 16

f32 = jnp.float32
bf16 = jnp.bfloat16


def from_device(value, sec_steps, strip_steps):
    secs, strips = lax.axis_size("sec"), lax.axis_size("strip")
    pairs = []
    for sec in range(secs - sec_steps):
        for strip in range(strips - strip_steps):
            pairs.append(((sec + sec_steps) * strips + strip + strip_steps, sec * strips + strip))
    return lax.ppermute(value, ("sec", "strip"), pairs)


def wave(phase):
    turns = np.arange(PATCH) * (2 * np.pi / PATCH)
    cos = np.round(np.cos(turns), 14)
    sin = np.round(np.sin(turns), 14)
    phase = np.mod(phase, PATCH)
    return cos[phase], sin[phase]


def split_table(table):
    high = table.astype(jnp.bfloat16)
    low = (table - high.astype(np.float64)).astype(jnp.bfloat16)
    return high, low


def stacked(table):
    return np.concatenate(split_table(table), axis=0)


def fine_table():
    c, s = wave(np.arange(PATCH)[:, None] * np.arange(PATCH)[None, :])
    table = np.zeros((2, 2, PATCH, 2, 2, PATCH))
    for p in range(2):
        table[0, p, :, 0, p] = c
        table[1, p, :, 0, p] = -s
        table[0, p, :, 1, p] = -s
        table[1, p, :, 1, p] = -c
    return stacked(table.reshape(4 * PATCH, 4 * PATCH))


def coarse_table():
    c, s = wave((np.arange(2 * PATCH) // 2)[:, None] * np.arange(PATCH)[None, :])
    table = np.zeros((2, 2, 2 * PATCH, 2, 2, PATCH))
    for p in range(2):
        table[p, 0, :, 0, p] = 0.5 * c
        table[p, 1, :, 0, p] = -0.5 * s
        table[p, 0, :, 1, p] = -0.5 * s
        table[p, 1, :, 1, p] = -0.5 * c
    return stacked(table.reshape(8 * PATCH, 4 * PATCH))


def shift_tables():
    spread = 1.869545
    t = np.arange(WINDOW) - WINDOW // 2
    c, s = wave(np.arange(PATCH)[:, None] * t[None, :])
    table = np.zeros((2, 2, 2, PATCH, 2, 4, WINDOW))
    for odd in range(2):
        for p in range(2):
            table[odd, 0, p, :, 0, 2 * p + odd] = c
            table[odd, 1, p, :, 0, 2 * p + odd] = -s
            table[odd, 0, p, :, 1, 2 * p + odd] = s
            table[odd, 1, p, :, 1, 2 * p + odd] = c
    along_t = (spread * table.reshape(8 * PATCH, 8 * WINDOW)).astype(jnp.bfloat16)
    c, s = wave(t[:, None] * np.arange(HALF)[None, :])
    weight = np.where(np.arange(HALF) == 0, 1.0, 2.0)
    nyquist = np.repeat(wave(HALF * t)[0][:, None], NYQ, axis=1)
    along_s = np.concatenate([c * weight, -s * weight, nyquist], axis=1) / (spread * PATCH**3)
    high, low = split_table(along_s)
    along_s = np.concatenate(
        [np.concatenate([high, high], axis=1), np.concatenate([low, np.zeros_like(low)], axis=1)], axis=0)
    return along_t, along_s


class Level:
    def __init__(self, pool, blocks, width, table):
        self.pool, self.first, self.blocks, self.table = pool, blocks[0], len(blocks), table
        self.quads = width // (4 * pool * STRIDE)
        self.tiles = 2 * self.quads
        self.body = self.blocks * HALF
        self.half = -(-self.quads * self.blocks // 8) * 8
        self.rows = self.tiles * self.body + 2 * self.half
        self.cross_body = self.quads * self.body
        self.cross_rows = self.cross_body + -(-self.half // 16) * 16

    def window(self, tile, p):
        quad, odd = divmod(tile, 2)
        return self.pool * LANES * quad + LANES * p + self.pool * STRIDE * odd

    def nyquist_row(self, tile, b):
        quad, odd = divmod(tile, 2)
        return odd * self.half + quad * self.blocks + b


def row_places(levels):
    at, places = 0, []
    for level in levels:
        places.append([at, at + level.body])
        at += level.body + 2 * level.half
    for level, place in zip(levels, places):
        place.append(at)
        at += level.body
    return places, at


def row_table(levels, ext):
    places, size = row_places(levels)
    table = np.zeros((size, ext))
    k = np.arange(HALF)[:, None]
    for level, (cos_at, nyquist_at, sin_at) in zip(levels, places):
        pool = level.pool
        x = np.arange(pool * PATCH) // pool
        c, s = wave(k * x[None, :])
        for b in range(level.blocks):
            first = (level.first + b) * pool * STRIDE
            columns = slice(first, first + x.size)
            table[cos_at + b * HALF : cos_at + (b + 1) * HALF, columns] = c / pool
            table[sin_at + b * HALF : sin_at + (b + 1) * HALF, columns] = s / pool
            for tile in range(level.tiles):
                table[nyquist_at + level.nyquist_row(tile, b), columns] = wave(HALF * x)[0] / pool
    return np.concatenate(split_table(table), axis=1)


def split(value):
    high = value.astype(bf16)
    return high, (value - high.astype(f32)).astype(bf16)


def dot(left, right):
    return jnp.dot(left, right, preferred_element_type=f32)


def dot3(high, low, table_ref, at):
    depth = high.shape[1]
    table_high = table_ref[at : at + depth]
    table_low = table_ref[at + depth : at + 2 * depth]
    return dot(
        jnp.concatenate([high, low, high], axis=1),
        jnp.concatenate([table_high, table_high, table_low], axis=0))


def cosine(turns):
    turns = turns + PATCH // 4
    part = (turns & (HALF - 1)) - PATCH // 4
    angle = part.astype(f32) * (2 * np.pi / PATCH)
    square = angle * angle
    value = jnp.full(square.shape, 1.0 / 479001600, f32)
    for term in (-1.0 / 3628800, 1.0 / 40320, -1.0 / 720, 1.0 / 24, -0.5, 1.0):
        value = value * square + term
    return jnp.where((turns & HALF) == 0, value, -value)


def write_row_table(row_ref, level):
    (cos_at, nyquist_at, sin_at), = row_places([level])[0]
    ext = row_ref.shape[1] // 2

    def put(at, value):
        high, low = split(value)
        row_ref[at : at + value.shape[0], :ext] = high
        row_ref[at : at + value.shape[0], ext:] = low

    def inside(x):
        return jnp.where((x >= 0) & (x < PATCH), 1.0, 0.0)

    k = lax.broadcasted_iota(jnp.int32, (HALF, ext), 0)
    for b in range(level.blocks):
        x = lax.broadcasted_iota(jnp.int32, (HALF, ext), 1) - (level.first + b) * STRIDE
        put(cos_at + b * HALF, cosine(k * x) * inside(x))
        put(sin_at + b * HALF, cosine(k * x - PATCH // 4) * inside(x))
    row = lax.broadcasted_iota(jnp.int32, (2 * level.half, ext), 0)
    x = lax.broadcasted_iota(jnp.int32, (2 * level.half, ext), 1)
    x = x - (level.first + lax.rem(lax.rem(row, level.half), level.blocks)) * STRIDE
    put(nyquist_at, cosine(x * HALF) * inside(x))


def write_fine_table(table_ref, at):
    y = lax.broadcasted_iota(jnp.int32, (PATCH, LANES), 0)
    lane = lax.broadcasted_iota(jnp.int32, (PATCH, LANES), 1)
    frequency = lane & (PATCH - 1)
    c, s = cosine(y * frequency), cosine(y * frequency - PATCH // 4)
    depth = 4 * PATCH
    for p in range(2):
        mine = (lane >= PATCH) if p else (lane < PATCH)
        cos, minus_cos, minus_sin = (jnp.where(mine, value, 0.0) for value in (c, -c, -s))
        for number, pair in enumerate(((cos, minus_sin), (minus_sin, minus_cos))):
            to = at + (2 * number + p) * PATCH
            for half, value in enumerate(pair):
                for level, part in enumerate(split(value)):
                    table_ref[to + level * depth : to + level * depth + PATCH, half * LANES : (half + 1) * LANES] = part


def all_rows(value):
    for step in (4, 2, 1):
        value = value + pltpu.roll(value, step, 0)
    return value


def left_of(level, place, half_ref, nyquist_ref):
    cos_at, nyquist_at, sin_at = place
    pieces = []
    for tile in range(level.tiles):
        columns = []
        for p in range(level.pool):
            at = level.window(tile, p)
            columns += [half_ref[start : start + level.body, at : at + LANES] for start in (cos_at, sin_at)]
        pieces.append(jnp.concatenate(columns, axis=1))
    pieces.append(nyquist_ref[...])
    return jnp.concatenate(pieces, axis=0)


def gather_nyquist(level, place, t_ref, targets):
    cos_at, nyquist_at, sin_at = place
    row = lax.broadcasted_iota(jnp.int32, (2 * level.half, LANES), 0)
    for p in range(level.pool):
        nyquist = jnp.zeros((2 * level.half, LANES), f32)
        for tile in range(level.tiles):
            at, first = level.window(tile, p), level.nyquist_row(tile, 0)
            value = t_ref[nyquist_at : nyquist_at + 2 * level.half, at : at + LANES]
            nyquist = jnp.where((row >= first) & (row < first + level.blocks), value, nyquist)
        for target, part in zip(targets, split(nyquist)):
            target[:, 2 * p * LANES : (2 * p + 1) * LANES] = part
            target[:, (2 * p + 1) * LANES : (2 * p + 2) * LANES] = jnp.zeros(part.shape, bf16)


def spectrum_power(level, f_ref, sections):
    sub = lax.broadcasted_iota(jnp.int32, (8, LANES), 0)
    lane = lax.broadcasted_iota(jnp.int32, (8, LANES), 1)
    dc = (sub == 0) & (lane % PATCH == 0)
    group = lax.broadcasted_iota(jnp.int32, (LANES, LANES), 0) // PATCH
    same = group == lax.broadcasted_iota(jnp.int32, (LANES, LANES), 1) // PATCH
    ones = jnp.where(same, 1.0, 0.0).astype(bf16)

    def square(at):
        re, im = f_ref[at : at + 8, :LANES], f_ref[at : at + 8, LANES:]
        return re * re + im * im

    sums = []
    for z in sections:
        end = z * level.rows + level.tiles * level.body
        tails = [square(end + at) for at in range(0, 2 * level.half, 8)]
        for tile in range(level.tiles):
            for b in range(level.blocks):
                base = z * level.rows + tile * level.body + b * HALF
                total = jnp.where(dc, 0.0, square(base))
                head = jnp.where(sub == 0, total, 0.0)
                for r in range(8, HALF, 8):
                    total = total + square(base + r)
                row = level.nyquist_row(tile, b)
                sums.append(2.0 * total - head + jnp.where(sub == row % 8, tails[row // 8], 0.0))
    high, low = split(jnp.concatenate(sums, axis=0))
    return dot(jnp.concatenate([high, low], axis=1), jnp.concatenate([ones, ones], axis=0))


def scale_spectrum(level, f_ref, sections, sums, spec_ref):
    sub = lax.broadcasted_iota(jnp.int32, (8, 2 * LANES), 0)
    lane = lax.broadcasted_iota(jnp.int32, (8, 2 * LANES), 1)
    dc = (sub == 0) & (lane % PATCH == 0)
    number = 0
    for z in sections:
        start = z * level.rows
        end = start + level.tiles * level.body
        tails = [f_ref[end + at : end + at + 8] for at in range(0, 2 * level.half, 8)]
        scaled = [jnp.zeros_like(tail) for tail in tails]
        for tile in range(level.tiles):
            for b in range(level.blocks):
                scale = lax.rsqrt(all_rows(sums[number : number + 8]) * (1.0 / PATCH**4) + 1e-05)
                number += 8
                scale = jnp.concatenate([scale, scale], axis=1)
                for r in range(0, HALF, 16):
                    at = start + tile * level.body + b * HALF + r
                    head = f_ref[at : at + 8]
                    if r == 0:
                        head = jnp.where(dc, 0.0, head)
                    both = jnp.concatenate([head * scale, f_ref[at + 8 : at + 16] * scale], axis=0)
                    spec_ref[at : at + 16] = both.astype(bf16)
                row = level.nyquist_row(tile, b)
                scaled[row // 8] = jnp.where(sub == row % 8, tails[row // 8] * scale, scaled[row // 8])
        spec_ref[end : end + 2 * level.half] = jnp.concatenate(scaled, axis=0).astype(bf16)


def transform_rows(levels, sections, strips, row_ref, scratch):
    t_ref, high_ref, low_ref = scratch[:3]
    odd_refs = scratch[3 : 3 + 2 * len(levels)]
    places, size = row_places(levels)
    for z in sections:
        x = jnp.concatenate([strip[0] for strip in strips[z]], axis=0)
        width = x.shape[1]
        x = jnp.concatenate([x, x], axis=0)
        for first in range(0, width, 2 * LANES):
            columns = slice(first, first + 2 * LANES)
            t = dot(row_ref[...], x[:, columns])
            for level, (cos_at, nyquist_at, sin_at) in zip(levels, places):
                for start in (cos_at, sin_at):
                    for ref, half in zip((high_ref, low_ref), split(t[start : start + level.body])):
                        ref[z, start : start + level.body, columns] = half
                rows = slice(nyquist_at, nyquist_at + 2 * level.half)
                t_ref[z, rows, columns] = t[rows]
        t_ref[z, :, width:] = jnp.zeros((size, LANES), f32)
        for ref in (high_ref, low_ref):
            ref[z, :, width:] = jnp.zeros((size, LANES), bf16)
    for index, (level, place) in enumerate(zip(levels, places)):
        odds = odd_refs[2 * index : 2 * index + 2]
        for z in sections:
            gather_nyquist(level, place, t_ref.at[z], [ref.at[z] for ref in odds])


def transform_columns(levels, sections, table_ref, scratch, spec_refs):
    high_ref, low_ref = scratch[1:3]
    odd_refs, f_refs = scratch[3 : 3 + 2 * len(levels)], scratch[3 + 2 * len(levels) :]
    places, size = row_places(levels)
    for index, (level, place) in enumerate(zip(levels, places)):
        lefts = [
            jnp.concatenate([left_of(level, place, ref.at[z], odd.at[z]) for z in sections], axis=0)
            for ref, odd in zip((high_ref, low_ref), odd_refs[2 * index : 2 * index + 2])]
        rows = slice(sections[0] * level.rows, (sections[-1] + 1) * level.rows)
        f_refs[index][rows] = dot3(*lefts, table_ref, level.table)
        sums = spectrum_power(level, f_refs[index], sections)
        scale_spectrum(level, f_refs[index], sections, sums, spec_refs[index])


def write_maps(levels, pairs, own_specs, specs, kept, table_ref, shift_at, map_at, scratch, outs, finished=()):
    count = len(levels)
    cross_refs, y_refs, maps_refs, rows_refs, stacks = (scratch[i * count : (i + 1) * count] for i in range(5))
    for level, own, spec, cross_ref, y_ref in zip(levels, own_specs, specs, cross_refs, y_refs):
        def cross(at, rows):
            a = own[at : at + rows].astype(f32)
            ar, ai = a[:, :LANES], a[:, LANES:]
            for d in range(pairs):
                b = spec[d * level.rows + at : d * level.rows + at + rows].astype(f32)
                br, bi = b[:, :LANES], b[:, LANES:]
                yield d * level.cross_rows, jnp.concatenate([ar * br + ai * bi, ar * bi - ai * br], axis=1)

        for tile in range(level.tiles):
            quad, odd = divmod(tile, 2)
            for r in range(0, level.body, 16):
                for to, value in cross(tile * level.body + r, 16):
                    to += quad * level.body + r
                    cross_ref[to : to + 16, 2 * odd * LANES : 2 * (odd + 1) * LANES] = value.astype(bf16)
        for to, value in cross(level.tiles * level.body, 2 * level.half):
            value = jnp.concatenate([value[: level.half], value[level.half :]], axis=1)
            spare = level.cross_rows - level.cross_body - level.half
            if spare:
                value = jnp.concatenate([value, jnp.zeros((spare, 4 * LANES), f32)], axis=0)
            cross_ref[to + level.cross_body : to + level.cross_rows] = value.astype(bf16)
        rows = pairs * level.cross_rows
        y_ref[:rows] = dot(cross_ref[:rows], table_ref[shift_at : shift_at + 4 * LANES])
    row = lax.broadcasted_iota(jnp.int32, (NYQ, LANES), 0)
    for level, y_ref, stack_ref, maps_ref in zip(levels, y_refs, stacks, maps_refs):
        for b in range(level.blocks):
            for d in range(pairs):
                first = d * level.cross_rows
                nyq_at = first + level.cross_body
                nyquist = y_ref[nyq_at : nyq_at + NYQ, :LANES]
                for quad in range(level.quads):
                    top = first + quad * level.body + b * HALF
                    column = (d * level.quads + quad) * LANES
                    for at, value in (
                        (0, y_ref[top : top + HALF, :LANES]),
                        (HALF, y_ref[top : top + HALF, LANES:]),
                        (2 * HALF, jnp.where(row == quad * level.blocks + b, nyquist, 0.0)),
                    ):
                        for half, part in enumerate(split(value)):
                            to = half * (2 * HALF + NYQ) + at
                            stack_ref[to : to + value.shape[0], column : column + LANES] = part
            columns = pairs * level.quads * LANES
            both = dot(table_ref[map_at : map_at + 2 * WINDOW, : stack_ref.shape[0]], stack_ref[:, :columns])
            maps = both[:WINDOW] + both[WINDOW:]
            for tile in range(pairs * level.quads):
                maps_ref[b * pairs * level.quads + tile] = maps[:, tile * LANES : (tile + 1) * LANES]

    def exchange(low, high, width):
        even = (lax.broadcasted_iota(jnp.int32, low.shape, 1) & width) == 0
        return (
            jnp.where(even, low, pltpu.roll(high, width, 1)),
            jnp.where(even, pltpu.roll(low, LANES - width, 1), high))

    for index, (level, maps_ref, rows_ref, out) in enumerate(zip(levels, maps_refs, rows_refs, outs)):
        tiles = level.blocks * pairs * level.quads
        for big in range(WINDOW // 4):
            rows = [maps_ref[:tiles, 4 * big + r, :] for r in range(4)]
            for step in (2, 1):
                for r in range(4):
                    if not r & step:
                        rows[r], rows[r + step] = exchange(rows[r], rows[r + step], step * WINDOW)
            for g in range(4):
                rows_ref[big, pl.ds(g, tiles, stride=4), :] = rows[g]
            for b in range(level.blocks):
                column = kept[index][: 4 * level.quads, level.first + b : level.first + b + 1]
                for d in range(pairs):
                    at = 4 * (b * pairs + d) * level.quads
                    out[d, b, :, big * LANES : (big + 1) * LANES] = rows_ref[big, at : at + 4 * level.quads] * column
        if finished:
            finished[index]()


def write_mask_columns(mask_ref, pad_ref, kept_ref):
    pad_ref[...] = jnp.zeros(pad_ref.shape, f32)
    pad_ref[: mask_ref.shape[1], : mask_ref.shape[2]] = mask_ref[0].astype(f32)
    kept_ref[...] = jnp.transpose(pad_ref[...])


def sections_ahead():
    return lax.axis_size("sec") - 1 - lax.axis_index("sec")


def for_pairs(run):
    ahead = sections_ahead()
    pl.when(ahead >= 2)(lambda: run(2))
    pl.when(ahead == 1)(lambda: run(1))
    pl.when(ahead < 1)(lambda: run(0))


def clear_maps(pairs, outs):
    for out in outs:
        if pairs < 2:
            out[pairs:] = jnp.zeros((2 - pairs,) + out.shape[1:], f32)


def section_scratch(levels, width, count):
    size = row_places(levels)[1]
    return [
        pltpu.VMEM((count, size, width + LANES), f32),
        pltpu.VMEM((count, size, width + LANES), bf16),
        pltpu.VMEM((count, size, width + LANES), bf16),
        *(pltpu.VMEM((count, 2 * level.half, 2 * level.pool * LANES), bf16)
          for level in levels for _ in range(2)),
        *(pltpu.VMEM((count * level.rows, 2 * LANES), f32) for level in levels),
    ]


def spec_scratch(levels, count):
    return [pltpu.VMEM((count * level.rows, 2 * LANES), bf16) for level in levels]


def pair_scratch(levels):
    def each(shape, dtype):
        return [pltpu.VMEM(shape(level), dtype) for level in levels]

    return [
        *each(lambda level: (2 * level.cross_rows, 4 * LANES), bf16),
        *each(lambda level: (2 * level.cross_rows, 2 * LANES), f32),
        *each(lambda level: (2 * level.blocks * level.quads, WINDOW, LANES), f32),
        *each(lambda level: (WINDOW // 4, 8 * level.blocks * level.quads, LANES), f32),
        *each(lambda level: (4 * HALF + 2 * NYQ, 2 * level.quads * LANES), bf16),
    ]


def copier(sems):
    used = []

    def start(source, target):
        copy = pltpu.make_async_copy(source, target, sems.at[len(used)])
        used.append(copy)
        copy.start()
        return copy.wait

    return start


def inner_kernel(
    levels, cuts,
    own_hbm, near, far, mask_hbm, mask_coarse_hbm, table_hbm,
    maps, own, table_ref, kept, kept_coarse,
    mask, mask_coarse, pad, pad_coarse, row_ref, *rest,
):
    *scratch, sems = rest
    start = copier(sems)

    def table(first, last):
        piece = pl.ds(first, last - first)
        return start(table_hbm.at[piece], table_ref.at[piece])

    fine_at, shift_at, map_at, coarse_at, end = cuts
    own_ready = start(own_hbm, own)
    copies = [table(shift_at, coarse_at), start(mask_hbm, mask), start(mask_coarse_hbm, mask_coarse)]
    outer_ready = table(coarse_at, end)
    size = 3 + 3 * len(levels)
    sections, spec_refs, rest = scratch[:size], scratch[size : size + 1], scratch[size + 1 :]
    strips = ((own,), (near,), (far,))
    rows = levels[0].rows

    def run(pairs):
        if pairs:
            write_row_table(row_ref, levels[0])
            write_fine_table(table_ref, fine_at)
            transform_rows(levels, range(1, pairs + 1), strips, row_ref, sections)
        own_ready()
        if pairs:
            transform_rows(levels, (0,), strips, row_ref, sections)
            transform_columns(levels, range(pairs + 1), table_ref, sections, spec_refs)
        for wait in copies:
            wait()
        if pairs:
            write_mask_columns(mask, pad, kept)
            write_mask_columns(mask_coarse, pad_coarse, kept_coarse)
            write_maps(
                levels, pairs, [spec_refs[0].at[pl.ds(0, rows)]], [spec_refs[0].at[pl.ds(rows, pairs * rows)]],
                (kept,), table_ref, shift_at, map_at, rest, (maps,))
        clear_maps(pairs, (maps,))
        outer_ready()

    for_pairs(run)


def own_kernel(levels, row_at, own, rim, table_ref, *rest):
    spec_refs, sections = rest[: len(levels)], rest[len(levels) :]
    row_ref = table_ref.at[pl.ds(row_at, row_places(levels)[1])]

    @pl.when(sections_ahead() >= 1)
    def _():
        transform_rows(levels, (0,), ((own, rim),), row_ref, sections)
        transform_columns(levels, (0,), table_ref, sections, spec_refs)


def outer_kernel(
    levels, cuts, inner, row_at,
    near, far, rim_near, rim_far, table_ref, own_fine, own_coarse, kept, kept_coarse, inner_maps,
    out_fine, out_coarse,
    maps, maps_coarse, *rest,
):
    *scratch, sems = rest
    inner_stored = copier(sems)(inner_maps, out_fine.at[0, :, pl.ds(0, inner)])
    fine_at, shift_at, map_at, coarse_at, end = cuts
    row_ref = table_ref.at[pl.ds(row_at, row_places(levels)[1])]
    size, count = 3 + 3 * len(levels), len(levels)
    sections, spec_refs, rest = scratch[:size], scratch[size : size + count], scratch[size + count :]
    strips = ((near, rim_near), (far, rim_far))

    def run(pairs):
        stores = [
            pltpu.make_async_copy(maps, out_fine.at[0, :, pl.ds(inner, levels[0].blocks)], sems.at[1]),
            pltpu.make_async_copy(maps_coarse, out_coarse.at[0], sems.at[2])]
        clear_maps(pairs, (maps, maps_coarse))
        if pairs:
            transform_rows(levels, range(pairs), strips, row_ref, sections)
            transform_columns(levels, range(pairs), table_ref, sections, spec_refs)
            write_maps(
                levels, pairs, (own_fine, own_coarse), spec_refs, (kept, kept_coarse), table_ref, shift_at, map_at,
                rest, (maps, maps_coarse), [store.start for store in stores])
        else:
            for store in stores:
                store.start()
        for store in stores:
            store.wait()

    for_pairs(run)
    inner_stored()


def correlate(own, near, far, rim, rim_near, rim_far, mask_fine, mask_coarse):
    strip_rows, width = own.shape[1:]
    fine, coarse = mask_fine.shape[1], mask_coarse.shape[1]
    inner = fine - 1
    shift, map_ = shift_tables()
    tables = [fine_table(), shift, map_, coarse_table()]
    cuts = [int(at) for at in np.cumsum([0] + [table.shape[0] for table in tables])]
    inner_levels = [Level(1, range(inner), width, cuts[0])]
    outer_levels = [Level(1, range(inner, fine), width, cuts[0]), Level(2, range(coarse), width, cuts[3])]
    row_at = cuts[4]
    tables.append(row_table(outer_levels, strip_rows + PATCH))
    columns = max(table.shape[1] for table in tables)
    table = np.concatenate([np.pad(table, ((0, 0), (0, columns - table.shape[1]))) for table in tables])
    cuts[4] = table.shape[0]

    shifts = WINDOW * WINDOW
    hbm = pl.BlockSpec(memory_space=pltpu.HBM)
    vmem = pl.BlockSpec(memory_space=pltpu.VMEM)
    params = pltpu.CompilerParams(vmem_limit_bytes=28 * 1024 * 1024)
    own, table, mask_fine, mask_coarse = (
        pltpu.with_memory_space_constraint(value, pltpu.HBM)
        for value in (own, jnp.asarray(table), mask_fine, mask_coarse))

    def cost(flops):
        return pl.CostEstimate(flops=flops, bytes_accessed=4 * 10**6, transcendentals=0)

    maps, own_kept, handed, *kept = pl.pallas_call(
        functools.partial(inner_kernel, inner_levels, cuts),
        out_shape=(
            jax.ShapeDtypeStruct((2, inner, 4 * inner_levels[0].quads, shifts), f32),
            jax.ShapeDtypeStruct(own.shape, bf16),
            jax.ShapeDtypeStruct(table.shape, bf16),
            *(jax.ShapeDtypeStruct((LANES, 8), f32) for _ in range(2)),
        ),
        in_specs=[hbm, vmem, vmem, hbm, hbm, hbm],
        out_specs=(vmem,) * 5,
        scratch_shapes=[
            pltpu.VMEM(mask_fine.shape, jnp.int32),
            pltpu.VMEM(mask_coarse.shape, jnp.int32),
            pltpu.VMEM((8, LANES), f32),
            pltpu.VMEM((8, LANES), f32),
            pltpu.VMEM((row_places(inner_levels)[1], 2 * strip_rows), bf16),
            *section_scratch(inner_levels, width, 3),
            *spec_scratch(inner_levels, 3),
            *pair_scratch(inner_levels),
            pltpu.SemaphoreType.DMA((5,)),
        ],
        compiler_params=params,
        cost_estimate=cost(3 * 10**9),
        name="inner_blocks",
    )(own, near, far, mask_fine, mask_coarse, table)
    own_specs = pl.pallas_call(
        functools.partial(own_kernel, outer_levels, row_at),
        out_shape=tuple(jax.ShapeDtypeStruct((level.rows, 2 * LANES), bf16) for level in outer_levels),
        in_specs=[vmem] * 3,
        out_specs=(vmem,) * 2,
        scratch_shapes=section_scratch(outer_levels, width, 1),
        compiler_params=params,
        cost_estimate=cost(2 * 10**9),
        name="own_outer_blocks",
    )(own_kept, rim, handed)
    return pl.pallas_call(
        functools.partial(outer_kernel, outer_levels, cuts, inner, row_at),
        out_shape=(
            jax.ShapeDtypeStruct((1, 2, fine, 4 * outer_levels[0].quads, shifts), f32),
            jax.ShapeDtypeStruct((1, 2, coarse, 4 * outer_levels[1].quads, shifts), f32),
        ),
        in_specs=[vmem] * 10,
        out_specs=(hbm, hbm),
        scratch_shapes=[
            *(pltpu.VMEM((2, level.blocks, 4 * level.quads, shifts), f32) for level in outer_levels),
            *section_scratch(outer_levels, width, 2),
            *spec_scratch(outer_levels, 2),
            *pair_scratch(outer_levels),
            pltpu.SemaphoreType.DMA((3,)),
        ],
        compiler_params=params,
        cost_estimate=cost(4 * 10**9),
        name="outer_blocks",
    )(near, far, rim_near, rim_far, handed, *own_specs, *kept, maps)


def local(sections, mask_fine, mask_coarse):
    far = from_device(sections, 2, 0)
    near = from_device(sections, 1, 0)
    rims = [from_device(sections, z, 1) for z in range(3)]
    return correlate(sections, near, far, *rims, mask_fine, mask_coarse)


def solution(mesh):
    in_specs = (
        P("sec", "strip", "groups"),
        P("sec", "strip", "groups"),
        P("sec", "strip", "groups"),
    )
    out_specs = (P("sec", None, "strip", "groups", None), P("sec", None, "strip", "groups", None))
    return jax.shard_map(local, mesh=mesh, in_specs=in_specs, out_specs=out_specs, check_vma=False)
```

```python
import functools

import jax
import jax.numpy as jnp
import numpy as np
from jax import lax
from jax.experimental import pallas as pl
from jax.experimental.pallas import tpu as pltpu
from jax.sharding import PartitionSpec as P

PATCH = 64
STRIDE = 32
WINDOW = 32
HALF = PATCH // 2
LANES = 128
NYQ = 16

f32 = jnp.float32
bf16 = jnp.bfloat16


def from_device(value, sec_steps, strip_steps):
    secs, strips = lax.axis_size("sec"), lax.axis_size("strip")
    pairs = []
    for sec in range(secs - sec_steps):
        for strip in range(strips - strip_steps):
            pairs.append(((sec + sec_steps) * strips + strip + strip_steps, sec * strips + strip))
    return lax.ppermute(value, ("sec", "strip"), pairs)


def wave(phase):
    turns = np.arange(PATCH) * (2 * np.pi / PATCH)
    cos = np.round(np.cos(turns), 14)
    sin = np.round(np.sin(turns), 14)
    phase = np.mod(phase, PATCH)
    return cos[phase], sin[phase]


def split_table(table):
    high = table.astype(jnp.bfloat16)
    low = (table - high.astype(np.float64)).astype(jnp.bfloat16)
    return high, low


def stacked(table):
    return np.concatenate(split_table(table), axis=0)


def fine_table():
    c, s = wave(np.arange(PATCH)[:, None] * np.arange(PATCH)[None, :])
    table = np.zeros((2, 2, PATCH, 2, 2, PATCH))
    for p in range(2):
        table[0, p, :, 0, p] = c
        table[1, p, :, 0, p] = -s
        table[0, p, :, 1, p] = -s
        table[1, p, :, 1, p] = -c
    return stacked(table.reshape(4 * PATCH, 4 * PATCH))


def coarse_table():
    c, s = wave((np.arange(2 * PATCH) // 2)[:, None] * np.arange(PATCH)[None, :])
    table = np.zeros((2, 2, 2 * PATCH, 2, 2, PATCH))
    for p in range(2):
        table[p, 0, :, 0, p] = 0.5 * c
        table[p, 1, :, 0, p] = -0.5 * s
        table[p, 0, :, 1, p] = -0.5 * s
        table[p, 1, :, 1, p] = -0.5 * c
    return stacked(table.reshape(8 * PATCH, 4 * PATCH))


def shift_tables():
    spread = 1.869545
    t = np.arange(WINDOW) - WINDOW // 2
    c, s = wave(np.arange(PATCH)[:, None] * t[None, :])
    table = np.zeros((2, 2, 2, PATCH, 2, 4, WINDOW))
    for odd in range(2):
        for p in range(2):
            table[odd, 0, p, :, 0, 2 * p + odd] = c
            table[odd, 1, p, :, 0, 2 * p + odd] = -s
            table[odd, 0, p, :, 1, 2 * p + odd] = s
            table[odd, 1, p, :, 1, 2 * p + odd] = c
    along_t = (spread * table.reshape(8 * PATCH, 8 * WINDOW)).astype(jnp.bfloat16)
    c, s = wave(t[:, None] * np.arange(HALF)[None, :])
    weight = np.where(np.arange(HALF) == 0, 1.0, 2.0)
    nyquist = np.repeat(wave(HALF * t)[0][:, None], NYQ, axis=1)
    along_s = np.concatenate([c * weight, -s * weight, nyquist], axis=1) / (spread * PATCH**3)
    high, low = split_table(along_s)
    along_s = np.concatenate(
        [np.concatenate([high, high], axis=1), np.concatenate([low, np.zeros_like(low)], axis=1)], axis=0)
    return along_t, along_s


class Level:
    def __init__(self, pool, blocks, width, table):
        self.pool, self.first, self.blocks, self.table = pool, blocks[0], len(blocks), table
        self.quads = width // (4 * pool * STRIDE)
        self.tiles = 2 * self.quads
        self.body = self.blocks * HALF
        self.half = -(-self.quads * self.blocks // 8) * 8
        self.rows = self.tiles * self.body + 2 * self.half
        self.cross_body = self.quads * self.body
        self.cross_rows = self.cross_body + -(-self.half // 16) * 16

    def window(self, tile, p):
        quad, odd = divmod(tile, 2)
        return self.pool * LANES * quad + LANES * p + self.pool * STRIDE * odd

    def nyquist_row(self, tile, b):
        quad, odd = divmod(tile, 2)
        return odd * self.half + quad * self.blocks + b


def row_places(levels):
    at, places = 0, []
    for level in levels:
        places.append([at, at + level.body])
        at += level.body + 2 * level.half
    for level, place in zip(levels, places):
        place.append(at)
        at += level.body
    return places, at


def row_table(levels, ext):
    places, size = row_places(levels)
    table = np.zeros((size, ext))
    k = np.arange(HALF)[:, None]
    for level, (cos_at, nyquist_at, sin_at) in zip(levels, places):
        pool = level.pool
        x = np.arange(pool * PATCH) // pool
        c, s = wave(k * x[None, :])
        for b in range(level.blocks):
            first = (level.first + b) * pool * STRIDE
            columns = slice(first, first + x.size)
            table[cos_at + b * HALF : cos_at + (b + 1) * HALF, columns] = c / pool
            table[sin_at + b * HALF : sin_at + (b + 1) * HALF, columns] = s / pool
            for tile in range(level.tiles):
                table[nyquist_at + level.nyquist_row(tile, b), columns] = wave(HALF * x)[0] / pool
    return np.concatenate(split_table(table), axis=1)


def split(value):
    high = value.astype(bf16)
    return high, (value - high.astype(f32)).astype(bf16)


def dot(left, right):
    return jnp.dot(left, right, preferred_element_type=f32)


def dot3(high, low, table_ref, at):
    depth = high.shape[1]
    table_high = table_ref[at : at + depth]
    table_low = table_ref[at + depth : at + 2 * depth]
    return dot(
        jnp.concatenate([high, low, high], axis=1),
        jnp.concatenate([table_high, table_high, table_low], axis=0))


def cosine(turns):
    turns = turns + PATCH // 4
    part = (turns & (HALF - 1)) - PATCH // 4
    angle = part.astype(f32) * (2 * np.pi / PATCH)
    square = angle * angle
    value = jnp.full(square.shape, 1.0 / 479001600, f32)
    for term in (-1.0 / 3628800, 1.0 / 40320, -1.0 / 720, 1.0 / 24, -0.5, 1.0):
        value = value * square + term
    return jnp.where((turns & HALF) == 0, value, -value)


def write_row_table(row_ref, level):
    (cos_at, nyquist_at, sin_at), = row_places([level])[0]
    ext = row_ref.shape[1] // 2

    def put(at, value):
        high, low = split(value)
        row_ref[at : at + value.shape[0], :ext] = high
        row_ref[at : at + value.shape[0], ext:] = low

    def inside(x):
        return jnp.where((x >= 0) & (x < PATCH), 1.0, 0.0)

    k = lax.broadcasted_iota(jnp.int32, (HALF, ext), 0)
    for b in range(level.blocks):
        x = lax.broadcasted_iota(jnp.int32, (HALF, ext), 1) - (level.first + b) * STRIDE
        put(cos_at + b * HALF, cosine(k * x) * inside(x))
        put(sin_at + b * HALF, cosine(k * x - PATCH // 4) * inside(x))
    row = lax.broadcasted_iota(jnp.int32, (2 * level.half, ext), 0)
    x = lax.broadcasted_iota(jnp.int32, (2 * level.half, ext), 1)
    x = x - (level.first + lax.rem(lax.rem(row, level.half), level.blocks)) * STRIDE
    put(nyquist_at, cosine(x * HALF) * inside(x))


def write_fine_table(table_ref, at):
    y = lax.broadcasted_iota(jnp.int32, (PATCH, LANES), 0)
    lane = lax.broadcasted_iota(jnp.int32, (PATCH, LANES), 1)
    frequency = lane & (PATCH - 1)
    c, s = cosine(y * frequency), cosine(y * frequency - PATCH // 4)
    depth = 4 * PATCH
    for p in range(2):
        mine = (lane >= PATCH) if p else (lane < PATCH)
        cos, minus_cos, minus_sin = (jnp.where(mine, value, 0.0) for value in (c, -c, -s))
        for number, pair in enumerate(((cos, minus_sin), (minus_sin, minus_cos))):
            to = at + (2 * number + p) * PATCH
            for half, value in enumerate(pair):
                for level, part in enumerate(split(value)):
                    table_ref[to + level * depth : to + level * depth + PATCH, half * LANES : (half + 1) * LANES] = part


def all_rows(value):
    value = value.reshape(value.shape[0] // 8, 8, value.shape[1])
    for step in (4, 2, 1):
        value = value + pltpu.roll(value, step, 1)
    return value


def left_of(level, place, half_ref, odd_ref):
    cos_at, nyquist_at, sin_at = place
    pieces = []
    for tile in range(level.tiles):
        if tile % 2:
            pieces.append(odd_ref[tile // 2 * level.body : (tile // 2 + 1) * level.body])
        else:
            columns = []
            for p in range(level.pool):
                at = level.window(tile, p)
                columns += [half_ref[start : start + level.body, at : at + LANES] for start in (cos_at, sin_at)]
            pieces.append(jnp.concatenate(columns, axis=1))
    pieces.append(odd_ref[level.quads * level.body :])
    return jnp.concatenate(pieces, axis=0)


def gather_windows(level, place, t_ref, halves, odds):
    cos_at, nyquist_at, sin_at = place
    body, end = level.body, level.quads * level.body
    row = lax.broadcasted_iota(jnp.int32, (2 * level.half, LANES), 0)
    for p in range(level.pool):
        for source, target in zip(halves, odds):
            for tile in range(1, level.tiles, 2):
                at = level.window(tile, p)
                for half, start in enumerate((cos_at, sin_at)):
                    to = tile // 2 * body
                    target[to : to + body, (2 * p + half) * LANES : (2 * p + half + 1) * LANES] = (
                        source[start : start + body, at : at + LANES])
        nyquist = jnp.zeros((2 * level.half, LANES), f32)
        for tile in range(level.tiles):
            at, first = level.window(tile, p), level.nyquist_row(tile, 0)
            value = t_ref[nyquist_at : nyquist_at + 2 * level.half, at : at + LANES]
            nyquist = jnp.where((row >= first) & (row < first + level.blocks), value, nyquist)
        for target, part in zip(odds, split(nyquist)):
            target[end:, 2 * p * LANES : (2 * p + 1) * LANES] = part
            target[end:, (2 * p + 1) * LANES : (2 * p + 2) * LANES] = jnp.zeros(part.shape, bf16)


def spectrum_power(level, f_ref, sections):
    sub = lax.broadcasted_iota(jnp.int32, (8, LANES), 0)
    lane = lax.broadcasted_iota(jnp.int32, (8, LANES), 1)
    dc = (sub == 0) & (lane % PATCH == 0)
    group = lax.broadcasted_iota(jnp.int32, (LANES, LANES), 0) // PATCH
    same = group == lax.broadcasted_iota(jnp.int32, (LANES, LANES), 1) // PATCH
    ones = jnp.where(same, 1.0, 0.0).astype(bf16)

    def square(at):
        re, im = f_ref[at : at + 8, :LANES], f_ref[at : at + 8, LANES:]
        return re * re + im * im

    sums = []
    for z in sections:
        end = z * level.rows + level.tiles * level.body
        tails = [square(end + at) for at in range(0, 2 * level.half, 8)]
        for tile in range(level.tiles):
            for b in range(level.blocks):
                base = z * level.rows + tile * level.body + b * HALF
                total = jnp.where(dc, 0.0, square(base))
                head = jnp.where(sub == 0, total, 0.0)
                for r in range(8, HALF, 8):
                    total = total + square(base + r)
                row = level.nyquist_row(tile, b)
                sums.append(2.0 * total - head + jnp.where(sub == row % 8, tails[row // 8], 0.0))
    high, low = split(jnp.concatenate(sums, axis=0))
    return dot(jnp.concatenate([high, low], axis=1), jnp.concatenate([ones, ones], axis=0))


def scale_spectrum(level, f_ref, sections, sums, spec_ref):
    scales = lax.rsqrt(all_rows(sums) * (1.0 / PATCH**4) + 1e-05)
    sub = lax.broadcasted_iota(jnp.int32, (8, 2 * LANES), 0)
    lane = lax.broadcasted_iota(jnp.int32, (8, 2 * LANES), 1)
    dc = (sub == 0) & (lane % PATCH == 0)
    number = 0
    for z in sections:
        start = z * level.rows
        end = start + level.tiles * level.body
        tails = [f_ref[end + at : end + at + 8] for at in range(0, 2 * level.half, 8)]
        scaled = [jnp.zeros_like(tail) for tail in tails]
        for tile in range(level.tiles):
            for b in range(level.blocks):
                scale = jnp.concatenate([scales[number], scales[number]], axis=1)
                number += 1
                for r in range(0, HALF, 16):
                    at = start + tile * level.body + b * HALF + r
                    head = f_ref[at : at + 8]
                    if r == 0:
                        head = jnp.where(dc, 0.0, head)
                    both = jnp.concatenate([head * scale, f_ref[at + 8 : at + 16] * scale], axis=0)
                    spec_ref[at : at + 16] = both.astype(bf16)
                row = level.nyquist_row(tile, b)
                scaled[row // 8] = jnp.where(sub == row % 8, tails[row // 8] * scale, scaled[row // 8])
        spec_ref[end : end + 2 * level.half] = jnp.concatenate(scaled, axis=0).astype(bf16)


def transform_rows(levels, sections, strips, row_ref, scratch):
    t_ref, high_ref, low_ref = scratch[:3]
    odd_refs = scratch[3 : 3 + 2 * len(levels)]
    places, size = row_places(levels)

    def keep(z, columns, t):
        for level, (cos_at, nyquist_at, sin_at) in zip(levels, places):
            for start in (cos_at, sin_at):
                for ref, half in zip((high_ref, low_ref), split(t[start : start + level.body])):
                    ref[z, start : start + level.body, columns] = half
            rows = slice(nyquist_at, nyquist_at + 2 * level.half)
            t_ref[z, rows, columns] = t[rows]

    waiting = None
    for z in sections:
        x = jnp.concatenate([strip[0] for strip in strips[z]], axis=0)
        width = x.shape[1]
        x = jnp.concatenate([x, x], axis=0)
        for first in range(0, width, 2 * LANES):
            columns = slice(first, first + 2 * LANES)
            t = dot(row_ref[...], x[:, columns])
            if waiting is not None:
                keep(*waiting)
            waiting = (z, columns, t)
        t_ref[z, :, width:] = jnp.zeros((size, LANES), f32)
        for ref in (high_ref, low_ref):
            ref[z, :, width:] = jnp.zeros((size, LANES), bf16)
    keep(*waiting)
    for index, (level, place) in enumerate(zip(levels, places)):
        odds = odd_refs[2 * index : 2 * index + 2]
        for z in sections:
            gather_windows(level, place, t_ref.at[z], (high_ref.at[z], low_ref.at[z]), [ref.at[z] for ref in odds])


def transform_columns(levels, sections, table_ref, scratch, spec_refs):
    high_ref, low_ref = scratch[1:3]
    odd_refs, f_refs = scratch[3 : 3 + 2 * len(levels)], scratch[3 + 2 * len(levels) :]
    places, size = row_places(levels)
    for index, (level, place) in enumerate(zip(levels, places)):
        lefts = [
            jnp.concatenate([left_of(level, place, ref.at[z], odd.at[z]) for z in sections], axis=0)
            for ref, odd in zip((high_ref, low_ref), odd_refs[2 * index : 2 * index + 2])]
        rows = slice(sections[0] * level.rows, (sections[-1] + 1) * level.rows)
        f_refs[index][rows] = dot3(*lefts, table_ref, level.table)
    sums = [spectrum_power(level, f_ref, sections) for level, f_ref in zip(levels, f_refs)]
    for level, f_ref, total, spec_ref in zip(levels, f_refs, sums, spec_refs):
        scale_spectrum(level, f_ref, sections, total, spec_ref)


def write_maps(levels, pairs, own_specs, specs, kept, table_ref, shift_at, map_at, scratch, outs, finished=()):
    count = len(levels)
    cross_refs, y_refs, maps_refs, rows_refs, stacks = (scratch[i * count : (i + 1) * count] for i in range(5))
    for level, own, spec, cross_ref, y_ref in zip(levels, own_specs, specs, cross_refs, y_refs):
        def cross(at, rows):
            a = own[at : at + rows].astype(f32)
            ar, ai = a[:, :LANES], a[:, LANES:]
            for d in range(pairs):
                b = spec[d * level.rows + at : d * level.rows + at + rows].astype(f32)
                br, bi = b[:, :LANES], b[:, LANES:]
                yield d * level.cross_rows, jnp.concatenate([ar * br + ai * bi, ar * bi - ai * br], axis=1)

        for tile in range(level.tiles):
            quad, odd = divmod(tile, 2)
            for r in range(0, level.body, 16):
                for to, value in cross(tile * level.body + r, 16):
                    to += quad * level.body + r
                    cross_ref[to : to + 16, 2 * odd * LANES : 2 * (odd + 1) * LANES] = value.astype(bf16)
        for to, value in cross(level.tiles * level.body, 2 * level.half):
            value = jnp.concatenate([value[: level.half], value[level.half :]], axis=1)
            spare = level.cross_rows - level.cross_body - level.half
            if spare:
                value = jnp.concatenate([value, jnp.zeros((spare, 4 * LANES), f32)], axis=0)
            cross_ref[to + level.cross_body : to + level.cross_rows] = value.astype(bf16)
        rows = pairs * level.cross_rows
        y_ref[:rows] = dot(cross_ref[:rows], table_ref[shift_at : shift_at + 4 * LANES])
    row = lax.broadcasted_iota(jnp.int32, (NYQ, LANES), 0)
    for level, y_ref, stack_ref, maps_ref in zip(levels, y_refs, stacks, maps_refs):
        for b in range(level.blocks):
            for d in range(pairs):
                first = d * level.cross_rows
                nyq_at = first + level.cross_body
                nyquist = y_ref[nyq_at : nyq_at + NYQ, :LANES]
                for quad in range(level.quads):
                    top = first + quad * level.body + b * HALF
                    column = (d * level.quads + quad) * LANES
                    for at, value in (
                        (0, y_ref[top : top + HALF, :LANES]),
                        (HALF, y_ref[top : top + HALF, LANES:]),
                        (2 * HALF, jnp.where(row == quad * level.blocks + b, nyquist, 0.0)),
                    ):
                        for half, part in enumerate(split(value)):
                            to = half * (2 * HALF + NYQ) + at
                            stack_ref[to : to + value.shape[0], column : column + LANES] = part
            columns = pairs * level.quads * LANES
            both = dot(table_ref[map_at : map_at + 2 * WINDOW, : stack_ref.shape[0]], stack_ref[:, :columns])
            maps = both[:WINDOW] + both[WINDOW:]
            for tile in range(pairs * level.quads):
                maps_ref[b * pairs * level.quads + tile] = maps[:, tile * LANES : (tile + 1) * LANES]

    def exchange(low, high, width):
        even = (lax.broadcasted_iota(jnp.int32, low.shape, 1) & width) == 0
        return (
            jnp.where(even, low, pltpu.roll(high, width, 1)),
            jnp.where(even, pltpu.roll(low, LANES - width, 1), high))

    bigs = range(WINDOW // 4)
    for index, (level, maps_ref, rows_ref, out) in enumerate(zip(levels, maps_refs, rows_refs, outs)):
        tiles = level.blocks * pairs * level.quads
        rows = [[maps_ref[:tiles, 4 * big + r, :] for r in range(4)] for big in bigs]
        for step in (2, 1):
            for r in range(4):
                if not r & step:
                    for big in bigs:
                        rows[big][r], rows[big][r + step] = exchange(
                            rows[big][r], rows[big][r + step], step * WINDOW)
        for big in bigs:
            for g in range(4):
                rows_ref[big, pl.ds(g, tiles, stride=4), :] = rows[big][g]
        for b in range(level.blocks):
            column = kept[index][: 4 * level.quads, level.first + b : level.first + b + 1]
            column = jnp.broadcast_to(column, (4 * level.quads, LANES))
            for d in range(pairs):
                at = 4 * (b * pairs + d) * level.quads
                for big in bigs:
                    out[d, b, :, big * LANES : (big + 1) * LANES] = rows_ref[big, at : at + 4 * level.quads] * column
        if finished:
            finished[index]()


def write_mask_columns(mask_ref, pad_ref, kept_ref):
    pad_ref[...] = jnp.zeros(pad_ref.shape, f32)
    pad_ref[: mask_ref.shape[1], : mask_ref.shape[2]] = mask_ref[0].astype(f32)
    kept_ref[...] = jnp.transpose(pad_ref[...])


def sections_ahead():
    return lax.axis_size("sec") - 1 - lax.axis_index("sec")


def for_pairs(run):
    ahead = sections_ahead()
    pl.when(ahead >= 2)(lambda: run(2))
    pl.when(ahead == 1)(lambda: run(1))
    pl.when(ahead < 1)(lambda: run(0))


def clear_maps(pairs, outs):
    for out in outs:
        if pairs < 2:
            out[pairs:] = jnp.zeros((2 - pairs,) + out.shape[1:], f32)


def section_scratch(levels, width, count):
    size = row_places(levels)[1]
    return [
        pltpu.VMEM((count, size, width + LANES), f32),
        pltpu.VMEM((count, size, width + LANES), bf16),
        pltpu.VMEM((count, size, width + LANES), bf16),
        *(pltpu.VMEM((count, level.quads * level.body + 2 * level.half, 2 * level.pool * LANES), bf16)
          for level in levels for _ in range(2)),
        *(pltpu.VMEM((count * level.rows, 2 * LANES), f32) for level in levels),
    ]


def spec_scratch(levels, count):
    return [pltpu.VMEM((count * level.rows, 2 * LANES), bf16) for level in levels]


def pair_scratch(levels):
    def each(shape, dtype):
        return [pltpu.VMEM(shape(level), dtype) for level in levels]

    return [
        *each(lambda level: (2 * level.cross_rows, 4 * LANES), bf16),
        *each(lambda level: (2 * level.cross_rows, 2 * LANES), f32),
        *each(lambda level: (2 * level.blocks * level.quads, WINDOW, LANES), f32),
        *each(lambda level: (WINDOW // 4, 8 * level.blocks * level.quads, LANES), f32),
        *each(lambda level: (4 * HALF + 2 * NYQ, 2 * level.quads * LANES), bf16),
    ]


def copier(sems):
    used = []

    def start(source, target):
        copy = pltpu.make_async_copy(source, target, sems.at[len(used)])
        used.append(copy)
        copy.start()
        return copy.wait

    return start


def inner_kernel(
    levels, cuts,
    own_hbm, near, far, mask_hbm, mask_coarse_hbm, table_hbm,
    maps, own, table_ref, kept, kept_coarse,
    mask, mask_coarse, pad, pad_coarse, row_ref, *rest,
):
    *scratch, sems = rest
    start = copier(sems)

    def table(first, last):
        piece = pl.ds(first, last - first)
        return start(table_hbm.at[piece], table_ref.at[piece])

    fine_at, shift_at, map_at, coarse_at, end = cuts
    own_ready = start(own_hbm, own)
    copies = [table(shift_at, coarse_at), start(mask_hbm, mask), start(mask_coarse_hbm, mask_coarse)]
    outer_ready = table(coarse_at, end)
    size = 3 + 3 * len(levels)
    sections, spec_refs, rest = scratch[:size], scratch[size : size + 1], scratch[size + 1 :]
    strips = ((own,), (near,), (far,))
    rows = levels[0].rows

    def run(pairs):
        if pairs:
            write_row_table(row_ref, levels[0])
            write_fine_table(table_ref, fine_at)
            transform_rows(levels, range(1, pairs + 1), strips, row_ref, sections)
        own_ready()
        if pairs:
            transform_rows(levels, (0,), strips, row_ref, sections)
            transform_columns(levels, range(pairs + 1), table_ref, sections, spec_refs)
        for wait in copies:
            wait()
        if pairs:
            write_mask_columns(mask, pad, kept)
            write_mask_columns(mask_coarse, pad_coarse, kept_coarse)
            write_maps(
                levels, pairs, [spec_refs[0].at[pl.ds(0, rows)]], [spec_refs[0].at[pl.ds(rows, pairs * rows)]],
                (kept,), table_ref, shift_at, map_at, rest, (maps,))
        clear_maps(pairs, (maps,))
        outer_ready()

    for_pairs(run)


def own_kernel(levels, row_at, own, rim, table_ref, *rest):
    spec_refs, sections = rest[: len(levels)], rest[len(levels) :]
    row_ref = table_ref.at[pl.ds(row_at, row_places(levels)[1])]

    @pl.when(sections_ahead() >= 1)
    def _():
        transform_rows(levels, (0,), ((own, rim),), row_ref, sections)
        transform_columns(levels, (0,), table_ref, sections, spec_refs)


def outer_kernel(
    levels, cuts, inner, row_at,
    near, far, rim_near, rim_far, table_ref, own_fine, own_coarse, kept, kept_coarse, inner_maps,
    out_fine, out_coarse,
    maps, maps_coarse, *rest,
):
    *scratch, sems = rest
    inner_stored = copier(sems)(inner_maps, out_fine.at[0, :, pl.ds(0, inner)])
    fine_at, shift_at, map_at, coarse_at, end = cuts
    row_ref = table_ref.at[pl.ds(row_at, row_places(levels)[1])]
    size, count = 3 + 3 * len(levels), len(levels)
    sections, spec_refs, rest = scratch[:size], scratch[size : size + count], scratch[size + count :]
    strips = ((near, rim_near), (far, rim_far))

    def run(pairs):
        stores = [
            pltpu.make_async_copy(maps, out_fine.at[0, :, pl.ds(inner, levels[0].blocks)], sems.at[1]),
            pltpu.make_async_copy(maps_coarse, out_coarse.at[0], sems.at[2])]
        clear_maps(pairs, (maps, maps_coarse))
        if pairs:
            transform_rows(levels, range(pairs), strips, row_ref, sections)
            transform_columns(levels, range(pairs), table_ref, sections, spec_refs)
            write_maps(
                levels, pairs, (own_fine, own_coarse), spec_refs, (kept, kept_coarse), table_ref, shift_at, map_at,
                rest, (maps, maps_coarse), [store.start for store in stores])
        else:
            for store in stores:
                store.start()
        for store in stores:
            store.wait()

    for_pairs(run)
    inner_stored()


def correlate(own, near, far, rim, rim_near, rim_far, mask_fine, mask_coarse):
    strip_rows, width = own.shape[1:]
    fine, coarse = mask_fine.shape[1], mask_coarse.shape[1]
    inner = fine - 1
    shift, map_ = shift_tables()
    tables = [fine_table(), shift, map_, coarse_table()]
    cuts = [int(at) for at in np.cumsum([0] + [table.shape[0] for table in tables])]
    inner_levels = [Level(1, range(inner), width, cuts[0])]
    outer_levels = [Level(1, range(inner, fine), width, cuts[0]), Level(2, range(coarse), width, cuts[3])]
    row_at = cuts[4]
    tables.append(row_table(outer_levels, strip_rows + PATCH))
    columns = max(table.shape[1] for table in tables)
    table = np.concatenate([np.pad(table, ((0, 0), (0, columns - table.shape[1]))) for table in tables])
    cuts[4] = table.shape[0]

    shifts = WINDOW * WINDOW
    hbm = pl.BlockSpec(memory_space=pltpu.HBM)
    vmem = pl.BlockSpec(memory_space=pltpu.VMEM)
    params = pltpu.CompilerParams(vmem_limit_bytes=28 * 1024 * 1024)
    own, table, mask_fine, mask_coarse = (
        pltpu.with_memory_space_constraint(value, pltpu.HBM)
        for value in (own, jnp.asarray(table), mask_fine, mask_coarse))

    def cost(flops):
        return pl.CostEstimate(flops=flops, bytes_accessed=4 * 10**6, transcendentals=0)

    maps, own_kept, handed, *kept = pl.pallas_call(
        functools.partial(inner_kernel, inner_levels, cuts),
        out_shape=(
            jax.ShapeDtypeStruct((2, inner, 4 * inner_levels[0].quads, shifts), f32),
            jax.ShapeDtypeStruct(own.shape, bf16),
            jax.ShapeDtypeStruct(table.shape, bf16),
            *(jax.ShapeDtypeStruct((LANES, 8), f32) for _ in range(2)),
        ),
        in_specs=[hbm, vmem, vmem, hbm, hbm, hbm],
        out_specs=(vmem,) * 5,
        scratch_shapes=[
            pltpu.VMEM(mask_fine.shape, jnp.int32),
            pltpu.VMEM(mask_coarse.shape, jnp.int32),
            pltpu.VMEM((8, LANES), f32),
            pltpu.VMEM((8, LANES), f32),
            pltpu.VMEM((row_places(inner_levels)[1], 2 * strip_rows), bf16),
            *section_scratch(inner_levels, width, 3),
            *spec_scratch(inner_levels, 3),
            *pair_scratch(inner_levels),
            pltpu.SemaphoreType.DMA((5,)),
        ],
        compiler_params=params,
        cost_estimate=cost(3 * 10**9),
        name="inner_blocks",
    )(own, near, far, mask_fine, mask_coarse, table)
    own_specs = pl.pallas_call(
        functools.partial(own_kernel, outer_levels, row_at),
        out_shape=tuple(jax.ShapeDtypeStruct((level.rows, 2 * LANES), bf16) for level in outer_levels),
        in_specs=[vmem] * 3,
        out_specs=(vmem,) * 2,
        scratch_shapes=section_scratch(outer_levels, width, 1),
        compiler_params=params,
        cost_estimate=cost(2 * 10**9),
        name="own_outer_blocks",
    )(own_kept, rim, handed)
    return pl.pallas_call(
        functools.partial(outer_kernel, outer_levels, cuts, inner, row_at),
        out_shape=(
            jax.ShapeDtypeStruct((1, 2, fine, 4 * outer_levels[0].quads, shifts), f32),
            jax.ShapeDtypeStruct((1, 2, coarse, 4 * outer_levels[1].quads, shifts), f32),
        ),
        in_specs=[vmem] * 10,
        out_specs=(hbm, hbm),
        scratch_shapes=[
            *(pltpu.VMEM((2, level.blocks, 4 * level.quads, shifts), f32) for level in outer_levels),
            *section_scratch(outer_levels, width, 2),
            *spec_scratch(outer_levels, 2),
            *pair_scratch(outer_levels),
            pltpu.SemaphoreType.DMA((3,)),
        ],
        compiler_params=params,
        cost_estimate=cost(4 * 10**9),
        name="outer_blocks",
    )(near, far, rim_near, rim_far, handed, *own_specs, *kept, maps)


def local(sections, mask_fine, mask_coarse):
    far = from_device(sections, 2, 0)
    near = from_device(sections, 1, 0)
    rims = [from_device(sections, z, 1) for z in range(3)]
    return correlate(sections, near, far, *rims, mask_fine, mask_coarse)


def solution(mesh):
    in_specs = (
        P("sec", "strip", "groups"),
        P("sec", "strip", "groups"),
        P("sec", "strip", "groups"),
    )
    out_specs = (P("sec", None, "strip", "groups", None), P("sec", None, "strip", "groups", None))
    return jax.shard_map(local, mesh=mesh, in_specs=in_specs, out_specs=out_specs, check_vma=False)
```

```python
import functools

import jax
import jax.numpy as jnp
import numpy as np
from jax import lax
from jax.experimental import pallas as pl
from jax.experimental.pallas import tpu as pltpu
from jax.sharding import PartitionSpec as P

PATCH = 64
STRIDE = 32
WINDOW = 32
HALF = PATCH // 2
LANES = 128
NYQ = 16

f32 = jnp.float32
bf16 = jnp.bfloat16


def from_device(value, sec_steps, strip_steps):
    secs, strips = lax.axis_size("sec"), lax.axis_size("strip")
    pairs = []
    for sec in range(secs - sec_steps):
        for strip in range(strips - strip_steps):
            pairs.append(((sec + sec_steps) * strips + strip + strip_steps, sec * strips + strip))
    return lax.ppermute(value, ("sec", "strip"), pairs)


def wave(phase):
    turns = np.arange(PATCH) * (2 * np.pi / PATCH)
    cos = np.round(np.cos(turns), 14)
    sin = np.round(np.sin(turns), 14)
    phase = np.mod(phase, PATCH)
    return cos[phase], sin[phase]


def split_table(table):
    high = table.astype(jnp.bfloat16)
    low = (table - high.astype(np.float64)).astype(jnp.bfloat16)
    return high, low


def stacked(table):
    return np.concatenate(split_table(table), axis=0)


def fine_table():
    c, s = wave(np.arange(PATCH)[:, None] * np.arange(PATCH)[None, :])
    table = np.zeros((2, 2, PATCH, 2, 2, PATCH))
    for p in range(2):
        table[0, p, :, 0, p] = c
        table[1, p, :, 0, p] = -s
        table[0, p, :, 1, p] = -s
        table[1, p, :, 1, p] = -c
    return stacked(table.reshape(4 * PATCH, 4 * PATCH))


def coarse_table():
    c, s = wave((np.arange(2 * PATCH) // 2)[:, None] * np.arange(PATCH)[None, :])
    re = np.concatenate([0.5 * c, -0.5 * s], axis=0)
    im = np.concatenate([-0.5 * s, -0.5 * c], axis=0)
    rows = []
    for pair in ((re, im), (im, re)):
        high, low = split_table(np.concatenate(pair, axis=1))
        rows += [np.concatenate([high, low], axis=1), np.concatenate([high, np.zeros_like(low)], axis=1)]
    return np.concatenate(rows, axis=0)


def shift_tables():
    spread = 1.869545
    t = np.arange(WINDOW) - WINDOW // 2
    c, s = wave(np.arange(PATCH)[:, None] * t[None, :])
    table = np.zeros((2, 2, 2, PATCH, 2, 4, WINDOW))
    for odd in range(2):
        for p in range(2):
            table[odd, 0, p, :, 0, 2 * p + odd] = c
            table[odd, 1, p, :, 0, 2 * p + odd] = -s
            table[odd, 0, p, :, 1, 2 * p + odd] = s
            table[odd, 1, p, :, 1, 2 * p + odd] = c
    along_t = (spread * table.reshape(8 * PATCH, 8 * WINDOW)).astype(jnp.bfloat16)
    c, s = wave(t[:, None] * np.arange(HALF)[None, :])
    weight = np.where(np.arange(HALF) == 0, 1.0, 2.0)
    nyquist = np.repeat(wave(HALF * t)[0][:, None], NYQ, axis=1)
    along_s = np.concatenate([c * weight, -s * weight, nyquist], axis=1) / (spread * PATCH**3)
    high, low = split_table(along_s)
    along_s = np.concatenate(
        [np.concatenate([high, high], axis=1), np.concatenate([low, np.zeros_like(low)], axis=1)], axis=0)
    return along_t, along_s


class Level:
    def __init__(self, pool, blocks, width, table):
        self.pool, self.first, self.blocks, self.table = pool, blocks[0], len(blocks), table
        self.quads = width // (4 * pool * STRIDE)
        self.tiles = 2 * self.quads
        self.body = self.blocks * HALF
        self.half = -(-self.quads * self.blocks // 8) * 8
        self.rows = self.tiles * self.body + 2 * self.half
        self.cross_body = self.quads * self.body
        self.cross_rows = self.cross_body + -(-self.half // 16) * 16

    def window(self, tile, p):
        quad, odd = divmod(tile, 2)
        return self.pool * LANES * quad + LANES * p + self.pool * STRIDE * odd

    def nyquist_row(self, tile, b):
        quad, odd = divmod(tile, 2)
        return odd * self.half + quad * self.blocks + b


def row_places(levels):
    at, places = 0, []
    for level in levels:
        places.append([at, at + level.body])
        at += level.body + 2 * level.half
    for level, place in zip(levels, places):
        place.append(at)
        at += level.body
    return places, at


def row_table(levels, ext):
    places, size = row_places(levels)
    table = np.zeros((size, ext))
    k = np.arange(HALF)[:, None]
    for level, (cos_at, nyquist_at, sin_at) in zip(levels, places):
        pool = level.pool
        x = np.arange(pool * PATCH) // pool
        c, s = wave(k * x[None, :])
        for b in range(level.blocks):
            first = (level.first + b) * pool * STRIDE
            columns = slice(first, first + x.size)
            table[cos_at + b * HALF : cos_at + (b + 1) * HALF, columns] = c / pool
            table[sin_at + b * HALF : sin_at + (b + 1) * HALF, columns] = s / pool
            for tile in range(level.tiles):
                table[nyquist_at + level.nyquist_row(tile, b), columns] = wave(HALF * x)[0] / pool
    return np.concatenate(split_table(table), axis=1)


def split(value):
    high = value.astype(bf16)
    return high, (value - high.astype(f32)).astype(bf16)


def dot(left, right):
    return jnp.dot(left, right, preferred_element_type=f32)


def dot3(high, low, table_ref, at):
    depth = high.shape[1]
    table_high = table_ref[at : at + depth]
    table_low = table_ref[at + depth : at + 2 * depth]
    return dot(
        jnp.concatenate([high, low, high], axis=1),
        jnp.concatenate([table_high, table_high, table_low], axis=0))


def cosine(turns):
    turns = turns + PATCH // 4
    part = (turns & (HALF - 1)) - PATCH // 4
    angle = part.astype(f32) * (2 * np.pi / PATCH)
    square = angle * angle
    value = jnp.full(square.shape, 1.0 / 479001600, f32)
    for term in (-1.0 / 3628800, 1.0 / 40320, -1.0 / 720, 1.0 / 24, -0.5, 1.0):
        value = value * square + term
    return jnp.where((turns & HALF) == 0, value, -value)


def write_row_table(row_ref, level):
    (cos_at, nyquist_at, sin_at), = row_places([level])[0]
    ext = row_ref.shape[1] // 2

    def put(at, value):
        high, low = split(value)
        row_ref[at : at + value.shape[0], :ext] = high
        row_ref[at : at + value.shape[0], ext:] = low

    def inside(x):
        return jnp.where((x >= 0) & (x < PATCH), 1.0, 0.0)

    k = lax.broadcasted_iota(jnp.int32, (HALF, ext), 0)
    for b in range(level.blocks):
        x = lax.broadcasted_iota(jnp.int32, (HALF, ext), 1) - (level.first + b) * STRIDE
        put(cos_at + b * HALF, cosine(k * x) * inside(x))
        put(sin_at + b * HALF, cosine(k * x - PATCH // 4) * inside(x))
    row = lax.broadcasted_iota(jnp.int32, (2 * level.half, ext), 0)
    x = lax.broadcasted_iota(jnp.int32, (2 * level.half, ext), 1)
    x = x - (level.first + lax.rem(lax.rem(row, level.half), level.blocks)) * STRIDE
    put(nyquist_at, cosine(x * HALF) * inside(x))


def write_fine_table(table_ref, at):
    y = lax.broadcasted_iota(jnp.int32, (PATCH, LANES), 0)
    lane = lax.broadcasted_iota(jnp.int32, (PATCH, LANES), 1)
    frequency = lane & (PATCH - 1)
    c, s = cosine(y * frequency), cosine(y * frequency - PATCH // 4)
    depth = 4 * PATCH
    for p in range(2):
        mine = (lane >= PATCH) if p else (lane < PATCH)
        cos, minus_cos, minus_sin = (jnp.where(mine, value, 0.0) for value in (c, -c, -s))
        for number, pair in enumerate(((cos, minus_sin), (minus_sin, minus_cos))):
            to = at + (2 * number + p) * PATCH
            for half, value in enumerate(pair):
                for level, part in enumerate(split(value)):
                    table_ref[to + level * depth : to + level * depth + PATCH, half * LANES : (half + 1) * LANES] = part


def all_rows(value):
    for step in (4, 2, 1):
        value = value + pltpu.roll(value, step, 0)
    return value


def left_of(level, place, half_ref, odd_ref):
    cos_at, nyquist_at, sin_at = place
    pieces = []
    for tile in range(level.tiles):
        if tile % 2:
            pieces.append(odd_ref[tile // 2 * level.body : (tile // 2 + 1) * level.body])
        else:
            columns = []
            for p in range(level.pool):
                at = level.window(tile, p)
                columns += [half_ref[start : start + level.body, at : at + LANES] for start in (cos_at, sin_at)]
            pieces.append(jnp.concatenate(columns, axis=1))
    pieces.append(odd_ref[level.quads * level.body :])
    return jnp.concatenate(pieces, axis=0)


def gather_windows(level, place, t_ref, halves, odds):
    cos_at, nyquist_at, sin_at = place
    body, end = level.body, level.quads * level.body
    row = lax.broadcasted_iota(jnp.int32, (2 * level.half, LANES), 0)
    for p in range(level.pool):
        for source, target in zip(halves, odds):
            for tile in range(1, level.tiles, 2):
                at = level.window(tile, p)
                for half, start in enumerate((cos_at, sin_at)):
                    to = tile // 2 * body
                    target[to : to + body, (2 * p + half) * LANES : (2 * p + half + 1) * LANES] = (
                        source[start : start + body, at : at + LANES])
        nyquist = jnp.zeros((2 * level.half, LANES), f32)
        for tile in range(level.tiles):
            at, first = level.window(tile, p), level.nyquist_row(tile, 0)
            value = t_ref[nyquist_at : nyquist_at + 2 * level.half, at : at + LANES]
            nyquist = jnp.where((row >= first) & (row < first + level.blocks), value, nyquist)
        for target, part in zip(odds, split(nyquist)):
            target[end:, 2 * p * LANES : (2 * p + 1) * LANES] = part
            target[end:, (2 * p + 1) * LANES : (2 * p + 2) * LANES] = jnp.zeros(part.shape, bf16)


def spectrum_power(level, f_ref, sections):
    sub = lax.broadcasted_iota(jnp.int32, (8, LANES), 0)
    lane = lax.broadcasted_iota(jnp.int32, (8, LANES), 1)
    dc = (sub == 0) & (lane % PATCH == 0)
    group = lax.broadcasted_iota(jnp.int32, (LANES, LANES), 0) // PATCH
    same = group == lax.broadcasted_iota(jnp.int32, (LANES, LANES), 1) // PATCH
    ones = jnp.where(same, 1.0, 0.0).astype(bf16)

    def square(at):
        re, im = f_ref[at : at + 8, :LANES], f_ref[at : at + 8, LANES:]
        return re * re + im * im

    sums = []
    for z in sections:
        end = z * level.rows + level.tiles * level.body
        tails = [square(end + at) for at in range(0, 2 * level.half, 8)]
        for tile in range(level.tiles):
            for b in range(level.blocks):
                base = z * level.rows + tile * level.body + b * HALF
                total = jnp.where(dc, 0.0, square(base))
                head = jnp.where(sub == 0, total, 0.0)
                for r in range(8, HALF, 8):
                    total = total + square(base + r)
                row = level.nyquist_row(tile, b)
                sums.append(2.0 * total - head + jnp.where(sub == row % 8, tails[row // 8], 0.0))
    high, low = split(jnp.concatenate(sums, axis=0))
    return dot(jnp.concatenate([high, low], axis=1), jnp.concatenate([ones, ones], axis=0))


def scale_spectrum(level, f_ref, sections, sums, spec_ref):
    sub = lax.broadcasted_iota(jnp.int32, (8, 2 * LANES), 0)
    lane = lax.broadcasted_iota(jnp.int32, (8, 2 * LANES), 1)
    dc = (sub == 0) & (lane % PATCH == 0)
    number = 0
    for z in sections:
        start = z * level.rows
        end = start + level.tiles * level.body
        tails = [f_ref[end + at : end + at + 8] for at in range(0, 2 * level.half, 8)]
        scaled = [jnp.zeros_like(tail) for tail in tails]
        for tile in range(level.tiles):
            for b in range(level.blocks):
                scale = lax.rsqrt(all_rows(sums[number : number + 8]) * (1.0 / PATCH**4) + 1e-05)
                number += 8
                scale = jnp.concatenate([scale, scale], axis=1)
                for r in range(0, HALF, 16):
                    at = start + tile * level.body + b * HALF + r
                    head = f_ref[at : at + 8]
                    if r == 0:
                        head = jnp.where(dc, 0.0, head)
                    both = jnp.concatenate([head * scale, f_ref[at + 8 : at + 16] * scale], axis=0)
                    spec_ref[at : at + 16] = both.astype(bf16)
                row = level.nyquist_row(tile, b)
                scaled[row // 8] = jnp.where(sub == row % 8, tails[row // 8] * scale, scaled[row // 8])
        spec_ref[end : end + 2 * level.half] = jnp.concatenate(scaled, axis=0).astype(bf16)


def transform_rows(levels, sections, strips, row_ref, scratch):
    t_ref, high_ref, low_ref = scratch[:3]
    odd_refs = scratch[3 : 3 + 2 * len(levels)]
    places, size = row_places(levels)
    for z in sections:
        x = jnp.concatenate([strip[0] for strip in strips[z]], axis=0)
        width = x.shape[1]
        x = jnp.concatenate([x, x], axis=0)
        for first in range(0, width, 2 * LANES):
            columns = slice(first, first + 2 * LANES)
            t = dot(row_ref[...], x[:, columns])
            for level, (cos_at, nyquist_at, sin_at) in zip(levels, places):
                for start in (cos_at, sin_at):
                    for ref, half in zip((high_ref, low_ref), split(t[start : start + level.body])):
                        ref[z, start : start + level.body, columns] = half
                rows = slice(nyquist_at, nyquist_at + 2 * level.half)
                t_ref[z, rows, columns] = t[rows]
        t_ref[z, :, width:] = jnp.zeros((size, LANES), f32)
        for ref in (high_ref, low_ref):
            ref[z, :, width:] = jnp.zeros((size, LANES), bf16)
    for index, (level, place) in enumerate(zip(levels, places)):
        odds = odd_refs[2 * index : 2 * index + 2]
        for z in sections:
            gather_windows(level, place, t_ref.at[z], (high_ref.at[z], low_ref.at[z]), [ref.at[z] for ref in odds])


def coarse_columns(high, low, table_ref, at):
    depth = 2 * LANES
    parts = []
    for p in range(2):
        columns = slice(p * depth, (p + 1) * depth)
        value = dot(
            jnp.concatenate([high[:, columns], low[:, columns]], axis=1),
            table_ref[at + 2 * p * depth : at + 2 * (p + 1) * depth])
        parts.append(value[:, :LANES] + value[:, LANES:])
    first = lax.broadcasted_iota(jnp.int32, parts[0].shape, 1) < PATCH
    re = jnp.where(first, parts[0], parts[1])
    im = pltpu.roll(jnp.where(first, parts[1], parts[0]), PATCH, 1)
    return jnp.concatenate([re, im], axis=1)


def transform_columns(levels, sections, table_ref, scratch, spec_refs):
    high_ref, low_ref = scratch[1:3]
    odd_refs, f_refs = scratch[3 : 3 + 2 * len(levels)], scratch[3 + 2 * len(levels) :]
    places, size = row_places(levels)
    for index, (level, place) in enumerate(zip(levels, places)):
        lefts = [
            jnp.concatenate([left_of(level, place, ref.at[z], odd.at[z]) for z in sections], axis=0)
            for ref, odd in zip((high_ref, low_ref), odd_refs[2 * index : 2 * index + 2])]
        rows = slice(sections[0] * level.rows, (sections[-1] + 1) * level.rows)
        if level.pool == 1:
            f_refs[index][rows] = dot3(*lefts, table_ref, level.table)
        else:
            f_refs[index][rows] = coarse_columns(*lefts, table_ref, level.table)
    for level, f_ref, spec_ref in zip(levels, f_refs, spec_refs):
        scale_spectrum(level, f_ref, sections, spectrum_power(level, f_ref, sections), spec_ref)


def write_maps(levels, pairs, own_specs, specs, kept, table_ref, shift_at, map_at, scratch, outs, finished=()):
    count = len(levels)
    cross_refs, y_refs, maps_refs, rows_refs, stacks = (scratch[i * count : (i + 1) * count] for i in range(5))
    for level, own, spec, cross_ref, y_ref in zip(levels, own_specs, specs, cross_refs, y_refs):
        def cross(at, rows):
            a = own[at : at + rows].astype(f32)
            ar, ai = a[:, :LANES], a[:, LANES:]
            for d in range(pairs):
                b = spec[d * level.rows + at : d * level.rows + at + rows].astype(f32)
                br, bi = b[:, :LANES], b[:, LANES:]
                yield d * level.cross_rows, jnp.concatenate([ar * br + ai * bi, ar * bi - ai * br], axis=1)

        for tile in range(level.tiles):
            quad, odd = divmod(tile, 2)
            for r in range(0, level.body, 16):
                for to, value in cross(tile * level.body + r, 16):
                    to += quad * level.body + r
                    cross_ref[to : to + 16, 2 * odd * LANES : 2 * (odd + 1) * LANES] = value.astype(bf16)
        for to, value in cross(level.tiles * level.body, 2 * level.half):
            value = jnp.concatenate([value[: level.half], value[level.half :]], axis=1)
            spare = level.cross_rows - level.cross_body - level.half
            if spare:
                value = jnp.concatenate([value, jnp.zeros((spare, 4 * LANES), f32)], axis=0)
            cross_ref[to + level.cross_body : to + level.cross_rows] = value.astype(bf16)
        rows = pairs * level.cross_rows
        y_ref[:rows] = dot(cross_ref[:rows], table_ref[shift_at : shift_at + 4 * LANES])
    row = lax.broadcasted_iota(jnp.int32, (NYQ, LANES), 0)
    for level, y_ref, stack_ref, maps_ref in zip(levels, y_refs, stacks, maps_refs):
        for b in range(level.blocks):
            for d in range(pairs):
                first = d * level.cross_rows
                nyq_at = first + level.cross_body
                nyquist = y_ref[nyq_at : nyq_at + NYQ, :LANES]
                for quad in range(level.quads):
                    top = first + quad * level.body + b * HALF
                    column = (d * level.quads + quad) * LANES
                    for at, value in (
                        (0, y_ref[top : top + HALF, :LANES]),
                        (HALF, y_ref[top : top + HALF, LANES:]),
                        (2 * HALF, jnp.where(row == quad * level.blocks + b, nyquist, 0.0)),
                    ):
                        for half, part in enumerate(split(value)):
                            to = half * (2 * HALF + NYQ) + at
                            stack_ref[to : to + value.shape[0], column : column + LANES] = part
            columns = pairs * level.quads * LANES
            both = dot(table_ref[map_at : map_at + 2 * WINDOW, : stack_ref.shape[0]], stack_ref[:, :columns])
            maps = both[:WINDOW] + both[WINDOW:]
            for tile in range(pairs * level.quads):
                maps_ref[b * pairs * level.quads + tile] = maps[:, tile * LANES : (tile + 1) * LANES]

    def exchange(low, high, width):
        even = (lax.broadcasted_iota(jnp.int32, low.shape, 1) & width) == 0
        return (
            jnp.where(even, low, pltpu.roll(high, width, 1)),
            jnp.where(even, pltpu.roll(low, LANES - width, 1), high))

    for index, (level, maps_ref, rows_ref, out) in enumerate(zip(levels, maps_refs, rows_refs, outs)):
        tiles = level.blocks * pairs * level.quads
        for big in range(WINDOW // 4):
            rows = [maps_ref[:tiles, 4 * big + r, :] for r in range(4)]
            for step in (2, 1):
                for r in range(4):
                    if not r & step:
                        rows[r], rows[r + step] = exchange(rows[r], rows[r + step], step * WINDOW)
            for g in range(4):
                rows_ref[big, pl.ds(g, tiles, stride=4), :] = rows[g]
            for b in range(level.blocks):
                column = kept[index][: 4 * level.quads, level.first + b : level.first + b + 1]
                for d in range(pairs):
                    at = 4 * (b * pairs + d) * level.quads
                    out[d, b, :, big * LANES : (big + 1) * LANES] = rows_ref[big, at : at + 4 * level.quads] * column
        if finished:
            finished[index]()


def write_mask_columns(mask_ref, pad_ref, kept_ref):
    pad_ref[...] = jnp.zeros(pad_ref.shape, f32)
    pad_ref[: mask_ref.shape[1], : mask_ref.shape[2]] = mask_ref[0].astype(f32)
    kept_ref[...] = jnp.transpose(pad_ref[...])


def sections_ahead():
    return lax.axis_size("sec") - 1 - lax.axis_index("sec")


def for_pairs(run):
    ahead = sections_ahead()
    pl.when(ahead >= 2)(lambda: run(2))
    pl.when(ahead == 1)(lambda: run(1))
    pl.when(ahead < 1)(lambda: run(0))


def clear_maps(pairs, outs):
    for out in outs:
        if pairs < 2:
            out[pairs:] = jnp.zeros((2 - pairs,) + out.shape[1:], f32)


def section_scratch(levels, width, count):
    size = row_places(levels)[1]
    return [
        pltpu.VMEM((count, size, width + LANES), f32),
        pltpu.VMEM((count, size, width + LANES), bf16),
        pltpu.VMEM((count, size, width + LANES), bf16),
        *(pltpu.VMEM((count, level.quads * level.body + 2 * level.half, 2 * level.pool * LANES), bf16)
          for level in levels for _ in range(2)),
        *(pltpu.VMEM((count * level.rows, 2 * LANES), f32) for level in levels),
    ]


def spec_scratch(levels, count):
    return [pltpu.VMEM((count * level.rows, 2 * LANES), bf16) for level in levels]


def pair_scratch(levels):
    def each(shape, dtype):
        return [pltpu.VMEM(shape(level), dtype) for level in levels]

    return [
        *each(lambda level: (2 * level.cross_rows, 4 * LANES), bf16),
        *each(lambda level: (2 * level.cross_rows, 2 * LANES), f32),
        *each(lambda level: (2 * level.blocks * level.quads, WINDOW, LANES), f32),
        *each(lambda level: (WINDOW // 4, 8 * level.blocks * level.quads, LANES), f32),
        *each(lambda level: (4 * HALF + 2 * NYQ, 2 * level.quads * LANES), bf16),
    ]


def copier(sems):
    used = []

    def start(source, target):
        copy = pltpu.make_async_copy(source, target, sems.at[len(used)])
        used.append(copy)
        copy.start()
        return copy.wait

    return start


def inner_kernel(
    levels, cuts,
    own_hbm, near, far, mask_hbm, mask_coarse_hbm, table_hbm,
    maps, own, table_ref, kept, kept_coarse,
    mask, mask_coarse, pad, pad_coarse, row_ref, *rest,
):
    *scratch, sems = rest
    start = copier(sems)

    def table(first, last):
        piece = pl.ds(first, last - first)
        return start(table_hbm.at[piece], table_ref.at[piece])

    fine_at, shift_at, map_at, coarse_at, end = cuts
    own_ready = start(own_hbm, own)
    copies = [table(shift_at, coarse_at), start(mask_hbm, mask), start(mask_coarse_hbm, mask_coarse)]
    outer_ready = table(coarse_at, end)
    size = 3 + 3 * len(levels)
    sections, spec_refs, rest = scratch[:size], scratch[size : size + 1], scratch[size + 1 :]
    strips = ((own,), (near,), (far,))
    rows = levels[0].rows

    def run(pairs):
        if pairs:
            write_row_table(row_ref, levels[0])
            write_fine_table(table_ref, fine_at)
            transform_rows(levels, range(1, pairs + 1), strips, row_ref, sections)
        own_ready()
        if pairs:
            transform_rows(levels, (0,), strips, row_ref, sections)
            transform_columns(levels, range(pairs + 1), table_ref, sections, spec_refs)
        for wait in copies:
            wait()
        if pairs:
            write_mask_columns(mask, pad, kept)
            write_mask_columns(mask_coarse, pad_coarse, kept_coarse)
            write_maps(
                levels, pairs, [spec_refs[0].at[pl.ds(0, rows)]], [spec_refs[0].at[pl.ds(rows, pairs * rows)]],
                (kept,), table_ref, shift_at, map_at, rest, (maps,))
        clear_maps(pairs, (maps,))
        outer_ready()

    for_pairs(run)


def own_kernel(levels, row_at, own, rim, table_ref, *rest):
    spec_refs, sections = rest[: len(levels)], rest[len(levels) :]
    row_ref = table_ref.at[pl.ds(row_at, row_places(levels)[1])]

    @pl.when(sections_ahead() >= 1)
    def _():
        transform_rows(levels, (0,), ((own, rim),), row_ref, sections)
        transform_columns(levels, (0,), table_ref, sections, spec_refs)


def outer_kernel(
    levels, cuts, inner, row_at,
    near, far, rim_near, rim_far, table_ref, own_fine, own_coarse, kept, kept_coarse, inner_maps,
    out_fine, out_coarse,
    maps, maps_coarse, *rest,
):
    *scratch, sems = rest
    inner_stored = copier(sems)(inner_maps, out_fine.at[0, :, pl.ds(0, inner)])
    fine_at, shift_at, map_at, coarse_at, end = cuts
    row_ref = table_ref.at[pl.ds(row_at, row_places(levels)[1])]
    size, count = 3 + 3 * len(levels), len(levels)
    sections, spec_refs, rest = scratch[:size], scratch[size : size + count], scratch[size + count :]
    strips = ((near, rim_near), (far, rim_far))

    def run(pairs):
        stores = [
            pltpu.make_async_copy(maps, out_fine.at[0, :, pl.ds(inner, levels[0].blocks)], sems.at[1]),
            pltpu.make_async_copy(maps_coarse, out_coarse.at[0], sems.at[2])]
        clear_maps(pairs, (maps, maps_coarse))
        if pairs:
            transform_rows(levels, range(pairs), strips, row_ref, sections)
            transform_columns(levels, range(pairs), table_ref, sections, spec_refs)
            write_maps(
                levels, pairs, (own_fine, own_coarse), spec_refs, (kept, kept_coarse), table_ref, shift_at, map_at,
                rest, (maps, maps_coarse), [store.start for store in stores])
        else:
            for store in stores:
                store.start()
        for store in stores:
            store.wait()

    for_pairs(run)
    inner_stored()


def correlate(own, near, far, rim, rim_near, rim_far, mask_fine, mask_coarse):
    strip_rows, width = own.shape[1:]
    fine, coarse = mask_fine.shape[1], mask_coarse.shape[1]
    inner = fine - 1
    shift, map_ = shift_tables()
    tables = [fine_table(), shift, map_, coarse_table()]
    cuts = [int(at) for at in np.cumsum([0] + [table.shape[0] for table in tables])]
    inner_levels = [Level(1, range(inner), width, cuts[0])]
    outer_levels = [Level(1, range(inner, fine), width, cuts[0]), Level(2, range(coarse), width, cuts[3])]
    row_at = cuts[4]
    tables.append(row_table(outer_levels, strip_rows + PATCH))
    columns = max(table.shape[1] for table in tables)
    table = np.concatenate([np.pad(table, ((0, 0), (0, columns - table.shape[1]))) for table in tables])
    cuts[4] = table.shape[0]

    shifts = WINDOW * WINDOW
    hbm = pl.BlockSpec(memory_space=pltpu.HBM)
    vmem = pl.BlockSpec(memory_space=pltpu.VMEM)
    params = pltpu.CompilerParams(vmem_limit_bytes=28 * 1024 * 1024)
    own, table, mask_fine, mask_coarse = (
        pltpu.with_memory_space_constraint(value, pltpu.HBM)
        for value in (own, jnp.asarray(table), mask_fine, mask_coarse))

    def cost(flops):
        return pl.CostEstimate(flops=flops, bytes_accessed=4 * 10**6, transcendentals=0)

    maps, own_kept, handed, *kept = pl.pallas_call(
        functools.partial(inner_kernel, inner_levels, cuts),
        out_shape=(
            jax.ShapeDtypeStruct((2, inner, 4 * inner_levels[0].quads, shifts), f32),
            jax.ShapeDtypeStruct(own.shape, bf16),
            jax.ShapeDtypeStruct(table.shape, bf16),
            *(jax.ShapeDtypeStruct((LANES, 8), f32) for _ in range(2)),
        ),
        in_specs=[hbm, vmem, vmem, hbm, hbm, hbm],
        out_specs=(vmem,) * 5,
        scratch_shapes=[
            pltpu.VMEM(mask_fine.shape, jnp.int32),
            pltpu.VMEM(mask_coarse.shape, jnp.int32),
            pltpu.VMEM((8, LANES), f32),
            pltpu.VMEM((8, LANES), f32),
            pltpu.VMEM((row_places(inner_levels)[1], 2 * strip_rows), bf16),
            *section_scratch(inner_levels, width, 3),
            *spec_scratch(inner_levels, 3),
            *pair_scratch(inner_levels),
            pltpu.SemaphoreType.DMA((5,)),
        ],
        compiler_params=params,
        cost_estimate=cost(3 * 10**9),
        name="inner_blocks",
    )(own, near, far, mask_fine, mask_coarse, table)
    own_specs = pl.pallas_call(
        functools.partial(own_kernel, outer_levels, row_at),
        out_shape=tuple(jax.ShapeDtypeStruct((level.rows, 2 * LANES), bf16) for level in outer_levels),
        in_specs=[vmem] * 3,
        out_specs=(vmem,) * 2,
        scratch_shapes=section_scratch(outer_levels, width, 1),
        compiler_params=params,
        cost_estimate=cost(2 * 10**9),
        name="own_outer_blocks",
    )(own_kept, rim, handed)
    return pl.pallas_call(
        functools.partial(outer_kernel, outer_levels, cuts, inner, row_at),
        out_shape=(
            jax.ShapeDtypeStruct((1, 2, fine, 4 * outer_levels[0].quads, shifts), f32),
            jax.ShapeDtypeStruct((1, 2, coarse, 4 * outer_levels[1].quads, shifts), f32),
        ),
        in_specs=[vmem] * 10,
        out_specs=(hbm, hbm),
        scratch_shapes=[
            *(pltpu.VMEM((2, level.blocks, 4 * level.quads, shifts), f32) for level in outer_levels),
            *section_scratch(outer_levels, width, 2),
            *spec_scratch(outer_levels, 2),
            *pair_scratch(outer_levels),
            pltpu.SemaphoreType.DMA((3,)),
        ],
        compiler_params=params,
        cost_estimate=cost(4 * 10**9),
        name="outer_blocks",
    )(near, far, rim_near, rim_far, handed, *own_specs, *kept, maps)


def local(sections, mask_fine, mask_coarse):
    far = from_device(sections, 2, 0)
    near = from_device(sections, 1, 0)
    rims = [from_device(sections, z, 1) for z in range(3)]
    return correlate(sections, near, far, *rims, mask_fine, mask_coarse)


def solution(mesh):
    in_specs = (
        P("sec", "strip", "groups"),
        P("sec", "strip", "groups"),
        P("sec", "strip", "groups"),
    )
    out_specs = (P("sec", None, "strip", "groups", None), P("sec", None, "strip", "groups", None))
    return jax.shard_map(local, mesh=mesh, in_specs=in_specs, out_specs=out_specs, check_vma=False)
```
